32 devices in a mesh: parts: 2 (over x), domain: 8 (over z, y), batch: 2 (over core).
Axes of the slice: x: 2, y: 2, z: 4, core: 2. Of those that a mesh axis runs over, the one named last changes fastest.
Arguments:
- positions: float32 [4, 3, 2048], P(('parts', 'batch'), None, 'domain'), parts along dimension 0, may hold values from 0 to 2
- features: float32 [4, 2048, 256], P(('parts', 'batch'), 'domain'), parts along dimension 0, may hold values from -6 to 6
- species: int32 [4, 2048], P(('parts', 'batch'), 'domain'), parts along dimension 0, may hold values from 0 to 3
- ref_forces: float32 [4, 3, 2048], P(('parts', 'batch'), None, 'domain'), parts along dimension 0, may hold values from -6 to 6
- centre_tile: int32 [4, 16], P(('parts', 'batch'), 'domain'), parts along dimension 0, may hold values from 0 to 3
- other_tile: int32 [4, 16], P(('parts', 'batch'), 'domain'), parts along dimension 0, may hold values from 0 to 7
- pair_live: int32 [4, 16], P(('parts', 'batch'), 'domain'), parts along dimension 0, may hold values 0 or 1
- send_tiles: int32 [4, 32], P(('parts', 'batch'), 'domain'), parts along dimension 0, may hold values from 0 to 3
- radial_w: float32 [8, 256], replicated, may hold values from -2 to 2
- mix_w: float32 [768, 256], replicated, may hold values from -0.21875 to 0.21875
- species_w: float32 [4, 256], replicated, may hold values from -6 to 6
- out_w: float32 [256], replicated, may hold values from -0.375 to 0.375
Outputs:
- forces: float32 [4, 3, 2048], P(('parts', 'batch'), None, 'domain'), parts along dimension 0
- grad_radial: float32 [16, 256], P('parts'), parts along dimension 0
- grad_mix: float32 [1536, 256], P('parts'), parts along dimension 0
- grad_species: float32 [8, 256], P('parts'), parts along dimension 0
- grad_out: float32 [512], P('parts'), parts along dimension 0
The draws below stay inside these ranges and needn't reach their ends.
There are 2 independent parts, one for each index of `parts`. The reference program is written for one: setup_inputs(seed, part) draws one part's arguments, and reference() takes and returns one part's arrays. A program takes and returns all parts, laid end to end along the dimension named above; an argument that names none is the same for every part. Nothing has to cross between parts.
All inputs are finite; a program needn't handle non-finite values. No bound on the sum of `pair_live` on one device may be relied on, other than what follows from the above.
Results may differ from the reference program's by a relative error of at most 0.0003.
Values sent between devices are 32-bit elements; how exact they have to be, the bound alone decides.
No kernel may reach another device: no remote copies, remote signals or barrier semaphores. Data moves between devices by JAX's collectives and lax.ppermute only.
A program may use at most 128 MiB of HBM per device.

```python
import math
import jax
import jax.numpy as jnp
from jax import lax

CH = 256
NB = 8
SPECIES = 4
TA = 64
SEND = 2
TILES_DEV = 4
PAIRS_DEV = 2
ATOMS = 2048
STRUCTS = 2
N_DOMAIN = 8


def touch_ends(array, rng, smallest, high):
    longest = array.shape.index(max(array.shape))
    spots = []
    for shift in (0, 1):
        where = [jax.random.randint(jax.random.fold_in(rng, axis), (), 0, length) for axis, length in enumerate(array.shape)]
        where[longest] = (where[longest] + shift) % array.shape[longest]
        spots.append(tuple(where))
    return array.at[spots[0]].set(smallest).at[spots[1]].set(high)


def shard_levels(stream_key, shape, cuts, least, high):
    loudness, own = 1.0, jax.random.fold_in(stream_key, 6)
    for axis_at, shards_of in cuts:
        steps = jnp.exp(jax.random.uniform(jax.random.fold_in(own, axis_at), (shards_of,), jnp.float32, least / len(cuts), high / len(cuts)))
        loudness = loudness * jnp.repeat(steps, shape[axis_at] // shards_of).reshape([-1 if axis == axis_at else 1 for axis in range(len(shape))])
    return loudness


def centred(own_key, shape, deviation, limit, shards=(), kind=jnp.bfloat16):
    loudness = shard_levels(own_key, shape, shards, -0.22, 0.18) if shards else 1.0
    values = jax.random.normal(own_key, shape, jnp.float32) * deviation * loudness
    return jnp.minimum(jnp.maximum(values, -limit), limit).astype(kind)


def setup_inputs(seed: int = 0, part: int = 0) -> dict:
    seeds = jax.random.split(jax.random.key(seed), 13)
    part_keys = jax.random.split(jax.random.fold_in(seeds[12], part), 13)
    return {
        "positions": jnp.clip(2.0 * jax.random.uniform(part_keys[0], (STRUCTS, 3, ATOMS), jnp.float32) ** shard_levels(part_keys[0], (STRUCTS, 3, ATOMS), ((0, 2), (2, 8)), -0.2, 0.2), 0.0, 2.0),
        "features": centred(part_keys[1], (STRUCTS, ATOMS, CH), 1.0, 6.0, ((0, 2), (1, 8)), jnp.float32),
        "species": touch_ends(jax.random.randint(part_keys[2], (STRUCTS, ATOMS), 0, SPECIES), jax.random.fold_in(part_keys[2], 1), 0, SPECIES - 1).astype(jnp.int32),
        "ref_forces": centred(part_keys[3], (STRUCTS, 3, ATOMS), 1.0, 6.0, ((0, 2), (2, 8)), jnp.float32),
        "centre_tile": touch_ends(jax.random.randint(part_keys[4], (STRUCTS, N_DOMAIN * PAIRS_DEV), 0, TILES_DEV), jax.random.fold_in(part_keys[4], 1), 0, TILES_DEV - 1).astype(jnp.int32),
        "other_tile": touch_ends(jax.random.randint(part_keys[5], (STRUCTS, N_DOMAIN * PAIRS_DEV), 0, TILES_DEV + 2 * SEND), jax.random.fold_in(part_keys[5], 1), 0, (TILES_DEV + 2 * SEND) - 1).astype(jnp.int32),
        "pair_live": touch_ends((jax.random.randint(part_keys[6], (STRUCTS, N_DOMAIN * PAIRS_DEV), 0, 4) < 3).astype(jnp.int32), jax.random.fold_in(part_keys[6], 1), 0, 1),
        "send_tiles": touch_ends(jax.random.randint(part_keys[7], (STRUCTS, N_DOMAIN * 2 * SEND), 0, TILES_DEV), jax.random.fold_in(part_keys[7], 1), 0, TILES_DEV - 1).astype(jnp.int32),
        "radial_w": centred(seeds[8], (NB, CH), NB ** -0.5, 2.0, (), jnp.float32),
        "mix_w": centred(seeds[9], (3 * CH, CH), (3 * CH) ** -0.5, 0.21875, (), jnp.float32),
        "species_w": centred(seeds[10], (SPECIES, CH), 1.0, 6.0, (), jnp.float32),
        "out_w": centred(seeds[11], (CH,), CH ** -0.5, 0.375, (), jnp.float32),
    }


cutoff = 2.5
soften = 0.25
env_scale = 0.25
precise = lax.Precision.HIGHEST

def harmonics(unit):
    along_x, along_y, along_z = (unit[0], unit[1], unit[2])
    root_three = math.sqrt(3.0)
    square_sum = along_x * along_x + along_y * along_y + along_z * along_z
    return jnp.stack([jnp.ones_like(along_x), along_x, along_y, along_z, root_three * along_x * along_y, root_three * along_y * along_z, root_three * along_z * along_x, 0.5 * root_three * (along_x * along_x - along_y * along_y), 0.5 * (3.0 * along_z * along_z - square_sum)], axis=0)

def pair_env(radial_w, centre_pos, other_pos, other_feat, weight_mask):
    offset = other_pos[:, None, :] - centre_pos[:, :, None]
    dist_sq = lax.optimization_barrier(jnp.sum(offset * offset, axis=0)) + soften
    distance = jnp.sqrt(dist_sq)
    angular = harmonics(offset / distance[None])
    smooth = jnp.maximum(1.0 - dist_sq / (cutoff * cutoff), 0.0) ** 3 * weight_mask
    basis_count = radial_w.shape[0]
    orders = jnp.arange(1, basis_count + 1).astype(jnp.float32)
    radial = jnp.sin(orders[:, None, None] * (math.pi / cutoff) * distance[None]) / distance[None] * smooth[None]
    atom_count = centre_pos.shape[1]
    pair_table = jnp.transpose(angular, (1, 0, 2))[:, :, None, :] * jnp.transpose(radial, (1, 0, 2))[:, None, :, :]
    pair_table = pair_table.reshape(atom_count * 9, basis_count * atom_count)
    mixed_feat = (radial_w[:, None, :] * other_feat[None, :, :]).reshape(basis_count * atom_count, radial_w.shape[1])
    return jnp.dot(pair_table, mixed_feat, precision=precise).reshape(atom_count, 9, radial_w.shape[1])

def local_energy(params, buf_pos, buf_feat, species_onehot, centre, other_slots, live_slots):
    radial_w, mix_w, species_w, out_w = params
    atom_count = buf_pos.shape[2]
    n_local = species_onehot.shape[0] // atom_count
    margin = (buf_pos.shape[0] - n_local) // 2
    identity = jnp.eye(atom_count, dtype=jnp.float32)

    def one_pair(centre_slot, other_slot, pair_alive):
        centre_pos = buf_pos[margin + centre_slot]
        other_pos = buf_pos[other_slot]
        other_feat = buf_feat[other_slot]
        same_tile = (other_slot == margin + centre_slot).astype(jnp.float32)
        weight_mask = pair_alive.astype(jnp.float32) * (1.0 - same_tile * identity)
        return pair_env(radial_w, centre_pos, other_pos, other_feat, weight_mask)
    per_pair = jax.vmap(one_pair)(centre, other_slots, live_slots)
    owner_map = (centre[:, None] == jnp.arange(n_local, dtype=jnp.int32)[None, :]).astype(jnp.float32)
    environ = jnp.einsum('pt,pamc->tamc', owner_map, per_pair, precision=precise) * env_scale
    squares = environ * environ
    channels = environ.shape[3]
    invariants = jnp.concatenate([squares[:, :, 0], lax.optimization_barrier(jnp.sum(squares[:, :, 1:4], axis=2)), lax.optimization_barrier(jnp.sum(squares[:, :, 4:9], axis=2))], axis=-1).reshape(n_local * atom_count, 3 * channels)
    hidden = jnp.dot(invariants, mix_w, precision=precise) + jnp.dot(species_onehot, species_w, precision=precise)
    return jnp.sum(jnp.dot(jax.nn.silu(hidden), out_w, precision=precise))

def position_grad(params, buf_pos, buf_feat, species_onehot, centre, other_slots, live_slots):
    return jax.grad(local_energy, argnums=1)(params, buf_pos, buf_feat, species_onehot, centre, other_slots, live_slots)

def reference(positions, features, species, ref_forces, centre_tile, other_tile, pair_live, send_tiles, radial_w, mix_w, species_w, out_w):
    params = (radial_w, mix_w, species_w, out_w)
    loss_scale = 1.0 / math.sqrt(3.0 * ATOMS * STRUCTS)
    all_tiles = N_DOMAIN * TILES_DEV
    devices = jnp.arange(N_DOMAIN, dtype=jnp.int32)
    lower_dev = (devices - 1) % N_DOMAIN
    upper_dev = (devices + 1) % N_DOMAIN
    forces_all = []
    grad_total = tuple((jnp.zeros_like(weight) for weight in params))
    for struct in range(STRUCTS):
        tile_pos = positions[struct].reshape(3, all_tiles, TA).transpose(1, 0, 2)
        tile_feat = features[struct].reshape(all_tiles, TA, CH)
        sent_list = send_tiles[struct].reshape(N_DOMAIN, 2 * SEND)
        from_lower = sent_list[lower_dev][:, SEND:] + lower_dev[:, None] * TILES_DEV
        from_upper = sent_list[upper_dev][:, :SEND] + upper_dev[:, None] * TILES_DEV
        owned_tiles = devices[:, None] * TILES_DEV + jnp.arange(TILES_DEV, dtype=jnp.int32)[None, :]
        buffer_index = jnp.concatenate([from_lower, owned_tiles, from_upper], axis=1).astype(jnp.int32)
        centres = centre_tile[struct].reshape(N_DOMAIN, PAIRS_DEV)
        others = other_tile[struct].reshape(N_DOMAIN, PAIRS_DEV)
        lives = pair_live[struct].reshape(N_DOMAIN, PAIRS_DEV)
        onehots = (species[struct].reshape(N_DOMAIN, TILES_DEV * TA)[:, :, None] == jnp.arange(SPECIES, dtype=jnp.int32)[None, None, :]).astype(jnp.float32)
        packed_items = (buffer_index, centres, others, lives, onehots)

        def forward(item_set):
            tile_index, centre, other_slots, live_slots, onehot = item_set
            return position_grad(params, tile_pos[tile_index], tile_feat[tile_index], onehot, centre, other_slots, live_slots)
        pos_grads = lax.map(forward, packed_items)
        summed = jnp.zeros((all_tiles, 3, TA), jnp.float32).at[buffer_index.reshape(-1)].add(pos_grads.reshape(-1, 3, TA))
        forces = -summed
        force_error = forces - ref_forces[struct].reshape(3, all_tiles, TA).transpose(1, 0, 2)

        def backward(item_set):
            tile_index, centre, other_slots, live_slots, onehot = item_set

            def through(param_set):
                return position_grad(param_set, tile_pos[tile_index], tile_feat[tile_index], onehot, centre, other_slots, live_slots)
            unused, pullback = jax.vjp(through, params)
            return pullback(-2.0 * loss_scale * force_error[tile_index])[0]
        per_device = lax.map(backward, packed_items)
        grad_total = tuple((accum + lax.optimization_barrier(jnp.sum(member, axis=0)) for accum, member in zip(grad_total, per_device)))
        forces_all.append(forces.transpose(1, 0, 2).reshape(3, ATOMS))
    return (jnp.stack(forces_all), grad_total[0], grad_total[1], grad_total[2], grad_total[3])
```

```python
import math

import jax
import jax.numpy as jnp
from jax import lax
from jax.experimental import pallas as pl
from jax.experimental.pallas import tpu as pltpu
from jax.sharding import PartitionSpec as P

TA = 64
SEND = 2
PAIRS = 2
COMPS = 9
BASIS = 8
SPECIES = 4
CHUNK = 2 * TA

cutoff = 2.5
soften = 0.25
env_scale = 0.25
root_three = math.sqrt(3.0)
F32 = jnp.float32
BF16 = jnp.bfloat16
NN = (((1,), (0,)), ((), ()))
NT = (((1,), (1,)), ((), ()))
TN = (((0,), (0,)), ((), ()))
GROUP = (0, 1, 1, 1, 2, 2, 2, 2, 2)


def split(value):
    high = value.astype(BF16)
    return high, (value - high.astype(F32)).astype(BF16)


def product(left, right, dims):
    (lh, ll), (rh, rl) = left, right

    def one(x, y):
        return lax.dot_general(x, y, dims, preferred_element_type=F32)

    return one(lh, rh) + (one(lh, rl) + one(ll, rh))


def flag(condition):
    return jnp.where(condition, 1.0, 0.0).astype(F32)


def lane_half():
    lane = lax.broadcasted_iota(jnp.int32, (1, CHUNK), 1)
    low = flag(lane < TA)
    return low, 1.0 - low


def twice(chunk, half):
    low, high = lane_half()
    swapped = pltpu.roll(chunk, TA, 1)
    return chunk * low + swapped * high if half == 0 else swapped * low + chunk * high


def pick(chunks, position):
    total = None
    for q, chunk in enumerate(chunks):
        for half in range(2):
            term = twice(chunk, half) * flag(position == 2 * q + half)
            total = term if total is None else total + term
    return total


def paired(first, second):
    low, high = lane_half()
    return first * low + second * high


def chunk_mask(position, q):
    low, high = lane_half()
    return low * flag(position == 2 * q) + high * flag(position == 2 * q + 1)


def geometry(lane_rows, columns, sign, live, same):
    offset = [(row - column) * sign for row, column in zip(lane_rows, columns)]
    dist_sq = offset[0] * offset[0] + offset[1] * offset[1] + offset[2] * offset[2] + soften
    distance = jnp.sqrt(dist_sq)
    inverse = 1.0 / distance
    unit = [x * inverse for x in offset]
    row = lax.broadcasted_iota(jnp.int32, (TA, CHUNK), 0)
    lane = lax.broadcasted_iota(jnp.int32, (TA, CHUNK), 1)
    lane = jnp.where(lane >= TA, lane - TA, lane)
    mask = live * (1.0 - same * flag(row == lane))
    base = jnp.maximum(1.0 - dist_sq * (1.0 / (cutoff * cutoff)), 0.0)
    weight = base * base * base * mask * inverse
    slope = -(6.0 / (cutoff * cutoff)) * base * base * mask - weight * inverse
    angle = distance * (math.pi / cutoff)
    return unit, inverse, weight, slope, jnp.sin(angle), jnp.cos(angle)


def harmonics(v):
    x, y, z = v
    return [
        None,
        x,
        y,
        z,
        root_three * x * y,
        root_three * y * z,
        root_three * z * x,
        0.5 * root_three * (x * x - y * y),
        z * z - 0.5 * (x * x + y * y),
    ]


def harmonics_tangent(v, t):
    x, y, z = v
    a, b, c = t
    return [
        None,
        a,
        b,
        c,
        root_three * (a * y + x * b),
        root_three * (b * z + y * c),
        root_three * (c * x + z * a),
        root_three * (x * a - y * b),
        2.0 * z * c - (x * a + y * b),
    ]


def paired_orders(sine, cosine, weight, slope):
    low, high = lane_half()
    double_s, double_c = 2.0 * sine * cosine, 1.0 - 2.0 * sine * sine
    now_s = sine * low + double_s * high
    now_c = cosine * low + double_c * high
    old_s = -sine * low
    old_c = cosine * low + high
    values, slopes = [], []
    for k in range(BASIS // 2):
        order = ((2 * k + 1) * low + (2 * k + 2) * high) * (math.pi / cutoff)
        values.append(now_s * weight)
        slopes.append(now_c * (weight * order) + now_s * slope)
        now_s, old_s = 2.0 * double_c * now_s - old_s, now_s
        now_c, old_c = 2.0 * double_c * now_c - old_c, now_c
    return values, slopes


def single_orders(sine, cosine, weight, slope):
    now_s, now_c = sine, cosine
    old_s, old_c = jnp.zeros_like(sine), jnp.ones_like(cosine)
    values, slopes = [], []
    for n in range(1, BASIS + 1):
        values.append(now_s * weight)
        slopes.append(now_c * (weight * (n * math.pi / cutoff)) + now_s * slope)
        now_s, old_s = 2.0 * cosine * now_s - old_s, now_s
        now_c, old_c = 2.0 * cosine * now_c - old_c, now_c
    return values, slopes


def columns_of(rows, square, turned):
    square[...] = jnp.zeros_like(square)
    square[0 : rows.shape[0], :] = rows
    turned[...] = square[...].T


def pair_rows(first, p):
    return twice(first, p)


def radial_feat(feat, radial, p, high_ref, low_ref):
    own = feat[p * TA : (p + 1) * TA, :]
    for n in range(BASIS):
        hi, lo = split(own * radial[n : n + 1, :])
        high_ref[n * TA : (n + 1) * TA, :] = hi
        low_ref[n * TA : (n + 1) * TA, :] = lo


def gather_kernel(send, pos, feat, ref, to_low, to_high):
    position = [pos[0, :, q * CHUNK : (q + 1) * CHUNK] for q in range(2)]
    error = [ref[0, :, q * CHUNK : (q + 1) * CHUNK] for q in range(2)]
    low, high = lane_half()
    for out, first in ((to_low, 0), (to_high, SEND)):
        tiles = [send[0, first + j] for j in range(SEND)]
        for j in range(SEND):
            start = pl.multiple_of(tiles[j] * TA, TA)
            out[j * TA : (j + 1) * TA, :] = feat[0, pl.ds(start, TA), :]
        out[SEND * TA :, :] = jnp.zeros((16, out.shape[1]), F32)
        out[SEND * TA : SEND * TA + 3, 0:CHUNK] = paired(
            pick(position, tiles[0]), pick(position, tiles[1])
        )
        out[SEND * TA : SEND * TA + 3, CHUNK:] = paired(pick(error, tiles[0]), pick(error, tiles[1]))
        for other in range(2 * SEND):
            same = low * flag(send[0, other] == tiles[0]) + high * flag(send[0, other] == tiles[1])
            out[SEND * TA + 8 + other : SEND * TA + 9 + other, 0:CHUNK] = same


def force_kernel(
    centre, other, live, send, pos, feat, species, from_low, from_high, radial_w, mix_w, species_w, out_w,
    env, dinv, gate, curve, inv, rows, fsel, own, to_high, to_low,
    square, turned, th, tl, xh, xl, raw, mh, ml,
):
    ghost = SEND * TA
    chunks = [
        from_low[ghost : ghost + 3, 0:CHUNK],
        pos[0, :, 0:CHUNK],
        pos[0, :, CHUNK:],
        from_high[ghost : ghost + 3, 0:CHUNK],
    ]
    kinds = [species[:, q * CHUNK : (q + 1) * CHUNK].astype(F32) for q in range(2)]
    centres = [centre[0, p] for p in range(PAIRS)]
    others = [other[0, p] for p in range(PAIRS)]
    sames = [flag(others[p] == centres[p] + SEND) for p in range(PAIRS)]
    shared = flag(centres[0] == centres[1])
    rows[...] = jnp.zeros_like(rows)
    rows[0:3, :] = paired(*(pick(chunks, others[p]) for p in range(PAIRS)))
    rows[3:6, :] = paired(*(pick(chunks[1:3], centres[p]) for p in range(PAIRS)))
    rows[6:7, :] = paired(*(pick(kinds, centres[p]) for p in range(PAIRS)))
    columns_of(rows[...], square, turned)

    for p in range(PAIRS):
        o = others[p]
        below = pl.multiple_of(jnp.clip(o, 0, 1) * TA, TA)
        inside = pl.multiple_of(jnp.clip(o - SEND, 0, 3) * TA, TA)
        above = pl.multiple_of(jnp.clip(o - SEND - 4, 0, 1) * TA, TA)
        fsel[p * TA : (p + 1) * TA, :] = (
            from_low[pl.ds(below, TA), :] * flag(o < SEND)
            + feat[0, pl.ds(inside, TA), :] * flag((o >= SEND) & (o < SEND + 4))
            + from_high[pl.ds(above, TA), :] * flag(o >= SEND + 4)
        )

    shapes = []
    for p in range(PAIRS):
        lane_rows = [twice(rows[i : i + 1, :], p) for i in range(3)]
        columns = [turned[p * TA : (p + 1) * TA, 3 + i : 4 + i] for i in range(3)]
        unit, inverse, weight, slope, sine, cosine = geometry(
            lane_rows, columns, 1.0, live[0, p].astype(F32), sames[p]
        )
        angular = harmonics(unit)
        values, slopes = paired_orders(sine, cosine, weight, slope)
        shapes.append((unit, inverse, angular, values, slopes))
        for m in range(COMPS):
            for k in range(BASIS // 2):
                entry = values[k] if m == 0 else angular[m] * values[k]
                hi, lo = split(entry)
                th[m * TA : (m + 1) * TA, k * CHUNK : (k + 1) * CHUNK] = hi
                tl[m * TA : (m + 1) * TA, k * CHUNK : (k + 1) * CHUNK] = lo
        radial_feat(fsel, radial_w, p, xh.at[p], xl.at[p])
        raw[p * COMPS * TA : (p + 1) * COMPS * TA, 0:256] = product(
            (th[...], tl[...]), (xh[p], xl[p]), NN
        )

    for m in range(COMPS):
        first = raw[m * TA : (m + 1) * TA, 0:256]
        second = raw[(COMPS + m) * TA : (COMPS + m + 1) * TA, 0:256]
        env[m * TA : (m + 1) * TA, :] = env_scale * (first + shared * second)
        env[(COMPS + m) * TA : (COMPS + m + 1) * TA, :] = env_scale * (second + shared * first)
    for p in range(PAIRS):
        sums = [None] * 3
        for m in range(COMPS):
            block = env[(p * COMPS + m) * TA : (p * COMPS + m + 1) * TA, :]
            sums[GROUP[m]] = block * block if sums[GROUP[m]] is None else sums[GROUP[m]] + block * block
        for g in range(3):
            inv[p * TA : (p + 1) * TA, g * 256 : (g + 1) * 256] = sums[g]
    hi, lo = split(mix_w[...])
    mh[...] = hi
    ml[...] = lo
    hidden = product(split(inv[...]), (mh[...], ml[...]), NN)
    kind = turned[:, 6:7]
    for s in range(species_w.shape[0]):
        hidden = hidden + flag(kind == float(s)) * species_w[s : s + 1, :]
    sigma = 1.0 / (1.0 + jnp.exp(-hidden))
    first_order = sigma * (1.0 + hidden * (1.0 - sigma))
    gate[...] = first_order
    curve[...] = sigma * (1.0 - sigma) * (2.0 + hidden * (1.0 - 2.0 * sigma)) * out_w[...]
    dinv[...] = product(split(first_order * out_w[...]), (mh[...], ml[...]), NT)

    grads_low = [jnp.zeros((3, CHUNK), F32) for _ in range(4)]
    low, high = lane_half()
    for p in range(PAIRS):
        unit, inverse, angular, values, slopes = shapes[p]
        for m in range(COMPS):
            block = env[(p * COMPS + m) * TA : (p * COMPS + m + 1) * TA, :]
            part = dinv[p * TA : (p + 1) * TA, GROUP[m] * 256 : (GROUP[m] + 1) * 256]
            hi, lo = split((2.0 * env_scale) * block * part)
            th[m * TA : (m + 1) * TA, 0:256] = hi
            tl[m * TA : (m + 1) * TA, 0:256] = lo
        raw[0 : COMPS * TA, :] = product((th[:, 0:256], tl[:, 0:256]), (xh[p], xl[p]), NT)
        d_radius = None
        d_angular = []
        for m in range(COMPS):
            along, across = None, None
            for k in range(BASIS // 2):
                block = raw[m * TA : (m + 1) * TA, k * CHUNK : (k + 1) * CHUNK]
                along = block * slopes[k] if along is None else along + block * slopes[k]
                across = block * values[k] if across is None else across + block * values[k]
            d_angular.append(across)
            term = along if m == 0 else along * angular[m]
            d_radius = term if d_radius is None else d_radius + term
        x, y, z = unit
        g = d_angular
        toward = [
            g[1] + root_three * (y * g[4] + z * g[6] + x * g[7]) - x * g[8],
            g[2] + root_three * (x * g[4] + z * g[5] - y * g[7]) - y * g[8],
            g[3] + root_three * (y * g[5] + x * g[6]) + 2.0 * (z * g[8]),
        ]
        radial_part = d_radius - inverse * (toward[0] * x + toward[1] * y + toward[2] * z)
        other_rows, centre_rows = [], []
        for i in range(3):
            d_offset = inverse * toward[i] + unit[i] * radial_part
            summed = jnp.sum(d_offset, axis=0, keepdims=True)
            other_rows.append(summed + pltpu.roll(summed, TA, 1))
            square[0:TA, :] = d_offset
            square[TA:, :] = d_offset
            centre_rows.append(-jnp.sum(square[...].T, axis=0, keepdims=True))
        for i in range(3):
            for q in range(4):
                at = chunk_mask(others[p], q) * other_rows[i]
                if q in (1, 2):
                    at = at + chunk_mask(centres[p] + SEND, q) * centre_rows[i]
                grads_low[q] = grads_low[q] + at * flag(
                    lax.broadcasted_iota(jnp.int32, (3, CHUNK), 0) == i
                )
    own[...] = jnp.zeros_like(own)
    own[0:3, 0:CHUNK] = grads_low[1]
    own[0:3, CHUNK:] = grads_low[2]
    own[3:6, 0:CHUNK] = grads_low[0]
    own[3:6, CHUNK:] = grads_low[3]
    for out, first, ghost_grad in ((to_low, 0, grads_low[0]), (to_high, SEND, grads_low[3])):
        out[...] = jnp.zeros_like(out)
        out[0:3, :] = paired(*(pick(grads_low[1:3], send[0, first + j]) for j in range(SEND)))
        out[3:6, :] = ghost_grad


def tangent_kernel(
    scale, centre, other, live, send, ref, from_low, from_high, own, low_one, low_two, high_one, high_two,
    rows, fsel, env, dinv, gate, curve, inv, radial_w, mix_w, out_w,
    forces, grad_mix, small, envdot, curl, both,
    square, turned, th, tl, xh, xl, raw, left, right,
):
    ghost = SEND * TA
    low, high = lane_half()
    centres = [centre[0, p] for p in range(PAIRS)]
    others = [other[0, p] for p in range(PAIRS)]
    sames = [flag(others[p] == centres[p] + SEND) for p in range(PAIRS)]
    shared = flag(centres[0] == centres[1])
    mine = [own[0:3, 0:CHUNK], own[0:3, CHUNK:]]
    arrived = [twice(low_one[3:6, :], j) for j in range(SEND)]
    arrived += [twice(high_one[3:6, :], j) for j in range(SEND)]
    for j in range(2 * SEND):
        for q in range(2):
            mine[q] = mine[q] + chunk_mask(send[0, j], q) * arrived[j]
    below = low_one[0:3, :]
    above = high_one[0:3, :]
    to_below = [twice(low_two[3:6, :], j) for j in range(SEND)]
    to_below += [twice(own[3:6, 0:CHUNK], j) for j in range(SEND)]
    to_above = [twice(own[3:6, CHUNK:], j) for j in range(SEND)]
    to_above += [twice(high_two[3:6, :], j) for j in range(SEND)]
    for j in range(2 * SEND):
        below = below + from_low[ghost + 8 + j : ghost + 9 + j, 0:CHUNK] * to_below[j]
        above = above + from_high[ghost + 8 + j : ghost + 9 + j, 0:CHUNK] * to_above[j]
    for q in range(2):
        forces[0, :, q * CHUNK : (q + 1) * CHUNK] = -mine[q]
    error = [
        below + from_low[ghost : ghost + 3, CHUNK:],
        mine[0] + ref[0, :, 0:CHUNK],
        mine[1] + ref[0, :, CHUNK:],
        above + from_high[ghost : ghost + 3, CHUNK:],
    ]
    error = [part * scale[0] for part in error]
    both[...] = jnp.zeros_like(both)
    both[0:8, :] = rows[...]
    both[8:11, :] = paired(*(pick(error, others[p]) for p in range(PAIRS)))
    both[11:14, :] = paired(*(pick(error[1:3], centres[p]) for p in range(PAIRS)))
    columns_of(both[...], square, turned)

    for p in range(PAIRS):
        lane_rows = [twice(both[i : i + 1, :], p) for i in range(3)]
        lane_move = [twice(both[8 + i : 9 + i, :], p) for i in range(3)]
        columns = [turned[p * TA : (p + 1) * TA, 3 + i : 4 + i] for i in range(3)]
        column_move = [turned[p * TA : (p + 1) * TA, 11 + i : 12 + i] for i in range(3)]
        unit, inverse, weight, slope, sine, cosine = geometry(
            lane_rows, columns, 1.0, live[0, p].astype(F32), sames[p]
        )
        move = [a - b for a, b in zip(lane_move, column_move)]
        stretch = unit[0] * move[0] + unit[1] * move[1] + unit[2] * move[2]
        turn = [(m - v * stretch) * inverse for m, v in zip(move, unit)]
        angular, turning = harmonics(unit), harmonics_tangent(unit, turn)
        values, slopes = paired_orders(sine, cosine, weight, slope)
        slopes = [s * stretch for s in slopes]
        for m in range(COMPS):
            for k in range(BASIS // 2):
                entry = slopes[k] if m == 0 else angular[m] * slopes[k] + turning[m] * values[k]
                hi, lo = split(entry)
                th[m * TA : (m + 1) * TA, k * CHUNK : (k + 1) * CHUNK] = hi
                tl[m * TA : (m + 1) * TA, k * CHUNK : (k + 1) * CHUNK] = lo
        radial_feat(fsel, radial_w, p, xh, xl)
        raw[p * COMPS * TA : (p + 1) * COMPS * TA, :] = product((th[...], tl[...]), (xh[...], xl[...]), NN)

    for m in range(COMPS):
        first = raw[m * TA : (m + 1) * TA, :]
        second = raw[(COMPS + m) * TA : (COMPS + m + 1) * TA, :]
        envdot[m * TA : (m + 1) * TA, :] = env_scale * (first + shared * second)
        envdot[(COMPS + m) * TA : (COMPS + m + 1) * TA, :] = env_scale * (second + shared * first)
    invdot = left
    half = PAIRS * TA
    for p in range(PAIRS):
        sums = [None] * 3
        for m in range(COMPS):
            at = slice((p * COMPS + m) * TA, (p * COMPS + m + 1) * TA)
            term = 2.0 * env[at, :] * envdot[at, :]
            sums[GROUP[m]] = term if sums[GROUP[m]] is None else sums[GROUP[m]] + term
        for g in range(3):
            invdot[half + p * TA : half + (p + 1) * TA, g * 256 : (g + 1) * 256] = sums[g]
    invdot[0:half, :] = inv[...]
    hidden_move = product(split(invdot[half:, :]), split(mix_w[...]), NN)
    bend = curve[...] * hidden_move
    curl[...] = bend
    once = 1.0 - shared * flag(lax.broadcasted_iota(jnp.int32, (half, 1), 0) >= TA)
    right[0:half, :] = bend * once
    right[half:, :] = gate[...] * out_w[...] * once
    grad_mix[...] = product(split(left[...]), split(right[...]), TN)
    small[...] = jnp.zeros_like(small)
    kind = turned[:, 6:7]
    for s in range(SPECIES):
        small[s : s + 1, :] = jnp.sum(right[0:half, :] * flag(kind == float(s)), axis=0, keepdims=True)
    small[SPECIES : SPECIES + 1, :] = jnp.sum(gate[...] * hidden_move * once, axis=0, keepdims=True)


def radial_kernel(
    centre, other, live, both, fsel, env, envdot, dinv, curl, mix_w,
    grad_radial,
    square, turned, lh, ll, gh, gl, turn_inv, raw,
):
    centres = [centre[0, p] for p in range(PAIRS)]
    others = [other[0, p] for p in range(PAIRS)]
    sames = [flag(others[p] == centres[p] + SEND) for p in range(PAIRS)]
    low, high = lane_half()
    columns_of(both[...], square, turned)
    turn_inv[...] = product(split(curl[...]), split(mix_w[...]), NT)
    total = [None] * BASIS
    for p in range(PAIRS):
        lane_rows = [twice(both[3 + i : 4 + i, :], p) for i in range(3)]
        lane_move = [twice(both[11 + i : 12 + i, :], p) for i in range(3)]
        columns = [turned[p * TA : (p + 1) * TA, i : i + 1] for i in range(3)]
        column_move = [turned[p * TA : (p + 1) * TA, 8 + i : 9 + i] for i in range(3)]
        unit, inverse, weight, slope, sine, cosine = geometry(
            lane_rows, columns, -1.0, live[0, p].astype(F32), sames[p]
        )
        move = [b - a for a, b in zip(lane_move, column_move)]
        stretch = unit[0] * move[0] + unit[1] * move[1] + unit[2] * move[2]
        turn = [(m - v * stretch) * inverse for m, v in zip(move, unit)]
        angular, turning = harmonics(unit), harmonics_tangent(unit, turn)
        values, slopes = single_orders(sine, cosine, weight, slope)
        for m in range(COMPS):
            if m == 0:
                on_value, on_slope = low, high * stretch
            else:
                on_value = angular[m] * low + turning[m] * high
                on_slope = angular[m] * high * stretch
            for n in range(BASIS):
                hi, lo = split(on_value * values[n] + on_slope * slopes[n])
                lh[n * TA : (n + 1) * TA, m * CHUNK : (m + 1) * CHUNK] = hi
                ll[n * TA : (n + 1) * TA, m * CHUNK : (m + 1) * CHUNK] = lo
            at = slice((p * COMPS + m) * TA, (p * COMPS + m + 1) * TA)
            group = slice(GROUP[m] * 256, (GROUP[m] + 1) * 256)
            here = slice(p * TA, (p + 1) * TA)
            steady = (2.0 * env_scale) * dinv[here, group]
            bent = (2.0 * env_scale) * turn_inv[here, group]
            hi, lo = split(env[at, :] * bent + envdot[at, :] * steady)
            gh[m * CHUNK : m * CHUNK + TA, :] = hi
            gl[m * CHUNK : m * CHUNK + TA, :] = lo
            hi, lo = split(env[at, :] * steady)
            gh[m * CHUNK + TA : (m + 1) * CHUNK, :] = hi
            gl[m * CHUNK + TA : (m + 1) * CHUNK, :] = lo
        raw[...] = product((lh[...], ll[...]), (gh[...], gl[...]), NN)
        for n in range(BASIS):
            term = jnp.sum(
                raw[n * TA : (n + 1) * TA, :] * fsel[p * TA : (p + 1) * TA, :], axis=0, keepdims=True
            )
            total[n] = term if total[n] is None else total[n] + term
    for n in range(BASIS):
        grad_radial[n : n + 1, :] = total[n]


def vmem():
    return pl.BlockSpec(memory_space=pltpu.VMEM)


def smem():
    return pl.BlockSpec(memory_space=pltpu.SMEM)


def call(kernel, name, outs, scratch, scalars, *operands, flops=0):
    return pl.pallas_call(
        kernel,
        name=name,
        out_shape=[jax.ShapeDtypeStruct(shape, F32) for shape in outs],
        in_specs=[smem()] * scalars + [vmem()] * (len(operands) - scalars),
        out_specs=[vmem()] * len(outs),
        scratch_shapes=[pltpu.VMEM(shape, kind) for shape, kind in scratch],
        compiler_params=pltpu.CompilerParams(vmem_limit_bytes=48 * 1024 * 1024),
        cost_estimate=pl.CostEstimate(flops=flops, bytes_accessed=1 << 20, transcendentals=0),
    )(*operands)


def shifted(block, axis, by):
    count = lax.axis_size(axis)
    return lax.ppermute(block, axis, [(i, (i + by) % count) for i in range(count)])


def on_device(
    positions,
    features,
    species,
    ref_forces,
    centre_tile,
    other_tile,
    pair_live,
    send_tiles,
    radial_w,
    mix_w,
    species_w,
    out_w,
):
    atoms = positions.shape[2]
    channels = features.shape[2]
    table = (COMPS * TA, BASIS * TA)
    sent = (SEND * TA + 16, channels)
    slots = PAIRS * TA
    turning = [((CHUNK, CHUNK), F32)] * 2
    out_row = out_w.reshape(1, channels)

    to_low, to_high = call(
        gather_kernel, "gather", [sent, sent], [], 1, send_tiles, positions, features, ref_forces
    )
    from_low = shifted(to_high, "domain", 1)
    from_high = shifted(to_low, "domain", -1)

    env, dinv, gate, curve, inv, rows, fsel, own, grads_up, grads_down = call(
        force_kernel,
        "force",
        [
            (PAIRS * COMPS * TA, channels),
            (slots, 3 * channels),
            (slots, channels),
            (slots, channels),
            (slots, 3 * channels),
            (8, CHUNK),
            (slots, channels),
            (8, atoms),
            (8, CHUNK),
            (8, CHUNK),
        ],
        turning
        + [(table, BF16)] * 2
        + [((PAIRS, BASIS * TA, channels), BF16)] * 2
        + [((PAIRS * COMPS * TA, BASIS * TA), F32)]
        + [((3 * channels, channels), BF16)] * 2,
        4,
        centre_tile, other_tile, pair_live, send_tiles,
        positions, features, species, from_low, from_high, radial_w, mix_w, species_w, out_row,
        flops=1 << 31,
    )
    low_one = shifted(grads_up, "domain", 1)
    low_two = shifted(grads_up, "domain", 2)
    high_one = shifted(grads_down, "domain", -1)
    high_two = shifted(grads_down, "domain", -2)

    total_count = 3.0 * atoms * lax.axis_size("domain") * lax.axis_size("batch")
    scale = jnp.full((1,), 2.0 / math.sqrt(total_count), F32)
    forces, grad_mix, small, envdot, curl, both = call(
        tangent_kernel,
        "tangent",
        [
            (1, 3, atoms),
            (3 * channels, channels),
            (8, channels),
            (PAIRS * COMPS * TA, channels),
            (slots, channels),
            (16, CHUNK),
        ],
        turning
        + [(table, BF16)] * 2
        + [((BASIS * TA, channels), BF16)] * 2
        + [((PAIRS * COMPS * TA, channels), F32)]
        + [((2 * slots, 3 * channels), F32), ((2 * slots, channels), F32)],
        5,
        scale, centre_tile, other_tile, pair_live, send_tiles,
        ref_forces, from_low, from_high, own, low_one, low_two, high_one, high_two,
        rows, fsel, env, dinv, gate, curve, inv, radial_w, mix_w, out_row,
        flops=1 << 31,
    )
    (grad_radial,) = call(
        radial_kernel,
        "radial",
        [(BASIS, channels)],
        turning
        + [((BASIS * TA, COMPS * CHUNK), BF16)] * 2
        + [((COMPS * CHUNK, channels), BF16)] * 2
        + [((slots, 3 * channels), F32), ((BASIS * TA, channels), F32)],
        3,
        centre_tile, other_tile, pair_live,
        both, fsel, env, envdot, dinv, curl, mix_w,
        flops=1 << 31,
    )
    packed = jnp.concatenate([grad_mix, grad_radial, small], axis=0)
    packed = lax.psum(packed, ("domain", "batch"))
    rows_mix = 3 * channels
    return (
        forces,
        packed[rows_mix : rows_mix + BASIS],
        packed[:rows_mix],
        packed[rows_mix + BASIS : rows_mix + BASIS + SPECIES],
        packed[rows_mix + BASIS + SPECIES],
    )


def solution(mesh):
    return jax.shard_map(
        on_device,
        mesh=mesh,
        in_specs=(
            P(("parts", "batch"), None, "domain"),
            P(("parts", "batch"), "domain", None),
            P(("parts", "batch"), "domain"),
            P(("parts", "batch"), None, "domain"),
            P(("parts", "batch"), "domain"),
            P(("parts", "batch"), "domain"),
            P(("parts", "batch"), "domain"),
            P(("parts", "batch"), "domain"),
            P(),
            P(),
            P(),
            P(),
        ),
        out_specs=(
            P(("parts", "batch"), None, "domain"),
            P("parts", None),
            P("parts", None),
            P("parts", None),
            P("parts"),
        ),
        check_vma=False,
    )
```

```python
import math

import jax
import jax.numpy as jnp
from jax import lax
from jax.experimental import pallas as pl
from jax.experimental.pallas import tpu as pltpu
from jax.sharding import PartitionSpec as P

TA = 64
SEND = 2
PAIRS = 2
COMPS = 9
BASIS = 8
SPECIES = 4
HALF = 128
CHUNK = 2 * TA

cutoff = 2.5
soften = 0.25
env_scale = 0.25
root_three = math.sqrt(3.0)
F32 = jnp.float32
BF16 = jnp.bfloat16
NN = (((1,), (0,)), ((), ()))
NT = (((1,), (1,)), ((), ()))
TN = (((0,), (0,)), ((), ()))
GROUP = (0, 1, 1, 1, 2, 2, 2, 2, 2)


def split(value):
    high = value.astype(BF16)
    return high, (value - high.astype(F32)).astype(BF16)


def product(left, right, dims):
    (lh, ll), (rh, rl) = left, right

    def one(x, y):
        return lax.dot_general(x, y, dims, preferred_element_type=F32)

    return one(lh, rh) + (one(lh, rl) + one(ll, rh))


def flag(condition):
    return jnp.where(condition, 1.0, 0.0).astype(F32)


def lane_half():
    lane = lax.broadcasted_iota(jnp.int32, (1, CHUNK), 1)
    low = flag(lane < TA)
    return low, 1.0 - low


def twice(chunk, half):
    low, high = lane_half()
    swapped = pltpu.roll(chunk, TA, 1)
    return chunk * low + swapped * high if half == 0 else swapped * low + chunk * high


def pick(chunks, position):
    total = None
    for q, chunk in enumerate(chunks):
        for half in range(2):
            term = twice(chunk, half) * flag(position == 2 * q + half)
            total = term if total is None else total + term
    return total


def paired(first, second):
    low, high = lane_half()
    return first * low + second * high


def chunk_mask(position, q):
    low, high = lane_half()
    return low * flag(position == 2 * q) + high * flag(position == 2 * q + 1)


def geometry(lane_rows, columns, sign, live, same):
    offset = [(row - column) * sign for row, column in zip(lane_rows, columns)]
    dist_sq = offset[0] * offset[0] + offset[1] * offset[1] + offset[2] * offset[2] + soften
    distance = jnp.sqrt(dist_sq)
    inverse = 1.0 / distance
    unit = [x * inverse for x in offset]
    row = lax.broadcasted_iota(jnp.int32, (TA, CHUNK), 0)
    lane = lax.broadcasted_iota(jnp.int32, (TA, CHUNK), 1)
    lane = jnp.where(lane >= TA, lane - TA, lane)
    mask = live * (1.0 - same * flag(row == lane))
    base = jnp.maximum(1.0 - dist_sq * (1.0 / (cutoff * cutoff)), 0.0)
    weight = base * base * base * mask * inverse
    slope = -(6.0 / (cutoff * cutoff)) * base * base * mask - weight * inverse
    angle = distance * (math.pi / cutoff)
    return unit, inverse, weight, slope, jnp.sin(angle), jnp.cos(angle)


def harmonics(v):
    x, y, z = v
    return [
        None,
        x,
        y,
        z,
        root_three * x * y,
        root_three * y * z,
        root_three * z * x,
        0.5 * root_three * (x * x - y * y),
        z * z - 0.5 * (x * x + y * y),
    ]


def harmonics_tangent(v, t):
    x, y, z = v
    a, b, c = t
    return [
        None,
        a,
        b,
        c,
        root_three * (a * y + x * b),
        root_three * (b * z + y * c),
        root_three * (c * x + z * a),
        root_three * (x * a - y * b),
        2.0 * z * c - (x * a + y * b),
    ]


def paired_orders(sine, cosine, weight, slope):
    low, high = lane_half()
    double_s, double_c = 2.0 * sine * cosine, 1.0 - 2.0 * sine * sine
    now_s = sine * low + double_s * high
    now_c = cosine * low + double_c * high
    old_s = -sine * low
    old_c = cosine * low + high
    values, slopes = [], []
    for k in range(BASIS // 2):
        order = ((2 * k + 1) * low + (2 * k + 2) * high) * (math.pi / cutoff)
        values.append(now_s * weight)
        slopes.append(now_c * (weight * order) + now_s * slope)
        now_s, old_s = 2.0 * double_c * now_s - old_s, now_s
        now_c, old_c = 2.0 * double_c * now_c - old_c, now_c
    return values, slopes


def single_orders(sine, cosine, weight, slope):
    now_s, now_c = sine, cosine
    old_s, old_c = jnp.zeros_like(sine), jnp.ones_like(cosine)
    values, slopes = [], []
    for n in range(1, BASIS + 1):
        values.append(now_s * weight)
        slopes.append(now_c * (weight * (n * math.pi / cutoff)) + now_s * slope)
        now_s, old_s = 2.0 * cosine * now_s - old_s, now_s
        now_c, old_c = 2.0 * cosine * now_c - old_c, now_c
    return values, slopes


def columns_of(rows, square, turned):
    square[...] = jnp.zeros_like(square)
    square[0 : rows.shape[0], :] = rows
    turned[...] = square[...].T


def pair_rows(first, p):
    return twice(first, p)


def radial_feat(feat, radial, p, high_ref, low_ref):
    own = feat[p * TA : (p + 1) * TA, :]
    for n in range(BASIS):
        hi, lo = split(own * radial[n : n + 1, :])
        high_ref[n * TA : (n + 1) * TA, :] = hi
        low_ref[n * TA : (n + 1) * TA, :] = lo


def gather_kernel(send, pos, feat, ref, to_low, to_high):
    position = [pos[0, :, q * CHUNK : (q + 1) * CHUNK] for q in range(2)]
    error = [ref[0, :, q * CHUNK : (q + 1) * CHUNK] for q in range(2)]
    low, high = lane_half()
    for out, first in ((to_low, 0), (to_high, SEND)):
        tiles = [send[0, first + j] for j in range(SEND)]
        for j in range(SEND):
            start = pl.multiple_of(tiles[j] * TA, TA)
            out[j * TA : (j + 1) * TA, :] = feat[0, pl.ds(start, TA), :]
        out[SEND * TA :, :] = jnp.zeros((16, out.shape[1]), F32)
        out[SEND * TA : SEND * TA + 3, 0:CHUNK] = paired(
            pick(position, tiles[0]), pick(position, tiles[1])
        )
        out[SEND * TA : SEND * TA + 3, CHUNK:] = paired(pick(error, tiles[0]), pick(error, tiles[1]))
        for other in range(2 * SEND):
            same = low * flag(send[0, other] == tiles[0]) + high * flag(send[0, other] == tiles[1])
            out[SEND * TA + 8 + other : SEND * TA + 9 + other, 0:CHUNK] = same


def force_kernel(
    centre, other, live, send, pos, feat, species, from_low, from_high, radial_w, mix_w, species_w, out_w,
    env, dinv, gate, curve, inv, rows, fsel, own, to_high, to_low,
    square, turned, th, tl, xh, xl, raw, mh, ml,
):
    ghost = SEND * TA
    chunks = [
        from_low[ghost : ghost + 3, 0:CHUNK],
        pos[0, :, 0:CHUNK],
        pos[0, :, CHUNK:],
        from_high[ghost : ghost + 3, 0:CHUNK],
    ]
    kinds = [species[:, q * CHUNK : (q + 1) * CHUNK].astype(F32) for q in range(2)]
    centres = [centre[0, p] for p in range(PAIRS)]
    others = [other[0, p] for p in range(PAIRS)]
    sames = [flag(others[p] == centres[p] + SEND) for p in range(PAIRS)]
    shared = flag(centres[0] == centres[1])
    rows[...] = jnp.zeros_like(rows)
    rows[0:3, :] = paired(*(pick(chunks, others[p]) for p in range(PAIRS)))
    rows[3:6, :] = paired(*(pick(chunks[1:3], centres[p]) for p in range(PAIRS)))
    rows[6:7, :] = paired(*(pick(kinds, centres[p]) for p in range(PAIRS)))
    columns_of(rows[...], square, turned)

    for p in range(PAIRS):
        o = others[p]
        below = pl.multiple_of(jnp.clip(o, 0, 1) * TA, TA)
        inside = pl.multiple_of(jnp.clip(o - SEND, 0, 3) * TA, TA)
        above = pl.multiple_of(jnp.clip(o - SEND - 4, 0, 1) * TA, TA)
        fsel[p * TA : (p + 1) * TA, :] = (
            from_low[pl.ds(below, TA), :] * flag(o < SEND)
            + feat[0, pl.ds(inside, TA), :] * flag((o >= SEND) & (o < SEND + 4))
            + from_high[pl.ds(above, TA), :] * flag(o >= SEND + 4)
        )

    shapes = []
    for p in range(PAIRS):
        lane_rows = [twice(rows[i : i + 1, :], p) for i in range(3)]
        columns = [turned[p * TA : (p + 1) * TA, 3 + i : 4 + i] for i in range(3)]
        unit, inverse, weight, slope, sine, cosine = geometry(
            lane_rows, columns, 1.0, live[0, p].astype(F32), sames[p]
        )
        angular = harmonics(unit)
        values, slopes = paired_orders(sine, cosine, weight, slope)
        shapes.append((unit, inverse, angular, values, slopes))
        for m in range(COMPS):
            for k in range(BASIS // 2):
                entry = values[k] if m == 0 else angular[m] * values[k]
                hi, lo = split(entry)
                th[m * TA : (m + 1) * TA, k * CHUNK : (k + 1) * CHUNK] = hi
                tl[m * TA : (m + 1) * TA, k * CHUNK : (k + 1) * CHUNK] = lo
        radial_feat(fsel, radial_w, p, xh.at[p], xl.at[p])
        raw[p * COMPS * TA : (p + 1) * COMPS * TA, 0:256] = product(
            (th[...], tl[...]), (xh[p], xl[p]), NN
        )

    for m in range(COMPS):
        first = raw[m * TA : (m + 1) * TA, 0:256]
        second = raw[(COMPS + m) * TA : (COMPS + m + 1) * TA, 0:256]
        env[m * TA : (m + 1) * TA, :] = env_scale * (first + shared * second)
        env[(COMPS + m) * TA : (COMPS + m + 1) * TA, :] = env_scale * (second + shared * first)
    for p in range(PAIRS):
        sums = [None] * 3
        for m in range(COMPS):
            block = env[(p * COMPS + m) * TA : (p * COMPS + m + 1) * TA, :]
            sums[GROUP[m]] = block * block if sums[GROUP[m]] is None else sums[GROUP[m]] + block * block
        for g in range(3):
            inv[p * TA : (p + 1) * TA, g * 256 : (g + 1) * 256] = sums[g]
    hi, lo = split(mix_w[...])
    mh[...] = hi
    ml[...] = lo
    hidden = product(split(inv[...]), (mh[...], ml[...]), NN)
    kind = turned[:, 6:7]
    for s in range(species_w.shape[0]):
        hidden = hidden + flag(kind == float(s)) * species_w[s : s + 1, :]
    sigma = 1.0 / (1.0 + jnp.exp(-hidden))
    first_order = sigma * (1.0 + hidden * (1.0 - sigma))
    gate[...] = first_order
    curve[...] = sigma * (1.0 - sigma) * (2.0 + hidden * (1.0 - 2.0 * sigma)) * out_w[...]
    dinv[...] = product(split(first_order * out_w[...]), (mh[...], ml[...]), NT)

    grads_low = [jnp.zeros((3, CHUNK), F32) for _ in range(4)]
    low, high = lane_half()
    for p in range(PAIRS):
        unit, inverse, angular, values, slopes = shapes[p]
        for m in range(COMPS):
            block = env[(p * COMPS + m) * TA : (p * COMPS + m + 1) * TA, :]
            part = dinv[p * TA : (p + 1) * TA, GROUP[m] * 256 : (GROUP[m] + 1) * 256]
            hi, lo = split((2.0 * env_scale) * block * part)
            th[m * TA : (m + 1) * TA, 0:256] = hi
            tl[m * TA : (m + 1) * TA, 0:256] = lo
        raw[0 : COMPS * TA, :] = product((th[:, 0:256], tl[:, 0:256]), (xh[p], xl[p]), NT)
        d_radius = None
        d_angular = []
        for m in range(COMPS):
            along, across = None, None
            for k in range(BASIS // 2):
                block = raw[m * TA : (m + 1) * TA, k * CHUNK : (k + 1) * CHUNK]
                along = block * slopes[k] if along is None else along + block * slopes[k]
                across = block * values[k] if across is None else across + block * values[k]
            d_angular.append(across)
            term = along if m == 0 else along * angular[m]
            d_radius = term if d_radius is None else d_radius + term
        x, y, z = unit
        g = d_angular
        toward = [
            g[1] + root_three * (y * g[4] + z * g[6] + x * g[7]) - x * g[8],
            g[2] + root_three * (x * g[4] + z * g[5] - y * g[7]) - y * g[8],
            g[3] + root_three * (y * g[5] + x * g[6]) + 2.0 * (z * g[8]),
        ]
        radial_part = d_radius - inverse * (toward[0] * x + toward[1] * y + toward[2] * z)
        other_rows, centre_rows = [], []
        for i in range(3):
            d_offset = inverse * toward[i] + unit[i] * radial_part
            summed = jnp.sum(d_offset, axis=0, keepdims=True)
            other_rows.append(summed + pltpu.roll(summed, TA, 1))
            square[0:TA, :] = d_offset
            square[TA:, :] = d_offset
            centre_rows.append(-jnp.sum(square[...].T, axis=0, keepdims=True))
        for i in range(3):
            for q in range(4):
                at = chunk_mask(others[p], q) * other_rows[i]
                if q in (1, 2):
                    at = at + chunk_mask(centres[p] + SEND, q) * centre_rows[i]
                grads_low[q] = grads_low[q] + at * flag(
                    lax.broadcasted_iota(jnp.int32, (3, CHUNK), 0) == i
                )
    own[...] = jnp.zeros_like(own)
    own[0:3, 0:CHUNK] = grads_low[1]
    own[0:3, CHUNK:] = grads_low[2]
    own[3:6, 0:CHUNK] = grads_low[0]
    own[3:6, CHUNK:] = grads_low[3]
    for out, first, ghost_grad in ((to_low, 0, grads_low[0]), (to_high, SEND, grads_low[3])):
        out[...] = jnp.zeros_like(out)
        out[0:3, :] = paired(*(pick(grads_low[1:3], send[0, first + j]) for j in range(SEND)))
        out[3:6, :] = ghost_grad


def tangent_kernel(
    scale, centre, other, live, send, ref, from_low, from_high, own, low_one, low_two, high_one, high_two,
    rows, fsel, env, dinv, gate, curve, inv, radial_w, mix_w, out_w,
    forces, keep, give, small, envdot, curl, both,
    square, turned, th, tl, xh, xl, raw, left, right,
):
    ghost = SEND * TA
    low, high = lane_half()
    centres = [centre[0, p] for p in range(PAIRS)]
    others = [other[0, p] for p in range(PAIRS)]
    sames = [flag(others[p] == centres[p] + SEND) for p in range(PAIRS)]
    shared = flag(centres[0] == centres[1])
    mine = [own[0:3, 0:CHUNK], own[0:3, CHUNK:]]
    arrived = [twice(low_one[3:6, :], j) for j in range(SEND)]
    arrived += [twice(high_one[3:6, :], j) for j in range(SEND)]
    for j in range(2 * SEND):
        for q in range(2):
            mine[q] = mine[q] + chunk_mask(send[0, j], q) * arrived[j]
    below = low_one[0:3, :]
    above = high_one[0:3, :]
    to_below = [twice(low_two[3:6, :], j) for j in range(SEND)]
    to_below += [twice(own[3:6, 0:CHUNK], j) for j in range(SEND)]
    to_above = [twice(own[3:6, CHUNK:], j) for j in range(SEND)]
    to_above += [twice(high_two[3:6, :], j) for j in range(SEND)]
    for j in range(2 * SEND):
        below = below + from_low[ghost + 8 + j : ghost + 9 + j, 0:CHUNK] * to_below[j]
        above = above + from_high[ghost + 8 + j : ghost + 9 + j, 0:CHUNK] * to_above[j]
    for q in range(2):
        forces[0, :, q * CHUNK : (q + 1) * CHUNK] = -mine[q]
    error = [
        below + from_low[ghost : ghost + 3, CHUNK:],
        mine[0] + ref[0, :, 0:CHUNK],
        mine[1] + ref[0, :, CHUNK:],
        above + from_high[ghost : ghost + 3, CHUNK:],
    ]
    error = [part * scale[0] for part in error]
    both[...] = jnp.zeros_like(both)
    both[0:8, :] = rows[...]
    both[8:11, :] = paired(*(pick(error, others[p]) for p in range(PAIRS)))
    both[11:14, :] = paired(*(pick(error[1:3], centres[p]) for p in range(PAIRS)))
    columns_of(both[...], square, turned)

    for p in range(PAIRS):
        lane_rows = [twice(both[i : i + 1, :], p) for i in range(3)]
        lane_move = [twice(both[8 + i : 9 + i, :], p) for i in range(3)]
        columns = [turned[p * TA : (p + 1) * TA, 3 + i : 4 + i] for i in range(3)]
        column_move = [turned[p * TA : (p + 1) * TA, 11 + i : 12 + i] for i in range(3)]
        unit, inverse, weight, slope, sine, cosine = geometry(
            lane_rows, columns, 1.0, live[0, p].astype(F32), sames[p]
        )
        move = [a - b for a, b in zip(lane_move, column_move)]
        stretch = unit[0] * move[0] + unit[1] * move[1] + unit[2] * move[2]
        turn = [(m - v * stretch) * inverse for m, v in zip(move, unit)]
        angular, turning = harmonics(unit), harmonics_tangent(unit, turn)
        values, slopes = paired_orders(sine, cosine, weight, slope)
        slopes = [s * stretch for s in slopes]
        for m in range(COMPS):
            for k in range(BASIS // 2):
                entry = slopes[k] if m == 0 else angular[m] * slopes[k] + turning[m] * values[k]
                hi, lo = split(entry)
                th[m * TA : (m + 1) * TA, k * CHUNK : (k + 1) * CHUNK] = hi
                tl[m * TA : (m + 1) * TA, k * CHUNK : (k + 1) * CHUNK] = lo
        radial_feat(fsel, radial_w, p, xh, xl)
        raw[p * COMPS * TA : (p + 1) * COMPS * TA, :] = product((th[...], tl[...]), (xh[...], xl[...]), NN)

    for m in range(COMPS):
        first = raw[m * TA : (m + 1) * TA, :]
        second = raw[(COMPS + m) * TA : (COMPS + m + 1) * TA, :]
        envdot[m * TA : (m + 1) * TA, :] = env_scale * (first + shared * second)
        envdot[(COMPS + m) * TA : (COMPS + m + 1) * TA, :] = env_scale * (second + shared * first)
    invdot = left
    half = PAIRS * TA
    for p in range(PAIRS):
        sums = [None] * 3
        for m in range(COMPS):
            at = slice((p * COMPS + m) * TA, (p * COMPS + m + 1) * TA)
            term = 2.0 * env[at, :] * envdot[at, :]
            sums[GROUP[m]] = term if sums[GROUP[m]] is None else sums[GROUP[m]] + term
        for g in range(3):
            invdot[half + p * TA : half + (p + 1) * TA, g * 256 : (g + 1) * 256] = sums[g]
    invdot[0:half, :] = inv[...]
    hidden_move = product(split(invdot[half:, :]), split(mix_w[...]), NN)
    bend = curve[...] * hidden_move
    curl[...] = bend
    once = 1.0 - shared * flag(lax.broadcasted_iota(jnp.int32, (half, 1), 0) >= TA)
    right[0:half, :] = bend * once
    right[half:, :] = gate[...] * out_w[...] * once
    core = lax.axis_index("batch")
    left_parts = split(left[...])
    for out, part in ((keep, core), (give, 1 - core)):
        lanes = pl.ds(pl.multiple_of(part * HALF, HALF), HALF)
        out[...] = product(left_parts, split(right[:, lanes]), TN)
    small[...] = jnp.zeros_like(small)
    kind = turned[:, 6:7]
    for s in range(SPECIES):
        small[s : s + 1, :] = jnp.sum(right[0:half, :] * flag(kind == float(s)), axis=0, keepdims=True)
    small[SPECIES : SPECIES + 1, :] = jnp.sum(gate[...] * hidden_move * once, axis=0, keepdims=True)


def radial_kernel(
    centre, other, live, both, fsel, env, envdot, dinv, curl, mix_w,
    grad_radial,
    square, turned, lh, ll, gh, gl, turn_inv, raw,
):
    centres = [centre[0, p] for p in range(PAIRS)]
    others = [other[0, p] for p in range(PAIRS)]
    sames = [flag(others[p] == centres[p] + SEND) for p in range(PAIRS)]
    low, high = lane_half()
    columns_of(both[...], square, turned)
    turn_inv[...] = product(split(curl[...]), split(mix_w[...]), NT)
    total = [None] * BASIS
    for p in range(PAIRS):
        lane_rows = [twice(both[3 + i : 4 + i, :], p) for i in range(3)]
        lane_move = [twice(both[11 + i : 12 + i, :], p) for i in range(3)]
        columns = [turned[p * TA : (p + 1) * TA, i : i + 1] for i in range(3)]
        column_move = [turned[p * TA : (p + 1) * TA, 8 + i : 9 + i] for i in range(3)]
        unit, inverse, weight, slope, sine, cosine = geometry(
            lane_rows, columns, -1.0, live[0, p].astype(F32), sames[p]
        )
        move = [b - a for a, b in zip(lane_move, column_move)]
        stretch = unit[0] * move[0] + unit[1] * move[1] + unit[2] * move[2]
        turn = [(m - v * stretch) * inverse for m, v in zip(move, unit)]
        angular, turning = harmonics(unit), harmonics_tangent(unit, turn)
        values, slopes = single_orders(sine, cosine, weight, slope)
        for m in range(COMPS):
            if m == 0:
                on_value, on_slope = low, high * stretch
            else:
                on_value = angular[m] * low + turning[m] * high
                on_slope = angular[m] * high * stretch
            for n in range(BASIS):
                hi, lo = split(on_value * values[n] + on_slope * slopes[n])
                lh[n * TA : (n + 1) * TA, m * CHUNK : (m + 1) * CHUNK] = hi
                ll[n * TA : (n + 1) * TA, m * CHUNK : (m + 1) * CHUNK] = lo
            at = slice((p * COMPS + m) * TA, (p * COMPS + m + 1) * TA)
            group = slice(GROUP[m] * 256, (GROUP[m] + 1) * 256)
            here = slice(p * TA, (p + 1) * TA)
            steady = (2.0 * env_scale) * dinv[here, group]
            bent = (2.0 * env_scale) * turn_inv[here, group]
            hi, lo = split(env[at, :] * bent + envdot[at, :] * steady)
            gh[m * CHUNK : m * CHUNK + TA, :] = hi
            gl[m * CHUNK : m * CHUNK + TA, :] = lo
            hi, lo = split(env[at, :] * steady)
            gh[m * CHUNK + TA : (m + 1) * CHUNK, :] = hi
            gl[m * CHUNK + TA : (m + 1) * CHUNK, :] = lo
        raw[...] = product((lh[...], ll[...]), (gh[...], gl[...]), NN)
        for n in range(BASIS):
            term = jnp.sum(
                raw[n * TA : (n + 1) * TA, :] * fsel[p * TA : (p + 1) * TA, :], axis=0, keepdims=True
            )
            total[n] = term if total[n] is None else total[n] + term
    for n in range(BASIS):
        grad_radial[n : n + 1, :] = total[n]


SMALL = 32


def pack_kernel(keep, taken, radial, small, packed):
    rows = keep.shape[0]
    packed[0:rows, :] = keep[...] + taken[...]
    packed[rows:, :] = jnp.zeros((packed.shape[0] - rows, HALF), F32)
    for h in range(2):
        lanes = slice(h * HALF, (h + 1) * HALF)
        packed[rows + 16 * h : rows + 16 * h + 8, :] = radial[:, lanes]
        packed[rows + 16 * h + 8 : rows + 16 * h + 16, :] = small[:, lanes]


def sum_kernel(spread, summed):
    count = lax.axis_size("domain")
    piece = spread.shape[0] // count
    total = spread[0:piece, :]
    for i in range(1, count):
        total = total + spread[i * piece : (i + 1) * piece, :]
    for i in range(count):
        summed[i * piece : (i + 1) * piece, :] = total


def join_kernel(whole, facing, mix, radial, kinds, out):
    rows = mix.shape[0]
    core = lax.axis_index("batch")
    for ref, part in ((whole, core), (facing, 1 - core)):
        mix[:, pl.ds(pl.multiple_of(part * HALF, HALF), HALF)] = ref[0:rows, :]
    for h in range(2):
        lanes = slice(h * HALF, (h + 1) * HALF)
        both = whole[rows + 16 * h : rows + 16 * h + 16, :] + facing[rows + 16 * h : rows + 16 * h + 16, :]
        radial[:, lanes] = both[0:BASIS]
        kinds[:, lanes] = both[BASIS : BASIS + SPECIES]
        out[:, lanes] = both[BASIS + SPECIES : BASIS + SPECIES + 1]


def vmem():
    return pl.BlockSpec(memory_space=pltpu.VMEM)


def smem():
    return pl.BlockSpec(memory_space=pltpu.SMEM)


def call(kernel, name, outs, scratch, scalars, *operands, flops=0):
    return pl.pallas_call(
        kernel,
        name=name,
        out_shape=[jax.ShapeDtypeStruct(shape, F32) for shape in outs],
        in_specs=[smem()] * scalars + [vmem()] * (len(operands) - scalars),
        out_specs=[vmem()] * len(outs),
        scratch_shapes=[pltpu.VMEM(shape, kind) for shape, kind in scratch],
        compiler_params=pltpu.CompilerParams(vmem_limit_bytes=48 * 1024 * 1024),
        cost_estimate=pl.CostEstimate(flops=flops, bytes_accessed=1 << 20, transcendentals=0),
    )(*operands)


def shifted(block, axis, by):
    count = lax.axis_size(axis)
    return lax.ppermute(block, axis, [(i, (i + by) % count) for i in range(count)])


def on_device(
    positions,
    features,
    species,
    ref_forces,
    centre_tile,
    other_tile,
    pair_live,
    send_tiles,
    radial_w,
    mix_w,
    species_w,
    out_w,
):
    atoms = positions.shape[2]
    channels = features.shape[2]
    table = (COMPS * TA, BASIS * TA)
    sent = (SEND * TA + 16, channels)
    slots = PAIRS * TA
    turning = [((CHUNK, CHUNK), F32)] * 2
    out_row = out_w.reshape(1, channels)

    to_low, to_high = call(
        gather_kernel, "gather", [sent, sent], [], 1, send_tiles, positions, features, ref_forces
    )
    from_low = shifted(to_high, "domain", 1)
    from_high = shifted(to_low, "domain", -1)

    env, dinv, gate, curve, inv, rows, fsel, own, grads_up, grads_down = call(
        force_kernel,
        "force",
        [
            (PAIRS * COMPS * TA, channels),
            (slots, 3 * channels),
            (slots, channels),
            (slots, channels),
            (slots, 3 * channels),
            (8, CHUNK),
            (slots, channels),
            (8, atoms),
            (8, CHUNK),
            (8, CHUNK),
        ],
        turning
        + [(table, BF16)] * 2
        + [((PAIRS, BASIS * TA, channels), BF16)] * 2
        + [((PAIRS * COMPS * TA, BASIS * TA), F32)]
        + [((3 * channels, channels), BF16)] * 2,
        4,
        centre_tile, other_tile, pair_live, send_tiles,
        positions, features, species, from_low, from_high, radial_w, mix_w, species_w, out_row,
        flops=1 << 31,
    )
    low_one = shifted(grads_up, "domain", 1)
    low_two = shifted(grads_up, "domain", 2)
    high_one = shifted(grads_down, "domain", -1)
    high_two = shifted(grads_down, "domain", -2)

    total_count = 3.0 * atoms * lax.axis_size("domain") * lax.axis_size("batch")
    scale = jnp.full((1,), 2.0 / math.sqrt(total_count), F32)
    forces, keep, give, small, envdot, curl, both = call(
        tangent_kernel,
        "tangent",
        [
            (1, 3, atoms),
            (3 * channels, HALF),
            (3 * channels, HALF),
            (8, channels),
            (PAIRS * COMPS * TA, channels),
            (slots, channels),
            (16, CHUNK),
        ],
        turning
        + [(table, BF16)] * 2
        + [((BASIS * TA, channels), BF16)] * 2
        + [((PAIRS * COMPS * TA, channels), F32)]
        + [((2 * slots, 3 * channels), F32), ((2 * slots, channels), F32)],
        5,
        scale, centre_tile, other_tile, pair_live, send_tiles,
        ref_forces, from_low, from_high, own, low_one, low_two, high_one, high_two,
        rows, fsel, env, dinv, gate, curve, inv, radial_w, mix_w, out_row,
        flops=1 << 31,
    )
    (grad_radial,) = call(
        radial_kernel,
        "radial",
        [(BASIS, channels)],
        turning
        + [((BASIS * TA, COMPS * CHUNK), BF16)] * 2
        + [((COMPS * CHUNK, channels), BF16)] * 2
        + [((slots, 3 * channels), F32), ((BASIS * TA, channels), F32)],
        3,
        centre_tile, other_tile, pair_live,
        both, fsel, env, envdot, dinv, curl, mix_w,
        flops=1 << 31,
    )
    count = lax.axis_size("domain")
    rows_mix = 3 * channels
    piece = -(-(rows_mix + SMALL) // (8 * count)) * 8
    taken = shifted(give, "batch", 1)
    (packed,) = call(pack_kernel, "pack", [(count * piece, HALF)], [], 0, keep, taken, grad_radial, small)
    spread = lax.all_to_all(packed, "domain", 0, 0, tiled=True)
    (summed,) = call(sum_kernel, "sum", [(count * piece, HALF)], [], 0, spread)
    whole = lax.all_to_all(summed, "domain", 0, 0, tiled=True)
    facing = shifted(whole, "batch", 1)
    mix, radial, kinds, out = call(
        join_kernel,
        "join",
        [(rows_mix, channels), (BASIS, channels), (SPECIES, channels), (1, channels)],
        [],
        0,
        whole,
        facing,
    )
    return forces, radial, mix, kinds, out.reshape(channels)


def solution(mesh):
    return jax.shard_map(
        on_device,
        mesh=mesh,
        in_specs=(
            P(("parts", "batch"), None, "domain"),
            P(("parts", "batch"), "domain", None),
            P(("parts", "batch"), "domain"),
            P(("parts", "batch"), None, "domain"),
            P(("parts", "batch"), "domain"),
            P(("parts", "batch"), "domain"),
            P(("parts", "batch"), "domain"),
            P(("parts", "batch"), "domain"),
            P(),
            P(),
            P(),
            P(),
        ),
        out_specs=(
            P(("parts", "batch"), None, "domain"),
            P("parts", None),
            P("parts", None),
            P("parts", None),
            P("parts"),
        ),
        check_vma=False,
    )
```

```python
import functools
import math

import jax
import jax.numpy as jnp
from jax import lax
from jax.experimental import pallas as pl
from jax.experimental.pallas import tpu as pltpu
from jax.sharding import PartitionSpec as P

TA = 64
SEND = 2
PAIRS = 2
COMPS = 9
BASIS = 8
SPECIES = 4
HALF = 128
CHUNK = 2 * TA

cutoff = 2.5
soften = 0.25
env_scale = 0.25
root_three = math.sqrt(3.0)
F32 = jnp.float32
BF16 = jnp.bfloat16
NN = (((1,), (0,)), ((), ()))
NT = (((1,), (1,)), ((), ()))
TN = (((0,), (0,)), ((), ()))
GROUP = (0, 1, 1, 1, 2, 2, 2, 2, 2)


def split(value):
    high = value.astype(BF16)
    return high, (value - high.astype(F32)).astype(BF16)


def product(left, right, dims):
    (lh, ll), (rh, rl) = left, right

    def one(x, y):
        return lax.dot_general(x, y, dims, preferred_element_type=F32)

    return one(lh, rh) + (one(lh, rl) + one(ll, rh))


def flag(condition):
    return jnp.where(condition, 1.0, 0.0).astype(F32)


def lane_half():
    lane = lax.broadcasted_iota(jnp.int32, (1, CHUNK), 1)
    low = flag(lane < TA)
    return low, 1.0 - low


def twice(chunk, half):
    low, high = lane_half()
    swapped = pltpu.roll(chunk, TA, 1)
    return chunk * low + swapped * high if half == 0 else swapped * low + chunk * high


def pick(chunks, position):
    total = None
    for q, chunk in enumerate(chunks):
        for half in range(2):
            term = twice(chunk, half) * flag(position == 2 * q + half)
            total = term if total is None else total + term
    return total


def paired(first, second):
    low, high = lane_half()
    return first * low + second * high


def chunk_mask(position, q):
    low, high = lane_half()
    return low * flag(position == 2 * q) + high * flag(position == 2 * q + 1)


def geometry(lane_rows, columns, sign, live, same):
    offset = [(row - column) * sign for row, column in zip(lane_rows, columns)]
    dist_sq = offset[0] * offset[0] + offset[1] * offset[1] + offset[2] * offset[2] + soften
    distance = jnp.sqrt(dist_sq)
    inverse = 1.0 / distance
    unit = [x * inverse for x in offset]
    row = lax.broadcasted_iota(jnp.int32, (TA, CHUNK), 0)
    lane = lax.broadcasted_iota(jnp.int32, (TA, CHUNK), 1)
    lane = jnp.where(lane >= TA, lane - TA, lane)
    mask = live * (1.0 - same * flag(row == lane))
    base = jnp.maximum(1.0 - dist_sq * (1.0 / (cutoff * cutoff)), 0.0)
    weight = base * base * base * mask * inverse
    slope = -(6.0 / (cutoff * cutoff)) * base * base * mask - weight * inverse
    angle = distance * (math.pi / cutoff)
    return unit, inverse, weight, slope, jnp.sin(angle), jnp.cos(angle)


def harmonics(v):
    x, y, z = v
    return [
        None,
        x,
        y,
        z,
        root_three * x * y,
        root_three * y * z,
        root_three * z * x,
        0.5 * root_three * (x * x - y * y),
        z * z - 0.5 * (x * x + y * y),
    ]


def harmonics_tangent(v, t):
    x, y, z = v
    a, b, c = t
    return [
        None,
        a,
        b,
        c,
        root_three * (a * y + x * b),
        root_three * (b * z + y * c),
        root_three * (c * x + z * a),
        root_three * (x * a - y * b),
        2.0 * z * c - (x * a + y * b),
    ]


def paired_orders(sine, cosine, weight, slope):
    low, high = lane_half()
    double_s, double_c = 2.0 * sine * cosine, 1.0 - 2.0 * sine * sine
    now_s = sine * low + double_s * high
    now_c = cosine * low + double_c * high
    old_s = -sine * low
    old_c = cosine * low + high
    values, slopes = [], []
    for k in range(BASIS // 2):
        order = ((2 * k + 1) * low + (2 * k + 2) * high) * (math.pi / cutoff)
        values.append(now_s * weight)
        slopes.append(now_c * (weight * order) + now_s * slope)
        now_s, old_s = 2.0 * double_c * now_s - old_s, now_s
        now_c, old_c = 2.0 * double_c * now_c - old_c, now_c
    return values, slopes


def single_orders(sine, cosine, weight, slope):
    now_s, now_c = sine, cosine
    old_s, old_c = jnp.zeros_like(sine), jnp.ones_like(cosine)
    values, slopes = [], []
    for n in range(1, BASIS + 1):
        values.append(now_s * weight)
        slopes.append(now_c * (weight * (n * math.pi / cutoff)) + now_s * slope)
        now_s, old_s = 2.0 * cosine * now_s - old_s, now_s
        now_c, old_c = 2.0 * cosine * now_c - old_c, now_c
    return values, slopes


def columns_of(rows, square, turned):
    square[...] = jnp.zeros_like(square)
    square[0 : rows.shape[0], :] = rows
    turned[...] = square[...].T


def pair_rows(first, p):
    return twice(first, p)


def radial_feat(feat, radial, p, high_ref, low_ref):
    own = feat[p * TA : (p + 1) * TA, :]
    for n in range(BASIS):
        hi, lo = split(own * radial[n : n + 1, :])
        high_ref[n * TA : (n + 1) * TA, :] = hi
        low_ref[n * TA : (n + 1) * TA, :] = lo


def gather_kernel(send, pos, feat, ref, to_low, to_high):
    position = [pos[0, :, q * CHUNK : (q + 1) * CHUNK] for q in range(2)]
    error = [ref[0, :, q * CHUNK : (q + 1) * CHUNK] for q in range(2)]
    low, high = lane_half()
    for out, first in ((to_low, 0), (to_high, SEND)):
        tiles = [send[0, first + j] for j in range(SEND)]
        for j in range(SEND):
            start = pl.multiple_of(tiles[j] * TA, TA)
            out[j * TA : (j + 1) * TA, :] = feat[0, pl.ds(start, TA), :]
        out[SEND * TA :, :] = jnp.zeros((16, out.shape[1]), F32)
        out[SEND * TA : SEND * TA + 3, 0:CHUNK] = paired(
            pick(position, tiles[0]), pick(position, tiles[1])
        )
        out[SEND * TA : SEND * TA + 3, CHUNK:] = paired(pick(error, tiles[0]), pick(error, tiles[1]))
        for other in range(2 * SEND):
            same = low * flag(send[0, other] == tiles[0]) + high * flag(send[0, other] == tiles[1])
            out[SEND * TA + 8 + other : SEND * TA + 9 + other, 0:CHUNK] = same


def force_kernel(
    centre, other, live, send, pos, feat, species, from_low, from_high, radial_w, mix_w, species_w, out_w,
    env, dinv, gate, curve, inv, rows, fsel, own, to_high, to_low,
    square, turned, th, tl, xh, xl, raw, mh, ml,
):
    ghost = SEND * TA
    chunks = [
        from_low[ghost : ghost + 3, 0:CHUNK],
        pos[0, :, 0:CHUNK],
        pos[0, :, CHUNK:],
        from_high[ghost : ghost + 3, 0:CHUNK],
    ]
    kinds = [species[:, q * CHUNK : (q + 1) * CHUNK].astype(F32) for q in range(2)]
    centres = [centre[0, p] for p in range(PAIRS)]
    others = [other[0, p] for p in range(PAIRS)]
    sames = [flag(others[p] == centres[p] + SEND) for p in range(PAIRS)]
    shared = flag(centres[0] == centres[1])
    rows[...] = jnp.zeros_like(rows)
    rows[0:3, :] = paired(*(pick(chunks, others[p]) for p in range(PAIRS)))
    rows[3:6, :] = paired(*(pick(chunks[1:3], centres[p]) for p in range(PAIRS)))
    rows[6:7, :] = paired(*(pick(kinds, centres[p]) for p in range(PAIRS)))
    columns_of(rows[...], square, turned)

    for p in range(PAIRS):
        o = others[p]
        below = pl.multiple_of(jnp.clip(o, 0, 1) * TA, TA)
        inside = pl.multiple_of(jnp.clip(o - SEND, 0, 3) * TA, TA)
        above = pl.multiple_of(jnp.clip(o - SEND - 4, 0, 1) * TA, TA)
        fsel[p * TA : (p + 1) * TA, :] = (
            from_low[pl.ds(below, TA), :] * flag(o < SEND)
            + feat[0, pl.ds(inside, TA), :] * flag((o >= SEND) & (o < SEND + 4))
            + from_high[pl.ds(above, TA), :] * flag(o >= SEND + 4)
        )

    shapes = []
    for p in range(PAIRS):
        lane_rows = [twice(rows[i : i + 1, :], p) for i in range(3)]
        columns = [turned[p * TA : (p + 1) * TA, 3 + i : 4 + i] for i in range(3)]
        unit, inverse, weight, slope, sine, cosine = geometry(
            lane_rows, columns, 1.0, live[0, p].astype(F32), sames[p]
        )
        angular = harmonics(unit)
        values, slopes = paired_orders(sine, cosine, weight, slope)
        shapes.append((unit, inverse, angular, values, slopes))
        for m in range(COMPS):
            for k in range(BASIS // 2):
                entry = values[k] if m == 0 else angular[m] * values[k]
                hi, lo = split(entry)
                th[m * TA : (m + 1) * TA, k * CHUNK : (k + 1) * CHUNK] = hi
                tl[m * TA : (m + 1) * TA, k * CHUNK : (k + 1) * CHUNK] = lo
        radial_feat(fsel, radial_w, p, xh.at[p], xl.at[p])
        raw[p * COMPS * TA : (p + 1) * COMPS * TA, 0:256] = product(
            (th[...], tl[...]), (xh[p], xl[p]), NN
        )

    for m in range(COMPS):
        first = raw[m * TA : (m + 1) * TA, 0:256]
        second = raw[(COMPS + m) * TA : (COMPS + m + 1) * TA, 0:256]
        env[m * TA : (m + 1) * TA, :] = env_scale * (first + shared * second)
        env[(COMPS + m) * TA : (COMPS + m + 1) * TA, :] = env_scale * (second + shared * first)
    for p in range(PAIRS):
        sums = [None] * 3
        for m in range(COMPS):
            block = env[(p * COMPS + m) * TA : (p * COMPS + m + 1) * TA, :]
            sums[GROUP[m]] = block * block if sums[GROUP[m]] is None else sums[GROUP[m]] + block * block
        for g in range(3):
            inv[p * TA : (p + 1) * TA, g * 256 : (g + 1) * 256] = sums[g]
    hi, lo = split(mix_w[...])
    mh[...] = hi
    ml[...] = lo
    hidden = product(split(inv[...]), (mh[...], ml[...]), NN)
    kind = turned[:, 6:7]
    for s in range(species_w.shape[0]):
        hidden = hidden + flag(kind == float(s)) * species_w[s : s + 1, :]
    sigma = 1.0 / (1.0 + jnp.exp(-hidden))
    first_order = sigma * (1.0 + hidden * (1.0 - sigma))
    gate[...] = first_order
    curve[...] = sigma * (1.0 - sigma) * (2.0 + hidden * (1.0 - 2.0 * sigma)) * out_w[...]
    dinv[...] = product(split(first_order * out_w[...]), (mh[...], ml[...]), NT)

    grads_low = [jnp.zeros((3, CHUNK), F32) for _ in range(4)]
    low, high = lane_half()
    for p in range(PAIRS):
        unit, inverse, angular, values, slopes = shapes[p]
        for m in range(COMPS):
            block = env[(p * COMPS + m) * TA : (p * COMPS + m + 1) * TA, :]
            part = dinv[p * TA : (p + 1) * TA, GROUP[m] * 256 : (GROUP[m] + 1) * 256]
            hi, lo = split((2.0 * env_scale) * block * part)
            th[m * TA : (m + 1) * TA, 0:256] = hi
            tl[m * TA : (m + 1) * TA, 0:256] = lo
        raw[0 : COMPS * TA, :] = product((th[:, 0:256], tl[:, 0:256]), (xh[p], xl[p]), NT)
        d_radius = None
        d_angular = []
        for m in range(COMPS):
            along, across = None, None
            for k in range(BASIS // 2):
                block = raw[m * TA : (m + 1) * TA, k * CHUNK : (k + 1) * CHUNK]
                along = block * slopes[k] if along is None else along + block * slopes[k]
                across = block * values[k] if across is None else across + block * values[k]
            d_angular.append(across)
            term = along if m == 0 else along * angular[m]
            d_radius = term if d_radius is None else d_radius + term
        x, y, z = unit
        g = d_angular
        toward = [
            g[1] + root_three * (y * g[4] + z * g[6] + x * g[7]) - x * g[8],
            g[2] + root_three * (x * g[4] + z * g[5] - y * g[7]) - y * g[8],
            g[3] + root_three * (y * g[5] + x * g[6]) + 2.0 * (z * g[8]),
        ]
        radial_part = d_radius - inverse * (toward[0] * x + toward[1] * y + toward[2] * z)
        other_rows, centre_rows = [], []
        for i in range(3):
            d_offset = inverse * toward[i] + unit[i] * radial_part
            summed = jnp.sum(d_offset, axis=0, keepdims=True)
            other_rows.append(summed + pltpu.roll(summed, TA, 1))
            square[0:TA, :] = d_offset
            square[TA:, :] = d_offset
            centre_rows.append(-jnp.sum(square[...].T, axis=0, keepdims=True))
        for i in range(3):
            for q in range(4):
                at = chunk_mask(others[p], q) * other_rows[i]
                if q in (1, 2):
                    at = at + chunk_mask(centres[p] + SEND, q) * centre_rows[i]
                grads_low[q] = grads_low[q] + at * flag(
                    lax.broadcasted_iota(jnp.int32, (3, CHUNK), 0) == i
                )
    own[...] = jnp.zeros_like(own)
    own[0:3, 0:CHUNK] = grads_low[1]
    own[0:3, CHUNK:] = grads_low[2]
    own[3:6, 0:CHUNK] = grads_low[0]
    own[3:6, CHUNK:] = grads_low[3]
    for out, first, ghost_grad in ((to_low, 0, grads_low[0]), (to_high, SEND, grads_low[3])):
        out[...] = jnp.zeros_like(out)
        out[0:3, :] = paired(*(pick(grads_low[1:3], send[0, first + j]) for j in range(SEND)))
        out[3:6, :] = ghost_grad


def tangent_kernel(
    scale, centre, other, live, send, ref, from_low, from_high, own, low_one, low_two, high_one, high_two,
    rows, fsel, env, dinv, gate, curve, inv, radial_w, mix_w, out_w,
    forces, keep, give, small, envdot, curl, both,
    square, turned, th, tl, xh, xl, raw, left, right,
):
    ghost = SEND * TA
    low, high = lane_half()
    centres = [centre[0, p] for p in range(PAIRS)]
    others = [other[0, p] for p in range(PAIRS)]
    sames = [flag(others[p] == centres[p] + SEND) for p in range(PAIRS)]
    shared = flag(centres[0] == centres[1])
    mine = [own[0:3, 0:CHUNK], own[0:3, CHUNK:]]
    arrived = [twice(low_one[3:6, :], j) for j in range(SEND)]
    arrived += [twice(high_one[3:6, :], j) for j in range(SEND)]
    for j in range(2 * SEND):
        for q in range(2):
            mine[q] = mine[q] + chunk_mask(send[0, j], q) * arrived[j]
    below = low_one[0:3, :]
    above = high_one[0:3, :]
    to_below = [twice(low_two[3:6, :], j) for j in range(SEND)]
    to_below += [twice(own[3:6, 0:CHUNK], j) for j in range(SEND)]
    to_above = [twice(own[3:6, CHUNK:], j) for j in range(SEND)]
    to_above += [twice(high_two[3:6, :], j) for j in range(SEND)]
    for j in range(2 * SEND):
        below = below + from_low[ghost + 8 + j : ghost + 9 + j, 0:CHUNK] * to_below[j]
        above = above + from_high[ghost + 8 + j : ghost + 9 + j, 0:CHUNK] * to_above[j]
    for q in range(2):
        forces[0, :, q * CHUNK : (q + 1) * CHUNK] = -mine[q]
    error = [
        below + from_low[ghost : ghost + 3, CHUNK:],
        mine[0] + ref[0, :, 0:CHUNK],
        mine[1] + ref[0, :, CHUNK:],
        above + from_high[ghost : ghost + 3, CHUNK:],
    ]
    error = [part * scale[0] for part in error]
    both[...] = jnp.zeros_like(both)
    both[0:8, :] = rows[...]
    both[8:11, :] = paired(*(pick(error, others[p]) for p in range(PAIRS)))
    both[11:14, :] = paired(*(pick(error[1:3], centres[p]) for p in range(PAIRS)))
    columns_of(both[...], square, turned)

    for p in range(PAIRS):
        lane_rows = [twice(both[i : i + 1, :], p) for i in range(3)]
        lane_move = [twice(both[8 + i : 9 + i, :], p) for i in range(3)]
        columns = [turned[p * TA : (p + 1) * TA, 3 + i : 4 + i] for i in range(3)]
        column_move = [turned[p * TA : (p + 1) * TA, 11 + i : 12 + i] for i in range(3)]
        unit, inverse, weight, slope, sine, cosine = geometry(
            lane_rows, columns, 1.0, live[0, p].astype(F32), sames[p]
        )
        move = [a - b for a, b in zip(lane_move, column_move)]
        stretch = unit[0] * move[0] + unit[1] * move[1] + unit[2] * move[2]
        turn = [(m - v * stretch) * inverse for m, v in zip(move, unit)]
        angular, turning = harmonics(unit), harmonics_tangent(unit, turn)
        values, slopes = paired_orders(sine, cosine, weight, slope)
        slopes = [s * stretch for s in slopes]
        for m in range(COMPS):
            for k in range(BASIS // 2):
                entry = slopes[k] if m == 0 else angular[m] * slopes[k] + turning[m] * values[k]
                hi, lo = split(entry)
                th[m * TA : (m + 1) * TA, k * CHUNK : (k + 1) * CHUNK] = hi
                tl[m * TA : (m + 1) * TA, k * CHUNK : (k + 1) * CHUNK] = lo
        radial_feat(fsel, radial_w, p, xh, xl)
        raw[p * COMPS * TA : (p + 1) * COMPS * TA, :] = product((th[...], tl[...]), (xh[...], xl[...]), NN)

    for m in range(COMPS):
        first = raw[m * TA : (m + 1) * TA, :]
        second = raw[(COMPS + m) * TA : (COMPS + m + 1) * TA, :]
        envdot[m * TA : (m + 1) * TA, :] = env_scale * (first + shared * second)
        envdot[(COMPS + m) * TA : (COMPS + m + 1) * TA, :] = env_scale * (second + shared * first)
    invdot = left
    half = PAIRS * TA
    for p in range(PAIRS):
        sums = [None] * 3
        for m in range(COMPS):
            at = slice((p * COMPS + m) * TA, (p * COMPS + m + 1) * TA)
            term = 2.0 * env[at, :] * envdot[at, :]
            sums[GROUP[m]] = term if sums[GROUP[m]] is None else sums[GROUP[m]] + term
        for g in range(3):
            invdot[half + p * TA : half + (p + 1) * TA, g * 256 : (g + 1) * 256] = sums[g]
    invdot[0:half, :] = inv[...]
    hidden_move = product(split(invdot[half:, :]), split(mix_w[...]), NN)
    bend = curve[...] * hidden_move
    curl[...] = bend
    once = 1.0 - shared * flag(lax.broadcasted_iota(jnp.int32, (half, 1), 0) >= TA)
    right[0:half, :] = bend * once
    right[half:, :] = gate[...] * out_w[...] * once
    core = lax.axis_index("batch")
    left_parts = split(left[...])
    for out, part in ((keep, core), (give, 1 - core)):
        lanes = pl.ds(pl.multiple_of(part * HALF, HALF), HALF)
        out[...] = product(left_parts, split(right[:, lanes]), TN)
    small[...] = jnp.zeros_like(small)
    kind = turned[:, 6:7]
    for s in range(SPECIES):
        small[s : s + 1, :] = jnp.sum(right[0:half, :] * flag(kind == float(s)), axis=0, keepdims=True)
    small[SPECIES : SPECIES + 1, :] = jnp.sum(gate[...] * hidden_move * once, axis=0, keepdims=True)


def radial_kernel(
    p, centre, other, live, both, fsel, env, envdot, dinv, curl, mix_w, after,
    grad_radial,
    square, turned, lh, ll, gh, gl, raw,
):
    same = flag(other[0, p] == centre[0, p] + SEND)
    low, high = lane_half()
    columns_of(both[...], square, turned)
    here = slice(p * TA, (p + 1) * TA)
    turn_inv = product(split(curl[here, :]), split(mix_w[...]), NT)
    lane_rows = [twice(both[3 + i : 4 + i, :], p) for i in range(3)]
    lane_move = [twice(both[11 + i : 12 + i, :], p) for i in range(3)]
    columns = [turned[here, i : i + 1] for i in range(3)]
    column_move = [turned[here, 8 + i : 9 + i] for i in range(3)]
    unit, inverse, weight, slope, sine, cosine = geometry(
        lane_rows, columns, -1.0, live[0, p].astype(F32), same
    )
    move = [b - a for a, b in zip(lane_move, column_move)]
    stretch = unit[0] * move[0] + unit[1] * move[1] + unit[2] * move[2]
    turn = [(m - v * stretch) * inverse for m, v in zip(move, unit)]
    angular, turning = harmonics(unit), harmonics_tangent(unit, turn)
    values, slopes = single_orders(sine, cosine, weight, slope)
    for m in range(COMPS):
        if m == 0:
            on_value, on_slope = low, high * stretch
        else:
            on_value = angular[m] * low + turning[m] * high
            on_slope = angular[m] * high * stretch
        for n in range(BASIS):
            hi, lo = split(on_value * values[n] + on_slope * slopes[n])
            lh[n * TA : (n + 1) * TA, m * CHUNK : (m + 1) * CHUNK] = hi
            ll[n * TA : (n + 1) * TA, m * CHUNK : (m + 1) * CHUNK] = lo
        at = slice((p * COMPS + m) * TA, (p * COMPS + m + 1) * TA)
        group = slice(GROUP[m] * 256, (GROUP[m] + 1) * 256)
        steady = (2.0 * env_scale) * dinv[here, group]
        bent = (2.0 * env_scale) * turn_inv[:, group]
        hi, lo = split(env[at, :] * bent + envdot[at, :] * steady)
        gh[m * CHUNK : m * CHUNK + TA, :] = hi
        gl[m * CHUNK : m * CHUNK + TA, :] = lo
        hi, lo = split(env[at, :] * steady)
        gh[m * CHUNK + TA : (m + 1) * CHUNK, :] = hi
        gl[m * CHUNK + TA : (m + 1) * CHUNK, :] = lo
    raw[...] = product((lh[...], ll[...]), (gh[...], gl[...]), NN)
    for n in range(BASIS):
        grad_radial[n : n + 1, :] = jnp.sum(
            raw[n * TA : (n + 1) * TA, :] * fsel[here, :], axis=0, keepdims=True
        )


SMALL = 32


def halves(rows):
    return (rows // 2, True) if rows % 16 == 0 else (rows, False)


def hand_on(total, bit, cut, keep_out, give_out):
    rows = keep_out.shape[0]
    if not cut:
        keep_out[...] = total(pl.ds(0, rows))
        give_out[0:rows, :] = total(pl.ds(0, rows))
        return
    mine = lax.bitwise_and(lax.shift_right_logical(lax.axis_index("domain"), bit), 1)
    for out, part in ((keep_out, mine), (give_out, 1 - mine)):
        out[0:rows, :] = total(pl.ds(pl.multiple_of(part * rows, 8), rows))


def first_kernel(cut, keep, taken, keep_out, give_out, token):
    hand_on(lambda at: keep[at, :] + taken[at, :], 0, cut, keep_out, give_out)
    token[...] = jnp.zeros_like(token)


def second_kernel(bit, cut, keep, taken, radial_0, radial_1, small, keep_out, give_out, tiny_out):
    hand_on(lambda at: keep[at, :] + taken[at, :], bit, cut, keep_out, give_out)
    rows = keep_out.shape[0]
    for h in range(2):
        lanes = slice(h * HALF, (h + 1) * HALF)
        tiny_out[16 * h : 16 * h + 8, :] = radial_0[:, lanes] + radial_1[:, lanes]
        tiny_out[16 * h + 8 : 16 * h + 16, :] = small[:, lanes]
    give_out[rows:, :] = tiny_out[...]


def later_kernel(bit, cut, keep, taken, tiny, keep_out, give_out, tiny_out):
    hand_on(lambda at: keep[at, :] + taken[at, :], bit, cut, keep_out, give_out)
    tiny_out[...] = tiny[...] + taken[keep.shape[0] :, :]
    give_out[keep_out.shape[0] :, :] = tiny_out[...]


def last_kernel(keep, taken, tiny, total, tiny_out):
    rows = keep.shape[0]
    total[...] = keep[...] + taken[0:rows, :]
    tiny_out[...] = tiny[...] + taken[rows:, :]


def grow_kernel(bit, tail, mine, theirs, tiny, grown):
    rows = theirs.shape[0]
    at = lax.bitwise_and(lax.shift_right_logical(lax.axis_index("domain"), bit), 1)
    for ref, part in ((mine, at), (theirs, 1 - at)):
        grown[pl.ds(pl.multiple_of(part * rows, 8), rows), :] = ref[...]
    if tail:
        grown[2 * rows :, :] = tiny[...]


def grow_last_kernel(mine, theirs, grown):
    rows = theirs.shape[0] - SMALL
    at = lax.bitwise_and(lax.axis_index("domain"), 1)
    for ref, part in ((mine, at), (theirs, 1 - at)):
        grown[pl.ds(pl.multiple_of(part * rows, 8), rows), :] = ref[0:rows, :]
    grown[2 * rows :, :] = mine[rows:, :] + theirs[rows:, :]


def join_kernel(whole, facing, mix, radial, kinds, out):
    rows = mix.shape[0]
    core = lax.axis_index("batch")
    for ref, part in ((whole, core), (facing, 1 - core)):
        mix[:, pl.ds(pl.multiple_of(part * HALF, HALF), HALF)] = ref[0:rows, :]
    for h in range(2):
        lanes = slice(h * HALF, (h + 1) * HALF)
        both = whole[rows + 16 * h : rows + 16 * h + 16, :] + facing[rows + 16 * h : rows + 16 * h + 16, :]
        radial[:, lanes] = both[0:BASIS]
        kinds[:, lanes] = both[BASIS : BASIS + SPECIES]
        out[:, lanes] = both[BASIS + SPECIES : BASIS + SPECIES + 1]


def vmem():
    return pl.BlockSpec(memory_space=pltpu.VMEM)


def smem():
    return pl.BlockSpec(memory_space=pltpu.SMEM)


def call(kernel, name, outs, scratch, scalars, *operands, flops=0):
    return pl.pallas_call(
        kernel,
        name=name,
        out_shape=[jax.ShapeDtypeStruct(shape, F32) for shape in outs],
        in_specs=[smem()] * scalars + [vmem()] * (len(operands) - scalars),
        out_specs=[vmem()] * len(outs),
        scratch_shapes=[pltpu.VMEM(shape, kind) for shape, kind in scratch],
        compiler_params=pltpu.CompilerParams(vmem_limit_bytes=48 * 1024 * 1024),
        cost_estimate=pl.CostEstimate(flops=flops, bytes_accessed=1 << 20, transcendentals=0),
    )(*operands)


def shifted(block, axis, by):
    count = lax.axis_size(axis)
    return lax.ppermute(block, axis, [(i, (i + by) % count) for i in range(count)])


def on_device(
    positions,
    features,
    species,
    ref_forces,
    centre_tile,
    other_tile,
    pair_live,
    send_tiles,
    radial_w,
    mix_w,
    species_w,
    out_w,
):
    atoms = positions.shape[2]
    channels = features.shape[2]
    table = (COMPS * TA, BASIS * TA)
    sent = (SEND * TA + 16, channels)
    slots = PAIRS * TA
    turning = [((CHUNK, CHUNK), F32)] * 2
    out_row = out_w.reshape(1, channels)

    to_low, to_high = call(
        gather_kernel, "gather", [sent, sent], [], 1, send_tiles, positions, features, ref_forces
    )
    from_low = shifted(to_high, "domain", 1)
    from_high = shifted(to_low, "domain", -1)

    env, dinv, gate, curve, inv, rows, fsel, own, grads_up, grads_down = call(
        force_kernel,
        "force",
        [
            (PAIRS * COMPS * TA, channels),
            (slots, 3 * channels),
            (slots, channels),
            (slots, channels),
            (slots, 3 * channels),
            (8, CHUNK),
            (slots, channels),
            (8, atoms),
            (8, CHUNK),
            (8, CHUNK),
        ],
        turning
        + [(table, BF16)] * 2
        + [((PAIRS, BASIS * TA, channels), BF16)] * 2
        + [((PAIRS * COMPS * TA, BASIS * TA), F32)]
        + [((3 * channels, channels), BF16)] * 2,
        4,
        centre_tile, other_tile, pair_live, send_tiles,
        positions, features, species, from_low, from_high, radial_w, mix_w, species_w, out_row,
        flops=1 << 31,
    )
    low_one = shifted(grads_up, "domain", 1)
    low_two = shifted(grads_up, "domain", 2)
    high_one = shifted(grads_down, "domain", -1)
    high_two = shifted(grads_down, "domain", -2)

    total_count = 3.0 * atoms * lax.axis_size("domain") * lax.axis_size("batch")
    scale = jnp.full((1,), 2.0 / math.sqrt(total_count), F32)
    forces, keep, give, small, envdot, curl, both = call(
        tangent_kernel,
        "tangent",
        [
            (1, 3, atoms),
            (3 * channels, HALF),
            (3 * channels, HALF),
            (8, channels),
            (PAIRS * COMPS * TA, channels),
            (slots, channels),
            (16, CHUNK),
        ],
        turning
        + [(table, BF16)] * 2
        + [((BASIS * TA, channels), BF16)] * 2
        + [((PAIRS * COMPS * TA, channels), F32)]
        + [((2 * slots, 3 * channels), F32), ((2 * slots, channels), F32)],
        5,
        scale, centre_tile, other_tile, pair_live, send_tiles,
        ref_forces, from_low, from_high, own, low_one, low_two, high_one, high_two,
        rows, fsel, env, dinv, gate, curve, inv, radial_w, mix_w, out_row,
        flops=1 << 31,
    )

    def radial(p, after):
        return call(
            functools.partial(radial_kernel, p),
            "radial",
            [(BASIS, channels)],
            turning
            + [((BASIS * TA, COMPS * CHUNK), BF16)] * 2
            + [((COMPS * CHUNK, channels), BF16)] * 2
            + [((BASIS * TA, channels), F32)],
            3,
            centre_tile, other_tile, pair_live,
            both, fsel, env, envdot, dinv, curl, mix_w, after,
            flops=1 << 31,
        )[0]

    count = lax.axis_size("domain")
    bits = count.bit_length() - 1
    rows_mix = 3 * channels

    def partner(block, bit):
        return lax.ppermute(block, "domain", [(i, i ^ (1 << bit)) for i in range(count)])

    taken = shifted(give, "batch", 1)
    radial_0 = radial(0, both)
    rows_now, cut = halves(rows_mix)
    cuts = [cut]
    keep, give, token = call(
        functools.partial(first_kernel, cut), "first",
        [(rows_now, HALF), (rows_now, HALF), (8, CHUNK)], [], 0, keep, taken,
    )
    taken = partner(give, 0)
    radial_1 = radial(1, token)
    tiny = None
    for bit in range(1, bits):
        rows_now, cut = halves(rows_now)
        cuts.append(cut)
        outs = [(rows_now, HALF), (rows_now + SMALL, HALF), (SMALL, HALF)]
        if bit == 1:
            keep, give, tiny = call(
                functools.partial(second_kernel, bit, cut), "second", outs, [], 0,
                keep, taken, radial_0, radial_1, small,
            )
        else:
            keep, give, tiny = call(
                functools.partial(later_kernel, bit, cut), "later", outs, [], 0, keep, taken, tiny
            )
        taken = partner(give, bit)
    mine, tiny = call(last_kernel, "last", [(rows_now, HALF), (SMALL, HALF)], [], 0, keep, taken, tiny)
    for bit in range(bits - 1, 0, -1):
        if cuts[bit]:
            theirs = partner(mine, bit)
            rows_now = 2 * rows_now
            tail = bit == 1
            (mine,) = call(
                functools.partial(grow_kernel, bit, tail), "grow",
                [(rows_now + SMALL * tail, HALF)], [], 0, mine, theirs, tiny,
            )
    theirs = partner(mine, 0)
    (whole,) = call(grow_last_kernel, "grow_last", [(rows_mix + SMALL, HALF)], [], 0, mine, theirs)
    facing = shifted(whole, "batch", 1)
    mix, radial_sum, kinds, out = call(
        join_kernel,
        "join",
        [(rows_mix, channels), (BASIS, channels), (SPECIES, channels), (1, channels)],
        [],
        0,
        whole,
        facing,
    )
    return forces, radial_sum, mix, kinds, out.reshape(channels)


def solution(mesh):
    return jax.shard_map(
        on_device,
        mesh=mesh,
        in_specs=(
            P(("parts", "batch"), None, "domain"),
            P(("parts", "batch"), "domain", None),
            P(("parts", "batch"), "domain"),
            P(("parts", "batch"), None, "domain"),
            P(("parts", "batch"), "domain"),
            P(("parts", "batch"), "domain"),
            P(("parts", "batch"), "domain"),
            P(("parts", "batch"), "domain"),
            P(),
            P(),
            P(),
            P(),
        ),
        out_specs=(
            P(("parts", "batch"), None, "domain"),
            P("parts", None),
            P("parts", None),
            P("parts", None),
            P("parts"),
        ),
        check_vma=False,
    )
```

```python
import functools
import math

import jax
import jax.numpy as jnp
from jax import lax
from jax.experimental import pallas as pl
from jax.experimental.pallas import tpu as pltpu
from jax.sharding import PartitionSpec as P

TA = 64
SEND = 2
PAIRS = 2
COMPS = 9
BASIS = 8
SPECIES = 4
HALF = 128
CHUNK = 2 * TA

cutoff = 2.5
soften = 0.25
env_scale = 0.25
root_three = math.sqrt(3.0)
F32 = jnp.float32
BF16 = jnp.bfloat16
NN = (((1,), (0,)), ((), ()))
NT = (((1,), (1,)), ((), ()))
TN = (((0,), (0,)), ((), ()))
GROUP = (0, 1, 1, 1, 2, 2, 2, 2, 2)


def split(value):
    high = value.astype(BF16)
    return high, (value - high.astype(F32)).astype(BF16)


def product(left, right, dims):
    (lh, ll), (rh, rl) = left, right

    def one(x, y):
        return lax.dot_general(x, y, dims, preferred_element_type=F32)

    return one(lh, rh) + (one(lh, rl) + one(ll, rh))


def flag(condition):
    return jnp.where(condition, 1.0, 0.0).astype(F32)


def lane_half():
    lane = lax.broadcasted_iota(jnp.int32, (1, CHUNK), 1)
    low = flag(lane < TA)
    return low, 1.0 - low


def twice(chunk, half):
    low, high = lane_half()
    swapped = pltpu.roll(chunk, TA, 1)
    return chunk * low + swapped * high if half == 0 else swapped * low + chunk * high


def pick(chunks, position):
    total = None
    for q, chunk in enumerate(chunks):
        for half in range(2):
            term = twice(chunk, half) * flag(position == 2 * q + half)
            total = term if total is None else total + term
    return total


def paired(first, second):
    low, high = lane_half()
    return first * low + second * high


def chunk_mask(position, q):
    low, high = lane_half()
    return low * flag(position == 2 * q) + high * flag(position == 2 * q + 1)


def geometry(lane_rows, columns, sign, live, same):
    offset = [(row - column) * sign for row, column in zip(lane_rows, columns)]
    dist_sq = offset[0] * offset[0] + offset[1] * offset[1] + offset[2] * offset[2] + soften
    distance = jnp.sqrt(dist_sq)
    inverse = 1.0 / distance
    unit = [x * inverse for x in offset]
    row = lax.broadcasted_iota(jnp.int32, (TA, CHUNK), 0)
    lane = lax.broadcasted_iota(jnp.int32, (TA, CHUNK), 1)
    lane = jnp.where(lane >= TA, lane - TA, lane)
    mask = live * (1.0 - same * flag(row == lane))
    base = jnp.maximum(1.0 - dist_sq * (1.0 / (cutoff * cutoff)), 0.0)
    weight = base * base * base * mask * inverse
    slope = -(6.0 / (cutoff * cutoff)) * base * base * mask - weight * inverse
    angle = distance * (math.pi / cutoff)
    return unit, inverse, weight, slope, jnp.sin(angle), jnp.cos(angle)


def harmonics(v):
    x, y, z = v
    return [
        None,
        x,
        y,
        z,
        root_three * x * y,
        root_three * y * z,
        root_three * z * x,
        0.5 * root_three * (x * x - y * y),
        z * z - 0.5 * (x * x + y * y),
    ]


def harmonics_tangent(v, t):
    x, y, z = v
    a, b, c = t
    return [
        None,
        a,
        b,
        c,
        root_three * (a * y + x * b),
        root_three * (b * z + y * c),
        root_three * (c * x + z * a),
        root_three * (x * a - y * b),
        2.0 * z * c - (x * a + y * b),
    ]


def paired_orders(sine, cosine, weight, slope):
    low, high = lane_half()
    double_s, double_c = 2.0 * sine * cosine, 1.0 - 2.0 * sine * sine
    now_s = sine * low + double_s * high
    now_c = cosine * low + double_c * high
    old_s = -sine * low
    old_c = cosine * low + high
    values, slopes = [], []
    for k in range(BASIS // 2):
        order = ((2 * k + 1) * low + (2 * k + 2) * high) * (math.pi / cutoff)
        values.append(now_s * weight)
        slopes.append(now_c * (weight * order) + now_s * slope)
        now_s, old_s = 2.0 * double_c * now_s - old_s, now_s
        now_c, old_c = 2.0 * double_c * now_c - old_c, now_c
    return values, slopes


def single_orders(sine, cosine, weight, slope):
    now_s, now_c = sine, cosine
    old_s, old_c = jnp.zeros_like(sine), jnp.ones_like(cosine)
    values, slopes = [], []
    for n in range(1, BASIS + 1):
        values.append(now_s * weight)
        slopes.append(now_c * (weight * (n * math.pi / cutoff)) + now_s * slope)
        now_s, old_s = 2.0 * cosine * now_s - old_s, now_s
        now_c, old_c = 2.0 * cosine * now_c - old_c, now_c
    return values, slopes


def columns_of(rows, square, turned):
    square[...] = jnp.zeros_like(square)
    square[0 : rows.shape[0], :] = rows
    turned[...] = square[...].T


def pair_rows(first, p):
    return twice(first, p)


def radial_feat(feat, radial, p, high_ref, low_ref):
    own = feat[p * TA : (p + 1) * TA, :]
    for n in range(BASIS):
        hi, lo = split(own * radial[n : n + 1, :])
        high_ref[n * TA : (n + 1) * TA, :] = hi
        low_ref[n * TA : (n + 1) * TA, :] = lo


OTHER, CENTRE, LIVE, SAME, SHARED, SENT = 0, 2, 4, 6, 8, 9


def fetch(pairs, sems):
    copies = [pltpu.make_async_copy(src, dst, sems.at[i]) for i, (src, dst) in enumerate(pairs)]
    for copy in copies:
        copy.start()
    return copies


def gather_kernel(send, pos, feat, ref, to_low, to_high, token, send_v, pos_v, feat_v, ref_v, sems):
    copies = fetch([(send, send_v), (pos, pos_v), (ref, ref_v), (feat, feat_v)], sems)
    for copy in copies[:3]:
        copy.wait()
    low, high = lane_half()
    sent = [send_v[0:1, j : j + 1].astype(F32) for j in range(2 * SEND)]
    for out, first in ((to_low, 0), (to_high, SEND)):
        tiles = sent[first : first + SEND]
        out[SEND * TA :, :] = jnp.zeros((16, out.shape[1]), F32)
        for i in range(3):
            at = SEND * TA + i
            for lanes, source in ((slice(0, CHUNK), pos_v), (slice(CHUNK, 2 * CHUNK), ref_v)):
                chunks = [source[i, :, q * CHUNK : (q + 1) * CHUNK] for q in range(2)]
                out[at : at + 1, lanes] = paired(pick(chunks, tiles[0]), pick(chunks, tiles[1]))
        for other in range(2 * SEND):
            same = low * flag(sent[other] == tiles[0]) + high * flag(sent[other] == tiles[1])
            out[SEND * TA + 8 + other : SEND * TA + 9 + other, 0:CHUNK] = same
    token[...] = jnp.zeros_like(token)
    copies[3].wait()
    for out, first in ((to_low, 0), (to_high, SEND)):
        for j in range(SEND):
            out[j * TA : (j + 1) * TA, :] = pick_rows(feat_v.at[0], sent[first + j], 0)


def pick_rows(ref, position, first):
    total = None
    for t in range(ref.shape[0] // TA):
        term = ref[t * TA : (t + 1) * TA, :] * flag(position == float(first + t))
        total = term if total is None else total + term
    return total


def stage_kernel(
    centre, other, live, send, pos, ref, species, feat, radial_w, mix_w, species_w, out_w, after,
    flags, atoms, own_feat, weights, mh, ml,
    centre_v, other_v, live_v, send_v, pos_v, ref_v, species_v, radial_v, mix_v, species_w_v, out_v, sems,
):
    copies = fetch(
        [
            (centre, centre_v), (other, other_v), (live, live_v), (send, send_v), (pos, pos_v), (ref, ref_v),
            (species, species_v), (radial_w, radial_v), (species_w, species_w_v), (out_w, out_v),
            (feat.at[0], own_feat), (mix_w, mix_v),
        ],
        sems,
    )
    for copy in copies[:-1]:
        copy.wait()
    flags[...] = jnp.zeros_like(flags)
    centres = [centre_v[0:1, p : p + 1].astype(F32) for p in range(PAIRS)]
    others = [other_v[0:1, p : p + 1].astype(F32) for p in range(PAIRS)]
    for p in range(PAIRS):
        for row, value in (
            (OTHER, others[p]),
            (CENTRE, centres[p]),
            (LIVE, live_v[0:1, p : p + 1].astype(F32)),
            (SAME, flag(others[p] == centres[p] + SEND)),
        ):
            flags[row + p : row + p + 1, :] = jnp.broadcast_to(value, (1, CHUNK))
    flags[SHARED : SHARED + 1, :] = jnp.broadcast_to(flag(centres[0] == centres[1]), (1, CHUNK))
    for j in range(2 * SEND):
        value = send_v[0:1, j : j + 1].astype(F32)
        flags[SENT + j : SENT + j + 1, :] = jnp.broadcast_to(value, (1, CHUNK))
    atoms[...] = jnp.zeros_like(atoms)
    for i in range(3):
        atoms[i : i + 1, :] = pos_v[i]
        atoms[4 + i : 5 + i, :] = ref_v[i]
    atoms[3:4, :] = species_v[...].astype(F32)
    weights[...] = jnp.zeros_like(weights)
    weights[0:BASIS, :] = radial_v[...]
    weights[BASIS : BASIS + SPECIES, :] = species_w_v[...]
    weights[BASIS + SPECIES : BASIS + SPECIES + 1, :] = out_v[...]
    copies[-1].wait()
    hi, lo = split(mix_v[...])
    mh[...] = hi
    ml[...] = lo


def force_kernel(
    flags, atoms, feat, weights, mh, ml, from_low, from_high,
    env, dinv, gate, curve, inv, rows, fsel, own, to_high, to_low, shape_store, xh, xl,
    square, turned, th, tl, eh, el, raw, back,
):
    ghost = SEND * TA
    chunks = [
        from_low[ghost : ghost + 3, 0:CHUNK],
        atoms[0:3, 0:CHUNK],
        atoms[0:3, CHUNK:],
        from_high[ghost : ghost + 3, 0:CHUNK],
    ]
    kinds = [atoms[3:4, q * CHUNK : (q + 1) * CHUNK] for q in range(2)]

    def number(row):
        return flags[row : row + 1, :]

    centres = [number(CENTRE + p) for p in range(PAIRS)]
    others = [number(OTHER + p) for p in range(PAIRS)]
    shared = flags[SHARED : SHARED + 1, 0:1]
    rows[...] = jnp.zeros_like(rows)
    rows[0:3, :] = paired(*(pick(chunks, others[p]) for p in range(PAIRS)))
    rows[3:6, :] = paired(*(pick(chunks[1:3], centres[p]) for p in range(PAIRS)))
    rows[6:7, :] = paired(*(pick(kinds, centres[p]) for p in range(PAIRS)))
    columns_of(rows[...], square, turned)

    for p in range(PAIRS):
        o = flags[OTHER + p : OTHER + p + 1, 0:1]
        fsel[p * TA : (p + 1) * TA, :] = (
            pick_rows(from_low.at[0:ghost], o, 0)
            + pick_rows(feat, o, SEND)
            + pick_rows(from_high.at[0:ghost], o, SEND + 4)
        )

    shapes = []
    for p in range(PAIRS):
        lane_rows = [twice(rows[i : i + 1, :], p) for i in range(3)]
        columns = [turned[p * TA : (p + 1) * TA, 3 + i : 4 + i] for i in range(3)]
        unit, inverse, weight, slope, sine, cosine = geometry(
            lane_rows, columns, 1.0, number(LIVE + p), number(SAME + p)
        )
        angular = harmonics(unit)
        values, slopes = paired_orders(sine, cosine, weight, slope)
        shapes.append((unit, inverse, angular, values, slopes))
        for i, part in enumerate(unit + [inverse] + values + slopes):
            shape_store[p, i] = part
        for m in range(COMPS):
            for k in range(BASIS // 2):
                entry = values[k] if m == 0 else angular[m] * values[k]
                hi, lo = split(entry)
                th[p, m * TA : (m + 1) * TA, k * CHUNK : (k + 1) * CHUNK] = hi
                tl[p, m * TA : (m + 1) * TA, k * CHUNK : (k + 1) * CHUNK] = lo
        radial_feat(fsel, weights, p, xh.at[p], xl.at[p])
        raw[p * COMPS * TA : (p + 1) * COMPS * TA, :] = product((th[p], tl[p]), (xh[p], xl[p]), NN)

    for m in range(COMPS):
        first = raw[m * TA : (m + 1) * TA, :]
        second = raw[(COMPS + m) * TA : (COMPS + m + 1) * TA, :]
        env[m * TA : (m + 1) * TA, :] = env_scale * (first + shared * second)
        env[(COMPS + m) * TA : (COMPS + m + 1) * TA, :] = env_scale * (second + shared * first)
    for p in range(PAIRS):
        sums = [None] * 3
        for m in range(COMPS):
            block = env[(p * COMPS + m) * TA : (p * COMPS + m + 1) * TA, :]
            sums[GROUP[m]] = block * block if sums[GROUP[m]] is None else sums[GROUP[m]] + block * block
        for g in range(3):
            inv[p * TA : (p + 1) * TA, g * 256 : (g + 1) * 256] = sums[g]
    hidden = product(split(inv[...]), (mh[...], ml[...]), NN)
    kind = turned[:, 6:7]
    for s in range(SPECIES):
        hidden = hidden + flag(kind == float(s)) * weights[BASIS + s : BASIS + s + 1, :]
    out_row = weights[BASIS + SPECIES : BASIS + SPECIES + 1, :]
    sigma = 1.0 / (1.0 + jnp.exp(-hidden))
    first_order = sigma * (1.0 + hidden * (1.0 - sigma))
    gate[...] = first_order
    curve[...] = sigma * (1.0 - sigma) * (2.0 + hidden * (1.0 - 2.0 * sigma)) * out_row
    dinv[...] = product(split(first_order * out_row), (mh[...], ml[...]), NT)

    tile_grads = [jnp.zeros((3, CHUNK), F32) for _ in range(4)]
    for p in range(PAIRS):
        unit, inverse, angular, values, slopes = shapes[p]
        for m in range(COMPS):
            block = env[(p * COMPS + m) * TA : (p * COMPS + m + 1) * TA, :]
            part = dinv[p * TA : (p + 1) * TA, GROUP[m] * 256 : (GROUP[m] + 1) * 256]
            hi, lo = split((2.0 * env_scale) * block * part)
            eh[p, m * TA : (m + 1) * TA, :] = hi
            el[p, m * TA : (m + 1) * TA, :] = lo
        back[p] = product((eh[p], el[p]), (xh[p], xl[p]), NT)
        d_radius = None
        d_angular = []
        for m in range(COMPS):
            along, across = None, None
            for k in range(BASIS // 2):
                block = back[p, m * TA : (m + 1) * TA, k * CHUNK : (k + 1) * CHUNK]
                along = block * slopes[k] if along is None else along + block * slopes[k]
                across = block * values[k] if across is None else across + block * values[k]
            d_angular.append(across)
            term = along if m == 0 else along * angular[m]
            d_radius = term if d_radius is None else d_radius + term
        x, y, z = unit
        g = d_angular
        toward = [
            g[1] + root_three * (y * g[4] + z * g[6] + x * g[7]) - x * g[8],
            g[2] + root_three * (x * g[4] + z * g[5] - y * g[7]) - y * g[8],
            g[3] + root_three * (y * g[5] + x * g[6]) + 2.0 * (z * g[8]),
        ]
        radial_part = d_radius - inverse * (toward[0] * x + toward[1] * y + toward[2] * z)
        for i in range(3):
            d_offset = inverse * toward[i] + unit[i] * radial_part
            summed = jnp.sum(d_offset, axis=0, keepdims=True)
            other_row = summed + pltpu.roll(summed, TA, 1)
            square[0:TA, :] = d_offset
            square[TA:, :] = d_offset
            centre_row = -jnp.sum(square[...].T, axis=0, keepdims=True)
            component = flag(lax.broadcasted_iota(jnp.int32, (3, CHUNK), 0) == i)
            for q in range(4):
                at = chunk_mask(others[p], q) * other_row
                if q in (1, 2):
                    at = at + chunk_mask(centres[p] + SEND, q) * centre_row
                tile_grads[q] = tile_grads[q] + at * component
    own[...] = jnp.zeros_like(own)
    own[0:3, 0:CHUNK] = tile_grads[1]
    own[0:3, CHUNK:] = tile_grads[2]
    own[3:6, 0:CHUNK] = tile_grads[0]
    own[3:6, CHUNK:] = tile_grads[3]
    for out, first, ghost_grad in ((to_low, 0, tile_grads[0]), (to_high, SEND, tile_grads[3])):
        out[...] = jnp.zeros_like(out)
        out[0:3, :] = paired(*(pick(tile_grads[1:3], number(SENT + first + j)) for j in range(SEND)))
        out[3:6, :] = ghost_grad


def tangent_kernel(
    scale, flags, atoms, weights, mh, ml, from_low, from_high, own, low_one, low_two, high_one, high_two,
    rows, env, gate, curve, inv, shape_store, xh, xl,
    forces, keep, give, small, envdot, curl, both,
    square, turned, th, tl, raw, left, right,
):
    ghost = SEND * TA
    def number(row):
        return flags[row : row + 1, :]

    centres = [number(CENTRE + p) for p in range(PAIRS)]
    others = [number(OTHER + p) for p in range(PAIRS)]
    shared = flags[SHARED : SHARED + 1, 0:1]
    mine = [own[0:3, 0:CHUNK], own[0:3, CHUNK:]]
    arrived = [twice(low_one[3:6, :], j) for j in range(SEND)]
    arrived += [twice(high_one[3:6, :], j) for j in range(SEND)]
    for j in range(2 * SEND):
        for q in range(2):
            mine[q] = mine[q] + chunk_mask(number(SENT + j), q) * arrived[j]
    below = low_one[0:3, :]
    above = high_one[0:3, :]
    to_below = [twice(low_two[3:6, :], j) for j in range(SEND)]
    to_below += [twice(own[3:6, 0:CHUNK], j) for j in range(SEND)]
    to_above = [twice(own[3:6, CHUNK:], j) for j in range(SEND)]
    to_above += [twice(high_two[3:6, :], j) for j in range(SEND)]
    for j in range(2 * SEND):
        below = below + from_low[ghost + 8 + j : ghost + 9 + j, 0:CHUNK] * to_below[j]
        above = above + from_high[ghost + 8 + j : ghost + 9 + j, 0:CHUNK] * to_above[j]
    for q in range(2):
        for i in range(3):
            forces[i, :, q * CHUNK : (q + 1) * CHUNK] = -mine[q][i : i + 1, :]
    error = [
        below + from_low[ghost : ghost + 3, CHUNK:],
        mine[0] + atoms[4:7, 0:CHUNK],
        mine[1] + atoms[4:7, CHUNK:],
        above + from_high[ghost : ghost + 3, CHUNK:],
    ]
    error = [part * scale for part in error]
    both[...] = jnp.zeros_like(both)
    both[0:8, :] = rows[...]
    both[8:11, :] = paired(*(pick(error, others[p]) for p in range(PAIRS)))
    both[11:14, :] = paired(*(pick(error[1:3], centres[p]) for p in range(PAIRS)))
    columns_of(both[...], square, turned)

    for p in range(PAIRS):
        lane_move = [twice(both[8 + i : 9 + i, :], p) for i in range(3)]
        column_move = [turned[p * TA : (p + 1) * TA, 11 + i : 12 + i] for i in range(3)]
        unit = [shape_store[p, i] for i in range(3)]
        inverse = shape_store[p, 3]
        values = [shape_store[p, 4 + k] for k in range(BASIS // 2)]
        slopes = [shape_store[p, 8 + k] for k in range(BASIS // 2)]
        move = [a - b for a, b in zip(lane_move, column_move)]
        stretch = unit[0] * move[0] + unit[1] * move[1] + unit[2] * move[2]
        turn = [(m - v * stretch) * inverse for m, v in zip(move, unit)]
        angular, turning = harmonics(unit), harmonics_tangent(unit, turn)
        slopes = [s * stretch for s in slopes]
        for m in range(COMPS):
            for k in range(BASIS // 2):
                entry = slopes[k] if m == 0 else angular[m] * slopes[k] + turning[m] * values[k]
                hi, lo = split(entry)
                th[p, m * TA : (m + 1) * TA, k * CHUNK : (k + 1) * CHUNK] = hi
                tl[p, m * TA : (m + 1) * TA, k * CHUNK : (k + 1) * CHUNK] = lo
        raw[p * COMPS * TA : (p + 1) * COMPS * TA, :] = product((th[p], tl[p]), (xh[p], xl[p]), NN)

    for m in range(COMPS):
        first = raw[m * TA : (m + 1) * TA, :]
        second = raw[(COMPS + m) * TA : (COMPS + m + 1) * TA, :]
        envdot[m * TA : (m + 1) * TA, :] = env_scale * (first + shared * second)
        envdot[(COMPS + m) * TA : (COMPS + m + 1) * TA, :] = env_scale * (second + shared * first)
    invdot = left
    half = PAIRS * TA
    for p in range(PAIRS):
        sums = [None] * 3
        for m in range(COMPS):
            at = slice((p * COMPS + m) * TA, (p * COMPS + m + 1) * TA)
            term = 2.0 * env[at, :] * envdot[at, :]
            sums[GROUP[m]] = term if sums[GROUP[m]] is None else sums[GROUP[m]] + term
        for g in range(3):
            invdot[half + p * TA : half + (p + 1) * TA, g * 256 : (g + 1) * 256] = sums[g]
    invdot[0:half, :] = inv[...]
    hidden_move = product(split(invdot[half:, :]), (mh[...], ml[...]), NN)
    bend = curve[...] * hidden_move
    curl[...] = bend
    once = 1.0 - shared * flag(lax.broadcasted_iota(jnp.int32, (half, 1), 0) >= TA)
    right[0:half, :] = bend * once
    right[half:, :] = gate[...] * weights[BASIS + SPECIES : BASIS + SPECIES + 1, :] * once
    core = lax.axis_index("batch")
    left_parts = split(left[...])
    for out, part in ((keep, core), (give, 1 - core)):
        lanes = pl.ds(pl.multiple_of(part * HALF, HALF), HALF)
        out[...] = product(left_parts, split(right[:, lanes]), TN)
    small[...] = jnp.zeros_like(small)
    kind = turned[:, 6:7]
    for s in range(SPECIES):
        small[s : s + 1, :] = jnp.sum(right[0:half, :] * flag(kind == float(s)), axis=0, keepdims=True)
    small[SPECIES : SPECIES + 1, :] = jnp.sum(gate[...] * hidden_move * once, axis=0, keepdims=True)


def radial_kernel(
    p, flags, both, fsel, env, envdot, dinv, curl, mh, ml, after,
    grad_radial,
    square, turned, lh, ll, gh, gl, raw,
):
    low, high = lane_half()
    columns_of(both[...], square, turned)
    here = slice(p * TA, (p + 1) * TA)
    turn_inv = product(split(curl[here, :]), (mh[...], ml[...]), NT)
    lane_rows = [twice(both[3 + i : 4 + i, :], p) for i in range(3)]
    lane_move = [twice(both[11 + i : 12 + i, :], p) for i in range(3)]
    columns = [turned[here, i : i + 1] for i in range(3)]
    column_move = [turned[here, 8 + i : 9 + i] for i in range(3)]
    unit, inverse, weight, slope, sine, cosine = geometry(
        lane_rows, columns, -1.0, flags[LIVE + p : LIVE + p + 1, :], flags[SAME + p : SAME + p + 1, :]
    )
    move = [b - a for a, b in zip(lane_move, column_move)]
    stretch = unit[0] * move[0] + unit[1] * move[1] + unit[2] * move[2]
    turn = [(m - v * stretch) * inverse for m, v in zip(move, unit)]
    angular, turning = harmonics(unit), harmonics_tangent(unit, turn)
    values, slopes = single_orders(sine, cosine, weight, slope)
    for m in range(COMPS):
        if m == 0:
            on_value, on_slope = low, high * stretch
        else:
            on_value = angular[m] * low + turning[m] * high
            on_slope = angular[m] * high * stretch
        for n in range(BASIS):
            hi, lo = split(on_value * values[n] + on_slope * slopes[n])
            lh[n * TA : (n + 1) * TA, m * CHUNK : (m + 1) * CHUNK] = hi
            ll[n * TA : (n + 1) * TA, m * CHUNK : (m + 1) * CHUNK] = lo
        at = slice((p * COMPS + m) * TA, (p * COMPS + m + 1) * TA)
        group = slice(GROUP[m] * 256, (GROUP[m] + 1) * 256)
        steady = (2.0 * env_scale) * dinv[here, group]
        bent = (2.0 * env_scale) * turn_inv[:, group]
        hi, lo = split(env[at, :] * bent + envdot[at, :] * steady)
        gh[m * CHUNK : m * CHUNK + TA, :] = hi
        gl[m * CHUNK : m * CHUNK + TA, :] = lo
        hi, lo = split(env[at, :] * steady)
        gh[m * CHUNK + TA : (m + 1) * CHUNK, :] = hi
        gl[m * CHUNK + TA : (m + 1) * CHUNK, :] = lo
    raw[...] = product((lh[...], ll[...]), (gh[...], gl[...]), NN)
    for n in range(BASIS):
        grad_radial[n : n + 1, :] = jnp.sum(
            raw[n * TA : (n + 1) * TA, :] * fsel[here, :], axis=0, keepdims=True
        )


SMALL = 32
LEVEL = 3


def place(shift, width):
    return lax.bitwise_and(lax.shift_right_logical(lax.axis_index("domain"), shift), width - 1)


def block_of(part, rows):
    return pl.ds(pl.multiple_of(part * rows, 8), rows)


def total_of(refs, at):
    total = refs[0][at, :]
    for ref in refs[1:]:
        total = total + ref[at, :]
    return total


def spread_kernel(shift, width, count, *refs):
    terms, outs = refs[:count], refs[count:]
    me = place(shift, width)
    for k in range(width - 1, -1, -1):
        outs[k][...] = total_of(terms, block_of(lax.bitwise_xor(me, k), outs[k].shape[0]))


def tail_kernel(count, *refs):
    terms, (radial_0, radial_1, small, out) = refs[:count], refs[count:]
    rows = terms[0].shape[0]
    out[0:rows, :] = total_of(terms, slice(0, rows))
    for h in range(2):
        lanes = slice(h * HALF, (h + 1) * HALF)
        at = rows + 16 * h
        out[at : at + 8, :] = radial_0[:, lanes] + radial_1[:, lanes]
        out[at + 8 : at + 16, :] = small[:, lanes]


def grow_kernel(shift, width, *refs):
    parts, out, tails = refs[:width], refs[width], refs[width + 1]
    rows = parts[0].shape[0] - SMALL
    me = place(shift, width)
    for k, ref in enumerate(parts):
        to = lax.bitwise_xor(me, k)
        out[block_of(to, rows), :] = ref[0:rows, :]
        tails[block_of(to, SMALL), :] = ref[rows:, :]
    total = tails[0:SMALL, :]
    for j in range(1, width):
        total = total + tails[j * SMALL : (j + 1) * SMALL, :]
    out[width * rows :, :] = total


def whole_kernel(shift, width, *refs):
    parts, out, held = refs[:width], refs[width], refs[width + 1]
    rows = parts[0].shape[0]
    me = place(shift, width)
    for k, ref in enumerate(parts):
        held[block_of(lax.bitwise_xor(me, k), rows), :] = ref[...]
    out[...] = total_of([held.at[j * rows : (j + 1) * rows] for j in range(width)], slice(0, rows))


def join_kernel(whole, facing, mix, radial, kinds, out):
    rows = mix.shape[0]
    core = lax.axis_index("batch")
    for ref, part in ((whole, core), (facing, 1 - core)):
        mix[:, pl.ds(pl.multiple_of(part * HALF, HALF), HALF)] = ref[0:rows, :]
    for h in range(2):
        lanes = slice(h * HALF, (h + 1) * HALF)
        both = whole[rows + 16 * h : rows + 16 * h + 16, :] + facing[rows + 16 * h : rows + 16 * h + 16, :]
        radial[:, lanes] = both[0:BASIS]
        kinds[:, lanes] = both[BASIS : BASIS + SPECIES]
        out[:, lanes] = both[BASIS + SPECIES : BASIS + SPECIES + 1]


def spec(space):
    return pl.BlockSpec(memory_space=space)


def call(kernel, name, outs, scratch, *operands, space=pltpu.VMEM, after=(), flops=0):
    if space is pltpu.HBM:
        operands = [pltpu.with_memory_space_constraint(operand, space) for operand in operands]
    outs = [out if len(out) == 2 and isinstance(out[0], tuple) else (out, F32) for out in outs]
    return pl.pallas_call(
        kernel,
        name=name,
        out_shape=[jax.ShapeDtypeStruct(*out) for out in outs],
        in_specs=[spec(space)] * len(operands) + [spec(pltpu.VMEM)] * len(after),
        out_specs=[spec(pltpu.VMEM)] * len(outs),
        scratch_shapes=[pltpu.VMEM(*item) if isinstance(item, tuple) else item for item in scratch],
        compiler_params=pltpu.CompilerParams(vmem_limit_bytes=28 * 1024 * 1024),
        cost_estimate=pl.CostEstimate(flops=flops, bytes_accessed=1 << 20, transcendentals=0),
    )(*operands, *after)


def shifted(block, axis, by):
    count = lax.axis_size(axis)
    return lax.ppermute(block, axis, [(i, (i + by) % count) for i in range(count)])


def partner(block, mask):
    return lax.ppermute(block, "domain", [(i, i ^ mask) for i in range(lax.axis_size("domain"))])


def on_device(
    positions,
    features,
    species,
    ref_forces,
    centre_tile,
    other_tile,
    pair_live,
    send_tiles,
    radial_w,
    mix_w,
    species_w,
    out_w,
):
    atoms_here = positions.shape[2]
    channels = features.shape[2]
    table = (COMPS * TA, BASIS * TA)
    sent = (SEND * TA + 16, channels)
    slots = PAIRS * TA
    line = (3, 1, atoms_here)
    turning = [((CHUNK, CHUNK), F32)] * 2
    out_row = out_w.reshape(1, channels)
    positions = positions.transpose(1, 0, 2)
    ref_forces = ref_forces.transpose(1, 0, 2)
    ints = [((1, n), jnp.int32) for n in (PAIRS, PAIRS, PAIRS, 2 * SEND)]

    to_low, to_high, token = call(
        gather_kernel,
        "gather",
        [sent, sent, (8, CHUNK)],
        [
            ints[3],
            (line, F32),
            ((1, atoms_here, channels), F32),
            (line, F32),
            pltpu.SemaphoreType.DMA((4,)),
        ],
        send_tiles, positions, features, ref_forces,
        space=pltpu.HBM,
    )
    from_low = shifted(to_high, "domain", 1)
    from_high = shifted(to_low, "domain", -1)
    flags, atoms, own_feat, weights, mh, ml = call(
        stage_kernel,
        "stage",
        [
            (16, CHUNK),
            (8, atoms_here),
            (atoms_here, channels),
            (16, channels),
            (mix_w.shape, BF16),
            (mix_w.shape, BF16),
        ],
        ints
        + [(line, F32), (line, F32), ((1, atoms_here), jnp.int32)]
        + [(radial_w.shape, F32), (mix_w.shape, F32), (species_w.shape, F32), (out_row.shape, F32)]
        + [pltpu.SemaphoreType.DMA((12,))],
        centre_tile, other_tile, pair_live, send_tiles, positions, ref_forces, species, features,
        radial_w, mix_w, species_w, out_row,
        space=pltpu.HBM,
        after=(token,),
    )

    factors = (PAIRS, BASIS * TA, channels)
    env, dinv, gate, curve, inv, rows, fsel, own, grads_up, grads_down, shape_store, xh, xl = call(
        force_kernel,
        "force",
        [
            (PAIRS * COMPS * TA, channels),
            (slots, 3 * channels),
            (slots, channels),
            (slots, channels),
            (slots, 3 * channels),
            (8, CHUNK),
            (slots, channels),
            (8, atoms_here),
            (8, CHUNK),
            (8, CHUNK),
            (PAIRS, 4 + BASIS, TA, CHUNK),
            (factors, BF16),
            (factors, BF16),
        ],
        turning
        + [((PAIRS, *table), BF16)] * 2
        + [((PAIRS, COMPS * TA, channels), BF16)] * 2
        + [((PAIRS * COMPS * TA, channels), F32), ((PAIRS, *table), F32)],
        flags, atoms, own_feat, weights, mh, ml, from_low, from_high,
        flops=1 << 31,
    )
    low_one = shifted(grads_up, "domain", 1)
    low_two = shifted(grads_up, "domain", 2)
    high_one = shifted(grads_down, "domain", -1)
    high_two = shifted(grads_down, "domain", -2)

    rows_mix = 3 * channels
    total_count = 3.0 * atoms_here * lax.axis_size("domain") * lax.axis_size("batch")
    forces, keep, give, small, envdot, curl, both = call(
        functools.partial(tangent_kernel, 2.0 / math.sqrt(total_count)),
        "tangent",
        [
            line,
            (rows_mix, HALF),
            (rows_mix, HALF),
            (8, channels),
            (PAIRS * COMPS * TA, channels),
            (slots, channels),
            (16, CHUNK),
        ],
        turning
        + [((PAIRS, *table), BF16)] * 2
        + [((PAIRS * COMPS * TA, channels), F32)]
        + [((2 * slots, 3 * channels), F32), ((2 * slots, channels), F32)],
        flags, atoms, weights, mh, ml, from_low, from_high, own, low_one, low_two, high_one, high_two,
        rows, env, gate, curve, inv, shape_store, xh, xl,
        flops=1 << 31,
    )

    def radial(p, after):
        return call(
            functools.partial(radial_kernel, p),
            "radial",
            [(BASIS, channels)],
            turning
            + [((BASIS * TA, COMPS * CHUNK), BF16)] * 2
            + [((COMPS * CHUNK, channels), BF16)] * 2
            + [((BASIS * TA, channels), F32)],
            flags, both, fsel, env, envdot, dinv, curl, mh, ml, after,
            flops=1 << 31,
        )[0]

    bits = lax.axis_size("domain").bit_length() - 1
    levels = [(shift, 1 << min(LEVEL, bits - shift)) for shift in range(0, bits, LEVEL)]
    terms = [keep, shifted(give, "batch", 1)]
    radials = [radial(0, both)]
    rows_now = rows_mix
    cut = []
    for shift, width in levels:
        if rows_now % (8 * width):
            break
        rows_now //= width
        cut.append((shift, width))
        blocks = call(
            functools.partial(spread_kernel, shift, width, len(terms)),
            "spread", [(rows_now, HALF)] * width, [], *terms,
        )
        terms = [blocks[0]] + [partner(blocks[k], k << shift) for k in range(width - 1, 0, -1)]
        if len(radials) < PAIRS:
            radials.append(radial(1, blocks[0]))
    (mine,) = call(
        functools.partial(tail_kernel, len(terms)),
        "tail", [(rows_now + SMALL, HALF)], [], *terms, *radials, small,
    )
    for shift, width in levels[len(cut) :]:
        parts = [mine] + [partner(mine, k << shift) for k in range(1, width)]
        (mine,) = call(
            functools.partial(whole_kernel, shift, width),
            "whole", [(rows_now + SMALL, HALF)], [((width * (rows_now + SMALL), HALF), F32)], *parts,
        )
    for shift, width in reversed(cut):
        parts = [mine] + [partner(mine, k << shift) for k in range(1, width)]
        rows_now *= width
        (mine,) = call(
            functools.partial(grow_kernel, shift, width),
            "grow", [(rows_now + SMALL, HALF)], [((width * SMALL, HALF), F32)], *parts,
        )
    facing = shifted(mine, "batch", 1)
    mix, radial_sum, kinds, out = call(
        join_kernel,
        "join",
        [(rows_mix, channels), (BASIS, channels), (SPECIES, channels), (1, channels)],
        [],
        mine,
        facing,
    )
    return forces.transpose(1, 0, 2), radial_sum, mix, kinds, out.reshape(channels)


def solution(mesh):
    return jax.shard_map(
        on_device,
        mesh=mesh,
        in_specs=(
            P(("parts", "batch"), None, "domain"),
            P(("parts", "batch"), "domain", None),
            P(("parts", "batch"), "domain"),
            P(("parts", "batch"), None, "domain"),
            P(("parts", "batch"), "domain"),
            P(("parts", "batch"), "domain"),
            P(("parts", "batch"), "domain"),
            P(("parts", "batch"), "domain"),
            P(),
            P(),
            P(),
            P(),
        ),
        out_specs=(
            P(("parts", "batch"), None, "domain"),
            P("parts", None),
            P("parts", None),
            P("parts", None),
            P("parts"),
        ),
        check_vma=False,
    )
```

```python
import functools
import math

import jax
import jax.numpy as jnp
from jax import lax
from jax.experimental import pallas as pl
from jax.experimental.pallas import tpu as pltpu
from jax.sharding import PartitionSpec as P

TA = 64
SEND = 2
PAIRS = 2
COMPS = 9
BASIS = 8
SPECIES = 4
HALF = 128
CHUNK = 2 * TA

cutoff = 2.5
soften = 0.25
env_scale = 0.25
root_three = math.sqrt(3.0)
F32 = jnp.float32
BF16 = jnp.bfloat16
NN = (((1,), (0,)), ((), ()))
NT = (((1,), (1,)), ((), ()))
TN = (((0,), (0,)), ((), ()))
GROUP = (0, 1, 1, 1, 2, 2, 2, 2, 2)


def split(value):
    high = value.astype(BF16)
    return high, (value - high.astype(F32)).astype(BF16)


def product(left, right, dims):
    (lh, ll), (rh, rl) = left, right

    def one(x, y):
        return lax.dot_general(x, y, dims, preferred_element_type=F32)

    return one(lh, rh) + (one(lh, rl) + one(ll, rh))


def flag(condition):
    return jnp.where(condition, 1.0, 0.0).astype(F32)


def place(shift, width):
    return lax.bitwise_and(lax.shift_right_logical(lax.axis_index("domain"), shift), width - 1)


def lane_half():
    lane = lax.broadcasted_iota(jnp.int32, (1, CHUNK), 1)
    low = flag(lane < TA)
    return low, 1.0 - low


def twice(chunk, half):
    low, high = lane_half()
    swapped = pltpu.roll(chunk, TA, 1)
    return chunk * low + swapped * high if half == 0 else swapped * low + chunk * high


def pick(chunks, position):
    total = None
    for q, chunk in enumerate(chunks):
        for half in range(2):
            term = twice(chunk, half) * flag(position == 2 * q + half)
            total = term if total is None else total + term
    return total


def paired(first, second):
    low, high = lane_half()
    return first * low + second * high


def chunk_mask(position, q):
    low, high = lane_half()
    return low * flag(position == 2 * q) + high * flag(position == 2 * q + 1)


def geometry(lane_rows, columns, sign, live, same):
    offset = [(row - column) * sign for row, column in zip(lane_rows, columns)]
    dist_sq = offset[0] * offset[0] + offset[1] * offset[1] + offset[2] * offset[2] + soften
    distance = jnp.sqrt(dist_sq)
    inverse = 1.0 / distance
    unit = [x * inverse for x in offset]
    row = lax.broadcasted_iota(jnp.int32, (TA, CHUNK), 0)
    lane = lax.broadcasted_iota(jnp.int32, (TA, CHUNK), 1)
    lane = jnp.where(lane >= TA, lane - TA, lane)
    mask = live * (1.0 - same * flag(row == lane))
    base = jnp.maximum(1.0 - dist_sq * (1.0 / (cutoff * cutoff)), 0.0)
    weight = base * base * base * mask * inverse
    slope = -(6.0 / (cutoff * cutoff)) * base * base * mask - weight * inverse
    angle = distance * (math.pi / cutoff)
    return unit, inverse, weight, slope, jnp.sin(angle), jnp.cos(angle)


def harmonics(v):
    x, y, z = v
    return [
        None,
        x,
        y,
        z,
        root_three * x * y,
        root_three * y * z,
        root_three * z * x,
        0.5 * root_three * (x * x - y * y),
        z * z - 0.5 * (x * x + y * y),
    ]


def harmonics_tangent(v, t):
    x, y, z = v
    a, b, c = t
    return [
        None,
        a,
        b,
        c,
        root_three * (a * y + x * b),
        root_three * (b * z + y * c),
        root_three * (c * x + z * a),
        root_three * (x * a - y * b),
        2.0 * z * c - (x * a + y * b),
    ]


def paired_orders(sine, cosine, weight, slope):
    low, high = lane_half()
    double_s, double_c = 2.0 * sine * cosine, 1.0 - 2.0 * sine * sine
    now_s = sine * low + double_s * high
    now_c = cosine * low + double_c * high
    old_s = -sine * low
    old_c = cosine * low + high
    values, slopes = [], []
    for k in range(BASIS // 2):
        order = ((2 * k + 1) * low + (2 * k + 2) * high) * (math.pi / cutoff)
        values.append(now_s * weight)
        slopes.append(now_c * (weight * order) + now_s * slope)
        now_s, old_s = 2.0 * double_c * now_s - old_s, now_s
        now_c, old_c = 2.0 * double_c * now_c - old_c, now_c
    return values, slopes


def single_orders(sine, cosine, weight, slope):
    now_s, now_c = sine, cosine
    old_s, old_c = jnp.zeros_like(sine), jnp.ones_like(cosine)
    values, slopes = [], []
    for n in range(1, BASIS + 1):
        values.append(now_s * weight)
        slopes.append(now_c * (weight * (n * math.pi / cutoff)) + now_s * slope)
        now_s, old_s = 2.0 * cosine * now_s - old_s, now_s
        now_c, old_c = 2.0 * cosine * now_c - old_c, now_c
    return values, slopes


def columns_of(rows, square, turned):
    square[...] = jnp.zeros_like(square)
    square[0 : rows.shape[0], :] = rows
    turned[...] = square[...].T


def pair_rows(first, p):
    return twice(first, p)


def radial_feat(feat, radial, p, high_ref, low_ref):
    own = feat[p * TA : (p + 1) * TA, :]
    for n in range(BASIS):
        hi, lo = split(own * radial[n : n + 1, :])
        high_ref[n * TA : (n + 1) * TA, :] = hi
        low_ref[n * TA : (n + 1) * TA, :] = lo


OTHER, CENTRE, LIVE, SAME, SHARED, SENT = 0, 2, 4, 6, 8, 9
GHOST_ROWS = 8


def fetch(pairs, sems):
    copies = [pltpu.make_async_copy(src, dst, sems.at[i]) for i, (src, dst) in enumerate(pairs)]
    for copy in copies:
        copy.start()
    return copies


def upward(shift):
    return 1.0 - flag(place(shift, 2) == 1)


def either(choice, first, second):
    return first * choice + second * (1.0 - choice)


def gather_kernel(send, pos, feat, ref, to_first, to_second, token, send_v, pos_v, feat_v, ref_v, sems):
    copies = fetch([(send, send_v), (pos, pos_v), (ref, ref_v), (feat, feat_v)], sems)
    for copy in copies[:3]:
        copy.wait()
    low, high = lane_half()
    up = upward(0)
    sent = [send_v[0:1, j : j + 1].astype(F32) for j in range(2 * SEND)]
    tiles_of = []
    for out, choice in ((to_first, 1.0 - up), (to_second, up)):
        tiles = [either(choice, sent[j], sent[SEND + j]) for j in range(SEND)]
        tiles_of.append(tiles)
        out[SEND * TA :, :] = jnp.zeros((GHOST_ROWS, out.shape[1]), F32)
        for i in range(3):
            at = SEND * TA + i
            for lanes, source in ((slice(0, CHUNK), pos_v), (slice(CHUNK, 2 * CHUNK), ref_v)):
                chunks = [source[i, :, q * CHUNK : (q + 1) * CHUNK] for q in range(2)]
                out[at : at + 1, lanes] = paired(pick(chunks, tiles[0]), pick(chunks, tiles[1]))
        for other in range(2 * SEND):
            same = low * flag(sent[other] == tiles[0]) + high * flag(sent[other] == tiles[1])
            out[SEND * TA + 3 + other : SEND * TA + 4 + other, 0:CHUNK] = same
    token[...] = jnp.zeros_like(token)
    copies[3].wait()
    for out, tiles in zip((to_first, to_second), tiles_of):
        for j in range(SEND):
            out[j * TA : (j + 1) * TA, :] = pick_rows(feat_v.at[0], tiles[j], 0.0)


def pick_rows(ref, position, first):
    total = None
    for t in range(ref.shape[0] // TA):
        term = ref[t * TA : (t + 1) * TA, :] * flag(position == first + float(t))
        total = term if total is None else total + term
    return total


def stage_kernel(
    centre, other, live, send, pos, ref, species, feat, radial_w, mix_w, species_w, out_w, after,
    flags, atoms, own_feat, weights, mh, ml,
    centre_v, other_v, live_v, send_v, pos_v, ref_v, species_v, radial_v, mix_v, species_w_v, out_v, sems,
):
    copies = fetch(
        [
            (centre, centre_v), (other, other_v), (live, live_v), (send, send_v), (pos, pos_v), (ref, ref_v),
            (species, species_v), (radial_w, radial_v), (species_w, species_w_v), (out_w, out_v),
            (feat.at[0], own_feat), (mix_w, mix_v),
        ],
        sems,
    )
    for copy in copies[:-1]:
        copy.wait()
    flags[...] = jnp.zeros_like(flags)
    centres = [centre_v[0:1, p : p + 1].astype(F32) for p in range(PAIRS)]
    others = [other_v[0:1, p : p + 1].astype(F32) for p in range(PAIRS)]
    for p in range(PAIRS):
        for row, value in (
            (OTHER, others[p]),
            (CENTRE, centres[p]),
            (LIVE, live_v[0:1, p : p + 1].astype(F32)),
            (SAME, flag(others[p] == centres[p] + SEND)),
        ):
            flags[row + p : row + p + 1, :] = jnp.broadcast_to(value, (1, CHUNK))
    flags[SHARED : SHARED + 1, :] = jnp.broadcast_to(flag(centres[0] == centres[1]), (1, CHUNK))
    for j in range(2 * SEND):
        value = send_v[0:1, j : j + 1].astype(F32)
        flags[SENT + j : SENT + j + 1, :] = jnp.broadcast_to(value, (1, CHUNK))
    atoms[...] = jnp.zeros_like(atoms)
    for i in range(3):
        atoms[i : i + 1, :] = pos_v[i]
        atoms[4 + i : 5 + i, :] = ref_v[i]
    atoms[3:4, :] = species_v[...].astype(F32)
    weights[...] = jnp.zeros_like(weights)
    weights[0:BASIS, :] = radial_v[...]
    weights[BASIS : BASIS + SPECIES, :] = species_w_v[...]
    weights[BASIS + SPECIES : BASIS + SPECIES + 1, :] = out_v[...]
    copies[-1].wait()
    hi, lo = split(mix_v[...])
    mh[...] = hi
    ml[...] = lo


def force_kernel(
    flags, atoms, feat, weights, mh, ml, from_first, from_second,
    env, dinv, gate, curve, inv, rows, fsel, own, one_first, one_second, two_first, two_second, shape_store, xh, xl,
    square, turned, th, tl, eh, el, raw, back,
):
    ghost = SEND * TA
    up = upward(0)
    near, far = from_first[ghost : ghost + 3, 0:CHUNK], from_second[ghost : ghost + 3, 0:CHUNK]
    chunks = [either(up, far, near), atoms[0:3, 0:CHUNK], atoms[0:3, CHUNK:], either(up, near, far)]
    kinds = [atoms[3:4, q * CHUNK : (q + 1) * CHUNK] for q in range(2)]

    def number(row):
        return flags[row : row + 1, :]

    centres = [number(CENTRE + p) for p in range(PAIRS)]
    others = [number(OTHER + p) for p in range(PAIRS)]
    shared = flags[SHARED : SHARED + 1, 0:1]
    rows[...] = jnp.zeros_like(rows)
    rows[0:3, :] = paired(*(pick(chunks, others[p]) for p in range(PAIRS)))
    rows[3:6, :] = paired(*(pick(chunks[1:3], centres[p]) for p in range(PAIRS)))
    rows[6:7, :] = paired(*(pick(kinds, centres[p]) for p in range(PAIRS)))
    columns_of(rows[...], square, turned)

    for p in range(PAIRS):
        o = flags[OTHER + p : OTHER + p + 1, 0:1]
        fsel[p * TA : (p + 1) * TA, :] = (
            pick_rows(from_first.at[0:ghost], o, (SEND + 4) * up)
            + pick_rows(feat, o, float(SEND))
            + pick_rows(from_second.at[0:ghost], o, (SEND + 4) * (1.0 - up))
        )

    shapes = []
    for p in range(PAIRS):
        lane_rows = [twice(rows[i : i + 1, :], p) for i in range(3)]
        columns = [turned[p * TA : (p + 1) * TA, 3 + i : 4 + i] for i in range(3)]
        unit, inverse, weight, slope, sine, cosine = geometry(
            lane_rows, columns, 1.0, number(LIVE + p), number(SAME + p)
        )
        angular = harmonics(unit)
        values, slopes = paired_orders(sine, cosine, weight, slope)
        shapes.append((unit, inverse, angular, values, slopes))
        for i, part in enumerate(unit + [inverse] + values + slopes):
            shape_store[p, i] = part
        for m in range(COMPS):
            for k in range(BASIS // 2):
                entry = values[k] if m == 0 else angular[m] * values[k]
                hi, lo = split(entry)
                th[p, m * TA : (m + 1) * TA, k * CHUNK : (k + 1) * CHUNK] = hi
                tl[p, m * TA : (m + 1) * TA, k * CHUNK : (k + 1) * CHUNK] = lo
        radial_feat(fsel, weights, p, xh.at[p], xl.at[p])
        raw[p * COMPS * TA : (p + 1) * COMPS * TA, :] = product((th[p], tl[p]), (xh[p], xl[p]), NN)

    for m in range(COMPS):
        first = raw[m * TA : (m + 1) * TA, :]
        second = raw[(COMPS + m) * TA : (COMPS + m + 1) * TA, :]
        env[m * TA : (m + 1) * TA, :] = env_scale * (first + shared * second)
        env[(COMPS + m) * TA : (COMPS + m + 1) * TA, :] = env_scale * (second + shared * first)
    for p in range(PAIRS):
        sums = [None] * 3
        for m in range(COMPS):
            block = env[(p * COMPS + m) * TA : (p * COMPS + m + 1) * TA, :]
            sums[GROUP[m]] = block * block if sums[GROUP[m]] is None else sums[GROUP[m]] + block * block
        for g in range(3):
            inv[p * TA : (p + 1) * TA, g * 256 : (g + 1) * 256] = sums[g]
    hidden = product(split(inv[...]), (mh[...], ml[...]), NN)
    kind = turned[:, 6:7]
    for s in range(SPECIES):
        hidden = hidden + flag(kind == float(s)) * weights[BASIS + s : BASIS + s + 1, :]
    out_row = weights[BASIS + SPECIES : BASIS + SPECIES + 1, :]
    sigma = 1.0 / (1.0 + jnp.exp(-hidden))
    first_order = sigma * (1.0 + hidden * (1.0 - sigma))
    gate[...] = first_order
    curve[...] = sigma * (1.0 - sigma) * (2.0 + hidden * (1.0 - 2.0 * sigma)) * out_row
    dinv[...] = product(split(first_order * out_row), (mh[...], ml[...]), NT)

    tile_grads = [jnp.zeros((3, CHUNK), F32) for _ in range(4)]
    for p in range(PAIRS):
        unit, inverse, angular, values, slopes = shapes[p]
        for m in range(COMPS):
            block = env[(p * COMPS + m) * TA : (p * COMPS + m + 1) * TA, :]
            part = dinv[p * TA : (p + 1) * TA, GROUP[m] * 256 : (GROUP[m] + 1) * 256]
            hi, lo = split((2.0 * env_scale) * block * part)
            eh[p, m * TA : (m + 1) * TA, :] = hi
            el[p, m * TA : (m + 1) * TA, :] = lo
        back[p] = product((eh[p], el[p]), (xh[p], xl[p]), NT)
        d_radius = None
        d_angular = []
        for m in range(COMPS):
            along, across = None, None
            for k in range(BASIS // 2):
                block = back[p, m * TA : (m + 1) * TA, k * CHUNK : (k + 1) * CHUNK]
                along = block * slopes[k] if along is None else along + block * slopes[k]
                across = block * values[k] if across is None else across + block * values[k]
            d_angular.append(across)
            term = along if m == 0 else along * angular[m]
            d_radius = term if d_radius is None else d_radius + term
        x, y, z = unit
        g = d_angular
        toward = [
            g[1] + root_three * (y * g[4] + z * g[6] + x * g[7]) - x * g[8],
            g[2] + root_three * (x * g[4] + z * g[5] - y * g[7]) - y * g[8],
            g[3] + root_three * (y * g[5] + x * g[6]) + 2.0 * (z * g[8]),
        ]
        radial_part = d_radius - inverse * (toward[0] * x + toward[1] * y + toward[2] * z)
        for i in range(3):
            d_offset = inverse * toward[i] + unit[i] * radial_part
            summed = jnp.sum(d_offset, axis=0, keepdims=True)
            other_row = summed + pltpu.roll(summed, TA, 1)
            square[0:TA, :] = d_offset
            square[TA:, :] = d_offset
            centre_row = -jnp.sum(square[...].T, axis=0, keepdims=True)
            component = flag(lax.broadcasted_iota(jnp.int32, (3, CHUNK), 0) == i)
            for q in range(4):
                at = chunk_mask(others[p], q) * other_row
                if q in (1, 2):
                    at = at + chunk_mask(centres[p] + SEND, q) * centre_row
                tile_grads[q] = tile_grads[q] + at * component
    own[...] = jnp.zeros_like(own)
    own[0:3, 0:CHUNK] = tile_grads[1]
    own[0:3, CHUNK:] = tile_grads[2]
    own[3:6, 0:CHUNK] = tile_grads[0]
    own[3:6, CHUNK:] = tile_grads[3]
    leaving = []
    for first, ghost_grad in ((0, tile_grads[0]), (SEND, tile_grads[3])):
        listed = paired(*(pick(tile_grads[1:3], number(SENT + first + j)) for j in range(SEND)))
        leaving.append((listed, ghost_grad))
    for shift, outs in ((0, (one_first, one_second)), (1, (two_first, two_second))):
        choice = upward(shift)
        for out, above in zip(outs, (choice, 1.0 - choice)):
            out[...] = jnp.zeros_like(out)
            out[0:3, :] = either(above, leaving[1][0], leaving[0][0])
            out[3:6, :] = either(above, leaving[1][1], leaving[0][1])


def tangent_kernel(
    scale, flags, atoms, weights, mh, ml, from_first, from_second, own, one_first, one_second, two_first, two_second,
    rows, env, gate, curve, inv, shape_store, xh, xl,
    forces, keep, give, small, envdot, curl, both,
    square, turned, th, tl, raw, left, right,
):
    ghost = SEND * TA
    def number(row):
        return flags[row : row + 1, :]

    centres = [number(CENTRE + p) for p in range(PAIRS)]
    others = [number(OTHER + p) for p in range(PAIRS)]
    shared = flags[SHARED : SHARED + 1, 0:1]
    mine = [own[0:3, 0:CHUNK], own[0:3, CHUNK:]]
    up, up_two = upward(0), upward(1)
    low_one = either(up, one_second[...], one_first[...])
    high_one = either(up, one_first[...], one_second[...])
    low_two = either(up_two, two_second[...], two_first[...])
    high_two = either(up_two, two_first[...], two_second[...])
    low_tail = either(up, from_second[ghost:, :], from_first[ghost:, :])
    high_tail = either(up, from_first[ghost:, :], from_second[ghost:, :])
    arrived = [twice(low_one[3:6, :], j) for j in range(SEND)]
    arrived += [twice(high_one[3:6, :], j) for j in range(SEND)]
    for j in range(2 * SEND):
        for q in range(2):
            mine[q] = mine[q] + chunk_mask(number(SENT + j), q) * arrived[j]
    below = low_one[0:3, :]
    above = high_one[0:3, :]
    to_below = [twice(low_two[3:6, :], j) for j in range(SEND)]
    to_below += [twice(own[3:6, 0:CHUNK], j) for j in range(SEND)]
    to_above = [twice(own[3:6, CHUNK:], j) for j in range(SEND)]
    to_above += [twice(high_two[3:6, :], j) for j in range(SEND)]
    for j in range(2 * SEND):
        below = below + low_tail[3 + j : 4 + j, 0:CHUNK] * to_below[j]
        above = above + high_tail[3 + j : 4 + j, 0:CHUNK] * to_above[j]
    for q in range(2):
        for i in range(3):
            forces[i, :, q * CHUNK : (q + 1) * CHUNK] = -mine[q][i : i + 1, :]
    error = [
        below + low_tail[0:3, CHUNK:],
        mine[0] + atoms[4:7, 0:CHUNK],
        mine[1] + atoms[4:7, CHUNK:],
        above + high_tail[0:3, CHUNK:],
    ]
    error = [part * scale for part in error]
    both[...] = jnp.zeros_like(both)
    both[0:8, :] = rows[...]
    both[8:11, :] = paired(*(pick(error, others[p]) for p in range(PAIRS)))
    both[11:14, :] = paired(*(pick(error[1:3], centres[p]) for p in range(PAIRS)))
    columns_of(both[...], square, turned)

    for p in range(PAIRS):
        lane_move = [twice(both[8 + i : 9 + i, :], p) for i in range(3)]
        column_move = [turned[p * TA : (p + 1) * TA, 11 + i : 12 + i] for i in range(3)]
        unit = [shape_store[p, i] for i in range(3)]
        inverse = shape_store[p, 3]
        values = [shape_store[p, 4 + k] for k in range(BASIS // 2)]
        slopes = [shape_store[p, 8 + k] for k in range(BASIS // 2)]
        move = [a - b for a, b in zip(lane_move, column_move)]
        stretch = unit[0] * move[0] + unit[1] * move[1] + unit[2] * move[2]
        turn = [(m - v * stretch) * inverse for m, v in zip(move, unit)]
        angular, turning = harmonics(unit), harmonics_tangent(unit, turn)
        slopes = [s * stretch for s in slopes]
        for m in range(COMPS):
            for k in range(BASIS // 2):
                entry = slopes[k] if m == 0 else angular[m] * slopes[k] + turning[m] * values[k]
                hi, lo = split(entry)
                th[p, m * TA : (m + 1) * TA, k * CHUNK : (k + 1) * CHUNK] = hi
                tl[p, m * TA : (m + 1) * TA, k * CHUNK : (k + 1) * CHUNK] = lo
        raw[p * COMPS * TA : (p + 1) * COMPS * TA, :] = product((th[p], tl[p]), (xh[p], xl[p]), NN)

    for m in range(COMPS):
        first = raw[m * TA : (m + 1) * TA, :]
        second = raw[(COMPS + m) * TA : (COMPS + m + 1) * TA, :]
        envdot[m * TA : (m + 1) * TA, :] = env_scale * (first + shared * second)
        envdot[(COMPS + m) * TA : (COMPS + m + 1) * TA, :] = env_scale * (second + shared * first)
    invdot = left
    half = PAIRS * TA
    for p in range(PAIRS):
        sums = [None] * 3
        for m in range(COMPS):
            at = slice((p * COMPS + m) * TA, (p * COMPS + m + 1) * TA)
            term = 2.0 * env[at, :] * envdot[at, :]
            sums[GROUP[m]] = term if sums[GROUP[m]] is None else sums[GROUP[m]] + term
        for g in range(3):
            invdot[half + p * TA : half + (p + 1) * TA, g * 256 : (g + 1) * 256] = sums[g]
    invdot[0:half, :] = inv[...]
    hidden_move = product(split(invdot[half:, :]), (mh[...], ml[...]), NN)
    bend = curve[...] * hidden_move
    curl[...] = bend
    once = 1.0 - shared * flag(lax.broadcasted_iota(jnp.int32, (half, 1), 0) >= TA)
    right[0:half, :] = bend * once
    right[half:, :] = gate[...] * weights[BASIS + SPECIES : BASIS + SPECIES + 1, :] * once
    core = lax.axis_index("batch")
    left_parts = split(left[...])
    for out, part in ((keep, core), (give, 1 - core)):
        lanes = pl.ds(pl.multiple_of(part * HALF, HALF), HALF)
        out[...] = product(left_parts, split(right[:, lanes]), TN)
    small[...] = jnp.zeros_like(small)
    kind = turned[:, 6:7]
    for s in range(SPECIES):
        small[s : s + 1, :] = jnp.sum(right[0:half, :] * flag(kind == float(s)), axis=0, keepdims=True)
    small[SPECIES : SPECIES + 1, :] = jnp.sum(gate[...] * hidden_move * once, axis=0, keepdims=True)


def radial_kernel(
    p, flags, both, fsel, env, envdot, dinv, curl, mh, ml, after,
    grad_radial,
    square, turned, lh, ll, gh, gl, raw,
):
    low, high = lane_half()
    columns_of(both[...], square, turned)
    here = slice(p * TA, (p + 1) * TA)
    turn_inv = product(split(curl[here, :]), (mh[...], ml[...]), NT)
    lane_rows = [twice(both[3 + i : 4 + i, :], p) for i in range(3)]
    lane_move = [twice(both[11 + i : 12 + i, :], p) for i in range(3)]
    columns = [turned[here, i : i + 1] for i in range(3)]
    column_move = [turned[here, 8 + i : 9 + i] for i in range(3)]
    unit, inverse, weight, slope, sine, cosine = geometry(
        lane_rows, columns, -1.0, flags[LIVE + p : LIVE + p + 1, :], flags[SAME + p : SAME + p + 1, :]
    )
    move = [b - a for a, b in zip(lane_move, column_move)]
    stretch = unit[0] * move[0] + unit[1] * move[1] + unit[2] * move[2]
    turn = [(m - v * stretch) * inverse for m, v in zip(move, unit)]
    angular, turning = harmonics(unit), harmonics_tangent(unit, turn)
    values, slopes = single_orders(sine, cosine, weight, slope)
    for m in range(COMPS):
        if m == 0:
            on_value, on_slope = low, high * stretch
        else:
            on_value = angular[m] * low + turning[m] * high
            on_slope = angular[m] * high * stretch
        for n in range(BASIS):
            hi, lo = split(on_value * values[n] + on_slope * slopes[n])
            lh[n * TA : (n + 1) * TA, m * CHUNK : (m + 1) * CHUNK] = hi
            ll[n * TA : (n + 1) * TA, m * CHUNK : (m + 1) * CHUNK] = lo
        at = slice((p * COMPS + m) * TA, (p * COMPS + m + 1) * TA)
        group = slice(GROUP[m] * 256, (GROUP[m] + 1) * 256)
        steady = (2.0 * env_scale) * dinv[here, group]
        bent = (2.0 * env_scale) * turn_inv[:, group]
        hi, lo = split(env[at, :] * bent + envdot[at, :] * steady)
        gh[m * CHUNK : m * CHUNK + TA, :] = hi
        gl[m * CHUNK : m * CHUNK + TA, :] = lo
        hi, lo = split(env[at, :] * steady)
        gh[m * CHUNK + TA : (m + 1) * CHUNK, :] = hi
        gl[m * CHUNK + TA : (m + 1) * CHUNK, :] = lo
    raw[...] = product((lh[...], ll[...]), (gh[...], gl[...]), NN)
    for n in range(BASIS):
        grad_radial[n : n + 1, :] = jnp.sum(
            raw[n * TA : (n + 1) * TA, :] * fsel[here, :], axis=0, keepdims=True
        )


SMALL = 32
FOUR = 4


def block_of(part, rows):
    return pl.ds(pl.multiple_of(part * rows, 8), rows)


def total_of(refs, at):
    total = refs[0][at, :]
    for ref in refs[1:]:
        total = total + ref[at, :]
    return total


def halve_kernel(keep, taken, keep_out, give_out):
    me = place(0, 2)
    for out, part in ((keep_out, me), (give_out, 1 - me)):
        out[...] = total_of([keep, taken], block_of(part, out.shape[0]))


def spread_kernel(keep, taken, radial_0, radial_1, small, *refs):
    outs, tiny = refs[:FOUR], refs[FOUR]
    for h in range(2):
        lanes = slice(h * HALF, (h + 1) * HALF)
        tiny[16 * h : 16 * h + 8, :] = radial_0[:, lanes] + radial_1[:, lanes]
        tiny[16 * h + 8 : 16 * h + 16, :] = small[:, lanes]
    me = place(1, FOUR)
    for k, out in enumerate(outs):
        rows, few = out.shape[0] - SMALL // FOUR, SMALL // FOUR
        to = lax.bitwise_xor(me, k)
        out[0:rows, :] = total_of([keep, taken], block_of(to, rows))
        out[rows:, :] = tiny[block_of(to, few), :]


def total_kernel(*refs):
    refs[-1][...] = total_of(refs[:-1], slice(None))


def grow_kernel(*refs):
    parts, out = refs[:FOUR], refs[FOUR]
    few = SMALL // FOUR
    rows = parts[0].shape[0] - few
    me = place(1, FOUR)
    for k, ref in enumerate(parts):
        to = lax.bitwise_xor(me, k)
        out[block_of(to, rows), :] = ref[0:rows, :]
        out[pl.ds(pl.multiple_of(FOUR * rows + to * few, 8), few), :] = ref[rows:, :]


def pair_kernel(mine, theirs, out):
    rows = mine.shape[0] - SMALL
    me = place(0, 2)
    for ref, part in ((mine, me), (theirs, 1 - me)):
        out[block_of(part, rows), :] = ref[0:rows, :]
    out[2 * rows :, :] = mine[rows:, :] + theirs[rows:, :]


def join_kernel(whole, facing, mix, radial, kinds, out):
    rows = mix.shape[0]
    core = lax.axis_index("batch")
    for ref, part in ((whole, core), (facing, 1 - core)):
        mix[:, pl.ds(pl.multiple_of(part * HALF, HALF), HALF)] = ref[0:rows, :]
    for h in range(2):
        lanes = slice(h * HALF, (h + 1) * HALF)
        both = whole[rows + 16 * h : rows + 16 * h + 16, :] + facing[rows + 16 * h : rows + 16 * h + 16, :]
        radial[:, lanes] = both[0:BASIS]
        kinds[:, lanes] = both[BASIS : BASIS + SPECIES]
        out[:, lanes] = both[BASIS + SPECIES : BASIS + SPECIES + 1]


def spec(space):
    return pl.BlockSpec(memory_space=space)


def call(kernel, name, outs, scratch, *operands, space=pltpu.VMEM, after=(), flops=0):
    if space is pltpu.HBM:
        operands = [pltpu.with_memory_space_constraint(operand, space) for operand in operands]
    outs = [out if len(out) == 2 and isinstance(out[0], tuple) else (out, F32) for out in outs]
    return pl.pallas_call(
        kernel,
        name=name,
        out_shape=[jax.ShapeDtypeStruct(*out) for out in outs],
        in_specs=[spec(space)] * len(operands) + [spec(pltpu.VMEM)] * len(after),
        out_specs=[spec(pltpu.VMEM)] * len(outs),
        scratch_shapes=[pltpu.VMEM(*item) if isinstance(item, tuple) else item for item in scratch],
        compiler_params=pltpu.CompilerParams(vmem_limit_bytes=28 * 1024 * 1024),
        cost_estimate=pl.CostEstimate(flops=flops, bytes_accessed=1 << 20, transcendentals=0),
    )(*operands, *after)


def shifted(block, axis, by):
    count = lax.axis_size(axis)
    return lax.ppermute(block, axis, [(i, (i + by) % count) for i in range(count)])


def exchanged(block, shift, first):
    count, step = lax.axis_size("domain"), 1 << shift
    up = [((i >> shift) & 1 == 0) == first for i in range(count)]
    return lax.ppermute(block, "domain", [(i, (i + step if up[i] else i - step) % count) for i in range(count)])


def partner(block, mask):
    return lax.ppermute(block, "domain", [(i, i ^ mask) for i in range(lax.axis_size("domain"))])


def on_device(
    positions,
    features,
    species,
    ref_forces,
    centre_tile,
    other_tile,
    pair_live,
    send_tiles,
    radial_w,
    mix_w,
    species_w,
    out_w,
):
    atoms_here = positions.shape[2]
    channels = features.shape[2]
    table = (COMPS * TA, BASIS * TA)
    sent = (SEND * TA + GHOST_ROWS, channels)
    slots = PAIRS * TA
    line = (3, 1, atoms_here)
    turning = [((CHUNK, CHUNK), F32)] * 2
    out_row = out_w.reshape(1, channels)
    positions = positions.transpose(1, 0, 2)
    ref_forces = ref_forces.transpose(1, 0, 2)
    ints = [((1, n), jnp.int32) for n in (PAIRS, PAIRS, PAIRS, 2 * SEND)]

    to_first, to_second, token = call(
        gather_kernel,
        "gather",
        [sent, sent, (8, CHUNK)],
        [
            ints[3],
            (line, F32),
            ((1, atoms_here, channels), F32),
            (line, F32),
            pltpu.SemaphoreType.DMA((4,)),
        ],
        send_tiles, positions, features, ref_forces,
        space=pltpu.HBM,
    )
    from_first = exchanged(to_first, 0, True)
    from_second = exchanged(to_second, 0, False)
    flags, atoms, own_feat, weights, mh, ml = call(
        stage_kernel,
        "stage",
        [
            (16, CHUNK),
            (8, atoms_here),
            (atoms_here, channels),
            (16, channels),
            (mix_w.shape, BF16),
            (mix_w.shape, BF16),
        ],
        ints
        + [(line, F32), (line, F32), ((1, atoms_here), jnp.int32)]
        + [(radial_w.shape, F32), (mix_w.shape, F32), (species_w.shape, F32), (out_row.shape, F32)]
        + [pltpu.SemaphoreType.DMA((12,))],
        centre_tile, other_tile, pair_live, send_tiles, positions, ref_forces, species, features,
        radial_w, mix_w, species_w, out_row,
        space=pltpu.HBM,
        after=(token,),
    )

    factors = (PAIRS, BASIS * TA, channels)
    env, dinv, gate, curve, inv, rows, fsel, own, *leaving, shape_store, xh, xl = call(
        force_kernel,
        "force",
        [
            (PAIRS * COMPS * TA, channels),
            (slots, 3 * channels),
            (slots, channels),
            (slots, channels),
            (slots, 3 * channels),
            (8, CHUNK),
            (slots, channels),
            (8, atoms_here),
            (8, CHUNK),
            (8, CHUNK),
            (8, CHUNK),
            (8, CHUNK),
            (PAIRS, 4 + BASIS, TA, CHUNK),
            (factors, BF16),
            (factors, BF16),
        ],
        turning
        + [((PAIRS, *table), BF16)] * 2
        + [((PAIRS, COMPS * TA, channels), BF16)] * 2
        + [((PAIRS * COMPS * TA, channels), F32), ((PAIRS, *table), F32)],
        flags, atoms, own_feat, weights, mh, ml, from_first, from_second,
        flops=1 << 31,
    )
    arriving = [exchanged(leaving[i], i // 2, i % 2 == 0) for i in (0, 2, 1, 3)]
    arriving = [arriving[i] for i in (0, 2, 1, 3)]

    rows_mix = 3 * channels
    total_count = 3.0 * atoms_here * lax.axis_size("domain") * lax.axis_size("batch")
    forces, keep, give, small, envdot, curl, both = call(
        functools.partial(tangent_kernel, 2.0 / math.sqrt(total_count)),
        "tangent",
        [
            line,
            (rows_mix, HALF),
            (rows_mix, HALF),
            (8, channels),
            (PAIRS * COMPS * TA, channels),
            (slots, channels),
            (16, CHUNK),
        ],
        turning
        + [((PAIRS, *table), BF16)] * 2
        + [((PAIRS * COMPS * TA, channels), F32)]
        + [((2 * slots, 3 * channels), F32), ((2 * slots, channels), F32)],
        flags, atoms, weights, mh, ml, from_first, from_second, own, *arriving,
        rows, env, gate, curve, inv, shape_store, xh, xl,
        flops=1 << 31,
    )

    def radial(p, after):
        return call(
            functools.partial(radial_kernel, p),
            "radial",
            [(BASIS, channels)],
            turning
            + [((BASIS * TA, COMPS * CHUNK), BF16)] * 2
            + [((COMPS * CHUNK, channels), BF16)] * 2
            + [((BASIS * TA, channels), F32)],
            flags, both, fsel, env, envdot, dinv, curl, mh, ml, after,
            flops=1 << 31,
        )[0]

    keep, give = call(
        halve_kernel, "halve", [(rows_mix // 2, HALF)] * 2, [], keep, shifted(give, "batch", 1)
    )
    taken = partner(give, 1)
    radials = [radial(p, keep) for p in range(PAIRS)]
    piece = rows_mix // (2 * FOUR) + SMALL // FOUR
    blocks = call(
        spread_kernel, "spread", [(piece, HALF)] * FOUR, [((SMALL, HALF), F32)],
        keep, taken, *radials, small,
    )
    terms = [blocks[0]] + [partner(blocks[k], 2 * k) for k in range(1, FOUR)]
    (mine,) = call(total_kernel, "total", [(piece, HALF)], [], *terms)
    bit = 2 * FOUR
    while bit < lax.axis_size("domain"):
        (mine,) = call(total_kernel, "total", [(piece, HALF)], [], mine, partner(mine, bit))
        bit *= 2
    parts = [mine] + [partner(mine, 2 * k) for k in range(1, FOUR)]
    (mine,) = call(grow_kernel, "grow", [(rows_mix // 2 + SMALL, HALF)], [], *parts)
    (mine,) = call(pair_kernel, "pair", [(rows_mix + SMALL, HALF)], [], mine, partner(mine, 1))
    facing = shifted(mine, "batch", 1)
    mix, radial_sum, kinds, out = call(
        join_kernel,
        "join",
        [(rows_mix, channels), (BASIS, channels), (SPECIES, channels), (1, channels)],
        [],
        mine,
        facing,
    )
    return forces.transpose(1, 0, 2), radial_sum, mix, kinds, out.reshape(channels)


def solution(mesh):
    return jax.shard_map(
        on_device,
        mesh=mesh,
        in_specs=(
            P(("parts", "batch"), None, "domain"),
            P(("parts", "batch"), "domain", None),
            P(("parts", "batch"), "domain"),
            P(("parts", "batch"), None, "domain"),
            P(("parts", "batch"), "domain"),
            P(("parts", "batch"), "domain"),
            P(("parts", "batch"), "domain"),
            P(("parts", "batch"), "domain"),
            P(),
            P(),
            P(),
            P(),
        ),
        out_specs=(
            P(("parts", "batch"), None, "domain"),
            P("parts", None),
            P("parts", None),
            P("parts", None),
            P("parts"),
        ),
        check_vma=False,
    )
```

```python
import functools
import math

import jax
import jax.numpy as jnp
from jax import lax
from jax.experimental import pallas as pl
from jax.experimental.pallas import tpu as pltpu
from jax.sharding import PartitionSpec as P

TA = 64
SEND = 2
PAIRS = 2
COMPS = 9
BASIS = 8
SPECIES = 4
HALF = 128
CHUNK = 2 * TA

cutoff = 2.5
soften = 0.25
env_scale = 0.25
root_three = math.sqrt(3.0)
F32 = jnp.float32
BF16 = jnp.bfloat16
NN = (((1,), (0,)), ((), ()))
NT = (((1,), (1,)), ((), ()))
TN = (((0,), (0,)), ((), ()))
GROUP = (0, 1, 1, 1, 2, 2, 2, 2, 2)


def split(value):
    high = value.astype(BF16)
    return high, (value - high.astype(F32)).astype(BF16)


def product(left, right, dims):
    (lh, ll), (rh, rl) = left, right

    def one(x, y):
        return lax.dot_general(x, y, dims, preferred_element_type=F32)

    return one(lh, rh) + (one(lh, rl) + one(ll, rh))


def flag(condition):
    return jnp.where(condition, 1.0, 0.0).astype(F32)


def place(shift, width):
    return lax.bitwise_and(lax.shift_right_logical(lax.axis_index("domain"), shift), width - 1)


def lane_half():
    lane = lax.broadcasted_iota(jnp.int32, (1, CHUNK), 1)
    low = flag(lane < TA)
    return low, 1.0 - low


def twice(chunk, half):
    low, high = lane_half()
    swapped = pltpu.roll(chunk, TA, 1)
    return chunk * low + swapped * high if half == 0 else swapped * low + chunk * high


def pick(chunks, position):
    total = None
    for q, chunk in enumerate(chunks):
        for half in range(2):
            term = twice(chunk, half) * flag(position == 2 * q + half)
            total = term if total is None else total + term
    return total


def paired(first, second):
    low, high = lane_half()
    return first * low + second * high


def chunk_mask(position, q):
    low, high = lane_half()
    return low * flag(position == 2 * q) + high * flag(position == 2 * q + 1)


def geometry(lane_rows, columns, sign, live, same):
    offset = [(row - column) * sign for row, column in zip(lane_rows, columns)]
    dist_sq = offset[0] * offset[0] + offset[1] * offset[1] + offset[2] * offset[2] + soften
    distance = jnp.sqrt(dist_sq)
    inverse = 1.0 / distance
    unit = [x * inverse for x in offset]
    row = lax.broadcasted_iota(jnp.int32, (TA, CHUNK), 0)
    lane = lax.broadcasted_iota(jnp.int32, (TA, CHUNK), 1)
    lane = jnp.where(lane >= TA, lane - TA, lane)
    mask = live * (1.0 - same * flag(row == lane))
    base = jnp.maximum(1.0 - dist_sq * (1.0 / (cutoff * cutoff)), 0.0)
    weight = base * base * base * mask * inverse
    slope = -(6.0 / (cutoff * cutoff)) * base * base * mask - weight * inverse
    angle = distance * (math.pi / cutoff)
    return unit, inverse, weight, slope, jnp.sin(angle), jnp.cos(angle)


def harmonics(v):
    x, y, z = v
    return [
        None,
        x,
        y,
        z,
        root_three * x * y,
        root_three * y * z,
        root_three * z * x,
        0.5 * root_three * (x * x - y * y),
        z * z - 0.5 * (x * x + y * y),
    ]


def harmonics_tangent(v, t):
    x, y, z = v
    a, b, c = t
    return [
        None,
        a,
        b,
        c,
        root_three * (a * y + x * b),
        root_three * (b * z + y * c),
        root_three * (c * x + z * a),
        root_three * (x * a - y * b),
        2.0 * z * c - (x * a + y * b),
    ]


def paired_orders(sine, cosine, weight, slope):
    low, high = lane_half()
    double_s, double_c = 2.0 * sine * cosine, 1.0 - 2.0 * sine * sine
    now_s = sine * low + double_s * high
    now_c = cosine * low + double_c * high
    old_s = -sine * low
    old_c = cosine * low + high
    values, slopes = [], []
    for k in range(BASIS // 2):
        order = ((2 * k + 1) * low + (2 * k + 2) * high) * (math.pi / cutoff)
        values.append(now_s * weight)
        slopes.append(now_c * (weight * order) + now_s * slope)
        now_s, old_s = 2.0 * double_c * now_s - old_s, now_s
        now_c, old_c = 2.0 * double_c * now_c - old_c, now_c
    return values, slopes


def single_orders(sine, cosine, weight, slope):
    now_s, now_c = sine, cosine
    old_s, old_c = jnp.zeros_like(sine), jnp.ones_like(cosine)
    values, slopes = [], []
    for n in range(1, BASIS + 1):
        values.append(now_s * weight)
        slopes.append(now_c * (weight * (n * math.pi / cutoff)) + now_s * slope)
        now_s, old_s = 2.0 * cosine * now_s - old_s, now_s
        now_c, old_c = 2.0 * cosine * now_c - old_c, now_c
    return values, slopes


def columns_of(rows, square, turned):
    square[...] = jnp.zeros_like(square)
    square[0 : rows.shape[0], :] = rows
    turned[...] = square[...].T


def pair_rows(first, p):
    return twice(first, p)


def radial_feat(feat, radial, p, high_ref, low_ref):
    own = feat[p * TA : (p + 1) * TA, :]
    for n in range(BASIS):
        hi, lo = split(own * radial[n : n + 1, :])
        high_ref[n * TA : (n + 1) * TA, :] = hi
        low_ref[n * TA : (n + 1) * TA, :] = lo


OTHER, CENTRE, LIVE, SAME, SHARED, SENT = 0, 2, 4, 6, 8, 9
GHOST_ROWS = 8


def fetch(pairs, sems):
    copies = [pltpu.make_async_copy(src, dst, sems.at[i]) for i, (src, dst) in enumerate(pairs)]
    for copy in copies:
        copy.start()
    return copies


def upward(shift):
    return 1.0 - flag(place(shift, 2) == 1)


def either(choice, first, second):
    return first * choice + second * (1.0 - choice)


def gather_kernel(send, pos, feat, ref, to_second, to_first, token, send_v, pos_v, feat_v, ref_v, sems):
    copies = fetch([(send, send_v), (pos, pos_v), (ref, ref_v), (feat, feat_v)], sems)
    for copy in copies[:3]:
        copy.wait()
    low, high = lane_half()
    up = upward(0)
    sent = [send_v[0:1, j : j + 1].astype(F32) for j in range(2 * SEND)]
    tiles_of = []
    for out, choice in ((to_first, 1.0 - up), (to_second, up)):
        tiles = [either(choice, sent[j], sent[SEND + j]) for j in range(SEND)]
        tiles_of.append(tiles)
        out[SEND * TA :, :] = jnp.zeros((GHOST_ROWS, out.shape[1]), F32)
        for i in range(3):
            at = SEND * TA + i
            for lanes, source in ((slice(0, CHUNK), pos_v), (slice(CHUNK, 2 * CHUNK), ref_v)):
                chunks = [source[i, :, q * CHUNK : (q + 1) * CHUNK] for q in range(2)]
                out[at : at + 1, lanes] = paired(pick(chunks, tiles[0]), pick(chunks, tiles[1]))
        for other in range(2 * SEND):
            same = low * flag(sent[other] == tiles[0]) + high * flag(sent[other] == tiles[1])
            out[SEND * TA + 3 + other : SEND * TA + 4 + other, 0:CHUNK] = same
    token[...] = jnp.zeros_like(token)
    copies[3].wait()
    for out, tiles in zip((to_first, to_second), tiles_of):
        for j in range(SEND):
            out[j * TA : (j + 1) * TA, :] = pick_rows(feat_v.at[0], tiles[j], 0.0)


def pick_rows(ref, position, first):
    total = None
    for t in range(ref.shape[0] // TA):
        term = ref[t * TA : (t + 1) * TA, :] * flag(position == first + float(t))
        total = term if total is None else total + term
    return total


def stage_kernel(
    centre, other, live, send, pos, ref, species, feat, radial_w, mix_w, species_w, out_w, after,
    flags, atoms, own_feat, weights, mh, ml,
    centre_v, other_v, live_v, send_v, pos_v, ref_v, species_v, radial_v, mix_v, species_w_v, out_v, sems,
):
    copies = fetch(
        [
            (centre, centre_v), (other, other_v), (live, live_v), (send, send_v), (pos, pos_v), (ref, ref_v),
            (species, species_v), (radial_w, radial_v), (species_w, species_w_v), (out_w, out_v),
            (feat.at[0], own_feat), (mix_w, mix_v),
        ],
        sems,
    )
    for copy in copies[:-1]:
        copy.wait()
    flags[...] = jnp.zeros_like(flags)
    centres = [centre_v[0:1, p : p + 1].astype(F32) for p in range(PAIRS)]
    others = [other_v[0:1, p : p + 1].astype(F32) for p in range(PAIRS)]
    for p in range(PAIRS):
        for row, value in (
            (OTHER, others[p]),
            (CENTRE, centres[p]),
            (LIVE, live_v[0:1, p : p + 1].astype(F32)),
            (SAME, flag(others[p] == centres[p] + SEND)),
        ):
            flags[row + p : row + p + 1, :] = jnp.broadcast_to(value, (1, CHUNK))
    flags[SHARED : SHARED + 1, :] = jnp.broadcast_to(flag(centres[0] == centres[1]), (1, CHUNK))
    for j in range(2 * SEND):
        value = send_v[0:1, j : j + 1].astype(F32)
        flags[SENT + j : SENT + j + 1, :] = jnp.broadcast_to(value, (1, CHUNK))
    atoms[...] = jnp.zeros_like(atoms)
    for i in range(3):
        atoms[i : i + 1, :] = pos_v[i]
        atoms[4 + i : 5 + i, :] = ref_v[i]
    atoms[3:4, :] = species_v[...].astype(F32)
    weights[...] = jnp.zeros_like(weights)
    weights[0:BASIS, :] = radial_v[...]
    weights[BASIS : BASIS + SPECIES, :] = species_w_v[...]
    weights[BASIS + SPECIES : BASIS + SPECIES + 1, :] = out_v[...]
    copies[-1].wait()
    hi, lo = split(mix_v[...])
    mh[...] = hi
    ml[...] = lo


def force_kernel(
    flags, atoms, feat, weights, mh, ml, from_second, from_first,
    env, dinv, gate, curve, inv, rows, fsel, own, one_first, one_second, two_first, two_second, shape_store, xh, xl,
    square, turned, th, tl, eh, el, raw, back,
):
    ghost = SEND * TA
    up = upward(0)
    near, far = from_first[ghost : ghost + 3, 0:CHUNK], from_second[ghost : ghost + 3, 0:CHUNK]
    chunks = [either(up, far, near), atoms[0:3, 0:CHUNK], atoms[0:3, CHUNK:], either(up, near, far)]
    kinds = [atoms[3:4, q * CHUNK : (q + 1) * CHUNK] for q in range(2)]

    def number(row):
        return flags[row : row + 1, :]

    centres = [number(CENTRE + p) for p in range(PAIRS)]
    others = [number(OTHER + p) for p in range(PAIRS)]
    shared = flags[SHARED : SHARED + 1, 0:1]
    rows[...] = jnp.zeros_like(rows)
    rows[0:3, :] = paired(*(pick(chunks, others[p]) for p in range(PAIRS)))
    rows[3:6, :] = paired(*(pick(chunks[1:3], centres[p]) for p in range(PAIRS)))
    rows[6:7, :] = paired(*(pick(kinds, centres[p]) for p in range(PAIRS)))
    columns_of(rows[...], square, turned)

    for p in range(PAIRS):
        o = flags[OTHER + p : OTHER + p + 1, 0:1]
        fsel[p * TA : (p + 1) * TA, :] = (
            pick_rows(from_first.at[0:ghost], o, (SEND + 4) * up)
            + pick_rows(feat, o, float(SEND))
            + pick_rows(from_second.at[0:ghost], o, (SEND + 4) * (1.0 - up))
        )

    shapes = []
    for p in range(PAIRS):
        lane_rows = [twice(rows[i : i + 1, :], p) for i in range(3)]
        columns = [turned[p * TA : (p + 1) * TA, 3 + i : 4 + i] for i in range(3)]
        unit, inverse, weight, slope, sine, cosine = geometry(
            lane_rows, columns, 1.0, number(LIVE + p), number(SAME + p)
        )
        angular = harmonics(unit)
        values, slopes = paired_orders(sine, cosine, weight, slope)
        shapes.append((unit, inverse, angular, values, slopes))
        for i, part in enumerate(unit + [inverse] + values + slopes):
            shape_store[p, i] = part
        for m in range(COMPS):
            for k in range(BASIS // 2):
                entry = values[k] if m == 0 else angular[m] * values[k]
                hi, lo = split(entry)
                th[p, m * TA : (m + 1) * TA, k * CHUNK : (k + 1) * CHUNK] = hi
                tl[p, m * TA : (m + 1) * TA, k * CHUNK : (k + 1) * CHUNK] = lo
        radial_feat(fsel, weights, p, xh.at[p], xl.at[p])
        raw[p * COMPS * TA : (p + 1) * COMPS * TA, :] = product((th[p], tl[p]), (xh[p], xl[p]), NN)

    for m in range(COMPS):
        first = raw[m * TA : (m + 1) * TA, :]
        second = raw[(COMPS + m) * TA : (COMPS + m + 1) * TA, :]
        env[m * TA : (m + 1) * TA, :] = env_scale * (first + shared * second)
        env[(COMPS + m) * TA : (COMPS + m + 1) * TA, :] = env_scale * (second + shared * first)
    for p in range(PAIRS):
        sums = [None] * 3
        for m in range(COMPS):
            block = env[(p * COMPS + m) * TA : (p * COMPS + m + 1) * TA, :]
            sums[GROUP[m]] = block * block if sums[GROUP[m]] is None else sums[GROUP[m]] + block * block
        for g in range(3):
            inv[p * TA : (p + 1) * TA, g * 256 : (g + 1) * 256] = sums[g]
    hidden = product(split(inv[...]), (mh[...], ml[...]), NN)
    kind = turned[:, 6:7]
    for s in range(SPECIES):
        hidden = hidden + flag(kind == float(s)) * weights[BASIS + s : BASIS + s + 1, :]
    out_row = weights[BASIS + SPECIES : BASIS + SPECIES + 1, :]
    sigma = 1.0 / (1.0 + jnp.exp(-hidden))
    first_order = sigma * (1.0 + hidden * (1.0 - sigma))
    gate[...] = first_order
    curve[...] = sigma * (1.0 - sigma) * (2.0 + hidden * (1.0 - 2.0 * sigma)) * out_row
    dinv[...] = product(split(first_order * out_row), (mh[...], ml[...]), NT)

    tile_grads = [jnp.zeros((3, CHUNK), F32) for _ in range(4)]
    for p in range(PAIRS):
        unit, inverse, angular, values, slopes = shapes[p]
        for m in range(COMPS):
            block = env[(p * COMPS + m) * TA : (p * COMPS + m + 1) * TA, :]
            part = dinv[p * TA : (p + 1) * TA, GROUP[m] * 256 : (GROUP[m] + 1) * 256]
            hi, lo = split((2.0 * env_scale) * block * part)
            eh[p, m * TA : (m + 1) * TA, :] = hi
            el[p, m * TA : (m + 1) * TA, :] = lo
        back[p] = product((eh[p], el[p]), (xh[p], xl[p]), NT)
        d_radius = None
        d_angular = []
        for m in range(COMPS):
            along, across = None, None
            for k in range(BASIS // 2):
                block = back[p, m * TA : (m + 1) * TA, k * CHUNK : (k + 1) * CHUNK]
                along = block * slopes[k] if along is None else along + block * slopes[k]
                across = block * values[k] if across is None else across + block * values[k]
            d_angular.append(across)
            term = along if m == 0 else along * angular[m]
            d_radius = term if d_radius is None else d_radius + term
        x, y, z = unit
        g = d_angular
        toward = [
            g[1] + root_three * (y * g[4] + z * g[6] + x * g[7]) - x * g[8],
            g[2] + root_three * (x * g[4] + z * g[5] - y * g[7]) - y * g[8],
            g[3] + root_three * (y * g[5] + x * g[6]) + 2.0 * (z * g[8]),
        ]
        radial_part = d_radius - inverse * (toward[0] * x + toward[1] * y + toward[2] * z)
        for i in range(3):
            d_offset = inverse * toward[i] + unit[i] * radial_part
            summed = jnp.sum(d_offset, axis=0, keepdims=True)
            other_row = summed + pltpu.roll(summed, TA, 1)
            square[0:TA, :] = d_offset
            square[TA:, :] = d_offset
            centre_row = -jnp.sum(square[...].T, axis=0, keepdims=True)
            component = flag(lax.broadcasted_iota(jnp.int32, (3, CHUNK), 0) == i)
            for q in range(4):
                at = chunk_mask(others[p], q) * other_row
                if q in (1, 2):
                    at = at + chunk_mask(centres[p] + SEND, q) * centre_row
                tile_grads[q] = tile_grads[q] + at * component
    own[...] = jnp.zeros_like(own)
    own[0:3, 0:CHUNK] = tile_grads[1]
    own[0:3, CHUNK:] = tile_grads[2]
    own[3:6, 0:CHUNK] = tile_grads[0]
    own[3:6, CHUNK:] = tile_grads[3]
    leaving = []
    for first, ghost_grad in ((0, tile_grads[0]), (SEND, tile_grads[3])):
        listed = paired(*(pick(tile_grads[1:3], number(SENT + first + j)) for j in range(SEND)))
        leaving.append((listed, ghost_grad))
    for shift, outs in ((0, (one_first, one_second)), (1, (two_first, two_second))):
        choice = upward(shift)
        for out, above in zip(outs, (choice, 1.0 - choice)):
            out[...] = jnp.zeros_like(out)
            out[0:3, :] = either(above, leaving[1][0], leaving[0][0])
            out[3:6, :] = either(above, leaving[1][1], leaving[0][1])


def tangent_kernel(
    scale, flags, atoms, weights, mh, ml, from_first, from_second, own, one_second, two_second, one_first, two_first,
    rows, env, gate, curve, inv, shape_store, xh, xl,
    forces, keep, give, small, envdot, curl, both,
    square, turned, th, tl, raw, left, right,
):
    ghost = SEND * TA
    def number(row):
        return flags[row : row + 1, :]

    centres = [number(CENTRE + p) for p in range(PAIRS)]
    others = [number(OTHER + p) for p in range(PAIRS)]
    shared = flags[SHARED : SHARED + 1, 0:1]
    mine = [own[0:3, 0:CHUNK], own[0:3, CHUNK:]]
    up, up_two = upward(0), upward(1)
    low_one = either(up, one_second[...], one_first[...])
    high_one = either(up, one_first[...], one_second[...])
    low_two = either(up_two, two_second[...], two_first[...])
    high_two = either(up_two, two_first[...], two_second[...])
    low_tail = either(up, from_second[ghost:, :], from_first[ghost:, :])
    high_tail = either(up, from_first[ghost:, :], from_second[ghost:, :])
    arrived = [twice(low_one[3:6, :], j) for j in range(SEND)]
    arrived += [twice(high_one[3:6, :], j) for j in range(SEND)]
    for j in range(2 * SEND):
        for q in range(2):
            mine[q] = mine[q] + chunk_mask(number(SENT + j), q) * arrived[j]
    below = low_one[0:3, :]
    above = high_one[0:3, :]
    to_below = [twice(low_two[3:6, :], j) for j in range(SEND)]
    to_below += [twice(own[3:6, 0:CHUNK], j) for j in range(SEND)]
    to_above = [twice(own[3:6, CHUNK:], j) for j in range(SEND)]
    to_above += [twice(high_two[3:6, :], j) for j in range(SEND)]
    for j in range(2 * SEND):
        below = below + low_tail[3 + j : 4 + j, 0:CHUNK] * to_below[j]
        above = above + high_tail[3 + j : 4 + j, 0:CHUNK] * to_above[j]
    for q in range(2):
        for i in range(3):
            forces[i, :, q * CHUNK : (q + 1) * CHUNK] = -mine[q][i : i + 1, :]
    error = [
        below + low_tail[0:3, CHUNK:],
        mine[0] + atoms[4:7, 0:CHUNK],
        mine[1] + atoms[4:7, CHUNK:],
        above + high_tail[0:3, CHUNK:],
    ]
    error = [part * scale for part in error]
    both[...] = jnp.zeros_like(both)
    both[0:8, :] = rows[...]
    both[8:11, :] = paired(*(pick(error, others[p]) for p in range(PAIRS)))
    both[11:14, :] = paired(*(pick(error[1:3], centres[p]) for p in range(PAIRS)))
    columns_of(both[...], square, turned)

    for p in range(PAIRS):
        lane_move = [twice(both[8 + i : 9 + i, :], p) for i in range(3)]
        column_move = [turned[p * TA : (p + 1) * TA, 11 + i : 12 + i] for i in range(3)]
        unit = [shape_store[p, i] for i in range(3)]
        inverse = shape_store[p, 3]
        values = [shape_store[p, 4 + k] for k in range(BASIS // 2)]
        slopes = [shape_store[p, 8 + k] for k in range(BASIS // 2)]
        move = [a - b for a, b in zip(lane_move, column_move)]
        stretch = unit[0] * move[0] + unit[1] * move[1] + unit[2] * move[2]
        turn = [(m - v * stretch) * inverse for m, v in zip(move, unit)]
        angular, turning = harmonics(unit), harmonics_tangent(unit, turn)
        slopes = [s * stretch for s in slopes]
        for m in range(COMPS):
            for k in range(BASIS // 2):
                entry = slopes[k] if m == 0 else angular[m] * slopes[k] + turning[m] * values[k]
                hi, lo = split(entry)
                th[p, m * TA : (m + 1) * TA, k * CHUNK : (k + 1) * CHUNK] = hi
                tl[p, m * TA : (m + 1) * TA, k * CHUNK : (k + 1) * CHUNK] = lo
        raw[p * COMPS * TA : (p + 1) * COMPS * TA, :] = product((th[p], tl[p]), (xh[p], xl[p]), NN)

    for m in range(COMPS):
        first = raw[m * TA : (m + 1) * TA, :]
        second = raw[(COMPS + m) * TA : (COMPS + m + 1) * TA, :]
        envdot[m * TA : (m + 1) * TA, :] = env_scale * (first + shared * second)
        envdot[(COMPS + m) * TA : (COMPS + m + 1) * TA, :] = env_scale * (second + shared * first)
    invdot = left
    half = PAIRS * TA
    for p in range(PAIRS):
        sums = [None] * 3
        for m in range(COMPS):
            at = slice((p * COMPS + m) * TA, (p * COMPS + m + 1) * TA)
            term = 2.0 * env[at, :] * envdot[at, :]
            sums[GROUP[m]] = term if sums[GROUP[m]] is None else sums[GROUP[m]] + term
        for g in range(3):
            invdot[half + p * TA : half + (p + 1) * TA, g * 256 : (g + 1) * 256] = sums[g]
    invdot[0:half, :] = inv[...]
    hidden_move = product(split(invdot[half:, :]), (mh[...], ml[...]), NN)
    bend = curve[...] * hidden_move
    curl[...] = bend
    once = 1.0 - shared * flag(lax.broadcasted_iota(jnp.int32, (half, 1), 0) >= TA)
    right[0:half, :] = bend * once
    right[half:, :] = gate[...] * weights[BASIS + SPECIES : BASIS + SPECIES + 1, :] * once
    core = lax.axis_index("batch")
    left_parts = split(left[...])
    for out, part in ((keep, core), (give, 1 - core)):
        lanes = pl.ds(pl.multiple_of(part * HALF, HALF), HALF)
        out[...] = product(left_parts, split(right[:, lanes]), TN)
    small[...] = jnp.zeros_like(small)
    kind = turned[:, 6:7]
    for s in range(SPECIES):
        small[s : s + 1, :] = jnp.sum(right[0:half, :] * flag(kind == float(s)), axis=0, keepdims=True)
    small[SPECIES : SPECIES + 1, :] = jnp.sum(gate[...] * hidden_move * once, axis=0, keepdims=True)


def radial_kernel(
    p, flags, both, fsel, env, envdot, dinv, curl, mh, ml, after,
    grad_radial,
    square, turned, lh, ll, gh, gl, raw,
):
    low, high = lane_half()
    columns_of(both[...], square, turned)
    here = slice(p * TA, (p + 1) * TA)
    turn_inv = product(split(curl[here, :]), (mh[...], ml[...]), NT)
    lane_rows = [twice(both[3 + i : 4 + i, :], p) for i in range(3)]
    lane_move = [twice(both[11 + i : 12 + i, :], p) for i in range(3)]
    columns = [turned[here, i : i + 1] for i in range(3)]
    column_move = [turned[here, 8 + i : 9 + i] for i in range(3)]
    unit, inverse, weight, slope, sine, cosine = geometry(
        lane_rows, columns, -1.0, flags[LIVE + p : LIVE + p + 1, :], flags[SAME + p : SAME + p + 1, :]
    )
    move = [b - a for a, b in zip(lane_move, column_move)]
    stretch = unit[0] * move[0] + unit[1] * move[1] + unit[2] * move[2]
    turn = [(m - v * stretch) * inverse for m, v in zip(move, unit)]
    angular, turning = harmonics(unit), harmonics_tangent(unit, turn)
    values, slopes = single_orders(sine, cosine, weight, slope)
    for m in range(COMPS):
        if m == 0:
            on_value, on_slope = low, high * stretch
        else:
            on_value = angular[m] * low + turning[m] * high
            on_slope = angular[m] * high * stretch
        for n in range(BASIS):
            hi, lo = split(on_value * values[n] + on_slope * slopes[n])
            lh[n * TA : (n + 1) * TA, m * CHUNK : (m + 1) * CHUNK] = hi
            ll[n * TA : (n + 1) * TA, m * CHUNK : (m + 1) * CHUNK] = lo
        at = slice((p * COMPS + m) * TA, (p * COMPS + m + 1) * TA)
        group = slice(GROUP[m] * 256, (GROUP[m] + 1) * 256)
        steady = (2.0 * env_scale) * dinv[here, group]
        bent = (2.0 * env_scale) * turn_inv[:, group]
        hi, lo = split(env[at, :] * bent + envdot[at, :] * steady)
        gh[m * CHUNK : m * CHUNK + TA, :] = hi
        gl[m * CHUNK : m * CHUNK + TA, :] = lo
        hi, lo = split(env[at, :] * steady)
        gh[m * CHUNK + TA : (m + 1) * CHUNK, :] = hi
        gl[m * CHUNK + TA : (m + 1) * CHUNK, :] = lo
    raw[...] = product((lh[...], ll[...]), (gh[...], gl[...]), NN)
    for n in range(BASIS):
        grad_radial[n : n + 1, :] = jnp.sum(
            raw[n * TA : (n + 1) * TA, :] * fsel[here, :], axis=0, keepdims=True
        )


SMALL = 32
FOUR = 4


def block_of(part, rows):
    return pl.ds(pl.multiple_of(part * rows, 8), rows)


def block_of_lanes(part):
    return pl.ds(pl.multiple_of(part * HALF, HALF), HALF)


def total_of(refs, at):
    total = refs[0][at, :]
    for ref in refs[1:]:
        total = total + ref[at, :]
    return total


def halve_kernel(keep, taken, keep_out, give_out):
    me = place(0, 2)
    for out, part in ((keep_out, me), (give_out, 1 - me)):
        out[...] = total_of([keep, taken], block_of(part, out.shape[0]))


def spread_kernel(keep, taken, radial_0, radial_1, small, *refs):
    outs, tiny = refs[:FOUR], refs[FOUR]
    for h in range(2):
        lanes = slice(h * HALF, (h + 1) * HALF)
        tiny[16 * h : 16 * h + 8, :] = radial_0[:, lanes] + radial_1[:, lanes]
        tiny[16 * h + 8 : 16 * h + 16, :] = small[:, lanes]
    me = place(1, FOUR)
    for k, out in enumerate(outs):
        rows, few = out.shape[0] - SMALL // FOUR, SMALL // FOUR
        to = lax.bitwise_xor(me, k)
        out[0:rows, :] = total_of([keep, taken], block_of(to, rows))
        out[rows:, :] = tiny[block_of(to, few), :]


def total_kernel(*refs):
    refs[-1][...] = total_of(refs[:-1], slice(None))


def grow_kernel(*refs):
    parts, out = refs[:FOUR], refs[FOUR]
    few = SMALL // FOUR
    rows = parts[0].shape[0] - few
    me = place(1, FOUR)
    for k, ref in enumerate(parts):
        to = lax.bitwise_xor(me, k)
        out[block_of(to, rows), :] = ref[0:rows, :]
        out[pl.ds(pl.multiple_of(FOUR * rows + to * few, 8), few), :] = ref[rows:, :]


def join_kernel(mine, theirs, facing_mine, facing_theirs, mix, radial, kinds, out):
    rows = mine.shape[0] - SMALL
    me, core = place(0, 2), lax.axis_index("batch")
    for lane_part, pair in ((core, (mine, theirs)), (1 - core, (facing_mine, facing_theirs))):
        lanes = block_of_lanes(lane_part)
        for ref, part in zip(pair, (me, 1 - me)):
            mix[block_of(part, rows), lanes] = ref[0:rows, :]
    both = (mine[rows:, :] + theirs[rows:, :]) + (facing_mine[rows:, :] + facing_theirs[rows:, :])
    for h in range(2):
        lanes = slice(h * HALF, (h + 1) * HALF)
        few = both[16 * h : 16 * h + 16, :]
        radial[:, lanes] = few[0:BASIS]
        kinds[:, lanes] = few[BASIS : BASIS + SPECIES]
        out[:, lanes] = few[BASIS + SPECIES : BASIS + SPECIES + 1]


def spec(space):
    return pl.BlockSpec(memory_space=space)


def call(kernel, name, outs, scratch, *operands, space=pltpu.VMEM, after=(), flops=0):
    if space is pltpu.HBM:
        operands = [pltpu.with_memory_space_constraint(operand, space) for operand in operands]
    outs = [out if len(out) == 2 and isinstance(out[0], tuple) else (out, F32) for out in outs]
    return pl.pallas_call(
        kernel,
        name=name,
        out_shape=[jax.ShapeDtypeStruct(*out) for out in outs],
        in_specs=[spec(space)] * len(operands) + [spec(pltpu.VMEM)] * len(after),
        out_specs=[spec(pltpu.VMEM)] * len(outs),
        scratch_shapes=[pltpu.VMEM(*item) if isinstance(item, tuple) else item for item in scratch],
        compiler_params=pltpu.CompilerParams(vmem_limit_bytes=28 * 1024 * 1024),
        cost_estimate=pl.CostEstimate(flops=flops, bytes_accessed=1 << 20, transcendentals=0),
    )(*operands, *after)


def shifted(block, axis, by):
    count = lax.axis_size(axis)
    return lax.ppermute(block, axis, [(i, (i + by) % count) for i in range(count)])


def exchanged(block, shift, first):
    count, step = lax.axis_size("domain"), 1 << shift
    up = [((i >> shift) & 1 == 0) == first for i in range(count)]
    return lax.ppermute(block, "domain", [(i, (i + step if up[i] else i - step) % count) for i in range(count)])


def partner(block, mask):
    return lax.ppermute(block, "domain", [(i, i ^ mask) for i in range(lax.axis_size("domain"))])


def on_device(
    positions,
    features,
    species,
    ref_forces,
    centre_tile,
    other_tile,
    pair_live,
    send_tiles,
    radial_w,
    mix_w,
    species_w,
    out_w,
):
    atoms_here = positions.shape[2]
    channels = features.shape[2]
    table = (COMPS * TA, BASIS * TA)
    sent = (SEND * TA + GHOST_ROWS, channels)
    slots = PAIRS * TA
    line = (3, 1, atoms_here)
    turning = [((CHUNK, CHUNK), F32)] * 2
    out_row = out_w.reshape(1, channels)
    positions = positions.transpose(1, 0, 2)
    ref_forces = ref_forces.transpose(1, 0, 2)
    ints = [((1, n), jnp.int32) for n in (PAIRS, PAIRS, PAIRS, 2 * SEND)]

    to_second, to_first, token = call(
        gather_kernel,
        "gather",
        [sent, sent, (8, CHUNK)],
        [
            ints[3],
            (line, F32),
            ((1, atoms_here, channels), F32),
            (line, F32),
            pltpu.SemaphoreType.DMA((4,)),
        ],
        send_tiles, positions, features, ref_forces,
        space=pltpu.HBM,
    )
    from_second = exchanged(to_second, 0, False)
    from_first = exchanged(to_first, 0, True)
    flags, atoms, own_feat, weights, mh, ml = call(
        stage_kernel,
        "stage",
        [
            (16, CHUNK),
            (8, atoms_here),
            (atoms_here, channels),
            (16, channels),
            (mix_w.shape, BF16),
            (mix_w.shape, BF16),
        ],
        ints
        + [(line, F32), (line, F32), ((1, atoms_here), jnp.int32)]
        + [(radial_w.shape, F32), (mix_w.shape, F32), (species_w.shape, F32), (out_row.shape, F32)]
        + [pltpu.SemaphoreType.DMA((12,))],
        centre_tile, other_tile, pair_live, send_tiles, positions, ref_forces, species, features,
        radial_w, mix_w, species_w, out_row,
        space=pltpu.HBM,
        after=(token,),
    )

    factors = (PAIRS, BASIS * TA, channels)
    env, dinv, gate, curve, inv, rows, fsel, own, *leaving, shape_store, xh, xl = call(
        force_kernel,
        "force",
        [
            (PAIRS * COMPS * TA, channels),
            (slots, 3 * channels),
            (slots, channels),
            (slots, channels),
            (slots, 3 * channels),
            (8, CHUNK),
            (slots, channels),
            (8, atoms_here),
            (8, CHUNK),
            (8, CHUNK),
            (8, CHUNK),
            (8, CHUNK),
            (PAIRS, 4 + BASIS, TA, CHUNK),
            (factors, BF16),
            (factors, BF16),
        ],
        turning
        + [((PAIRS, *table), BF16)] * 2
        + [((PAIRS, COMPS * TA, channels), BF16)] * 2
        + [((PAIRS * COMPS * TA, channels), F32), ((PAIRS, *table), F32)],
        flags, atoms, own_feat, weights, mh, ml, from_second, from_first,
        flops=1 << 31,
    )
    arriving = [exchanged(leaving[i], i // 2, i % 2 == 0) for i in (1, 3, 0, 2)]

    rows_mix = 3 * channels
    total_count = 3.0 * atoms_here * lax.axis_size("domain") * lax.axis_size("batch")
    forces, keep, give, small, envdot, curl, both = call(
        functools.partial(tangent_kernel, 2.0 / math.sqrt(total_count)),
        "tangent",
        [
            line,
            (rows_mix, HALF),
            (rows_mix, HALF),
            (8, channels),
            (PAIRS * COMPS * TA, channels),
            (slots, channels),
            (16, CHUNK),
        ],
        turning
        + [((PAIRS, *table), BF16)] * 2
        + [((PAIRS * COMPS * TA, channels), F32)]
        + [((2 * slots, 3 * channels), F32), ((2 * slots, channels), F32)],
        flags, atoms, weights, mh, ml, from_first, from_second, own, *arriving,
        rows, env, gate, curve, inv, shape_store, xh, xl,
        flops=1 << 31,
    )

    def radial(p, after):
        return call(
            functools.partial(radial_kernel, p),
            "radial",
            [(BASIS, channels)],
            turning
            + [((BASIS * TA, COMPS * CHUNK), BF16)] * 2
            + [((COMPS * CHUNK, channels), BF16)] * 2
            + [((BASIS * TA, channels), F32)],
            flags, both, fsel, env, envdot, dinv, curl, mh, ml, after,
            flops=1 << 31,
        )[0]

    keep, give = call(
        halve_kernel, "halve", [(rows_mix // 2, HALF)] * 2, [], keep, shifted(give, "batch", 1)
    )
    taken = partner(give, 1)
    radials = [radial(p, keep) for p in range(PAIRS)]
    piece = rows_mix // (2 * FOUR) + SMALL // FOUR
    blocks = call(
        spread_kernel, "spread", [(piece, HALF)] * FOUR, [((SMALL, HALF), F32)],
        keep, taken, *radials, small,
    )
    terms = [blocks[0]] + [partner(blocks[k], 2 * k) for k in range(FOUR - 1, 0, -1)]
    (mine,) = call(total_kernel, "total", [(piece, HALF)], [], *terms)
    bit = 2 * FOUR
    while bit < lax.axis_size("domain"):
        (mine,) = call(total_kernel, "total", [(piece, HALF)], [], mine, partner(mine, bit))
        bit *= 2
    parts = [mine] + [partner(mine, 2 * k) for k in range(1, FOUR)]
    (mine,) = call(grow_kernel, "grow", [(rows_mix // 2 + SMALL, HALF)], [], *parts)
    theirs = partner(mine, 1)
    facing = [shifted(part, "batch", 1) for part in (mine, theirs)]
    mix, radial_sum, kinds, out = call(
        join_kernel,
        "join",
        [(rows_mix, channels), (BASIS, channels), (SPECIES, channels), (1, channels)],
        [],
        mine,
        theirs,
        *facing,
    )
    return forces.transpose(1, 0, 2), radial_sum, mix, kinds, out.reshape(channels)


def solution(mesh):
    return jax.shard_map(
        on_device,
        mesh=mesh,
        in_specs=(
            P(("parts", "batch"), None, "domain"),
            P(("parts", "batch"), "domain", None),
            P(("parts", "batch"), "domain"),
            P(("parts", "batch"), None, "domain"),
            P(("parts", "batch"), "domain"),
            P(("parts", "batch"), "domain"),
            P(("parts", "batch"), "domain"),
            P(("parts", "batch"), "domain"),
            P(),
            P(),
            P(),
            P(),
        ),
        out_specs=(
            P(("parts", "batch"), None, "domain"),
            P("parts", None),
            P("parts", None),
            P("parts", None),
            P("parts"),
        ),
        check_vma=False,
    )
```

```python
import functools
import math

import jax
import jax.numpy as jnp
from jax import lax
from jax.experimental import pallas as pl
from jax.experimental.pallas import tpu as pltpu
from jax.sharding import PartitionSpec as P

TA = 64
SEND = 2
PAIRS = 2
COMPS = 9
BASIS = 8
SPECIES = 4
HALF = 128
CHUNK = 2 * TA

cutoff = 2.5
soften = 0.25
env_scale = 0.25
root_three = math.sqrt(3.0)
F32 = jnp.float32
BF16 = jnp.bfloat16
NN = (((1,), (0,)), ((), ()))
NT = (((1,), (1,)), ((), ()))
TN = (((0,), (0,)), ((), ()))
GROUP = (0, 1, 1, 1, 2, 2, 2, 2, 2)


def split(value):
    high = value.astype(BF16)
    return high, (value - high.astype(F32)).astype(BF16)


def product(left, right, dims):
    (lh, ll), (rh, rl) = left, right

    def one(x, y):
        return lax.dot_general(x, y, dims, preferred_element_type=F32)

    return one(lh, rh) + (one(lh, rl) + one(ll, rh))


def flag(condition):
    return jnp.where(condition, 1.0, 0.0).astype(F32)


def place(shift, width):
    return lax.bitwise_and(lax.shift_right_logical(lax.axis_index("domain"), shift), width - 1)


def lane_half():
    lane = lax.broadcasted_iota(jnp.int32, (1, CHUNK), 1)
    low = flag(lane < TA)
    return low, 1.0 - low


def twice(chunk, half):
    low, high = lane_half()
    swapped = pltpu.roll(chunk, TA, 1)
    return chunk * low + swapped * high if half == 0 else swapped * low + chunk * high


def pick(chunks, position):
    total = None
    for q, chunk in enumerate(chunks):
        for half in range(2):
            term = twice(chunk, half) * flag(position == 2 * q + half)
            total = term if total is None else total + term
    return total


def paired(first, second):
    low, high = lane_half()
    return first * low + second * high


def chunk_mask(position, q):
    low, high = lane_half()
    return low * flag(position == 2 * q) + high * flag(position == 2 * q + 1)


def geometry(lane_rows, columns, sign, live, same):
    offset = [(row - column) * sign for row, column in zip(lane_rows, columns)]
    dist_sq = offset[0] * offset[0] + offset[1] * offset[1] + offset[2] * offset[2] + soften
    distance = jnp.sqrt(dist_sq)
    inverse = 1.0 / distance
    unit = [x * inverse for x in offset]
    row = lax.broadcasted_iota(jnp.int32, (TA, CHUNK), 0)
    lane = lax.broadcasted_iota(jnp.int32, (TA, CHUNK), 1)
    lane = jnp.where(lane >= TA, lane - TA, lane)
    mask = live * (1.0 - same * flag(row == lane))
    base = jnp.maximum(1.0 - dist_sq * (1.0 / (cutoff * cutoff)), 0.0)
    weight = base * base * base * mask * inverse
    slope = -(6.0 / (cutoff * cutoff)) * base * base * mask - weight * inverse
    angle = distance * (math.pi / cutoff)
    return unit, inverse, weight, slope, jnp.sin(angle), jnp.cos(angle)


def harmonics(v):
    x, y, z = v
    return [
        None,
        x,
        y,
        z,
        root_three * x * y,
        root_three * y * z,
        root_three * z * x,
        0.5 * root_three * (x * x - y * y),
        z * z - 0.5 * (x * x + y * y),
    ]


def harmonics_tangent(v, t):
    x, y, z = v
    a, b, c = t
    return [
        None,
        a,
        b,
        c,
        root_three * (a * y + x * b),
        root_three * (b * z + y * c),
        root_three * (c * x + z * a),
        root_three * (x * a - y * b),
        2.0 * z * c - (x * a + y * b),
    ]


def paired_orders(sine, cosine, weight, slope):
    low, high = lane_half()
    double_s, double_c = 2.0 * sine * cosine, 1.0 - 2.0 * sine * sine
    now_s = sine * low + double_s * high
    now_c = cosine * low + double_c * high
    old_s = -sine * low
    old_c = cosine * low + high
    values, slopes = [], []
    for k in range(BASIS // 2):
        order = ((2 * k + 1) * low + (2 * k + 2) * high) * (math.pi / cutoff)
        values.append(now_s * weight)
        slopes.append(now_c * (weight * order) + now_s * slope)
        now_s, old_s = 2.0 * double_c * now_s - old_s, now_s
        now_c, old_c = 2.0 * double_c * now_c - old_c, now_c
    return values, slopes


def single_orders(sine, cosine, weight, slope):
    now_s, now_c = sine, cosine
    old_s, old_c = jnp.zeros_like(sine), jnp.ones_like(cosine)
    values, slopes = [], []
    for n in range(1, BASIS + 1):
        values.append(now_s * weight)
        slopes.append(now_c * (weight * (n * math.pi / cutoff)) + now_s * slope)
        now_s, old_s = 2.0 * cosine * now_s - old_s, now_s
        now_c, old_c = 2.0 * cosine * now_c - old_c, now_c
    return values, slopes


def columns_of(rows, square, turned):
    square[...] = jnp.zeros_like(square)
    square[0 : rows.shape[0], :] = rows
    turned[...] = square[...].T


def pair_rows(first, p):
    return twice(first, p)


def radial_feat(feat, radial, p, high_ref, low_ref):
    own = feat[p * TA : (p + 1) * TA, :]
    for n in range(BASIS):
        hi, lo = split(own * radial[n : n + 1, :])
        high_ref[n * TA : (n + 1) * TA, :] = hi
        low_ref[n * TA : (n + 1) * TA, :] = lo


OTHER, CENTRE, LIVE, SAME, SHARED, SENT = 0, 2, 4, 6, 8, 9
GHOST_ROWS = 8


def fetch(pairs, sems):
    copies = [pltpu.make_async_copy(src, dst, sems.at[i]) for i, (src, dst) in enumerate(pairs)]
    for copy in copies:
        copy.start()
    return copies


def upward(shift):
    return 1.0 - flag(place(shift, 2) == 1)


def either(choice, first, second):
    return first * choice + second * (1.0 - choice)


def gather_kernel(send, pos, feat, ref, to_second, to_first, token, send_v, pos_v, feat_v, ref_v, sems):
    copies = fetch([(send, send_v), (pos, pos_v), (ref, ref_v), (feat, feat_v)], sems)
    for copy in copies[:3]:
        copy.wait()
    low, high = lane_half()
    up = upward(0)
    sent = [send_v[0:1, j : j + 1].astype(F32) for j in range(2 * SEND)]
    tiles_of = []
    for out, choice in ((to_first, 1.0 - up), (to_second, up)):
        tiles = [either(choice, sent[j], sent[SEND + j]) for j in range(SEND)]
        tiles_of.append(tiles)
        out[SEND * TA :, :] = jnp.zeros((GHOST_ROWS, out.shape[1]), F32)
        for i in range(3):
            at = SEND * TA + i
            for lanes, source in ((slice(0, CHUNK), pos_v), (slice(CHUNK, 2 * CHUNK), ref_v)):
                chunks = [source[i, :, q * CHUNK : (q + 1) * CHUNK] for q in range(2)]
                out[at : at + 1, lanes] = paired(pick(chunks, tiles[0]), pick(chunks, tiles[1]))
        for other in range(2 * SEND):
            same = low * flag(sent[other] == tiles[0]) + high * flag(sent[other] == tiles[1])
            out[SEND * TA + 3 + other : SEND * TA + 4 + other, 0:CHUNK] = same
    token[...] = jnp.zeros_like(token)
    copies[3].wait()
    for out, tiles in zip((to_first, to_second), tiles_of):
        for j in range(SEND):
            out[j * TA : (j + 1) * TA, :] = pick_rows(feat_v.at[0], tiles[j], 0.0)


def pick_rows(ref, position, first):
    total = None
    for t in range(ref.shape[0] // TA):
        term = ref[t * TA : (t + 1) * TA, :] * flag(position == first + float(t))
        total = term if total is None else total + term
    return total


def stage_kernel(
    centre, other, live, send, pos, ref, species, feat, radial_w, mix_w, species_w, out_w, after,
    flags, atoms, own_feat, weights, mh, ml,
    centre_v, other_v, live_v, send_v, pos_v, ref_v, species_v, radial_v, mix_v, species_w_v, out_v, sems,
):
    copies = fetch(
        [
            (centre, centre_v), (other, other_v), (live, live_v), (send, send_v), (pos, pos_v), (ref, ref_v),
            (species, species_v), (radial_w, radial_v), (species_w, species_w_v), (out_w, out_v),
            (feat.at[0], own_feat), (mix_w, mix_v),
        ],
        sems,
    )
    for copy in copies[:-1]:
        copy.wait()
    flags[...] = jnp.zeros_like(flags)
    centres = [centre_v[0:1, p : p + 1].astype(F32) for p in range(PAIRS)]
    others = [other_v[0:1, p : p + 1].astype(F32) for p in range(PAIRS)]
    for p in range(PAIRS):
        for row, value in (
            (OTHER, others[p]),
            (CENTRE, centres[p]),
            (LIVE, live_v[0:1, p : p + 1].astype(F32)),
            (SAME, flag(others[p] == centres[p] + SEND)),
        ):
            flags[row + p : row + p + 1, :] = jnp.broadcast_to(value, (1, CHUNK))
    flags[SHARED : SHARED + 1, :] = jnp.broadcast_to(flag(centres[0] == centres[1]), (1, CHUNK))
    for j in range(2 * SEND):
        value = send_v[0:1, j : j + 1].astype(F32)
        flags[SENT + j : SENT + j + 1, :] = jnp.broadcast_to(value, (1, CHUNK))
    atoms[...] = jnp.zeros_like(atoms)
    for i in range(3):
        atoms[i : i + 1, :] = pos_v[i]
        atoms[4 + i : 5 + i, :] = ref_v[i]
    atoms[3:4, :] = species_v[...].astype(F32)
    weights[...] = jnp.zeros_like(weights)
    weights[0:BASIS, :] = radial_v[...]
    weights[BASIS : BASIS + SPECIES, :] = species_w_v[...]
    weights[BASIS + SPECIES : BASIS + SPECIES + 1, :] = out_v[...]
    copies[-1].wait()
    hi, lo = split(mix_v[...])
    mh[...] = hi
    ml[...] = lo


def force_kernel(
    flags, atoms, feat, weights, mh, ml, from_second, from_first,
    env, dinv, gate, curve, inv, rows, fsel, own, leaving, shape_store, xh, xl,
    square, turned, th, tl, eh, el, raw, back,
):
    ghost = SEND * TA
    up = upward(0)
    near, far = from_first[ghost : ghost + 3, 0:CHUNK], from_second[ghost : ghost + 3, 0:CHUNK]
    chunks = [either(up, far, near), atoms[0:3, 0:CHUNK], atoms[0:3, CHUNK:], either(up, near, far)]
    kinds = [atoms[3:4, q * CHUNK : (q + 1) * CHUNK] for q in range(2)]

    def number(row):
        return flags[row : row + 1, :]

    centres = [number(CENTRE + p) for p in range(PAIRS)]
    others = [number(OTHER + p) for p in range(PAIRS)]
    shared = flags[SHARED : SHARED + 1, 0:1]
    rows[...] = jnp.zeros_like(rows)
    rows[0:3, :] = paired(*(pick(chunks, others[p]) for p in range(PAIRS)))
    rows[3:6, :] = paired(*(pick(chunks[1:3], centres[p]) for p in range(PAIRS)))
    rows[6:7, :] = paired(*(pick(kinds, centres[p]) for p in range(PAIRS)))
    columns_of(rows[...], square, turned)

    for p in range(PAIRS):
        o = flags[OTHER + p : OTHER + p + 1, 0:1]
        fsel[p * TA : (p + 1) * TA, :] = (
            pick_rows(from_first.at[0:ghost], o, (SEND + 4) * up)
            + pick_rows(feat, o, float(SEND))
            + pick_rows(from_second.at[0:ghost], o, (SEND + 4) * (1.0 - up))
        )

    shapes = []
    for p in range(PAIRS):
        lane_rows = [twice(rows[i : i + 1, :], p) for i in range(3)]
        columns = [turned[p * TA : (p + 1) * TA, 3 + i : 4 + i] for i in range(3)]
        unit, inverse, weight, slope, sine, cosine = geometry(
            lane_rows, columns, 1.0, number(LIVE + p), number(SAME + p)
        )
        angular = harmonics(unit)
        values, slopes = paired_orders(sine, cosine, weight, slope)
        shapes.append((unit, inverse, angular, values, slopes))
        for i, part in enumerate(unit + [inverse] + values + slopes):
            shape_store[p, i] = part
        for m in range(COMPS):
            for k in range(BASIS // 2):
                entry = values[k] if m == 0 else angular[m] * values[k]
                hi, lo = split(entry)
                th[p, m * TA : (m + 1) * TA, k * CHUNK : (k + 1) * CHUNK] = hi
                tl[p, m * TA : (m + 1) * TA, k * CHUNK : (k + 1) * CHUNK] = lo
        radial_feat(fsel, weights, p, xh.at[p], xl.at[p])
        raw[p * COMPS * TA : (p + 1) * COMPS * TA, :] = product((th[p], tl[p]), (xh[p], xl[p]), NN)

    for m in range(COMPS):
        first = raw[m * TA : (m + 1) * TA, :]
        second = raw[(COMPS + m) * TA : (COMPS + m + 1) * TA, :]
        env[m * TA : (m + 1) * TA, :] = env_scale * (first + shared * second)
        env[(COMPS + m) * TA : (COMPS + m + 1) * TA, :] = env_scale * (second + shared * first)
    for p in range(PAIRS):
        sums = [None] * 3
        for m in range(COMPS):
            block = env[(p * COMPS + m) * TA : (p * COMPS + m + 1) * TA, :]
            sums[GROUP[m]] = block * block if sums[GROUP[m]] is None else sums[GROUP[m]] + block * block
        for g in range(3):
            inv[p * TA : (p + 1) * TA, g * 256 : (g + 1) * 256] = sums[g]
    hidden = product(split(inv[...]), (mh[...], ml[...]), NN)
    kind = turned[:, 6:7]
    for s in range(SPECIES):
        hidden = hidden + flag(kind == float(s)) * weights[BASIS + s : BASIS + s + 1, :]
    out_row = weights[BASIS + SPECIES : BASIS + SPECIES + 1, :]
    sigma = 1.0 / (1.0 + jnp.exp(-hidden))
    first_order = sigma * (1.0 + hidden * (1.0 - sigma))
    gate[...] = first_order
    curve[...] = sigma * (1.0 - sigma) * (2.0 + hidden * (1.0 - 2.0 * sigma)) * out_row
    dinv[...] = product(split(first_order * out_row), (mh[...], ml[...]), NT)

    tile_grads = [jnp.zeros((3, CHUNK), F32) for _ in range(4)]
    for p in range(PAIRS):
        unit, inverse, angular, values, slopes = shapes[p]
        for m in range(COMPS):
            block = env[(p * COMPS + m) * TA : (p * COMPS + m + 1) * TA, :]
            part = dinv[p * TA : (p + 1) * TA, GROUP[m] * 256 : (GROUP[m] + 1) * 256]
            hi, lo = split((2.0 * env_scale) * block * part)
            eh[p, m * TA : (m + 1) * TA, :] = hi
            el[p, m * TA : (m + 1) * TA, :] = lo
        back[p] = product((eh[p], el[p]), (xh[p], xl[p]), NT)
        d_radius = None
        d_angular = []
        for m in range(COMPS):
            along, across = None, None
            for k in range(BASIS // 2):
                block = back[p, m * TA : (m + 1) * TA, k * CHUNK : (k + 1) * CHUNK]
                along = block * slopes[k] if along is None else along + block * slopes[k]
                across = block * values[k] if across is None else across + block * values[k]
            d_angular.append(across)
            term = along if m == 0 else along * angular[m]
            d_radius = term if d_radius is None else d_radius + term
        x, y, z = unit
        g = d_angular
        toward = [
            g[1] + root_three * (y * g[4] + z * g[6] + x * g[7]) - x * g[8],
            g[2] + root_three * (x * g[4] + z * g[5] - y * g[7]) - y * g[8],
            g[3] + root_three * (y * g[5] + x * g[6]) + 2.0 * (z * g[8]),
        ]
        radial_part = d_radius - inverse * (toward[0] * x + toward[1] * y + toward[2] * z)
        for i in range(3):
            d_offset = inverse * toward[i] + unit[i] * radial_part
            summed = jnp.sum(d_offset, axis=0, keepdims=True)
            other_row = summed + pltpu.roll(summed, TA, 1)
            square[0:TA, :] = d_offset
            square[TA:, :] = d_offset
            centre_row = -jnp.sum(square[...].T, axis=0, keepdims=True)
            component = flag(lax.broadcasted_iota(jnp.int32, (3, CHUNK), 0) == i)
            for q in range(4):
                at = chunk_mask(others[p], q) * other_row
                if q in (1, 2):
                    at = at + chunk_mask(centres[p] + SEND, q) * centre_row
                tile_grads[q] = tile_grads[q] + at * component
    own[...] = jnp.zeros_like(own)
    own[0:3, 0:CHUNK] = tile_grads[1]
    own[0:3, CHUNK:] = tile_grads[2]
    own[3:6, 0:CHUNK] = tile_grads[0]
    own[3:6, CHUNK:] = tile_grads[3]
    block = jnp.zeros((3, CHUNK), F32)
    for k, (first, ghost_grad) in enumerate(((0, tile_grads[0]), (SEND, tile_grads[3]))):
        listed = paired(*(pick(tile_grads[1:3], number(SENT + first + j)) for j in range(SEND)))
        for to in range(leaving.shape[0]):
            leaving[to, 8 * k : 8 * k + 3, :] = listed
            leaving[to, 8 * k + 3 : 8 * k + 6, :] = ghost_grad
            leaving[to, 8 * k + 6 : 8 * k + 8, :] = block[0:2]


def tangent_kernel(
    scale, flags, atoms, weights, mh, ml, from_first, from_second, own, arriving,
    rows, env, gate, curve, inv, shape_store, xh, xl,
    forces, keep, give, small, envdot, curl, both,
    square, turned, th, tl, raw, left, right,
):
    ghost = SEND * TA
    def number(row):
        return flags[row : row + 1, :]

    centres = [number(CENTRE + p) for p in range(PAIRS)]
    others = [number(OTHER + p) for p in range(PAIRS)]
    shared = flags[SHARED : SHARED + 1, 0:1]
    mine = [own[0:3, 0:CHUNK], own[0:3, CHUNK:]]
    up = upward(0)
    count = lax.axis_size("domain")
    here = lax.axis_index("domain")
    low_one, low_two = (arriving[lax.rem(here + count - k, count), 8:16, :] for k in (1, 2))
    high_one, high_two = (arriving[lax.rem(here + k, count), 0:8, :] for k in (1, 2))
    low_tail = either(up, from_second[ghost:, :], from_first[ghost:, :])
    high_tail = either(up, from_first[ghost:, :], from_second[ghost:, :])
    arrived = [twice(low_one[3:6, :], j) for j in range(SEND)]
    arrived += [twice(high_one[3:6, :], j) for j in range(SEND)]
    for j in range(2 * SEND):
        for q in range(2):
            mine[q] = mine[q] + chunk_mask(number(SENT + j), q) * arrived[j]
    below = low_one[0:3, :]
    above = high_one[0:3, :]
    to_below = [twice(low_two[3:6, :], j) for j in range(SEND)]
    to_below += [twice(own[3:6, 0:CHUNK], j) for j in range(SEND)]
    to_above = [twice(own[3:6, CHUNK:], j) for j in range(SEND)]
    to_above += [twice(high_two[3:6, :], j) for j in range(SEND)]
    for j in range(2 * SEND):
        below = below + low_tail[3 + j : 4 + j, 0:CHUNK] * to_below[j]
        above = above + high_tail[3 + j : 4 + j, 0:CHUNK] * to_above[j]
    for q in range(2):
        for i in range(3):
            forces[i, :, q * CHUNK : (q + 1) * CHUNK] = -mine[q][i : i + 1, :]
    error = [
        below + low_tail[0:3, CHUNK:],
        mine[0] + atoms[4:7, 0:CHUNK],
        mine[1] + atoms[4:7, CHUNK:],
        above + high_tail[0:3, CHUNK:],
    ]
    error = [part * scale for part in error]
    both[...] = jnp.zeros_like(both)
    both[0:8, :] = rows[...]
    both[8:11, :] = paired(*(pick(error, others[p]) for p in range(PAIRS)))
    both[11:14, :] = paired(*(pick(error[1:3], centres[p]) for p in range(PAIRS)))
    columns_of(both[...], square, turned)

    for p in range(PAIRS):
        lane_move = [twice(both[8 + i : 9 + i, :], p) for i in range(3)]
        column_move = [turned[p * TA : (p + 1) * TA, 11 + i : 12 + i] for i in range(3)]
        unit = [shape_store[p, i] for i in range(3)]
        inverse = shape_store[p, 3]
        values = [shape_store[p, 4 + k] for k in range(BASIS // 2)]
        slopes = [shape_store[p, 8 + k] for k in range(BASIS // 2)]
        move = [a - b for a, b in zip(lane_move, column_move)]
        stretch = unit[0] * move[0] + unit[1] * move[1] + unit[2] * move[2]
        turn = [(m - v * stretch) * inverse for m, v in zip(move, unit)]
        angular, turning = harmonics(unit), harmonics_tangent(unit, turn)
        slopes = [s * stretch for s in slopes]
        for m in range(COMPS):
            for k in range(BASIS // 2):
                entry = slopes[k] if m == 0 else angular[m] * slopes[k] + turning[m] * values[k]
                hi, lo = split(entry)
                th[p, m * TA : (m + 1) * TA, k * CHUNK : (k + 1) * CHUNK] = hi
                tl[p, m * TA : (m + 1) * TA, k * CHUNK : (k + 1) * CHUNK] = lo
        raw[p * COMPS * TA : (p + 1) * COMPS * TA, :] = product((th[p], tl[p]), (xh[p], xl[p]), NN)

    for m in range(COMPS):
        first = raw[m * TA : (m + 1) * TA, :]
        second = raw[(COMPS + m) * TA : (COMPS + m + 1) * TA, :]
        envdot[m * TA : (m + 1) * TA, :] = env_scale * (first + shared * second)
        envdot[(COMPS + m) * TA : (COMPS + m + 1) * TA, :] = env_scale * (second + shared * first)
    invdot = left
    half = PAIRS * TA
    for p in range(PAIRS):
        sums = [None] * 3
        for m in range(COMPS):
            at = slice((p * COMPS + m) * TA, (p * COMPS + m + 1) * TA)
            term = 2.0 * env[at, :] * envdot[at, :]
            sums[GROUP[m]] = term if sums[GROUP[m]] is None else sums[GROUP[m]] + term
        for g in range(3):
            invdot[half + p * TA : half + (p + 1) * TA, g * 256 : (g + 1) * 256] = sums[g]
    invdot[0:half, :] = inv[...]
    hidden_move = product(split(invdot[half:, :]), (mh[...], ml[...]), NN)
    bend = curve[...] * hidden_move
    curl[...] = bend
    once = 1.0 - shared * flag(lax.broadcasted_iota(jnp.int32, (half, 1), 0) >= TA)
    right[0:half, :] = bend * once
    right[half:, :] = gate[...] * weights[BASIS + SPECIES : BASIS + SPECIES + 1, :] * once
    core = lax.axis_index("batch")
    left_parts = split(left[...])
    for out, part in ((keep, core), (give, 1 - core)):
        lanes = pl.ds(pl.multiple_of(part * HALF, HALF), HALF)
        out[...] = product(left_parts, split(right[:, lanes]), TN)
    small[...] = jnp.zeros_like(small)
    kind = turned[:, 6:7]
    for s in range(SPECIES):
        small[s : s + 1, :] = jnp.sum(right[0:half, :] * flag(kind == float(s)), axis=0, keepdims=True)
    small[SPECIES : SPECIES + 1, :] = jnp.sum(gate[...] * hidden_move * once, axis=0, keepdims=True)


def radial_kernel(
    p, flags, both, fsel, env, envdot, dinv, curl, mh, ml, after,
    grad_radial,
    square, turned, lh, ll, gh, gl, raw,
):
    low, high = lane_half()
    columns_of(both[...], square, turned)
    here = slice(p * TA, (p + 1) * TA)
    turn_inv = product(split(curl[here, :]), (mh[...], ml[...]), NT)
    lane_rows = [twice(both[3 + i : 4 + i, :], p) for i in range(3)]
    lane_move = [twice(both[11 + i : 12 + i, :], p) for i in range(3)]
    columns = [turned[here, i : i + 1] for i in range(3)]
    column_move = [turned[here, 8 + i : 9 + i] for i in range(3)]
    unit, inverse, weight, slope, sine, cosine = geometry(
        lane_rows, columns, -1.0, flags[LIVE + p : LIVE + p + 1, :], flags[SAME + p : SAME + p + 1, :]
    )
    move = [b - a for a, b in zip(lane_move, column_move)]
    stretch = unit[0] * move[0] + unit[1] * move[1] + unit[2] * move[2]
    turn = [(m - v * stretch) * inverse for m, v in zip(move, unit)]
    angular, turning = harmonics(unit), harmonics_tangent(unit, turn)
    values, slopes = single_orders(sine, cosine, weight, slope)
    for m in range(COMPS):
        if m == 0:
            on_value, on_slope = low, high * stretch
        else:
            on_value = angular[m] * low + turning[m] * high
            on_slope = angular[m] * high * stretch
        for n in range(BASIS):
            hi, lo = split(on_value * values[n] + on_slope * slopes[n])
            lh[n * TA : (n + 1) * TA, m * CHUNK : (m + 1) * CHUNK] = hi
            ll[n * TA : (n + 1) * TA, m * CHUNK : (m + 1) * CHUNK] = lo
        at = slice((p * COMPS + m) * TA, (p * COMPS + m + 1) * TA)
        group = slice(GROUP[m] * 256, (GROUP[m] + 1) * 256)
        steady = (2.0 * env_scale) * dinv[here, group]
        bent = (2.0 * env_scale) * turn_inv[:, group]
        hi, lo = split(env[at, :] * bent + envdot[at, :] * steady)
        gh[m * CHUNK : m * CHUNK + TA, :] = hi
        gl[m * CHUNK : m * CHUNK + TA, :] = lo
        hi, lo = split(env[at, :] * steady)
        gh[m * CHUNK + TA : (m + 1) * CHUNK, :] = hi
        gl[m * CHUNK + TA : (m + 1) * CHUNK, :] = lo
    raw[...] = product((lh[...], ll[...]), (gh[...], gl[...]), NN)
    for n in range(BASIS):
        grad_radial[n : n + 1, :] = jnp.sum(
            raw[n * TA : (n + 1) * TA, :] * fsel[here, :], axis=0, keepdims=True
        )


SMALL = 32
FOUR = 4


def block_of(part, rows):
    return pl.ds(pl.multiple_of(part * rows, 8), rows)


def block_of_lanes(part):
    return pl.ds(pl.multiple_of(part * HALF, HALF), HALF)


def total_of(refs, at):
    total = refs[0][at, :]
    for ref in refs[1:]:
        total = total + ref[at, :]
    return total


def halve_kernel(keep, taken, keep_out, give_out):
    me = place(0, 2)
    for out, part in ((keep_out, me), (give_out, 1 - me)):
        out[...] = total_of([keep, taken], block_of(part, out.shape[0]))


def spread_kernel(keep, taken, radial_0, radial_1, small, *refs):
    outs, tiny = refs[:FOUR], refs[FOUR]
    for h in range(2):
        lanes = slice(h * HALF, (h + 1) * HALF)
        tiny[16 * h : 16 * h + 8, :] = radial_0[:, lanes] + radial_1[:, lanes]
        tiny[16 * h + 8 : 16 * h + 16, :] = small[:, lanes]
    me = place(1, FOUR)
    for k, out in enumerate(outs):
        rows, few = out.shape[0] - SMALL // FOUR, SMALL // FOUR
        to = lax.bitwise_xor(me, k)
        out[0:rows, :] = total_of([keep, taken], block_of(to, rows))
        out[rows:, :] = tiny[block_of(to, few), :]


def total_kernel(*refs):
    refs[-1][...] = total_of(refs[:-1], slice(None))


def grow_kernel(*refs):
    parts, out = refs[:FOUR], refs[FOUR]
    few = SMALL // FOUR
    rows = parts[0].shape[0] - few
    me = place(1, FOUR)
    for k, ref in enumerate(parts):
        to = lax.bitwise_xor(me, k)
        out[block_of(to, rows), :] = ref[0:rows, :]
        out[pl.ds(pl.multiple_of(FOUR * rows + to * few, 8), few), :] = ref[rows:, :]


def join_kernel(mine, theirs, facing_mine, facing_theirs, mix, radial, kinds, out):
    rows = mine.shape[0] - SMALL
    me, core = place(0, 2), lax.axis_index("batch")
    for lane_part, pair in ((core, (mine, theirs)), (1 - core, (facing_mine, facing_theirs))):
        lanes = block_of_lanes(lane_part)
        for ref, part in zip(pair, (me, 1 - me)):
            mix[block_of(part, rows), lanes] = ref[0:rows, :]
    both = (mine[rows:, :] + theirs[rows:, :]) + (facing_mine[rows:, :] + facing_theirs[rows:, :])
    for h in range(2):
        lanes = slice(h * HALF, (h + 1) * HALF)
        few = both[16 * h : 16 * h + 16, :]
        radial[:, lanes] = few[0:BASIS]
        kinds[:, lanes] = few[BASIS : BASIS + SPECIES]
        out[:, lanes] = few[BASIS + SPECIES : BASIS + SPECIES + 1]


def spec(space):
    return pl.BlockSpec(memory_space=space)


def call(kernel, name, outs, scratch, *operands, space=pltpu.VMEM, after=(), flops=0):
    if space is pltpu.HBM:
        operands = [pltpu.with_memory_space_constraint(operand, space) for operand in operands]
    outs = [out if len(out) == 2 and isinstance(out[0], tuple) else (out, F32) for out in outs]
    return pl.pallas_call(
        kernel,
        name=name,
        out_shape=[jax.ShapeDtypeStruct(*out) for out in outs],
        in_specs=[spec(space)] * len(operands) + [spec(pltpu.VMEM)] * len(after),
        out_specs=[spec(pltpu.VMEM)] * len(outs),
        scratch_shapes=[pltpu.VMEM(*item) if isinstance(item, tuple) else item for item in scratch],
        compiler_params=pltpu.CompilerParams(vmem_limit_bytes=28 * 1024 * 1024),
        cost_estimate=pl.CostEstimate(flops=flops, bytes_accessed=1 << 20, transcendentals=0),
    )(*operands, *after)


def shifted(block, axis, by):
    count = lax.axis_size(axis)
    return lax.ppermute(block, axis, [(i, (i + by) % count) for i in range(count)])


def exchanged(block, shift, first):
    count, step = lax.axis_size("domain"), 1 << shift
    up = [((i >> shift) & 1 == 0) == first for i in range(count)]
    return lax.ppermute(block, "domain", [(i, (i + step if up[i] else i - step) % count) for i in range(count)])


def partner(block, mask):
    return lax.ppermute(block, "domain", [(i, i ^ mask) for i in range(lax.axis_size("domain"))])


def on_device(
    positions,
    features,
    species,
    ref_forces,
    centre_tile,
    other_tile,
    pair_live,
    send_tiles,
    radial_w,
    mix_w,
    species_w,
    out_w,
):
    atoms_here = positions.shape[2]
    channels = features.shape[2]
    table = (COMPS * TA, BASIS * TA)
    sent = (SEND * TA + GHOST_ROWS, channels)
    slots = PAIRS * TA
    line = (3, 1, atoms_here)
    turning = [((CHUNK, CHUNK), F32)] * 2
    out_row = out_w.reshape(1, channels)
    positions = positions.transpose(1, 0, 2)
    ref_forces = ref_forces.transpose(1, 0, 2)
    ints = [((1, n), jnp.int32) for n in (PAIRS, PAIRS, PAIRS, 2 * SEND)]

    to_second, to_first, token = call(
        gather_kernel,
        "gather",
        [sent, sent, (8, CHUNK)],
        [
            ints[3],
            (line, F32),
            ((1, atoms_here, channels), F32),
            (line, F32),
            pltpu.SemaphoreType.DMA((4,)),
        ],
        send_tiles, positions, features, ref_forces,
        space=pltpu.HBM,
    )
    from_second = exchanged(to_second, 0, False)
    from_first = exchanged(to_first, 0, True)
    flags, atoms, own_feat, weights, mh, ml = call(
        stage_kernel,
        "stage",
        [
            (16, CHUNK),
            (8, atoms_here),
            (atoms_here, channels),
            (16, channels),
            (mix_w.shape, BF16),
            (mix_w.shape, BF16),
        ],
        ints
        + [(line, F32), (line, F32), ((1, atoms_here), jnp.int32)]
        + [(radial_w.shape, F32), (mix_w.shape, F32), (species_w.shape, F32), (out_row.shape, F32)]
        + [pltpu.SemaphoreType.DMA((12,))],
        centre_tile, other_tile, pair_live, send_tiles, positions, ref_forces, species, features,
        radial_w, mix_w, species_w, out_row,
        space=pltpu.HBM,
        after=(token,),
    )

    factors = (PAIRS, BASIS * TA, channels)
    env, dinv, gate, curve, inv, rows, fsel, own, leaving, shape_store, xh, xl = call(
        force_kernel,
        "force",
        [
            (PAIRS * COMPS * TA, channels),
            (slots, 3 * channels),
            (slots, channels),
            (slots, channels),
            (slots, 3 * channels),
            (8, CHUNK),
            (slots, channels),
            (8, atoms_here),
            (lax.axis_size("domain"), 16, CHUNK),
            (PAIRS, 4 + BASIS, TA, CHUNK),
            (factors, BF16),
            (factors, BF16),
        ],
        turning
        + [((PAIRS, *table), BF16)] * 2
        + [((PAIRS, COMPS * TA, channels), BF16)] * 2
        + [((PAIRS * COMPS * TA, channels), F32), ((PAIRS, *table), F32)],
        flags, atoms, own_feat, weights, mh, ml, from_second, from_first,
        flops=1 << 31,
    )
    arriving = lax.all_to_all(leaving, "domain", 0, 0)

    rows_mix = 3 * channels
    total_count = 3.0 * atoms_here * lax.axis_size("domain") * lax.axis_size("batch")
    forces, keep, give, small, envdot, curl, both = call(
        functools.partial(tangent_kernel, 2.0 / math.sqrt(total_count)),
        "tangent",
        [
            line,
            (rows_mix, HALF),
            (rows_mix, HALF),
            (8, channels),
            (PAIRS * COMPS * TA, channels),
            (slots, channels),
            (16, CHUNK),
        ],
        turning
        + [((PAIRS, *table), BF16)] * 2
        + [((PAIRS * COMPS * TA, channels), F32)]
        + [((2 * slots, 3 * channels), F32), ((2 * slots, channels), F32)],
        flags, atoms, weights, mh, ml, from_first, from_second, own, arriving,
        rows, env, gate, curve, inv, shape_store, xh, xl,
        flops=1 << 31,
    )

    def radial(p, after):
        return call(
            functools.partial(radial_kernel, p),
            "radial",
            [(BASIS, channels)],
            turning
            + [((BASIS * TA, COMPS * CHUNK), BF16)] * 2
            + [((COMPS * CHUNK, channels), BF16)] * 2
            + [((BASIS * TA, channels), F32)],
            flags, both, fsel, env, envdot, dinv, curl, mh, ml, after,
            flops=1 << 31,
        )[0]

    keep, give = call(
        halve_kernel, "halve", [(rows_mix // 2, HALF)] * 2, [], keep, shifted(give, "batch", 1)
    )
    taken = partner(give, 1)
    radials = [radial(p, keep) for p in range(PAIRS)]
    piece = rows_mix // (2 * FOUR) + SMALL // FOUR
    blocks = call(
        spread_kernel, "spread", [(piece, HALF)] * FOUR, [((SMALL, HALF), F32)],
        keep, taken, *radials, small,
    )
    terms = [blocks[0]] + [partner(blocks[k], 2 * k) for k in range(FOUR - 1, 0, -1)]
    (mine,) = call(total_kernel, "total", [(piece, HALF)], [], *terms)
    bit = 2 * FOUR
    while bit < lax.axis_size("domain"):
        (mine,) = call(total_kernel, "total", [(piece, HALF)], [], mine, partner(mine, bit))
        bit *= 2
    parts = [mine] + [partner(mine, 2 * k) for k in range(1, FOUR)]
    (mine,) = call(grow_kernel, "grow", [(rows_mix // 2 + SMALL, HALF)], [], *parts)
    theirs = partner(mine, 1)
    facing = [shifted(part, "batch", 1) for part in (mine, theirs)]
    mix, radial_sum, kinds, out = call(
        join_kernel,
        "join",
        [(rows_mix, channels), (BASIS, channels), (SPECIES, channels), (1, channels)],
        [],
        mine,
        theirs,
        *facing,
    )
    return forces.transpose(1, 0, 2), radial_sum, mix, kinds, out.reshape(channels)


def solution(mesh):
    return jax.shard_map(
        on_device,
        mesh=mesh,
        in_specs=(
            P(("parts", "batch"), None, "domain"),
            P(("parts", "batch"), "domain", None),
            P(("parts", "batch"), "domain"),
            P(("parts", "batch"), None, "domain"),
            P(("parts", "batch"), "domain"),
            P(("parts", "batch"), "domain"),
            P(("parts", "batch"), "domain"),
            P(("parts", "batch"), "domain"),
            P(),
            P(),
            P(),
            P(),
        ),
        out_specs=(
            P(("parts", "batch"), None, "domain"),
            P("parts", None),
            P("parts", None),
            P("parts", None),
            P("parts"),
        ),
        check_vma=False,
    )
```

```python
import functools
import math

import jax
import jax.numpy as jnp
from jax import lax
from jax.experimental import pallas as pl
from jax.experimental.pallas import tpu as pltpu
from jax.sharding import PartitionSpec as P

TA = 64
SEND = 2
PAIRS = 2
COMPS = 9
WIDE = 10 * TA
BASIS = 8
SPECIES = 4
HALF = 128
CHUNK = 2 * TA

cutoff = 2.5
soften = 0.25
env_scale = 0.25
root_three = math.sqrt(3.0)
F32 = jnp.float32
BF16 = jnp.bfloat16
NN = (((1,), (0,)), ((), ()))
NT = (((1,), (1,)), ((), ()))
TN = (((0,), (0,)), ((), ()))
GROUP = (0, 1, 1, 1, 2, 2, 2, 2, 2)


def split(value):
    high = value.astype(BF16)
    return high, (value - high.astype(F32)).astype(BF16)


def product(left, right, dims):
    (lh, ll), (rh, rl) = left, right

    def one(x, y):
        return lax.dot_general(x, y, dims, preferred_element_type=F32)

    return one(lh, rh) + (one(lh, rl) + one(ll, rh))


def flag(condition):
    return jnp.where(condition, 1.0, 0.0).astype(F32)


def place(shift, width):
    return lax.bitwise_and(lax.shift_right_logical(lax.axis_index("domain"), shift), width - 1)


def lane_half():
    lane = lax.broadcasted_iota(jnp.int32, (1, CHUNK), 1)
    low = flag(lane < TA)
    return low, 1.0 - low


def twice(chunk, half):
    low, high = lane_half()
    swapped = pltpu.roll(chunk, TA, 1)
    return chunk * low + swapped * high if half == 0 else swapped * low + chunk * high


def pick(chunks, position):
    total = None
    for q, chunk in enumerate(chunks):
        for half in range(2):
            term = twice(chunk, half) * flag(position == 2 * q + half)
            total = term if total is None else total + term
    return total


def paired(first, second):
    low, high = lane_half()
    return first * low + second * high


def chunk_mask(position, q):
    low, high = lane_half()
    return low * flag(position == 2 * q) + high * flag(position == 2 * q + 1)


def geometry(lane_rows, columns, sign, live, same):
    offset = [(row - column) * sign for row, column in zip(lane_rows, columns)]
    dist_sq = offset[0] * offset[0] + offset[1] * offset[1] + offset[2] * offset[2] + soften
    distance = jnp.sqrt(dist_sq)
    inverse = 1.0 / distance
    unit = [x * inverse for x in offset]
    row = lax.broadcasted_iota(jnp.int32, (TA, CHUNK), 0)
    lane = lax.broadcasted_iota(jnp.int32, (TA, CHUNK), 1)
    lane = jnp.where(lane >= TA, lane - TA, lane)
    mask = live * (1.0 - same * flag(row == lane))
    base = jnp.maximum(1.0 - dist_sq * (1.0 / (cutoff * cutoff)), 0.0)
    weight = base * base * base * mask * inverse
    slope = -(6.0 / (cutoff * cutoff)) * base * base * mask - weight * inverse
    angle = distance * (math.pi / cutoff)
    return unit, inverse, weight, slope, jnp.sin(angle), jnp.cos(angle)


def harmonics(v):
    x, y, z = v
    return [
        None,
        x,
        y,
        z,
        root_three * x * y,
        root_three * y * z,
        root_three * z * x,
        0.5 * root_three * (x * x - y * y),
        z * z - 0.5 * (x * x + y * y),
    ]


def harmonics_tangent(v, t):
    x, y, z = v
    a, b, c = t
    return [
        None,
        a,
        b,
        c,
        root_three * (a * y + x * b),
        root_three * (b * z + y * c),
        root_three * (c * x + z * a),
        root_three * (x * a - y * b),
        2.0 * z * c - (x * a + y * b),
    ]


def paired_orders(sine, cosine, weight, slope):
    low, high = lane_half()
    double_s, double_c = 2.0 * sine * cosine, 1.0 - 2.0 * sine * sine
    now_s = sine * low + double_s * high
    now_c = cosine * low + double_c * high
    old_s = -sine * low
    old_c = cosine * low + high
    values, slopes = [], []
    for k in range(BASIS // 2):
        order = ((2 * k + 1) * low + (2 * k + 2) * high) * (math.pi / cutoff)
        values.append(now_s * weight)
        slopes.append(now_c * (weight * order) + now_s * slope)
        now_s, old_s = 2.0 * double_c * now_s - old_s, now_s
        now_c, old_c = 2.0 * double_c * now_c - old_c, now_c
    return values, slopes


def single_orders(sine, cosine, weight, slope):
    now_s, now_c = sine, cosine
    old_s, old_c = jnp.zeros_like(sine), jnp.ones_like(cosine)
    values, slopes = [], []
    for n in range(1, BASIS + 1):
        values.append(now_s * weight)
        slopes.append(now_c * (weight * (n * math.pi / cutoff)) + now_s * slope)
        now_s, old_s = 2.0 * cosine * now_s - old_s, now_s
        now_c, old_c = 2.0 * cosine * now_c - old_c, now_c
    return values, slopes


def columns_of(rows, square, turned):
    square[...] = jnp.zeros_like(square)
    square[0 : rows.shape[0], :] = rows
    turned[...] = square[...].T


def pair_rows(first, p):
    return twice(first, p)


def radial_feat(feat, radial, p, high_ref, low_ref):
    own = feat[p * TA : (p + 1) * TA, :]
    for n in range(BASIS):
        hi, lo = split(own * radial[n : n + 1, :])
        high_ref[n * TA : (n + 1) * TA, :] = hi
        low_ref[n * TA : (n + 1) * TA, :] = lo


OTHER, CENTRE, LIVE, SAME, SHARED, SENT = 0, 2, 4, 6, 8, 9
GHOST_ROWS = 8


def fetch(pairs, sems):
    copies = [pltpu.make_async_copy(src, dst, sems.at[i]) for i, (src, dst) in enumerate(pairs)]
    for copy in copies:
        copy.start()
    return copies


def upward(shift):
    return 1.0 - flag(place(shift, 2) == 1)


def either(choice, first, second):
    return first * choice + second * (1.0 - choice)


def gather_kernel(send, pos, feat, ref, to_second, to_first, token, send_v, pos_v, feat_v, ref_v, sems):
    copies = fetch([(send, send_v), (pos, pos_v), (ref, ref_v), (feat, feat_v)], sems)
    for copy in copies[:3]:
        copy.wait()
    low, high = lane_half()
    up = upward(0)
    sent = [send_v[0:1, j : j + 1].astype(F32) for j in range(2 * SEND)]
    tiles_of = []
    for out, choice in ((to_first, 1.0 - up), (to_second, up)):
        tiles = [either(choice, sent[j], sent[SEND + j]) for j in range(SEND)]
        tiles_of.append(tiles)
        out[SEND * TA :, :] = jnp.zeros((GHOST_ROWS, out.shape[1]), F32)
        for i in range(3):
            at = SEND * TA + i
            for lanes, source in ((slice(0, CHUNK), pos_v), (slice(CHUNK, 2 * CHUNK), ref_v)):
                chunks = [source[i, :, q * CHUNK : (q + 1) * CHUNK] for q in range(2)]
                out[at : at + 1, lanes] = paired(pick(chunks, tiles[0]), pick(chunks, tiles[1]))
        for other in range(2 * SEND):
            same = low * flag(sent[other] == tiles[0]) + high * flag(sent[other] == tiles[1])
            out[SEND * TA + 3 + other : SEND * TA + 4 + other, 0:CHUNK] = same
    token[...] = jnp.zeros_like(token)
    copies[3].wait()
    for out, tiles in zip((to_first, to_second), tiles_of):
        for j in range(SEND):
            out[j * TA : (j + 1) * TA, :] = pick_rows(feat_v.at[0], tiles[j], 0.0)


def pick_rows(ref, position, first):
    total = None
    for t in range(ref.shape[0] // TA):
        term = ref[t * TA : (t + 1) * TA, :] * flag(position == first + float(t))
        total = term if total is None else total + term
    return total


def stage_kernel(
    centre, other, live, send, pos, ref, species, feat, radial_w, mix_w, species_w, out_w, after,
    flags, atoms, own_feat, weights, mh, ml,
    centre_v, other_v, live_v, send_v, pos_v, ref_v, species_v, radial_v, mix_v, species_w_v, out_v, sems,
):
    copies = fetch(
        [
            (centre, centre_v), (other, other_v), (live, live_v), (send, send_v), (pos, pos_v), (ref, ref_v),
            (species, species_v), (radial_w, radial_v), (species_w, species_w_v), (out_w, out_v),
            (feat.at[0], own_feat), (mix_w, mix_v),
        ],
        sems,
    )
    for copy in copies[:-1]:
        copy.wait()
    flags[...] = jnp.zeros_like(flags)
    centres = [centre_v[0:1, p : p + 1].astype(F32) for p in range(PAIRS)]
    others = [other_v[0:1, p : p + 1].astype(F32) for p in range(PAIRS)]
    for p in range(PAIRS):
        for row, value in (
            (OTHER, others[p]),
            (CENTRE, centres[p]),
            (LIVE, live_v[0:1, p : p + 1].astype(F32)),
            (SAME, flag(others[p] == centres[p] + SEND)),
        ):
            flags[row + p : row + p + 1, :] = jnp.broadcast_to(value, (1, CHUNK))
    flags[SHARED : SHARED + 1, :] = jnp.broadcast_to(flag(centres[0] == centres[1]), (1, CHUNK))
    for j in range(2 * SEND):
        value = send_v[0:1, j : j + 1].astype(F32)
        flags[SENT + j : SENT + j + 1, :] = jnp.broadcast_to(value, (1, CHUNK))
    atoms[...] = jnp.zeros_like(atoms)
    for i in range(3):
        atoms[i : i + 1, :] = pos_v[i]
        atoms[4 + i : 5 + i, :] = ref_v[i]
    atoms[3:4, :] = species_v[...].astype(F32)
    weights[...] = jnp.zeros_like(weights)
    weights[0:BASIS, :] = radial_v[...]
    weights[BASIS : BASIS + SPECIES, :] = species_w_v[...]
    weights[BASIS + SPECIES : BASIS + SPECIES + 1, :] = out_v[...]
    copies[-1].wait()
    hi, lo = split(mix_v[...])
    mh[...] = hi
    ml[...] = lo


def force_kernel(
    flags, atoms, feat, weights, mh, ml, from_second, from_first,
    env, dinv, gate, curve, inv, rows, fsel, own, one_first, one_second, two_first, two_second, shape_store, xh, xl, eh, el,
    square, turned, th, tl, raw, back,
):
    ghost = SEND * TA
    up = upward(0)
    near, far = from_first[ghost : ghost + 3, 0:CHUNK], from_second[ghost : ghost + 3, 0:CHUNK]
    chunks = [either(up, far, near), atoms[0:3, 0:CHUNK], atoms[0:3, CHUNK:], either(up, near, far)]
    kinds = [atoms[3:4, q * CHUNK : (q + 1) * CHUNK] for q in range(2)]

    def number(row):
        return flags[row : row + 1, :]

    centres = [number(CENTRE + p) for p in range(PAIRS)]
    others = [number(OTHER + p) for p in range(PAIRS)]
    shared = flags[SHARED : SHARED + 1, 0:1]
    rows[...] = jnp.zeros_like(rows)
    rows[0:3, :] = paired(*(pick(chunks, others[p]) for p in range(PAIRS)))
    rows[3:6, :] = paired(*(pick(chunks[1:3], centres[p]) for p in range(PAIRS)))
    rows[6:7, :] = paired(*(pick(kinds, centres[p]) for p in range(PAIRS)))
    columns_of(rows[...], square, turned)

    for p in range(PAIRS):
        o = flags[OTHER + p : OTHER + p + 1, 0:1]
        fsel[p * TA : (p + 1) * TA, :] = (
            pick_rows(from_first.at[0:ghost], o, (SEND + 4) * up)
            + pick_rows(feat, o, float(SEND))
            + pick_rows(from_second.at[0:ghost], o, (SEND + 4) * (1.0 - up))
        )

    shapes = []
    for p in range(PAIRS):
        lane_rows = [twice(rows[i : i + 1, :], p) for i in range(3)]
        columns = [turned[p * TA : (p + 1) * TA, 3 + i : 4 + i] for i in range(3)]
        unit, inverse, weight, slope, sine, cosine = geometry(
            lane_rows, columns, 1.0, number(LIVE + p), number(SAME + p)
        )
        angular = harmonics(unit)
        values, slopes = paired_orders(sine, cosine, weight, slope)
        shapes.append((unit, inverse, angular, values, slopes))
        for i, part in enumerate(unit + [inverse] + values + slopes):
            shape_store[p, i] = part
        for m in range(COMPS):
            for k in range(BASIS // 2):
                entry = values[k] if m == 0 else angular[m] * values[k]
                hi, lo = split(entry)
                th[p, m * TA : (m + 1) * TA, k * CHUNK : (k + 1) * CHUNK] = hi
                tl[p, m * TA : (m + 1) * TA, k * CHUNK : (k + 1) * CHUNK] = lo
        radial_feat(fsel, weights, p, xh.at[p], xl.at[p])
        raw[p * COMPS * TA : (p + 1) * COMPS * TA, :] = product((th[p], tl[p]), (xh[p], xl[p]), NN)

    for m in range(COMPS):
        first = raw[m * TA : (m + 1) * TA, :]
        second = raw[(COMPS + m) * TA : (COMPS + m + 1) * TA, :]
        env[m * TA : (m + 1) * TA, :] = env_scale * (first + shared * second)
        env[(COMPS + m) * TA : (COMPS + m + 1) * TA, :] = env_scale * (second + shared * first)
    for p in range(PAIRS):
        sums = [None] * 3
        for m in range(COMPS):
            block = env[(p * COMPS + m) * TA : (p * COMPS + m + 1) * TA, :]
            sums[GROUP[m]] = block * block if sums[GROUP[m]] is None else sums[GROUP[m]] + block * block
        for g in range(3):
            inv[p * TA : (p + 1) * TA, g * 256 : (g + 1) * 256] = sums[g]
    hidden = product(split(inv[...]), (mh[...], ml[...]), NN)
    kind = turned[:, 6:7]
    for s in range(SPECIES):
        hidden = hidden + flag(kind == float(s)) * weights[BASIS + s : BASIS + s + 1, :]
    out_row = weights[BASIS + SPECIES : BASIS + SPECIES + 1, :]
    sigma = 1.0 / (1.0 + jnp.exp(-hidden))
    first_order = sigma * (1.0 + hidden * (1.0 - sigma))
    gate[...] = first_order
    curve[...] = sigma * (1.0 - sigma) * (2.0 + hidden * (1.0 - 2.0 * sigma)) * out_row
    dinv[...] = product(split(first_order * out_row), (mh[...], ml[...]), NT)

    tile_grads = [jnp.zeros((3, CHUNK), F32) for _ in range(4)]
    for p in range(PAIRS):
        unit, inverse, angular, values, slopes = shapes[p]
        for m in range(COMPS):
            block = env[(p * COMPS + m) * TA : (p * COMPS + m + 1) * TA, :]
            part = dinv[p * TA : (p + 1) * TA, GROUP[m] * 256 : (GROUP[m] + 1) * 256]
            hi, lo = split((2.0 * env_scale) * block * part)
            eh[p, m * TA : (m + 1) * TA, :] = hi
            el[p, m * TA : (m + 1) * TA, :] = lo
        for ref in (eh, el):
            ref[p, COMPS * TA :, :] = jnp.zeros((WIDE - COMPS * TA, ref.shape[2]), BF16)
        steady = (eh[p, 0 : COMPS * TA, :], el[p, 0 : COMPS * TA, :])
        back[p] = product(steady, (xh[p], xl[p]), NT)
        d_radius = None
        d_angular = []
        for m in range(COMPS):
            along, across = None, None
            for k in range(BASIS // 2):
                block = back[p, m * TA : (m + 1) * TA, k * CHUNK : (k + 1) * CHUNK]
                along = block * slopes[k] if along is None else along + block * slopes[k]
                across = block * values[k] if across is None else across + block * values[k]
            d_angular.append(across)
            term = along if m == 0 else along * angular[m]
            d_radius = term if d_radius is None else d_radius + term
        x, y, z = unit
        g = d_angular
        toward = [
            g[1] + root_three * (y * g[4] + z * g[6] + x * g[7]) - x * g[8],
            g[2] + root_three * (x * g[4] + z * g[5] - y * g[7]) - y * g[8],
            g[3] + root_three * (y * g[5] + x * g[6]) + 2.0 * (z * g[8]),
        ]
        radial_part = d_radius - inverse * (toward[0] * x + toward[1] * y + toward[2] * z)
        for i in range(3):
            d_offset = inverse * toward[i] + unit[i] * radial_part
            summed = jnp.sum(d_offset, axis=0, keepdims=True)
            other_row = summed + pltpu.roll(summed, TA, 1)
            square[0:TA, :] = d_offset
            square[TA:, :] = d_offset
            centre_row = -jnp.sum(square[...].T, axis=0, keepdims=True)
            component = flag(lax.broadcasted_iota(jnp.int32, (3, CHUNK), 0) == i)
            for q in range(4):
                at = chunk_mask(others[p], q) * other_row
                if q in (1, 2):
                    at = at + chunk_mask(centres[p] + SEND, q) * centre_row
                tile_grads[q] = tile_grads[q] + at * component
    own[...] = jnp.zeros_like(own)
    own[0:3, 0:CHUNK] = tile_grads[1]
    own[0:3, CHUNK:] = tile_grads[2]
    own[3:6, 0:CHUNK] = tile_grads[0]
    own[3:6, CHUNK:] = tile_grads[3]
    leaving = []
    for first, ghost_grad in ((0, tile_grads[0]), (SEND, tile_grads[3])):
        listed = paired(*(pick(tile_grads[1:3], number(SENT + first + j)) for j in range(SEND)))
        leaving.append((listed, ghost_grad))
    for shift, outs in ((0, (one_first, one_second)), (1, (two_first, two_second))):
        choice = upward(shift)
        for out, above in zip(outs, (choice, 1.0 - choice)):
            out[...] = jnp.zeros_like(out)
            out[0:3, :] = either(above, leaving[1][0], leaving[0][0])
            out[3:6, :] = either(above, leaving[1][1], leaving[0][1])


def tangent_kernel(
    scale, flags, atoms, weights, mh, ml, from_first, from_second, own, one_second, two_second, one_first, two_first,
    rows, env, gate, curve, inv, shape_store, xh, xl, after,
    forces, keep, give, small, envdot, curl, both,
    square, turned, th, tl, raw, left, right,
):
    ghost = SEND * TA
    def number(row):
        return flags[row : row + 1, :]

    centres = [number(CENTRE + p) for p in range(PAIRS)]
    others = [number(OTHER + p) for p in range(PAIRS)]
    shared = flags[SHARED : SHARED + 1, 0:1]
    mine = [own[0:3, 0:CHUNK], own[0:3, CHUNK:]]
    up, up_two = upward(0), upward(1)
    low_one = either(up, one_second[...], one_first[...])
    high_one = either(up, one_first[...], one_second[...])
    low_two = either(up_two, two_second[...], two_first[...])
    high_two = either(up_two, two_first[...], two_second[...])
    low_tail = either(up, from_second[ghost:, :], from_first[ghost:, :])
    high_tail = either(up, from_first[ghost:, :], from_second[ghost:, :])
    arrived = [twice(low_one[3:6, :], j) for j in range(SEND)]
    arrived += [twice(high_one[3:6, :], j) for j in range(SEND)]
    for j in range(2 * SEND):
        for q in range(2):
            mine[q] = mine[q] + chunk_mask(number(SENT + j), q) * arrived[j]
    below = low_one[0:3, :]
    above = high_one[0:3, :]
    to_below = [twice(low_two[3:6, :], j) for j in range(SEND)]
    to_below += [twice(own[3:6, 0:CHUNK], j) for j in range(SEND)]
    to_above = [twice(own[3:6, CHUNK:], j) for j in range(SEND)]
    to_above += [twice(high_two[3:6, :], j) for j in range(SEND)]
    for j in range(2 * SEND):
        below = below + low_tail[3 + j : 4 + j, 0:CHUNK] * to_below[j]
        above = above + high_tail[3 + j : 4 + j, 0:CHUNK] * to_above[j]
    for q in range(2):
        for i in range(3):
            forces[i, :, q * CHUNK : (q + 1) * CHUNK] = -mine[q][i : i + 1, :]
    error = [
        below + low_tail[0:3, CHUNK:],
        mine[0] + atoms[4:7, 0:CHUNK],
        mine[1] + atoms[4:7, CHUNK:],
        above + high_tail[0:3, CHUNK:],
    ]
    error = [part * scale for part in error]
    both[...] = jnp.zeros_like(both)
    both[0:8, :] = rows[...]
    both[8:11, :] = paired(*(pick(error, others[p]) for p in range(PAIRS)))
    both[11:14, :] = paired(*(pick(error[1:3], centres[p]) for p in range(PAIRS)))
    columns_of(both[...], square, turned)

    for p in range(PAIRS):
        lane_move = [twice(both[8 + i : 9 + i, :], p) for i in range(3)]
        column_move = [turned[p * TA : (p + 1) * TA, 11 + i : 12 + i] for i in range(3)]
        unit = [shape_store[p, i] for i in range(3)]
        inverse = shape_store[p, 3]
        values = [shape_store[p, 4 + k] for k in range(BASIS // 2)]
        slopes = [shape_store[p, 8 + k] for k in range(BASIS // 2)]
        move = [a - b for a, b in zip(lane_move, column_move)]
        stretch = unit[0] * move[0] + unit[1] * move[1] + unit[2] * move[2]
        turn = [(m - v * stretch) * inverse for m, v in zip(move, unit)]
        angular, turning = harmonics(unit), harmonics_tangent(unit, turn)
        slopes = [s * stretch for s in slopes]
        for m in range(COMPS):
            for k in range(BASIS // 2):
                entry = slopes[k] if m == 0 else angular[m] * slopes[k] + turning[m] * values[k]
                hi, lo = split(entry)
                th[p, m * TA : (m + 1) * TA, k * CHUNK : (k + 1) * CHUNK] = hi
                tl[p, m * TA : (m + 1) * TA, k * CHUNK : (k + 1) * CHUNK] = lo
        raw[p * COMPS * TA : (p + 1) * COMPS * TA, :] = product((th[p], tl[p]), (xh[p], xl[p]), NN)

    for m in range(COMPS):
        first = raw[m * TA : (m + 1) * TA, :]
        second = raw[(COMPS + m) * TA : (COMPS + m + 1) * TA, :]
        envdot[m * TA : (m + 1) * TA, :] = env_scale * (first + shared * second)
        envdot[(COMPS + m) * TA : (COMPS + m + 1) * TA, :] = env_scale * (second + shared * first)
    invdot = left
    half = PAIRS * TA
    for p in range(PAIRS):
        sums = [None] * 3
        for m in range(COMPS):
            at = slice((p * COMPS + m) * TA, (p * COMPS + m + 1) * TA)
            term = 2.0 * env[at, :] * envdot[at, :]
            sums[GROUP[m]] = term if sums[GROUP[m]] is None else sums[GROUP[m]] + term
        for g in range(3):
            invdot[half + p * TA : half + (p + 1) * TA, g * 256 : (g + 1) * 256] = sums[g]
    invdot[0:half, :] = inv[...]
    hidden_move = product(split(invdot[half:, :]), (mh[...], ml[...]), NN)
    bend = curve[...] * hidden_move
    curl[...] = bend
    once = 1.0 - shared * flag(lax.broadcasted_iota(jnp.int32, (half, 1), 0) >= TA)
    right[0:half, :] = bend * once
    right[half:, :] = gate[...] * weights[BASIS + SPECIES : BASIS + SPECIES + 1, :] * once
    raw[0 : left.shape[1], :] = product(split(left[...]), split(right[...]), TN)
    core = lax.axis_index("batch")
    for out, part in ((keep, core), (give, 1 - core)):
        out[...] = raw[0 : left.shape[1], block_of_lanes(part)]
    small[...] = jnp.zeros_like(small)
    kind = turned[:, 6:7]
    for s in range(SPECIES):
        small[s : s + 1, :] = jnp.sum(right[0:half, :] * flag(kind == float(s)), axis=0, keepdims=True)
    small[SPECIES : SPECIES + 1, :] = jnp.sum(gate[...] * hidden_move * once, axis=0, keepdims=True)


def table_kernel(flags, rows, shape_store, lh, ll, token, square, turned):
    low, high = lane_half()
    token[...] = jnp.zeros_like(token)
    columns_of(rows[...], square, turned)
    for p in range(PAIRS):
        lane_rows = [twice(rows[3 + i : 4 + i, :], p) for i in range(3)]
        columns = [turned[p * TA : (p + 1) * TA, i : i + 1] for i in range(3)]
        unit, inverse, weight, slope, sine, cosine = geometry(
            lane_rows, columns, -1.0, flags[LIVE + p : LIVE + p + 1, :], flags[SAME + p : SAME + p + 1, :]
        )
        angular = harmonics(unit)
        values, slopes = single_orders(sine, cosine, weight, slope)
        for i, part in enumerate(unit + [inverse] + values + slopes):
            shape_store[p, i] = part
        for m in range(0, COMPS + 1, 2):
            factor = low if m == 0 else angular[m] * low
            if m + 1 < COMPS:
                factor = factor + angular[m + 1] * high
            for n in range(BASIS):
                hi, lo = split(factor * values[n])
                lh[p, n * TA : (n + 1) * TA, m * TA : (m + 2) * TA] = hi
                ll[p, n * TA : (n + 1) * TA, m * TA : (m + 2) * TA] = lo


def radial_kernel(
    p, both, shape_store, lh, ll, eh, el, fsel, env, envdot, dinv, curl, mh, ml, after,
    grad_radial,
    square, turned, sh, sl, gh, gl, raw,
):
    low, high = lane_half()
    columns_of(both[...], square, turned)
    here = slice(p * TA, (p + 1) * TA)
    turn_inv = product(split(curl[here, :]), (mh[...], ml[...]), NT)
    lane_move = [twice(both[11 + i : 12 + i, :], p) for i in range(3)]
    column_move = [turned[here, 8 + i : 9 + i] for i in range(3)]
    unit = [shape_store[p, i] for i in range(3)]
    inverse = shape_store[p, 3]
    move = [b - a for a, b in zip(lane_move, column_move)]
    stretch = unit[0] * move[0] + unit[1] * move[1] + unit[2] * move[2]
    turn = [(m - v * stretch) * inverse for m, v in zip(move, unit)]
    angular, turning = harmonics(unit), harmonics_tangent(unit, turn)
    sh[:, 0:CHUNK] = lh[p, :, WIDE - CHUNK :]
    sl[:, 0:CHUNK] = ll[p, :, WIDE - CHUNK :]
    for m in range(0, COMPS + 1, 2):
        if m == 0:
            on_value, on_slope = turning[1] * high, low + angular[1] * high
        else:
            on_value, on_slope = turning[m] * low, angular[m] * low
            if m + 1 < COMPS:
                on_value = on_value + turning[m + 1] * high
                on_slope = on_slope + angular[m + 1] * high
        on_slope = on_slope * stretch
        lanes = slice(CHUNK + m * TA, CHUNK + (m + 2) * TA)
        for n in range(BASIS):
            hi, lo = split(on_value * shape_store[p, 4 + n] + on_slope * shape_store[p, 4 + BASIS + n])
            sh[n * TA : (n + 1) * TA, lanes] = hi
            sl[n * TA : (n + 1) * TA, lanes] = lo
    for m in range(COMPS):
        at = slice((p * COMPS + m) * TA, (p * COMPS + m + 1) * TA)
        group = slice(GROUP[m] * 256, (GROUP[m] + 1) * 256)
        steady = (2.0 * env_scale) * dinv[here, group]
        bent = (2.0 * env_scale) * turn_inv[:, group]
        hi, lo = split(env[at, :] * bent + envdot[at, :] * steady)
        gh[m * TA : (m + 1) * TA, :] = hi
        gl[m * TA : (m + 1) * TA, :] = lo
    for ref, tail in ((gh, eh), (gl, el)):
        ref[COMPS * TA : WIDE, :] = jnp.zeros((WIDE - COMPS * TA, ref.shape[1]), BF16)
        ref[WIDE:, :] = tail[p]
    first = WIDE - CHUNK
    raw[...] = product((lh[p, :, 0:first], ll[p, :, 0:first]), (gh[0:first, :], gl[0:first, :]), NN) + product(
        (sh[...], sl[...]), (gh[first:, :], gl[first:, :]), NN
    )
    for n in range(BASIS):
        grad_radial[n : n + 1, :] = jnp.sum(
            raw[n * TA : (n + 1) * TA, :] * fsel[here, :], axis=0, keepdims=True
        )


SMALL = 32
FOUR = 4


def block_of(part, rows):
    return pl.ds(pl.multiple_of(part * rows, 8), rows)


def block_of_lanes(part):
    return pl.ds(pl.multiple_of(part * HALF, HALF), HALF)


def total_of(refs, at):
    total = refs[0][at, :]
    for ref in refs[1:]:
        total = total + ref[at, :]
    return total


def halve_kernel(keep, taken, keep_out, give_out):
    me = place(0, 2)
    for out, part in ((keep_out, me), (give_out, 1 - me)):
        out[...] = total_of([keep, taken], block_of(part, out.shape[0]))


def spread_kernel(keep, taken, radial_0, radial_1, small, *refs):
    outs, tiny = refs[:FOUR], refs[FOUR]
    for h in range(2):
        lanes = slice(h * HALF, (h + 1) * HALF)
        tiny[16 * h : 16 * h + 8, :] = radial_0[:, lanes] + radial_1[:, lanes]
        tiny[16 * h + 8 : 16 * h + 16, :] = small[:, lanes]
    me = place(1, FOUR)
    for k, out in enumerate(outs):
        rows, few = out.shape[0] - SMALL // FOUR, SMALL // FOUR
        to = lax.bitwise_xor(me, k)
        out[0:rows, :] = total_of([keep, taken], block_of(to, rows))
        out[rows:, :] = tiny[block_of(to, few), :]


def total_kernel(*refs):
    refs[-1][...] = total_of(refs[:-1], slice(None))


def grow_kernel(*refs):
    parts, out = refs[:FOUR], refs[FOUR]
    few = SMALL // FOUR
    rows = parts[0].shape[0] - few
    me = place(1, FOUR)
    for k, ref in enumerate(parts):
        to = lax.bitwise_xor(me, k)
        out[block_of(to, rows), :] = ref[0:rows, :]
        out[pl.ds(pl.multiple_of(FOUR * rows + to * few, 8), few), :] = ref[rows:, :]


def join_kernel(mine, theirs, facing_mine, facing_theirs, mix, radial, kinds, out):
    rows = mine.shape[0] - SMALL
    me, core = place(0, 2), lax.axis_index("batch")
    for lane_part, pair in ((core, (mine, theirs)), (1 - core, (facing_mine, facing_theirs))):
        lanes = block_of_lanes(lane_part)
        for ref, part in zip(pair, (me, 1 - me)):
            mix[block_of(part, rows), lanes] = ref[0:rows, :]
    both = (mine[rows:, :] + theirs[rows:, :]) + (facing_mine[rows:, :] + facing_theirs[rows:, :])
    for h in range(2):
        lanes = slice(h * HALF, (h + 1) * HALF)
        few = both[16 * h : 16 * h + 16, :]
        radial[:, lanes] = few[0:BASIS]
        kinds[:, lanes] = few[BASIS : BASIS + SPECIES]
        out[:, lanes] = few[BASIS + SPECIES : BASIS + SPECIES + 1]


def spec(space):
    return pl.BlockSpec(memory_space=space)


def call(kernel, name, outs, scratch, *operands, space=pltpu.VMEM, after=(), flops=0):
    if space is pltpu.HBM:
        operands = [pltpu.with_memory_space_constraint(operand, space) for operand in operands]
    outs = [out if len(out) == 2 and isinstance(out[0], tuple) else (out, F32) for out in outs]
    return pl.pallas_call(
        kernel,
        name=name,
        out_shape=[jax.ShapeDtypeStruct(*out) for out in outs],
        in_specs=[spec(space)] * len(operands) + [spec(pltpu.VMEM)] * len(after),
        out_specs=[spec(pltpu.VMEM)] * len(outs),
        scratch_shapes=[pltpu.VMEM(*item) if isinstance(item, tuple) else item for item in scratch],
        compiler_params=pltpu.CompilerParams(vmem_limit_bytes=28 * 1024 * 1024),
        cost_estimate=pl.CostEstimate(flops=flops, bytes_accessed=1 << 20, transcendentals=0),
    )(*operands, *after)


def shifted(block, axis, by):
    count = lax.axis_size(axis)
    return lax.ppermute(block, axis, [(i, (i + by) % count) for i in range(count)])


def exchanged(block, shift, first):
    count, step = lax.axis_size("domain"), 1 << shift
    up = [((i >> shift) & 1 == 0) == first for i in range(count)]
    return lax.ppermute(block, "domain", [(i, (i + step if up[i] else i - step) % count) for i in range(count)])


def partner(block, mask):
    return lax.ppermute(block, "domain", [(i, i ^ mask) for i in range(lax.axis_size("domain"))])


def on_device(
    positions,
    features,
    species,
    ref_forces,
    centre_tile,
    other_tile,
    pair_live,
    send_tiles,
    radial_w,
    mix_w,
    species_w,
    out_w,
):
    atoms_here = positions.shape[2]
    channels = features.shape[2]
    table = (COMPS * TA, BASIS * TA)
    sent = (SEND * TA + GHOST_ROWS, channels)
    slots = PAIRS * TA
    line = (3, 1, atoms_here)
    turning = [((CHUNK, CHUNK), F32)] * 2
    out_row = out_w.reshape(1, channels)
    positions = positions.transpose(1, 0, 2)
    ref_forces = ref_forces.transpose(1, 0, 2)
    ints = [((1, n), jnp.int32) for n in (PAIRS, PAIRS, PAIRS, 2 * SEND)]

    to_second, to_first, token = call(
        gather_kernel,
        "gather",
        [sent, sent, (8, CHUNK)],
        [
            ints[3],
            (line, F32),
            ((1, atoms_here, channels), F32),
            (line, F32),
            pltpu.SemaphoreType.DMA((4,)),
        ],
        send_tiles, positions, features, ref_forces,
        space=pltpu.HBM,
    )
    from_second = exchanged(to_second, 0, False)
    from_first = exchanged(to_first, 0, True)
    flags, atoms, own_feat, weights, mh, ml = call(
        stage_kernel,
        "stage",
        [
            (16, CHUNK),
            (8, atoms_here),
            (atoms_here, channels),
            (16, channels),
            (mix_w.shape, BF16),
            (mix_w.shape, BF16),
        ],
        ints
        + [(line, F32), (line, F32), ((1, atoms_here), jnp.int32)]
        + [(radial_w.shape, F32), (mix_w.shape, F32), (species_w.shape, F32), (out_row.shape, F32)]
        + [pltpu.SemaphoreType.DMA((12,))],
        centre_tile, other_tile, pair_live, send_tiles, positions, ref_forces, species, features,
        radial_w, mix_w, species_w, out_row,
        space=pltpu.HBM,
        after=(token,),
    )

    factors = (PAIRS, BASIS * TA, channels)
    env, dinv, gate, curve, inv, rows, fsel, own, *leaving, shape_store, xh, xl, eh, el = call(
        force_kernel,
        "force",
        [
            (PAIRS * COMPS * TA, channels),
            (slots, 3 * channels),
            (slots, channels),
            (slots, channels),
            (slots, 3 * channels),
            (8, CHUNK),
            (slots, channels),
            (8, atoms_here),
            (8, CHUNK),
            (8, CHUNK),
            (8, CHUNK),
            (8, CHUNK),
            (PAIRS, 4 + BASIS, TA, CHUNK),
            (factors, BF16),
            (factors, BF16),
            ((PAIRS, WIDE, channels), BF16),
            ((PAIRS, WIDE, channels), BF16),
        ],
        turning
        + [((PAIRS, *table), BF16)] * 2
        + [((PAIRS * COMPS * TA, channels), F32), ((PAIRS, *table), F32)],
        flags, atoms, own_feat, weights, mh, ml, from_second, from_first,
        flops=1 << 31,
    )
    arriving = [exchanged(leaving[i], i // 2, i % 2 == 0) for i in (1, 3, 0, 2)]

    table_shape, lh, ll, token = call(
        table_kernel,
        "table",
        [
            (PAIRS, 4 + 2 * BASIS, TA, CHUNK),
            ((PAIRS, BASIS * TA, WIDE), BF16),
            ((PAIRS, BASIS * TA, WIDE), BF16),
            (8, CHUNK),
        ],
        turning,
        flags, rows,
        flops=1 << 30,
    )

    rows_mix = 3 * channels
    total_count = 3.0 * atoms_here * lax.axis_size("domain") * lax.axis_size("batch")
    forces, keep, give, small, envdot, curl, both = call(
        functools.partial(tangent_kernel, 2.0 / math.sqrt(total_count)),
        "tangent",
        [
            line,
            (rows_mix, HALF),
            (rows_mix, HALF),
            (8, channels),
            (PAIRS * COMPS * TA, channels),
            (slots, channels),
            (16, CHUNK),
        ],
        turning
        + [((PAIRS, *table), BF16)] * 2
        + [((PAIRS * COMPS * TA, channels), F32)]
        + [((2 * slots, 3 * channels), F32), ((2 * slots, channels), F32)],
        flags, atoms, weights, mh, ml, from_first, from_second, own, *arriving,
        rows, env, gate, curve, inv, shape_store, xh, xl, token,
        flops=1 << 31,
    )

    def radial(p, after):
        return call(
            functools.partial(radial_kernel, p),
            "radial",
            [(BASIS, channels)],
            turning
            + [((BASIS * TA, CHUNK + WIDE), BF16)] * 2
            + [((2 * WIDE, channels), BF16)] * 2
            + [((BASIS * TA, channels), F32)],
            both, table_shape, lh, ll, eh, el, fsel, env, envdot, dinv, curl, mh, ml, after,
            flops=1 << 31,
        )[0]

    radials = [radial(0, both)]
    keep, give = call(
        halve_kernel, "halve", [(rows_mix // 2, HALF)] * 2, [], keep, shifted(give, "batch", 1)
    )
    taken = partner(give, 1)
    radials.append(radial(1, keep))
    piece = rows_mix // (2 * FOUR) + SMALL // FOUR
    blocks = call(
        spread_kernel, "spread", [(piece, HALF)] * FOUR, [((SMALL, HALF), F32)],
        keep, taken, *radials, small,
    )
    terms = [blocks[0]] + [partner(blocks[k], 2 * k) for k in range(FOUR - 1, 0, -1)]
    (mine,) = call(total_kernel, "total", [(piece, HALF)], [], *terms)
    bit = 2 * FOUR
    while bit < lax.axis_size("domain"):
        (mine,) = call(total_kernel, "total", [(piece, HALF)], [], mine, partner(mine, bit))
        bit *= 2
    parts = [mine] + [partner(mine, 2 * k) for k in range(1, FOUR)]
    (mine,) = call(grow_kernel, "grow", [(rows_mix // 2 + SMALL, HALF)], [], *parts)
    theirs = partner(mine, 1)
    facing = [shifted(part, "batch", 1) for part in (mine, theirs)]
    mix, radial_sum, kinds, out = call(
        join_kernel,
        "join",
        [(rows_mix, channels), (BASIS, channels), (SPECIES, channels), (1, channels)],
        [],
        mine,
        theirs,
        *facing,
    )
    return forces.transpose(1, 0, 2), radial_sum, mix, kinds, out.reshape(channels)


def solution(mesh):
    return jax.shard_map(
        on_device,
        mesh=mesh,
        in_specs=(
            P(("parts", "batch"), None, "domain"),
            P(("parts", "batch"), "domain", None),
            P(("parts", "batch"), "domain"),
            P(("parts", "batch"), None, "domain"),
            P(("parts", "batch"), "domain"),
            P(("parts", "batch"), "domain"),
            P(("parts", "batch"), "domain"),
            P(("parts", "batch"), "domain"),
            P(),
            P(),
            P(),
            P(),
        ),
        out_specs=(
            P(("parts", "batch"), None, "domain"),
            P("parts", None),
            P("parts", None),
            P("parts", None),
            P("parts"),
        ),
        check_vma=False,
    )
```

```python
import functools
import math

import jax
import jax.numpy as jnp
from jax import lax
from jax.experimental import pallas as pl
from jax.experimental.pallas import tpu as pltpu
from jax.sharding import PartitionSpec as P

TA = 64
SEND = 2
PAIRS = 2
COMPS = 9
WIDE = 10 * TA
BASIS = 8
SPECIES = 4
HALF = 128
CHUNK = 2 * TA

cutoff = 2.5
soften = 0.25
env_scale = 0.25
root_three = math.sqrt(3.0)
F32 = jnp.float32
BF16 = jnp.bfloat16
NN = (((1,), (0,)), ((), ()))
NT = (((1,), (1,)), ((), ()))
TN = (((0,), (0,)), ((), ()))
GROUP = (0, 1, 1, 1, 2, 2, 2, 2, 2)


def split(value):
    high = value.astype(BF16)
    return high, (value - high.astype(F32)).astype(BF16)


def product(left, right, dims):
    (lh, ll), (rh, rl) = left, right

    def one(x, y):
        return lax.dot_general(x, y, dims, preferred_element_type=F32)

    return one(lh, rh) + (one(lh, rl) + one(ll, rh))


def flag(condition):
    return jnp.where(condition, 1.0, 0.0).astype(F32)


def place(shift, width):
    return lax.bitwise_and(lax.shift_right_logical(lax.axis_index("domain"), shift), width - 1)


def lane_half():
    lane = lax.broadcasted_iota(jnp.int32, (1, CHUNK), 1)
    low = flag(lane < TA)
    return low, 1.0 - low


def twice(chunk, half):
    low, high = lane_half()
    swapped = pltpu.roll(chunk, TA, 1)
    return chunk * low + swapped * high if half == 0 else swapped * low + chunk * high


def pick(chunks, position):
    total = None
    for q, chunk in enumerate(chunks):
        for half in range(2):
            term = twice(chunk, half) * flag(position == 2 * q + half)
            total = term if total is None else total + term
    return total


def paired(first, second):
    low, high = lane_half()
    return first * low + second * high


def chunk_mask(position, q):
    low, high = lane_half()
    return low * flag(position == 2 * q) + high * flag(position == 2 * q + 1)


def geometry(lane_rows, columns, sign, live, same):
    offset = [(row - column) * sign for row, column in zip(lane_rows, columns)]
    dist_sq = offset[0] * offset[0] + offset[1] * offset[1] + offset[2] * offset[2] + soften
    distance = jnp.sqrt(dist_sq)
    inverse = 1.0 / distance
    unit = [x * inverse for x in offset]
    row = lax.broadcasted_iota(jnp.int32, (TA, CHUNK), 0)
    lane = lax.broadcasted_iota(jnp.int32, (TA, CHUNK), 1)
    lane = jnp.where(lane >= TA, lane - TA, lane)
    mask = live * (1.0 - same * flag(row == lane))
    base = jnp.maximum(1.0 - dist_sq * (1.0 / (cutoff * cutoff)), 0.0)
    weight = base * base * base * mask * inverse
    slope = -(6.0 / (cutoff * cutoff)) * base * base * mask - weight * inverse
    angle = distance * (math.pi / cutoff)
    return unit, inverse, weight, slope, jnp.sin(angle), jnp.cos(angle)


def harmonics(v):
    x, y, z = v
    return [
        None,
        x,
        y,
        z,
        root_three * x * y,
        root_three * y * z,
        root_three * z * x,
        0.5 * root_three * (x * x - y * y),
        z * z - 0.5 * (x * x + y * y),
    ]


def harmonics_tangent(v, t):
    x, y, z = v
    a, b, c = t
    return [
        None,
        a,
        b,
        c,
        root_three * (a * y + x * b),
        root_three * (b * z + y * c),
        root_three * (c * x + z * a),
        root_three * (x * a - y * b),
        2.0 * z * c - (x * a + y * b),
    ]


def paired_orders(sine, cosine, weight, slope):
    low, high = lane_half()
    double_s, double_c = 2.0 * sine * cosine, 1.0 - 2.0 * sine * sine
    now_s = sine * low + double_s * high
    now_c = cosine * low + double_c * high
    old_s = -sine * low
    old_c = cosine * low + high
    values, slopes = [], []
    for k in range(BASIS // 2):
        order = ((2 * k + 1) * low + (2 * k + 2) * high) * (math.pi / cutoff)
        values.append(now_s * weight)
        slopes.append(now_c * (weight * order) + now_s * slope)
        now_s, old_s = 2.0 * double_c * now_s - old_s, now_s
        now_c, old_c = 2.0 * double_c * now_c - old_c, now_c
    return values, slopes


def single_orders(sine, cosine, weight, slope):
    now_s, now_c = sine, cosine
    old_s, old_c = jnp.zeros_like(sine), jnp.ones_like(cosine)
    values, slopes = [], []
    for n in range(1, BASIS + 1):
        values.append(now_s * weight)
        slopes.append(now_c * (weight * (n * math.pi / cutoff)) + now_s * slope)
        now_s, old_s = 2.0 * cosine * now_s - old_s, now_s
        now_c, old_c = 2.0 * cosine * now_c - old_c, now_c
    return values, slopes


def columns_of(rows, square, turned):
    square[...] = jnp.zeros_like(square)
    square[0 : rows.shape[0], :] = rows
    turned[...] = square[...].T


def pair_rows(first, p):
    return twice(first, p)


def radial_feat(feat, radial, p, high_ref, low_ref):
    own = feat[p * TA : (p + 1) * TA, :]
    for n in range(BASIS):
        hi, lo = split(own * radial[n : n + 1, :])
        high_ref[n * TA : (n + 1) * TA, :] = hi
        low_ref[n * TA : (n + 1) * TA, :] = lo


OTHER, CENTRE, LIVE, SAME, SHARED, SENT = 0, 2, 4, 6, 8, 9
GHOST_ROWS = 8


def fetch(pairs, sems):
    copies = [pltpu.make_async_copy(src, dst, sems.at[i]) for i, (src, dst) in enumerate(pairs)]
    for copy in copies:
        copy.start()
    return copies


def upward(shift):
    return 1.0 - flag(place(shift, 2) == 1)


def either(choice, first, second):
    return first * choice + second * (1.0 - choice)


def gather_kernel(send, pos, feat, ref, to_second, to_first, token, send_v, pos_v, feat_v, ref_v, sems):
    copies = fetch([(send, send_v), (pos, pos_v), (ref, ref_v), (feat, feat_v)], sems)
    for copy in copies[:3]:
        copy.wait()
    low, high = lane_half()
    up = upward(0)
    sent = [send_v[0:1, j : j + 1].astype(F32) for j in range(2 * SEND)]
    tiles_of = []
    for out, choice in ((to_first, 1.0 - up), (to_second, up)):
        tiles = [either(choice, sent[j], sent[SEND + j]) for j in range(SEND)]
        tiles_of.append(tiles)
        out[SEND * TA :, :] = jnp.zeros((GHOST_ROWS, out.shape[1]), F32)
        for i in range(3):
            at = SEND * TA + i
            for lanes, source in ((slice(0, CHUNK), pos_v), (slice(CHUNK, 2 * CHUNK), ref_v)):
                chunks = [source[i, :, q * CHUNK : (q + 1) * CHUNK] for q in range(2)]
                out[at : at + 1, lanes] = paired(pick(chunks, tiles[0]), pick(chunks, tiles[1]))
        for other in range(2 * SEND):
            same = low * flag(sent[other] == tiles[0]) + high * flag(sent[other] == tiles[1])
            out[SEND * TA + 3 + other : SEND * TA + 4 + other, 0:CHUNK] = same
    token[...] = jnp.zeros_like(token)
    copies[3].wait()
    for out, tiles in zip((to_first, to_second), tiles_of):
        for j in range(SEND):
            out[j * TA : (j + 1) * TA, :] = pick_rows(feat_v.at[0], tiles[j], 0.0)


def pick_rows(ref, position, first):
    total = None
    for t in range(ref.shape[0] // TA):
        term = ref[t * TA : (t + 1) * TA, :] * flag(position == first + float(t))
        total = term if total is None else total + term
    return total


def stage_kernel(
    centre, other, live, send, pos, ref, species, feat, radial_w, mix_w, species_w, out_w, after,
    flags, atoms, own_feat, weights, mh, ml,
    centre_v, other_v, live_v, send_v, pos_v, ref_v, species_v, radial_v, mix_v, species_w_v, out_v, sems,
):
    copies = fetch(
        [
            (centre, centre_v), (other, other_v), (live, live_v), (send, send_v), (pos, pos_v), (ref, ref_v),
            (species, species_v), (radial_w, radial_v), (species_w, species_w_v), (out_w, out_v),
            (feat.at[0], own_feat), (mix_w, mix_v),
        ],
        sems,
    )
    for copy in copies[:-1]:
        copy.wait()
    flags[...] = jnp.zeros_like(flags)
    centres = [centre_v[0:1, p : p + 1].astype(F32) for p in range(PAIRS)]
    others = [other_v[0:1, p : p + 1].astype(F32) for p in range(PAIRS)]
    for p in range(PAIRS):
        for row, value in (
            (OTHER, others[p]),
            (CENTRE, centres[p]),
            (LIVE, live_v[0:1, p : p + 1].astype(F32)),
            (SAME, flag(others[p] == centres[p] + SEND)),
        ):
            flags[row + p : row + p + 1, :] = jnp.broadcast_to(value, (1, CHUNK))
    flags[SHARED : SHARED + 1, :] = jnp.broadcast_to(flag(centres[0] == centres[1]), (1, CHUNK))
    for j in range(2 * SEND):
        value = send_v[0:1, j : j + 1].astype(F32)
        flags[SENT + j : SENT + j + 1, :] = jnp.broadcast_to(value, (1, CHUNK))
    atoms[...] = jnp.zeros_like(atoms)
    for i in range(3):
        atoms[i : i + 1, :] = pos_v[i]
        atoms[4 + i : 5 + i, :] = ref_v[i]
    atoms[3:4, :] = species_v[...].astype(F32)
    weights[...] = jnp.zeros_like(weights)
    weights[0:BASIS, :] = radial_v[...]
    weights[BASIS : BASIS + SPECIES, :] = species_w_v[...]
    weights[BASIS + SPECIES : BASIS + SPECIES + 1, :] = out_v[...]
    copies[-1].wait()
    hi, lo = split(mix_v[...])
    mh[...] = hi
    ml[...] = lo


def force_kernel(
    flags, atoms, feat, weights, mh, ml, from_second, from_first,
    env, dinv, gate, curve, inv, rows, fsel, own, one_first, one_second, two_first, two_second, shape_store, xh, xl, eh, el,
    square, turned, th, tl, raw, back,
):
    ghost = SEND * TA
    up = upward(0)
    near, far = from_first[ghost : ghost + 3, 0:CHUNK], from_second[ghost : ghost + 3, 0:CHUNK]
    chunks = [either(up, far, near), atoms[0:3, 0:CHUNK], atoms[0:3, CHUNK:], either(up, near, far)]
    kinds = [atoms[3:4, q * CHUNK : (q + 1) * CHUNK] for q in range(2)]

    def number(row):
        return flags[row : row + 1, :]

    centres = [number(CENTRE + p) for p in range(PAIRS)]
    others = [number(OTHER + p) for p in range(PAIRS)]
    shared = flags[SHARED : SHARED + 1, 0:1]
    rows[...] = jnp.zeros_like(rows)
    rows[0:3, :] = paired(*(pick(chunks, others[p]) for p in range(PAIRS)))
    rows[3:6, :] = paired(*(pick(chunks[1:3], centres[p]) for p in range(PAIRS)))
    rows[6:7, :] = paired(*(pick(kinds, centres[p]) for p in range(PAIRS)))
    columns_of(rows[...], square, turned)

    for p in range(PAIRS):
        o = flags[OTHER + p : OTHER + p + 1, 0:1]
        fsel[p * TA : (p + 1) * TA, :] = (
            pick_rows(from_first.at[0:ghost], o, (SEND + 4) * up)
            + pick_rows(feat, o, float(SEND))
            + pick_rows(from_second.at[0:ghost], o, (SEND + 4) * (1.0 - up))
        )

    shapes = []
    for p in range(PAIRS):
        lane_rows = [twice(rows[i : i + 1, :], p) for i in range(3)]
        columns = [turned[p * TA : (p + 1) * TA, 3 + i : 4 + i] for i in range(3)]
        unit, inverse, weight, slope, sine, cosine = geometry(
            lane_rows, columns, 1.0, number(LIVE + p), number(SAME + p)
        )
        angular = harmonics(unit)
        values, slopes = paired_orders(sine, cosine, weight, slope)
        shapes.append((unit, inverse, angular, values, slopes))
        for i, part in enumerate(unit + [inverse] + values + slopes):
            shape_store[p, i] = part
        for m in range(COMPS):
            for k in range(BASIS // 2):
                entry = values[k] if m == 0 else angular[m] * values[k]
                hi, lo = split(entry)
                th[p, m * TA : (m + 1) * TA, k * CHUNK : (k + 1) * CHUNK] = hi
                tl[p, m * TA : (m + 1) * TA, k * CHUNK : (k + 1) * CHUNK] = lo
        radial_feat(fsel, weights, p, xh.at[p], xl.at[p])
        raw[p * COMPS * TA : (p + 1) * COMPS * TA, :] = product((th[p], tl[p]), (xh[p], xl[p]), NN)

    for m in range(COMPS):
        first = raw[m * TA : (m + 1) * TA, :]
        second = raw[(COMPS + m) * TA : (COMPS + m + 1) * TA, :]
        env[m * TA : (m + 1) * TA, :] = env_scale * (first + shared * second)
        env[(COMPS + m) * TA : (COMPS + m + 1) * TA, :] = env_scale * (second + shared * first)
    for p in range(PAIRS):
        sums = [None] * 3
        for m in range(COMPS):
            block = env[(p * COMPS + m) * TA : (p * COMPS + m + 1) * TA, :]
            sums[GROUP[m]] = block * block if sums[GROUP[m]] is None else sums[GROUP[m]] + block * block
        for g in range(3):
            inv[p * TA : (p + 1) * TA, g * 256 : (g + 1) * 256] = sums[g]
    hidden = product(split(inv[...]), (mh[...], ml[...]), NN)
    kind = turned[:, 6:7]
    for s in range(SPECIES):
        hidden = hidden + flag(kind == float(s)) * weights[BASIS + s : BASIS + s + 1, :]
    out_row = weights[BASIS + SPECIES : BASIS + SPECIES + 1, :]
    sigma = 1.0 / (1.0 + jnp.exp(-hidden))
    first_order = sigma * (1.0 + hidden * (1.0 - sigma))
    gate[...] = first_order
    curve[...] = sigma * (1.0 - sigma) * (2.0 + hidden * (1.0 - 2.0 * sigma)) * out_row
    dinv[...] = product(split(first_order * out_row), (mh[...], ml[...]), NT)

    tile_grads = [jnp.zeros((3, CHUNK), F32) for _ in range(4)]
    for p in range(PAIRS):
        unit, inverse, angular, values, slopes = shapes[p]
        for m in range(COMPS):
            block = env[(p * COMPS + m) * TA : (p * COMPS + m + 1) * TA, :]
            part = dinv[p * TA : (p + 1) * TA, GROUP[m] * 256 : (GROUP[m] + 1) * 256]
            hi, lo = split((2.0 * env_scale) * block * part)
            eh[p, m * TA : (m + 1) * TA, :] = hi
            el[p, m * TA : (m + 1) * TA, :] = lo
        for ref in (eh, el):
            ref[p, COMPS * TA :, :] = jnp.zeros((WIDE - COMPS * TA, ref.shape[2]), BF16)
        steady = (eh[p, 0 : COMPS * TA, :], el[p, 0 : COMPS * TA, :])
        back[p] = product(steady, (xh[p], xl[p]), NT)
        d_radius = None
        d_angular = []
        for m in range(COMPS):
            along, across = None, None
            for k in range(BASIS // 2):
                block = back[p, m * TA : (m + 1) * TA, k * CHUNK : (k + 1) * CHUNK]
                along = block * slopes[k] if along is None else along + block * slopes[k]
                across = block * values[k] if across is None else across + block * values[k]
            d_angular.append(across)
            term = along if m == 0 else along * angular[m]
            d_radius = term if d_radius is None else d_radius + term
        x, y, z = unit
        g = d_angular
        toward = [
            g[1] + root_three * (y * g[4] + z * g[6] + x * g[7]) - x * g[8],
            g[2] + root_three * (x * g[4] + z * g[5] - y * g[7]) - y * g[8],
            g[3] + root_three * (y * g[5] + x * g[6]) + 2.0 * (z * g[8]),
        ]
        radial_part = d_radius - inverse * (toward[0] * x + toward[1] * y + toward[2] * z)
        for i in range(3):
            d_offset = inverse * toward[i] + unit[i] * radial_part
            summed = jnp.sum(d_offset, axis=0, keepdims=True)
            other_row = summed + pltpu.roll(summed, TA, 1)
            square[0:TA, :] = d_offset
            square[TA:, :] = d_offset
            centre_row = -jnp.sum(square[...].T, axis=0, keepdims=True)
            component = flag(lax.broadcasted_iota(jnp.int32, (3, CHUNK), 0) == i)
            for q in range(4):
                at = chunk_mask(others[p], q) * other_row
                if q in (1, 2):
                    at = at + chunk_mask(centres[p] + SEND, q) * centre_row
                tile_grads[q] = tile_grads[q] + at * component
    own[...] = jnp.zeros_like(own)
    own[0:3, 0:CHUNK] = tile_grads[1]
    own[0:3, CHUNK:] = tile_grads[2]
    own[3:6, 0:CHUNK] = tile_grads[0]
    own[3:6, CHUNK:] = tile_grads[3]
    leaving = []
    for first, ghost_grad in ((0, tile_grads[0]), (SEND, tile_grads[3])):
        listed = paired(*(pick(tile_grads[1:3], number(SENT + first + j)) for j in range(SEND)))
        leaving.append((listed, ghost_grad))
    for shift, outs in ((0, (one_first, one_second)), (1, (two_first, two_second))):
        choice = upward(shift)
        for out, above in zip(outs, (choice, 1.0 - choice)):
            out[...] = jnp.zeros_like(out)
            out[0:3, :] = either(above, leaving[1][0], leaving[0][0])
            out[3:6, :] = either(above, leaving[1][1], leaving[0][1])


def tangent_kernel(
    scale, flags, atoms, weights, mh, ml, from_first, from_second, own, one_second, two_second, one_first, two_first,
    rows, env, gate, curve, inv, shape_store, xh, xl, after,
    forces, keep, give, small, envdot, curl, both,
    square, turned, th, tl, raw, left, right,
):
    ghost = SEND * TA
    def number(row):
        return flags[row : row + 1, :]

    centres = [number(CENTRE + p) for p in range(PAIRS)]
    others = [number(OTHER + p) for p in range(PAIRS)]
    shared = flags[SHARED : SHARED + 1, 0:1]
    mine = [own[0:3, 0:CHUNK], own[0:3, CHUNK:]]
    up, up_two = upward(0), upward(1)
    low_one = either(up, one_second[...], one_first[...])
    high_one = either(up, one_first[...], one_second[...])
    low_two = either(up_two, two_second[...], two_first[...])
    high_two = either(up_two, two_first[...], two_second[...])
    low_tail = either(up, from_second[ghost:, :], from_first[ghost:, :])
    high_tail = either(up, from_first[ghost:, :], from_second[ghost:, :])
    arrived = [twice(low_one[3:6, :], j) for j in range(SEND)]
    arrived += [twice(high_one[3:6, :], j) for j in range(SEND)]
    for j in range(2 * SEND):
        for q in range(2):
            mine[q] = mine[q] + chunk_mask(number(SENT + j), q) * arrived[j]
    below = low_one[0:3, :]
    above = high_one[0:3, :]
    to_below = [twice(low_two[3:6, :], j) for j in range(SEND)]
    to_below += [twice(own[3:6, 0:CHUNK], j) for j in range(SEND)]
    to_above = [twice(own[3:6, CHUNK:], j) for j in range(SEND)]
    to_above += [twice(high_two[3:6, :], j) for j in range(SEND)]
    for j in range(2 * SEND):
        below = below + low_tail[3 + j : 4 + j, 0:CHUNK] * to_below[j]
        above = above + high_tail[3 + j : 4 + j, 0:CHUNK] * to_above[j]
    for q in range(2):
        for i in range(3):
            forces[i, :, q * CHUNK : (q + 1) * CHUNK] = -mine[q][i : i + 1, :]
    error = [
        below + low_tail[0:3, CHUNK:],
        mine[0] + atoms[4:7, 0:CHUNK],
        mine[1] + atoms[4:7, CHUNK:],
        above + high_tail[0:3, CHUNK:],
    ]
    error = [part * scale for part in error]
    both[...] = jnp.zeros_like(both)
    both[0:8, :] = rows[...]
    both[8:11, :] = paired(*(pick(error, others[p]) for p in range(PAIRS)))
    both[11:14, :] = paired(*(pick(error[1:3], centres[p]) for p in range(PAIRS)))
    columns_of(both[...], square, turned)

    for p in range(PAIRS):
        lane_move = [twice(both[8 + i : 9 + i, :], p) for i in range(3)]
        column_move = [turned[p * TA : (p + 1) * TA, 11 + i : 12 + i] for i in range(3)]
        unit = [shape_store[p, i] for i in range(3)]
        inverse = shape_store[p, 3]
        values = [shape_store[p, 4 + k] for k in range(BASIS // 2)]
        slopes = [shape_store[p, 8 + k] for k in range(BASIS // 2)]
        move = [a - b for a, b in zip(lane_move, column_move)]
        stretch = unit[0] * move[0] + unit[1] * move[1] + unit[2] * move[2]
        turn = [(m - v * stretch) * inverse for m, v in zip(move, unit)]
        angular, turning = harmonics(unit), harmonics_tangent(unit, turn)
        slopes = [s * stretch for s in slopes]
        for m in range(COMPS):
            for k in range(BASIS // 2):
                entry = slopes[k] if m == 0 else angular[m] * slopes[k] + turning[m] * values[k]
                hi, lo = split(entry)
                th[p, m * TA : (m + 1) * TA, k * CHUNK : (k + 1) * CHUNK] = hi
                tl[p, m * TA : (m + 1) * TA, k * CHUNK : (k + 1) * CHUNK] = lo
        raw[p * COMPS * TA : (p + 1) * COMPS * TA, :] = product((th[p], tl[p]), (xh[p], xl[p]), NN)

    for m in range(COMPS):
        first = raw[m * TA : (m + 1) * TA, :]
        second = raw[(COMPS + m) * TA : (COMPS + m + 1) * TA, :]
        envdot[m * TA : (m + 1) * TA, :] = env_scale * (first + shared * second)
        envdot[(COMPS + m) * TA : (COMPS + m + 1) * TA, :] = env_scale * (second + shared * first)
    invdot = left
    half = PAIRS * TA
    for p in range(PAIRS):
        sums = [None] * 3
        for m in range(COMPS):
            at = slice((p * COMPS + m) * TA, (p * COMPS + m + 1) * TA)
            term = 2.0 * env[at, :] * envdot[at, :]
            sums[GROUP[m]] = term if sums[GROUP[m]] is None else sums[GROUP[m]] + term
        for g in range(3):
            invdot[half + p * TA : half + (p + 1) * TA, g * 256 : (g + 1) * 256] = sums[g]
    invdot[0:half, :] = inv[...]
    hidden_move = product(split(invdot[half:, :]), (mh[...], ml[...]), NN)
    bend = curve[...] * hidden_move
    curl[...] = bend
    once = 1.0 - shared * flag(lax.broadcasted_iota(jnp.int32, (half, 1), 0) >= TA)
    right[0:half, :] = bend * once
    right[half:, :] = gate[...] * weights[BASIS + SPECIES : BASIS + SPECIES + 1, :] * once
    raw[0 : left.shape[1], :] = product(split(left[...]), split(right[...]), TN)
    core = lax.axis_index("batch")
    for out, part in ((keep, core), (give, 1 - core)):
        out[...] = raw[0 : left.shape[1], block_of_lanes(part)]
    small[...] = jnp.zeros_like(small)
    kind = turned[:, 6:7]
    for s in range(SPECIES):
        small[s : s + 1, :] = jnp.sum(right[0:half, :] * flag(kind == float(s)), axis=0, keepdims=True)
    small[SPECIES : SPECIES + 1, :] = jnp.sum(gate[...] * hidden_move * once, axis=0, keepdims=True)


def table_kernel(flags, rows, shape_store, lh, ll, token, square, turned):
    low, high = lane_half()
    token[...] = jnp.zeros_like(token)
    columns_of(rows[...], square, turned)
    for p in range(PAIRS):
        lane_rows = [twice(rows[3 + i : 4 + i, :], p) for i in range(3)]
        columns = [turned[p * TA : (p + 1) * TA, i : i + 1] for i in range(3)]
        unit, inverse, weight, slope, sine, cosine = geometry(
            lane_rows, columns, -1.0, flags[LIVE + p : LIVE + p + 1, :], flags[SAME + p : SAME + p + 1, :]
        )
        angular = harmonics(unit)
        values, slopes = single_orders(sine, cosine, weight, slope)
        for i, part in enumerate(unit + [inverse] + values + slopes):
            shape_store[p, i] = part
        for m in range(0, COMPS + 1, 2):
            factor = low if m == 0 else angular[m] * low
            if m + 1 < COMPS:
                factor = factor + angular[m + 1] * high
            for n in range(BASIS):
                hi, lo = split(factor * values[n])
                lh[p, n * TA : (n + 1) * TA, m * TA : (m + 2) * TA] = hi
                ll[p, n * TA : (n + 1) * TA, m * TA : (m + 2) * TA] = lo


def radial_kernel(
    p, both, shape_store, lh, ll, eh, el, fsel, env, envdot, dinv, curl, mh, ml, after,
    grad_radial,
    square, turned, sh, sl, gh, gl, raw,
):
    low, high = lane_half()
    columns_of(both[...], square, turned)
    here = slice(p * TA, (p + 1) * TA)
    turn_inv = product(split(curl[here, :]), (mh[...], ml[...]), NT)
    lane_move = [twice(both[11 + i : 12 + i, :], p) for i in range(3)]
    column_move = [turned[here, 8 + i : 9 + i] for i in range(3)]
    unit = [shape_store[p, i] for i in range(3)]
    inverse = shape_store[p, 3]
    move = [b - a for a, b in zip(lane_move, column_move)]
    stretch = unit[0] * move[0] + unit[1] * move[1] + unit[2] * move[2]
    turn = [(m - v * stretch) * inverse for m, v in zip(move, unit)]
    angular, turning = harmonics(unit), harmonics_tangent(unit, turn)
    sh[:, 0:CHUNK] = lh[p, :, WIDE - CHUNK :]
    sl[:, 0:CHUNK] = ll[p, :, WIDE - CHUNK :]
    for m in range(0, COMPS + 1, 2):
        if m == 0:
            on_value, on_slope = turning[1] * high, low + angular[1] * high
        else:
            on_value, on_slope = turning[m] * low, angular[m] * low
            if m + 1 < COMPS:
                on_value = on_value + turning[m + 1] * high
                on_slope = on_slope + angular[m + 1] * high
        on_slope = on_slope * stretch
        lanes = slice(CHUNK + m * TA, CHUNK + (m + 2) * TA)
        for n in range(BASIS):
            hi, lo = split(on_value * shape_store[p, 4 + n] + on_slope * shape_store[p, 4 + BASIS + n])
            sh[n * TA : (n + 1) * TA, lanes] = hi
            sl[n * TA : (n + 1) * TA, lanes] = lo
    for m in range(COMPS):
        at = slice((p * COMPS + m) * TA, (p * COMPS + m + 1) * TA)
        group = slice(GROUP[m] * 256, (GROUP[m] + 1) * 256)
        steady = (2.0 * env_scale) * dinv[here, group]
        bent = (2.0 * env_scale) * turn_inv[:, group]
        hi, lo = split(env[at, :] * bent + envdot[at, :] * steady)
        gh[m * TA : (m + 1) * TA, :] = hi
        gl[m * TA : (m + 1) * TA, :] = lo
    for ref, tail in ((gh, eh), (gl, el)):
        ref[COMPS * TA : WIDE, :] = jnp.zeros((WIDE - COMPS * TA, ref.shape[1]), BF16)
        ref[WIDE:, :] = tail[p]
    first = WIDE - CHUNK
    raw[...] = product((lh[p, :, 0:first], ll[p, :, 0:first]), (gh[0:first, :], gl[0:first, :]), NN) + product(
        (sh[...], sl[...]), (gh[first:, :], gl[first:, :]), NN
    )
    for n in range(BASIS):
        grad_radial[n : n + 1, :] = jnp.sum(
            raw[n * TA : (n + 1) * TA, :] * fsel[here, :], axis=0, keepdims=True
        )


SMALL = 32
PAD = 8
FOUR = 4


def block_of(part, rows):
    return pl.ds(pl.multiple_of(part * rows, 8), rows)


def block_from(start, rows):
    return pl.ds(pl.multiple_of(start, 8), rows)


def block_of_lanes(part):
    return pl.ds(pl.multiple_of(part * HALF, HALF), HALF)


def total_of(refs, at):
    total = refs[0][at, :]
    for ref in refs[1:]:
        total = total + ref[at, :]
    return total


def halve_kernel(keep, taken, after, *outs):
    half, piece = keep.shape[0] // 2, keep.shape[0] // (2 * FOUR)
    mine, me = place(0, 2), place(1, FOUR)
    for i, out in enumerate(outs):
        part = mine if i < 2 else 1 - mine
        for j in range(2):
            k = 1 + 2 * (i % 2) - j
            at = block_from(part * half + lax.bitwise_xor(me, k) * piece, piece)
            out[j * piece : (j + 1) * piece, :] = keep[at, :] + taken[at, :]
        if out.shape[0] > 2 * piece:
            out[2 * piece :, :] = jnp.zeros((out.shape[0] - 2 * piece, HALF), F32)


def spread_kernel(first, keep, taken, radial_0, radial_1, small, after, out_0, out_1, tiny):
    for h in range(2):
        lanes = slice(h * HALF, (h + 1) * HALF)
        tiny[16 * h : 16 * h + 8, :] = radial_0[:, lanes] + radial_1[:, lanes]
        tiny[16 * h + 8 : 16 * h + 16, :] = small[:, lanes]
    me = place(1, FOUR)
    few = SMALL // FOUR
    rows = keep.shape[0] // 2
    for j, out in enumerate((out_0, out_1)):
        out[0:rows, :] = total_of([keep, taken], slice(j * rows, (j + 1) * rows))
        out[rows : rows + few, :] = tiny[block_of(lax.bitwise_xor(me, first - j), few), :]
        if out.shape[0] > rows + few:
            out[rows + few :, :] = jnp.zeros((out.shape[0] - rows - few, HALF), F32)


def total_kernel(*refs):
    refs[-1][...] = total_of(refs[:-1], slice(0, refs[-1].shape[0]))


def near_kernel(mine, third, out):
    rows = mine.shape[0] - SMALL // FOUR
    out[0:rows, :] = mine[0:rows, :]
    out[rows : 2 * rows, :] = third[0:rows, :]
    out[2 * rows :, :] = jnp.zeros((out.shape[0] - 2 * rows, HALF), F32)


def rest_kernel(mine, first, second, third, after, out):
    few = SMALL // FOUR
    rows = mine.shape[0] - few
    out[0:rows, :] = second[0:rows, :]
    out[rows : 2 * rows, :] = first[0:rows, :]
    me = place(1, FOUR)
    for k, ref in enumerate((mine, first, second, third)):
        out[block_from(2 * rows + lax.bitwise_xor(me, k) * few, few), :] = ref[rows:, :]


def pair_kernel(near, rest, their_near, their_rest, out):
    piece = (rest.shape[0] - SMALL) // 2
    half = FOUR * piece
    mine, me = place(0, 2), place(1, FOUR)
    for refs, part in (((near, rest), mine), ((their_near, their_rest), 1 - mine)):
        for ref, ks in zip(refs, ((0, 3), (2, 1))):
            for j, k in enumerate(ks):
                at = block_from(part * half + lax.bitwise_xor(me, k) * piece, piece)
                out[at, :] = ref[j * piece : (j + 1) * piece, :]
    out[2 * half :, :] = rest[2 * piece :, :] + their_rest[2 * piece :, :]


def join_kernel(whole, facing, mix, radial, kinds, out):
    rows = mix.shape[0]
    core = lax.axis_index("batch")
    for ref, part in ((whole, core), (facing, 1 - core)):
        mix[:, block_of_lanes(part)] = ref[0:rows, :]
    both = whole[rows:, :] + facing[rows:, :]
    for h in range(2):
        lanes = slice(h * HALF, (h + 1) * HALF)
        few = both[16 * h : 16 * h + 16, :]
        radial[:, lanes] = few[0:BASIS]
        kinds[:, lanes] = few[BASIS : BASIS + SPECIES]
        out[:, lanes] = few[BASIS + SPECIES : BASIS + SPECIES + 1]


def spec(space):
    return pl.BlockSpec(memory_space=space)


def call(kernel, name, outs, scratch, *operands, space=pltpu.VMEM, after=(), flops=0):
    if space is pltpu.HBM:
        operands = [pltpu.with_memory_space_constraint(operand, space) for operand in operands]
    outs = [out if len(out) == 2 and isinstance(out[0], tuple) else (out, F32) for out in outs]
    return pl.pallas_call(
        kernel,
        name=name,
        out_shape=[jax.ShapeDtypeStruct(*out) for out in outs],
        in_specs=[spec(space)] * len(operands) + [spec(pltpu.VMEM)] * len(after),
        out_specs=[spec(pltpu.VMEM)] * len(outs),
        scratch_shapes=[pltpu.VMEM(*item) if isinstance(item, tuple) else item for item in scratch],
        compiler_params=pltpu.CompilerParams(vmem_limit_bytes=28 * 1024 * 1024),
        cost_estimate=pl.CostEstimate(flops=flops, bytes_accessed=1 << 20 if flops else 1 << 10, transcendentals=0),
    )(*operands, *after)


def shifted(block, axis, by):
    count = lax.axis_size(axis)
    return lax.ppermute(block, axis, [(i, (i + by) % count) for i in range(count)])


def exchanged(block, shift, first):
    count, step = lax.axis_size("domain"), 1 << shift
    up = [((i >> shift) & 1 == 0) == first for i in range(count)]
    return lax.ppermute(block, "domain", [(i, (i + step if up[i] else i - step) % count) for i in range(count)])


def partner(block, mask):
    return lax.ppermute(block, "domain", [(i, i ^ mask) for i in range(lax.axis_size("domain"))])


def on_device(
    positions,
    features,
    species,
    ref_forces,
    centre_tile,
    other_tile,
    pair_live,
    send_tiles,
    radial_w,
    mix_w,
    species_w,
    out_w,
):
    atoms_here = positions.shape[2]
    channels = features.shape[2]
    table = (COMPS * TA, BASIS * TA)
    sent = (SEND * TA + GHOST_ROWS, channels)
    slots = PAIRS * TA
    line = (3, 1, atoms_here)
    turning = [((CHUNK, CHUNK), F32)] * 2
    out_row = out_w.reshape(1, channels)
    positions = positions.transpose(1, 0, 2)
    ref_forces = ref_forces.transpose(1, 0, 2)
    ints = [((1, n), jnp.int32) for n in (PAIRS, PAIRS, PAIRS, 2 * SEND)]

    to_second, to_first, token = call(
        gather_kernel,
        "gather",
        [sent, sent, (8, CHUNK)],
        [
            ints[3],
            (line, F32),
            ((1, atoms_here, channels), F32),
            (line, F32),
            pltpu.SemaphoreType.DMA((4,)),
        ],
        send_tiles, positions, features, ref_forces,
        space=pltpu.HBM,
    )
    from_second = exchanged(to_second, 0, False)
    from_first = exchanged(to_first, 0, True)
    flags, atoms, own_feat, weights, mh, ml = call(
        stage_kernel,
        "stage",
        [
            (16, CHUNK),
            (8, atoms_here),
            (atoms_here, channels),
            (16, channels),
            (mix_w.shape, BF16),
            (mix_w.shape, BF16),
        ],
        ints
        + [(line, F32), (line, F32), ((1, atoms_here), jnp.int32)]
        + [(radial_w.shape, F32), (mix_w.shape, F32), (species_w.shape, F32), (out_row.shape, F32)]
        + [pltpu.SemaphoreType.DMA((12,))],
        centre_tile, other_tile, pair_live, send_tiles, positions, ref_forces, species, features,
        radial_w, mix_w, species_w, out_row,
        space=pltpu.HBM,
        after=(token,),
    )

    factors = (PAIRS, BASIS * TA, channels)
    env, dinv, gate, curve, inv, rows, fsel, own, *leaving, shape_store, xh, xl, eh, el = call(
        force_kernel,
        "force",
        [
            (PAIRS * COMPS * TA, channels),
            (slots, 3 * channels),
            (slots, channels),
            (slots, channels),
            (slots, 3 * channels),
            (8, CHUNK),
            (slots, channels),
            (8, atoms_here),
            (8, CHUNK),
            (8, CHUNK),
            (8, CHUNK),
            (8, CHUNK),
            (PAIRS, 4 + BASIS, TA, CHUNK),
            (factors, BF16),
            (factors, BF16),
            ((PAIRS, WIDE, channels), BF16),
            ((PAIRS, WIDE, channels), BF16),
        ],
        turning
        + [((PAIRS, *table), BF16)] * 2
        + [((PAIRS * COMPS * TA, channels), F32), ((PAIRS, *table), F32)],
        flags, atoms, own_feat, weights, mh, ml, from_second, from_first,
        flops=1 << 31,
    )
    arriving = [exchanged(leaving[i], i // 2, i % 2 == 0) for i in (1, 3, 0, 2)]

    table_shape, lh, ll, token = call(
        table_kernel,
        "table",
        [
            (PAIRS, 4 + 2 * BASIS, TA, CHUNK),
            ((PAIRS, BASIS * TA, WIDE), BF16),
            ((PAIRS, BASIS * TA, WIDE), BF16),
            (8, CHUNK),
        ],
        turning,
        flags, rows,
        flops=1 << 30,
    )

    rows_mix = 3 * channels
    total_count = 3.0 * atoms_here * lax.axis_size("domain") * lax.axis_size("batch")
    forces, keep, give, small, envdot, curl, both = call(
        functools.partial(tangent_kernel, 2.0 / math.sqrt(total_count)),
        "tangent",
        [
            line,
            (rows_mix, HALF),
            (rows_mix, HALF),
            (8, channels),
            (PAIRS * COMPS * TA, channels),
            (slots, channels),
            (16, CHUNK),
        ],
        turning
        + [((PAIRS, *table), BF16)] * 2
        + [((PAIRS * COMPS * TA, channels), F32)]
        + [((2 * slots, 3 * channels), F32), ((2 * slots, channels), F32)],
        flags, atoms, weights, mh, ml, from_first, from_second, own, *arriving,
        rows, env, gate, curve, inv, shape_store, xh, xl, token,
        flops=1 << 31,
    )

    def radial(p, after):
        return call(
            functools.partial(radial_kernel, p),
            "radial",
            [(BASIS, channels)],
            turning
            + [((BASIS * TA, CHUNK + WIDE), BF16)] * 2
            + [((2 * WIDE, channels), BF16)] * 2
            + [((BASIS * TA, channels), F32)],
            both, table_shape, lh, ll, eh, el, fsel, env, envdot, dinv, curl, mh, ml, after,
            flops=1 << 31 if p == 0 else 0,
        )[0]

    radials = [radial(0, both)]
    piece = rows_mix // (2 * FOUR)
    few = SMALL // FOUR
    near, far, give_near, give_far = call(
        halve_kernel, "halve", [(2 * piece, HALF)] * 3 + [(2 * piece + PAD, HALF)], [],
        keep, shifted(give, "batch", 1), radials[0],
    )
    radials.append(radial(1, far))
    blocks = []
    after = radials[1]
    taken_near = partner(give_near, 1)
    taken_far = partner(give_far, 1)
    for first, kept, taken in ((3, far, taken_far), (1, near, taken_near)):
        blocks += call(
            functools.partial(spread_kernel, first),
            "spread", [(piece + few + PAD * k, HALF) for k in (first - 1, max(first - 2, 0))], [((SMALL, HALF), F32)],
            kept, taken, *radials, small, after,
        )
        after = blocks[0]
    terms = [blocks[3]] + [partner(blocks[3 - k], 2 * k) for k in range(FOUR - 1, 0, -1)]
    (mine,) = call(total_kernel, "total", [(piece + few, HALF)], [], *terms)
    bit = 2 * FOUR
    while bit < lax.axis_size("domain"):
        (mine,) = call(total_kernel, "total", [(piece + few, HALF)], [], mine, partner(mine, bit))
        bit *= 2
    parts = [mine] + [partner(mine, 2 * k) for k in range(1, FOUR)]
    (near,) = call(near_kernel, "near", [(2 * piece + SMALL + PAD, HALF)], [], mine, parts[3])
    their_near = partner(near, 1)
    (rest,) = call(rest_kernel, "rest", [(2 * piece + SMALL, HALF)], [], *parts, near)
    their_rest = partner(rest, 1)
    (whole,) = call(
        pair_kernel, "pair", [(rows_mix + SMALL, HALF)], [], near, rest, their_near, their_rest
    )
    facing = shifted(whole, "batch", 1)
    mix, radial_sum, kinds, out = call(
        join_kernel,
        "join",
        [(rows_mix, channels), (BASIS, channels), (SPECIES, channels), (1, channels)],
        [],
        whole,
        facing,
    )
    return forces.transpose(1, 0, 2), radial_sum, mix, kinds, out.reshape(channels)


def solution(mesh):
    return jax.shard_map(
        on_device,
        mesh=mesh,
        in_specs=(
            P(("parts", "batch"), None, "domain"),
            P(("parts", "batch"), "domain", None),
            P(("parts", "batch"), "domain"),
            P(("parts", "batch"), None, "domain"),
            P(("parts", "batch"), "domain"),
            P(("parts", "batch"), "domain"),
            P(("parts", "batch"), "domain"),
            P(("parts", "batch"), "domain"),
            P(),
            P(),
            P(),
            P(),
        ),
        out_specs=(
            P(("parts", "batch"), None, "domain"),
            P("parts", None),
            P("parts", None),
            P("parts", None),
            P("parts"),
        ),
        check_vma=False,
    )
```

```python
import functools
import math

import jax
import jax.numpy as jnp
from jax import lax
from jax.experimental import pallas as pl
from jax.experimental.pallas import tpu as pltpu
from jax.sharding import PartitionSpec as P

TA = 64
SEND = 2
PAIRS = 2
COMPS = 9
WIDE = 10 * TA
BASIS = 8
SPECIES = 4
HALF = 128
CHUNK = 2 * TA

cutoff = 2.5
soften = 0.25
env_scale = 0.25
root_three = math.sqrt(3.0)
F32 = jnp.float32
BF16 = jnp.bfloat16
NN = (((1,), (0,)), ((), ()))
NT = (((1,), (1,)), ((), ()))
TN = (((0,), (0,)), ((), ()))
GROUP = (0, 1, 1, 1, 2, 2, 2, 2, 2)


def split(value):
    high = value.astype(BF16)
    return high, (value - high.astype(F32)).astype(BF16)


def product(left, right, dims):
    (lh, ll), (rh, rl) = left, right

    def one(x, y):
        return lax.dot_general(x, y, dims, preferred_element_type=F32)

    return one(lh, rh) + (one(lh, rl) + one(ll, rh))


def long_product(left, right, dims):
    return lax.dot_general(left, right, dims, preferred_element_type=F32)


def put_left(ref, p, rows, lane, width, value):
    hi, lo = split(value)
    span = ref.shape[2] // 3
    for third, part in enumerate((hi, lo, hi)):
        at = third * span + lane
        ref[p, rows, at : at + width] = part


def flag(condition):
    return jnp.where(condition, 1.0, 0.0).astype(F32)


def place(shift, width):
    return lax.bitwise_and(lax.shift_right_logical(lax.axis_index("domain"), shift), width - 1)


def lane_half():
    lane = lax.broadcasted_iota(jnp.int32, (1, CHUNK), 1)
    low = flag(lane < TA)
    return low, 1.0 - low


def twice(chunk, half):
    low, high = lane_half()
    swapped = pltpu.roll(chunk, TA, 1)
    return chunk * low + swapped * high if half == 0 else swapped * low + chunk * high


def pick(chunks, position):
    total = None
    for q, chunk in enumerate(chunks):
        for half in range(2):
            term = twice(chunk, half) * flag(position == 2 * q + half)
            total = term if total is None else total + term
    return total


def paired(first, second):
    low, high = lane_half()
    return first * low + second * high


def chunk_mask(position, q):
    low, high = lane_half()
    return low * flag(position == 2 * q) + high * flag(position == 2 * q + 1)


def geometry(lane_rows, columns, sign, live, same):
    offset = [(row - column) * sign for row, column in zip(lane_rows, columns)]
    dist_sq = offset[0] * offset[0] + offset[1] * offset[1] + offset[2] * offset[2] + soften
    distance = jnp.sqrt(dist_sq)
    inverse = 1.0 / distance
    unit = [x * inverse for x in offset]
    row = lax.broadcasted_iota(jnp.int32, (TA, CHUNK), 0)
    lane = lax.broadcasted_iota(jnp.int32, (TA, CHUNK), 1)
    lane = jnp.where(lane >= TA, lane - TA, lane)
    mask = live * (1.0 - same * flag(row == lane))
    base = jnp.maximum(1.0 - dist_sq * (1.0 / (cutoff * cutoff)), 0.0)
    weight = base * base * base * mask * inverse
    slope = -(6.0 / (cutoff * cutoff)) * base * base * mask - weight * inverse
    angle = distance * (math.pi / cutoff)
    return unit, inverse, weight, slope, jnp.sin(angle), jnp.cos(angle)


def harmonics(v):
    x, y, z = v
    return [
        None,
        x,
        y,
        z,
        root_three * x * y,
        root_three * y * z,
        root_three * z * x,
        0.5 * root_three * (x * x - y * y),
        z * z - 0.5 * (x * x + y * y),
    ]


def harmonics_tangent(v, t):
    x, y, z = v
    a, b, c = t
    return [
        None,
        a,
        b,
        c,
        root_three * (a * y + x * b),
        root_three * (b * z + y * c),
        root_three * (c * x + z * a),
        root_three * (x * a - y * b),
        2.0 * z * c - (x * a + y * b),
    ]


def paired_orders(sine, cosine, weight, slope):
    low, high = lane_half()
    double_s, double_c = 2.0 * sine * cosine, 1.0 - 2.0 * sine * sine
    now_s = sine * low + double_s * high
    now_c = cosine * low + double_c * high
    old_s = -sine * low
    old_c = cosine * low + high
    values, slopes = [], []
    for k in range(BASIS // 2):
        order = ((2 * k + 1) * low + (2 * k + 2) * high) * (math.pi / cutoff)
        values.append(now_s * weight)
        slopes.append(now_c * (weight * order) + now_s * slope)
        now_s, old_s = 2.0 * double_c * now_s - old_s, now_s
        now_c, old_c = 2.0 * double_c * now_c - old_c, now_c
    return values, slopes


def single_orders(sine, cosine, weight, slope):
    now_s, now_c = sine, cosine
    old_s, old_c = jnp.zeros_like(sine), jnp.ones_like(cosine)
    values, slopes = [], []
    for n in range(1, BASIS + 1):
        values.append(now_s * weight)
        slopes.append(now_c * (weight * (n * math.pi / cutoff)) + now_s * slope)
        now_s, old_s = 2.0 * cosine * now_s - old_s, now_s
        now_c, old_c = 2.0 * cosine * now_c - old_c, now_c
    return values, slopes


def columns_of(rows, square, turned):
    square[...] = jnp.zeros_like(square)
    square[0 : rows.shape[0], :] = rows
    turned[...] = square[...].T


def pair_rows(first, p):
    return twice(first, p)


def radial_feat(feat, radial, p, tall, wide):
    own = feat[p * TA : (p + 1) * TA, :]
    span, channels = BASIS * TA, feat.shape[1]
    for n in range(BASIS):
        hi, lo = split(own * radial[n : n + 1, :])
        for third, part in enumerate((hi, hi, lo)):
            tall[p, third * span + n * TA : third * span + (n + 1) * TA, :] = part
            wide[p, n * TA : (n + 1) * TA, third * channels : (third + 1) * channels] = part


OTHER, CENTRE, LIVE, SAME, SHARED, SENT = 0, 2, 4, 6, 8, 9
GHOST_ROWS = 8


def fetch(pairs, sems):
    copies = [pltpu.make_async_copy(src, dst, sems.at[i]) for i, (src, dst) in enumerate(pairs)]
    for copy in copies:
        copy.start()
    return copies


def upward(shift):
    return 1.0 - flag(place(shift, 2) == 1)


def either(choice, first, second):
    return first * choice + second * (1.0 - choice)


def gather_kernel(send, pos, feat, ref, to_second, to_first, token, send_v, pos_v, feat_v, ref_v, sems):
    copies = fetch([(send, send_v), (pos, pos_v), (ref, ref_v), (feat, feat_v)], sems)
    for copy in copies[:3]:
        copy.wait()
    low, high = lane_half()
    up = upward(0)
    sent = [send_v[0:1, j : j + 1].astype(F32) for j in range(2 * SEND)]
    tiles_of = []
    for out, choice in ((to_first, 1.0 - up), (to_second, up)):
        tiles = [either(choice, sent[j], sent[SEND + j]) for j in range(SEND)]
        tiles_of.append(tiles)
        out[SEND * TA :, :] = jnp.zeros((GHOST_ROWS, out.shape[1]), F32)
        for i in range(3):
            at = SEND * TA + i
            for lanes, source in ((slice(0, CHUNK), pos_v), (slice(CHUNK, 2 * CHUNK), ref_v)):
                chunks = [source[i, :, q * CHUNK : (q + 1) * CHUNK] for q in range(2)]
                out[at : at + 1, lanes] = paired(pick(chunks, tiles[0]), pick(chunks, tiles[1]))
        for other in range(2 * SEND):
            same = low * flag(sent[other] == tiles[0]) + high * flag(sent[other] == tiles[1])
            out[SEND * TA + 3 + other : SEND * TA + 4 + other, 0:CHUNK] = same
    token[...] = jnp.zeros_like(token)
    copies[3].wait()
    for out, tiles in zip((to_first, to_second), tiles_of):
        for j in range(SEND):
            out[j * TA : (j + 1) * TA, :] = pick_rows(feat_v.at[0], tiles[j], 0.0)


def pick_rows(ref, position, first):
    total = None
    for t in range(ref.shape[0] // TA):
        term = ref[t * TA : (t + 1) * TA, :] * flag(position == first + float(t))
        total = term if total is None else total + term
    return total


def stage_kernel(
    centre, other, live, send, pos, ref, species, feat, radial_w, mix_w, species_w, out_w, after,
    flags, atoms, own_feat, weights, mh, ml,
    centre_v, other_v, live_v, send_v, pos_v, ref_v, species_v, radial_v, mix_v, species_w_v, out_v, sems,
):
    copies = fetch(
        [
            (centre, centre_v), (other, other_v), (live, live_v), (send, send_v), (pos, pos_v), (ref, ref_v),
            (species, species_v), (radial_w, radial_v), (species_w, species_w_v), (out_w, out_v),
            (feat.at[0], own_feat), (mix_w, mix_v),
        ],
        sems,
    )
    for copy in copies[:-1]:
        copy.wait()
    flags[...] = jnp.zeros_like(flags)
    centres = [centre_v[0:1, p : p + 1].astype(F32) for p in range(PAIRS)]
    others = [other_v[0:1, p : p + 1].astype(F32) for p in range(PAIRS)]
    for p in range(PAIRS):
        for row, value in (
            (OTHER, others[p]),
            (CENTRE, centres[p]),
            (LIVE, live_v[0:1, p : p + 1].astype(F32)),
            (SAME, flag(others[p] == centres[p] + SEND)),
        ):
            flags[row + p : row + p + 1, :] = jnp.broadcast_to(value, (1, CHUNK))
    flags[SHARED : SHARED + 1, :] = jnp.broadcast_to(flag(centres[0] == centres[1]), (1, CHUNK))
    for j in range(2 * SEND):
        value = send_v[0:1, j : j + 1].astype(F32)
        flags[SENT + j : SENT + j + 1, :] = jnp.broadcast_to(value, (1, CHUNK))
    atoms[...] = jnp.zeros_like(atoms)
    for i in range(3):
        atoms[i : i + 1, :] = pos_v[i]
        atoms[4 + i : 5 + i, :] = ref_v[i]
    atoms[3:4, :] = species_v[...].astype(F32)
    weights[...] = jnp.zeros_like(weights)
    weights[0:BASIS, :] = radial_v[...]
    weights[BASIS : BASIS + SPECIES, :] = species_w_v[...]
    weights[BASIS + SPECIES : BASIS + SPECIES + 1, :] = out_v[...]
    copies[-1].wait()
    hi, lo = split(mix_v[...])
    mh[...] = hi
    ml[...] = lo


def force_kernel(
    flags, atoms, feat, weights, mh, ml, from_second, from_first,
    env, dinv, gate, curve, inv, rows, fsel, own, one_first, one_second, two_first, two_second, shape_store, tall, eh, el,
    square, turned, table, wide, steady, raw, back,
):
    ghost = SEND * TA
    up = upward(0)
    near, far = from_first[ghost : ghost + 3, 0:CHUNK], from_second[ghost : ghost + 3, 0:CHUNK]
    chunks = [either(up, far, near), atoms[0:3, 0:CHUNK], atoms[0:3, CHUNK:], either(up, near, far)]
    kinds = [atoms[3:4, q * CHUNK : (q + 1) * CHUNK] for q in range(2)]

    def number(row):
        return flags[row : row + 1, :]

    centres = [number(CENTRE + p) for p in range(PAIRS)]
    others = [number(OTHER + p) for p in range(PAIRS)]
    shared = flags[SHARED : SHARED + 1, 0:1]
    rows[...] = jnp.zeros_like(rows)
    rows[0:3, :] = paired(*(pick(chunks, others[p]) for p in range(PAIRS)))
    rows[3:6, :] = paired(*(pick(chunks[1:3], centres[p]) for p in range(PAIRS)))
    rows[6:7, :] = paired(*(pick(kinds, centres[p]) for p in range(PAIRS)))
    columns_of(rows[...], square, turned)

    for p in range(PAIRS):
        o = flags[OTHER + p : OTHER + p + 1, 0:1]
        fsel[p * TA : (p + 1) * TA, :] = (
            pick_rows(from_first.at[0:ghost], o, (SEND + 4) * up)
            + pick_rows(feat, o, float(SEND))
            + pick_rows(from_second.at[0:ghost], o, (SEND + 4) * (1.0 - up))
        )

    shapes = []
    for p in range(PAIRS):
        lane_rows = [twice(rows[i : i + 1, :], p) for i in range(3)]
        columns = [turned[p * TA : (p + 1) * TA, 3 + i : 4 + i] for i in range(3)]
        unit, inverse, weight, slope, sine, cosine = geometry(
            lane_rows, columns, 1.0, number(LIVE + p), number(SAME + p)
        )
        angular = harmonics(unit)
        values, slopes = paired_orders(sine, cosine, weight, slope)
        shapes.append((unit, inverse, angular, values, slopes))
        for i, part in enumerate(unit + [inverse] + values + slopes):
            shape_store[p, i] = part
        for m in range(COMPS):
            for k in range(BASIS // 2):
                entry = values[k] if m == 0 else angular[m] * values[k]
                put_left(table, p, slice(m * TA, (m + 1) * TA), k * CHUNK, CHUNK, entry)
        radial_feat(fsel, weights, p, tall, wide)
        raw[p * COMPS * TA : (p + 1) * COMPS * TA, :] = long_product(table[p], tall[p], NN)

    for m in range(COMPS):
        first = raw[m * TA : (m + 1) * TA, :]
        second = raw[(COMPS + m) * TA : (COMPS + m + 1) * TA, :]
        env[m * TA : (m + 1) * TA, :] = env_scale * (first + shared * second)
        env[(COMPS + m) * TA : (COMPS + m + 1) * TA, :] = env_scale * (second + shared * first)
    for p in range(PAIRS):
        sums = [None] * 3
        for m in range(COMPS):
            block = env[(p * COMPS + m) * TA : (p * COMPS + m + 1) * TA, :]
            sums[GROUP[m]] = block * block if sums[GROUP[m]] is None else sums[GROUP[m]] + block * block
        for g in range(3):
            inv[p * TA : (p + 1) * TA, g * 256 : (g + 1) * 256] = sums[g]
    hidden = product(split(inv[...]), (mh[...], ml[...]), NN)
    kind = turned[:, 6:7]
    for s in range(SPECIES):
        hidden = hidden + flag(kind == float(s)) * weights[BASIS + s : BASIS + s + 1, :]
    out_row = weights[BASIS + SPECIES : BASIS + SPECIES + 1, :]
    sigma = 1.0 / (1.0 + jnp.exp(-hidden))
    first_order = sigma * (1.0 + hidden * (1.0 - sigma))
    gate[...] = first_order
    curve[...] = sigma * (1.0 - sigma) * (2.0 + hidden * (1.0 - 2.0 * sigma)) * out_row
    dinv[...] = product(split(first_order * out_row), (mh[...], ml[...]), NT)

    tile_grads = [jnp.zeros((3, CHUNK), F32) for _ in range(4)]
    for p in range(PAIRS):
        unit, inverse, angular, values, slopes = shapes[p]
        for m in range(COMPS):
            block = env[(p * COMPS + m) * TA : (p * COMPS + m + 1) * TA, :]
            part = dinv[p * TA : (p + 1) * TA, GROUP[m] * 256 : (GROUP[m] + 1) * 256]
            at = slice(m * TA, (m + 1) * TA)
            hi, lo = split((2.0 * env_scale) * block * part)
            eh[p, at, :] = hi
            el[p, at, :] = lo
            for third, piece in enumerate((hi, lo, hi)):
                steady[p, at, third * 256 : (third + 1) * 256] = piece
        for ref in (eh, el):
            ref[p, COMPS * TA :, :] = jnp.zeros((WIDE - COMPS * TA, ref.shape[2]), BF16)
        back[p] = long_product(steady[p], wide[p], NT)
        d_radius = None
        d_angular = []
        for m in range(COMPS):
            along, across = None, None
            for k in range(BASIS // 2):
                block = back[p, m * TA : (m + 1) * TA, k * CHUNK : (k + 1) * CHUNK]
                along = block * slopes[k] if along is None else along + block * slopes[k]
                across = block * values[k] if across is None else across + block * values[k]
            d_angular.append(across)
            term = along if m == 0 else along * angular[m]
            d_radius = term if d_radius is None else d_radius + term
        x, y, z = unit
        g = d_angular
        toward = [
            g[1] + root_three * (y * g[4] + z * g[6] + x * g[7]) - x * g[8],
            g[2] + root_three * (x * g[4] + z * g[5] - y * g[7]) - y * g[8],
            g[3] + root_three * (y * g[5] + x * g[6]) + 2.0 * (z * g[8]),
        ]
        radial_part = d_radius - inverse * (toward[0] * x + toward[1] * y + toward[2] * z)
        for i in range(3):
            d_offset = inverse * toward[i] + unit[i] * radial_part
            summed = jnp.sum(d_offset, axis=0, keepdims=True)
            other_row = summed + pltpu.roll(summed, TA, 1)
            square[0:TA, :] = d_offset
            square[TA:, :] = d_offset
            centre_row = -jnp.sum(square[...].T, axis=0, keepdims=True)
            component = flag(lax.broadcasted_iota(jnp.int32, (3, CHUNK), 0) == i)
            for q in range(4):
                at = chunk_mask(others[p], q) * other_row
                if q in (1, 2):
                    at = at + chunk_mask(centres[p] + SEND, q) * centre_row
                tile_grads[q] = tile_grads[q] + at * component
    own[...] = jnp.zeros_like(own)
    own[0:3, 0:CHUNK] = tile_grads[1]
    own[0:3, CHUNK:] = tile_grads[2]
    own[3:6, 0:CHUNK] = tile_grads[0]
    own[3:6, CHUNK:] = tile_grads[3]
    leaving = []
    for first, ghost_grad in ((0, tile_grads[0]), (SEND, tile_grads[3])):
        listed = paired(*(pick(tile_grads[1:3], number(SENT + first + j)) for j in range(SEND)))
        leaving.append((listed, ghost_grad))
    for shift, outs in ((0, (one_first, one_second)), (1, (two_first, two_second))):
        choice = upward(shift)
        for out, above in zip(outs, (choice, 1.0 - choice)):
            out[...] = jnp.zeros_like(out)
            out[0:3, :] = either(above, leaving[1][0], leaving[0][0])
            out[3:6, :] = either(above, leaving[1][1], leaving[0][1])


def tangent_kernel(
    scale, flags, atoms, weights, mh, ml, from_first, from_second, own, one_second, two_second, one_first, two_first,
    rows, env, gate, curve, inv, shape_store, tall, after,
    forces, keep, give, small, envdot, curl, both,
    square, turned, table, raw, left, right,
):
    ghost = SEND * TA
    def number(row):
        return flags[row : row + 1, :]

    centres = [number(CENTRE + p) for p in range(PAIRS)]
    others = [number(OTHER + p) for p in range(PAIRS)]
    shared = flags[SHARED : SHARED + 1, 0:1]
    mine = [own[0:3, 0:CHUNK], own[0:3, CHUNK:]]
    up, up_two = upward(0), upward(1)
    low_one = either(up, one_second[...], one_first[...])
    high_one = either(up, one_first[...], one_second[...])
    low_two = either(up_two, two_second[...], two_first[...])
    high_two = either(up_two, two_first[...], two_second[...])
    low_tail = either(up, from_second[ghost:, :], from_first[ghost:, :])
    high_tail = either(up, from_first[ghost:, :], from_second[ghost:, :])
    arrived = [twice(low_one[3:6, :], j) for j in range(SEND)]
    arrived += [twice(high_one[3:6, :], j) for j in range(SEND)]
    for j in range(2 * SEND):
        for q in range(2):
            mine[q] = mine[q] + chunk_mask(number(SENT + j), q) * arrived[j]
    below = low_one[0:3, :]
    above = high_one[0:3, :]
    to_below = [twice(low_two[3:6, :], j) for j in range(SEND)]
    to_below += [twice(own[3:6, 0:CHUNK], j) for j in range(SEND)]
    to_above = [twice(own[3:6, CHUNK:], j) for j in range(SEND)]
    to_above += [twice(high_two[3:6, :], j) for j in range(SEND)]
    for j in range(2 * SEND):
        below = below + low_tail[3 + j : 4 + j, 0:CHUNK] * to_below[j]
        above = above + high_tail[3 + j : 4 + j, 0:CHUNK] * to_above[j]
    for q in range(2):
        for i in range(3):
            forces[i, :, q * CHUNK : (q + 1) * CHUNK] = -mine[q][i : i + 1, :]
    error = [
        below + low_tail[0:3, CHUNK:],
        mine[0] + atoms[4:7, 0:CHUNK],
        mine[1] + atoms[4:7, CHUNK:],
        above + high_tail[0:3, CHUNK:],
    ]
    error = [part * scale for part in error]
    both[...] = jnp.zeros_like(both)
    both[0:8, :] = rows[...]
    both[8:11, :] = paired(*(pick(error, others[p]) for p in range(PAIRS)))
    both[11:14, :] = paired(*(pick(error[1:3], centres[p]) for p in range(PAIRS)))
    columns_of(both[...], square, turned)

    for p in range(PAIRS):
        lane_move = [twice(both[8 + i : 9 + i, :], p) for i in range(3)]
        column_move = [turned[p * TA : (p + 1) * TA, 11 + i : 12 + i] for i in range(3)]
        unit = [shape_store[p, i] for i in range(3)]
        inverse = shape_store[p, 3]
        values = [shape_store[p, 4 + k] for k in range(BASIS // 2)]
        slopes = [shape_store[p, 8 + k] for k in range(BASIS // 2)]
        move = [a - b for a, b in zip(lane_move, column_move)]
        stretch = unit[0] * move[0] + unit[1] * move[1] + unit[2] * move[2]
        turn = [(m - v * stretch) * inverse for m, v in zip(move, unit)]
        angular, turning = harmonics(unit), harmonics_tangent(unit, turn)
        slopes = [s * stretch for s in slopes]
        for m in range(COMPS):
            for k in range(BASIS // 2):
                entry = slopes[k] if m == 0 else angular[m] * slopes[k] + turning[m] * values[k]
                put_left(table, p, slice(m * TA, (m + 1) * TA), k * CHUNK, CHUNK, entry)
        raw[p * COMPS * TA : (p + 1) * COMPS * TA, :] = long_product(table[p], tall[p], NN)

    for m in range(COMPS):
        first = raw[m * TA : (m + 1) * TA, :]
        second = raw[(COMPS + m) * TA : (COMPS + m + 1) * TA, :]
        envdot[m * TA : (m + 1) * TA, :] = env_scale * (first + shared * second)
        envdot[(COMPS + m) * TA : (COMPS + m + 1) * TA, :] = env_scale * (second + shared * first)
    invdot = left
    half = PAIRS * TA
    for p in range(PAIRS):
        sums = [None] * 3
        for m in range(COMPS):
            at = slice((p * COMPS + m) * TA, (p * COMPS + m + 1) * TA)
            term = 2.0 * env[at, :] * envdot[at, :]
            sums[GROUP[m]] = term if sums[GROUP[m]] is None else sums[GROUP[m]] + term
        for g in range(3):
            invdot[half + p * TA : half + (p + 1) * TA, g * 256 : (g + 1) * 256] = sums[g]
    invdot[0:half, :] = inv[...]
    hidden_move = product(split(invdot[half:, :]), (mh[...], ml[...]), NN)
    bend = curve[...] * hidden_move
    curl[...] = bend
    once = 1.0 - shared * flag(lax.broadcasted_iota(jnp.int32, (half, 1), 0) >= TA)
    right[0:half, :] = bend * once
    right[half:, :] = gate[...] * weights[BASIS + SPECIES : BASIS + SPECIES + 1, :] * once
    raw[0 : left.shape[1], :] = product(split(left[...]), split(right[...]), TN)
    core = lax.axis_index("batch")
    for out, part in ((keep, core), (give, 1 - core)):
        out[...] = raw[0 : left.shape[1], block_of_lanes(part)]
    small[...] = jnp.zeros_like(small)
    kind = turned[:, 6:7]
    for s in range(SPECIES):
        small[s : s + 1, :] = jnp.sum(right[0:half, :] * flag(kind == float(s)), axis=0, keepdims=True)
    small[SPECIES : SPECIES + 1, :] = jnp.sum(gate[...] * hidden_move * once, axis=0, keepdims=True)


def table_kernel(flags, rows, shape_store, lh, ll, token, square, turned):
    low, high = lane_half()
    token[...] = jnp.zeros_like(token)
    columns_of(rows[...], square, turned)
    for p in range(PAIRS):
        lane_rows = [twice(rows[3 + i : 4 + i, :], p) for i in range(3)]
        columns = [turned[p * TA : (p + 1) * TA, i : i + 1] for i in range(3)]
        unit, inverse, weight, slope, sine, cosine = geometry(
            lane_rows, columns, -1.0, flags[LIVE + p : LIVE + p + 1, :], flags[SAME + p : SAME + p + 1, :]
        )
        angular = harmonics(unit)
        values, slopes = single_orders(sine, cosine, weight, slope)
        for i, part in enumerate(unit + [inverse] + values + slopes):
            shape_store[p, i] = part
        for m in range(0, COMPS + 1, 2):
            factor = low if m == 0 else angular[m] * low
            if m + 1 < COMPS:
                factor = factor + angular[m + 1] * high
            for n in range(BASIS):
                hi, lo = split(factor * values[n])
                lh[p, n * TA : (n + 1) * TA, m * TA : (m + 2) * TA] = hi
                ll[p, n * TA : (n + 1) * TA, m * TA : (m + 2) * TA] = lo


def radial_kernel(
    p, both, shape_store, lh, ll, eh, el, fsel, env, envdot, dinv, curl, mh, ml, after,
    grad_radial,
    square, turned, sh, sl, gh, gl, raw,
):
    low, high = lane_half()
    columns_of(both[...], square, turned)
    here = slice(p * TA, (p + 1) * TA)
    turn_inv = product(split(curl[here, :]), (mh[...], ml[...]), NT)
    lane_move = [twice(both[11 + i : 12 + i, :], p) for i in range(3)]
    column_move = [turned[here, 8 + i : 9 + i] for i in range(3)]
    unit = [shape_store[p, i] for i in range(3)]
    inverse = shape_store[p, 3]
    move = [b - a for a, b in zip(lane_move, column_move)]
    stretch = unit[0] * move[0] + unit[1] * move[1] + unit[2] * move[2]
    turn = [(m - v * stretch) * inverse for m, v in zip(move, unit)]
    angular, turning = harmonics(unit), harmonics_tangent(unit, turn)
    sh[:, 0:CHUNK] = lh[p, :, WIDE - CHUNK :]
    sl[:, 0:CHUNK] = ll[p, :, WIDE - CHUNK :]
    for m in range(0, COMPS + 1, 2):
        if m == 0:
            on_value, on_slope = turning[1] * high, low + angular[1] * high
        else:
            on_value, on_slope = turning[m] * low, angular[m] * low
            if m + 1 < COMPS:
                on_value = on_value + turning[m + 1] * high
                on_slope = on_slope + angular[m + 1] * high
        on_slope = on_slope * stretch
        lanes = slice(CHUNK + m * TA, CHUNK + (m + 2) * TA)
        for n in range(BASIS):
            hi, lo = split(on_value * shape_store[p, 4 + n] + on_slope * shape_store[p, 4 + BASIS + n])
            sh[n * TA : (n + 1) * TA, lanes] = hi
            sl[n * TA : (n + 1) * TA, lanes] = lo
    for m in range(COMPS):
        at = slice((p * COMPS + m) * TA, (p * COMPS + m + 1) * TA)
        group = slice(GROUP[m] * 256, (GROUP[m] + 1) * 256)
        steady = (2.0 * env_scale) * dinv[here, group]
        bent = (2.0 * env_scale) * turn_inv[:, group]
        hi, lo = split(env[at, :] * bent + envdot[at, :] * steady)
        gh[m * TA : (m + 1) * TA, :] = hi
        gl[m * TA : (m + 1) * TA, :] = lo
    for ref, tail in ((gh, eh), (gl, el)):
        ref[COMPS * TA : WIDE, :] = jnp.zeros((WIDE - COMPS * TA, ref.shape[1]), BF16)
        ref[WIDE:, :] = tail[p]
    first = WIDE - CHUNK
    raw[...] = product((lh[p, :, 0:first], ll[p, :, 0:first]), (gh[0:first, :], gl[0:first, :]), NN) + product(
        (sh[...], sl[...]), (gh[first:, :], gl[first:, :]), NN
    )
    for n in range(BASIS):
        grad_radial[n : n + 1, :] = jnp.sum(
            raw[n * TA : (n + 1) * TA, :] * fsel[here, :], axis=0, keepdims=True
        )


SMALL = 32
PAD = 8
FOUR = 4


def block_of(part, rows):
    return pl.ds(pl.multiple_of(part * rows, 8), rows)


def block_from(start, rows):
    return pl.ds(pl.multiple_of(start, 8), rows)


def block_of_lanes(part):
    return pl.ds(pl.multiple_of(part * HALF, HALF), HALF)


def total_of(refs, at):
    total = refs[0][at, :]
    for ref in refs[1:]:
        total = total + ref[at, :]
    return total


def halve_kernel(keep, taken, after, *outs):
    half, piece = keep.shape[0] // 2, keep.shape[0] // (2 * FOUR)
    mine, me = place(0, 2), place(1, FOUR)
    for i, out in enumerate(outs):
        part = mine if i < 2 else 1 - mine
        for j in range(2):
            k = 1 + 2 * (i % 2) - j
            at = block_from(part * half + lax.bitwise_xor(me, k) * piece, piece)
            out[j * piece : (j + 1) * piece, :] = keep[at, :] + taken[at, :]
        if out.shape[0] > 2 * piece:
            out[2 * piece :, :] = jnp.zeros((out.shape[0] - 2 * piece, HALF), F32)


def spread_kernel(first, keep, taken, radial_0, radial_1, small, after, out_0, out_1, tiny):
    for h in range(2):
        lanes = slice(h * HALF, (h + 1) * HALF)
        tiny[16 * h : 16 * h + 8, :] = radial_0[:, lanes] + radial_1[:, lanes]
        tiny[16 * h + 8 : 16 * h + 16, :] = small[:, lanes]
    me = place(1, FOUR)
    few = SMALL // FOUR
    rows = keep.shape[0] // 2
    for j, out in enumerate((out_0, out_1)):
        out[0:rows, :] = total_of([keep, taken], slice(j * rows, (j + 1) * rows))
        out[rows : rows + few, :] = tiny[block_of(lax.bitwise_xor(me, first - j), few), :]
        if out.shape[0] > rows + few:
            out[rows + few :, :] = jnp.zeros((out.shape[0] - rows - few, HALF), F32)


def total_kernel(*refs):
    refs[-1][...] = total_of(refs[:-1], slice(0, refs[-1].shape[0]))


def near_kernel(mine, third, out):
    rows = mine.shape[0] - SMALL // FOUR
    out[0:rows, :] = mine[0:rows, :]
    out[rows : 2 * rows, :] = third[0:rows, :]
    out[2 * rows :, :] = jnp.zeros((out.shape[0] - 2 * rows, HALF), F32)


def rest_kernel(mine, first, second, third, after, out):
    few = SMALL // FOUR
    rows = mine.shape[0] - few
    out[0:rows, :] = second[0:rows, :]
    out[rows : 2 * rows, :] = first[0:rows, :]
    me = place(1, FOUR)
    for k, ref in enumerate((mine, first, second, third)):
        out[block_from(2 * rows + lax.bitwise_xor(me, k) * few, few), :] = ref[rows:, :]


def pair_kernel(near, rest, their_near, their_rest, out):
    piece = (rest.shape[0] - SMALL) // 2
    half = FOUR * piece
    mine, me = place(0, 2), place(1, FOUR)
    for refs, part in (((near, rest), mine), ((their_near, their_rest), 1 - mine)):
        for ref, ks in zip(refs, ((0, 3), (2, 1))):
            for j, k in enumerate(ks):
                at = block_from(part * half + lax.bitwise_xor(me, k) * piece, piece)
                out[at, :] = ref[j * piece : (j + 1) * piece, :]
    out[2 * half :, :] = rest[2 * piece :, :] + their_rest[2 * piece :, :]


def join_kernel(whole, facing, mix, radial, kinds, out, sems):
    rows = mix.shape[0]
    core = lax.axis_index("batch")
    copies = fetch(
        [
            (ref.at[0:rows, :], mix.at[:, block_of_lanes(part)])
            for ref, part in ((whole, core), (facing, 1 - core))
        ],
        sems,
    )
    both = whole[rows:, :] + facing[rows:, :]
    for h in range(2):
        lanes = slice(h * HALF, (h + 1) * HALF)
        few = both[16 * h : 16 * h + 16, :]
        radial[:, lanes] = few[0:BASIS]
        kinds[:, lanes] = few[BASIS : BASIS + SPECIES]
        out[:, lanes] = few[BASIS + SPECIES : BASIS + SPECIES + 1]
    for copy in copies:
        copy.wait()


def spec(space):
    return pl.BlockSpec(memory_space=space)


def call(kernel, name, outs, scratch, *operands, space=pltpu.VMEM, after=(), flops=0, loose=0):
    if space is pltpu.HBM:
        operands = [pltpu.with_memory_space_constraint(operand, space) for operand in operands]
    outs = [out if len(out) == 2 and isinstance(out[0], tuple) else (out, F32) for out in outs]
    return pl.pallas_call(
        kernel,
        name=name,
        out_shape=[jax.ShapeDtypeStruct(*out) for out in outs],
        in_specs=[spec(space)] * len(operands) + [spec(pltpu.VMEM)] * len(after),
        out_specs=[spec(pl.ANY)] * loose + [spec(pltpu.VMEM)] * (len(outs) - loose),
        scratch_shapes=[pltpu.VMEM(*item) if isinstance(item, tuple) else item for item in scratch],
        compiler_params=pltpu.CompilerParams(vmem_limit_bytes=28 * 1024 * 1024),
        cost_estimate=pl.CostEstimate(flops=flops, bytes_accessed=1 << 20 if flops else 1 << 10, transcendentals=0),
    )(*operands, *after)


def shifted(block, axis, by):
    count = lax.axis_size(axis)
    return lax.ppermute(block, axis, [(i, (i + by) % count) for i in range(count)])


def exchanged(block, shift, first):
    count, step = lax.axis_size("domain"), 1 << shift
    up = [((i >> shift) & 1 == 0) == first for i in range(count)]
    return lax.ppermute(block, "domain", [(i, (i + step if up[i] else i - step) % count) for i in range(count)])


def partner(block, mask):
    return lax.ppermute(block, "domain", [(i, i ^ mask) for i in range(lax.axis_size("domain"))])


def on_device(
    positions,
    features,
    species,
    ref_forces,
    centre_tile,
    other_tile,
    pair_live,
    send_tiles,
    radial_w,
    mix_w,
    species_w,
    out_w,
):
    atoms_here = positions.shape[2]
    channels = features.shape[2]
    table = (COMPS * TA, BASIS * TA)
    sent = (SEND * TA + GHOST_ROWS, channels)
    slots = PAIRS * TA
    line = (3, 1, atoms_here)
    turning = [((CHUNK, CHUNK), F32)] * 2
    out_row = out_w.reshape(1, channels)
    positions = positions.transpose(1, 0, 2)
    ref_forces = ref_forces.transpose(1, 0, 2)
    ints = [((1, n), jnp.int32) for n in (PAIRS, PAIRS, PAIRS, 2 * SEND)]

    to_second, to_first, token = call(
        gather_kernel,
        "gather",
        [sent, sent, (8, CHUNK)],
        [
            ints[3],
            (line, F32),
            ((1, atoms_here, channels), F32),
            (line, F32),
            pltpu.SemaphoreType.DMA((4,)),
        ],
        send_tiles, positions, features, ref_forces,
        space=pltpu.HBM,
    )
    from_second = exchanged(to_second, 0, False)
    from_first = exchanged(to_first, 0, True)
    flags, atoms, own_feat, weights, mh, ml = call(
        stage_kernel,
        "stage",
        [
            (16, CHUNK),
            (8, atoms_here),
            (atoms_here, channels),
            (16, channels),
            (mix_w.shape, BF16),
            (mix_w.shape, BF16),
        ],
        ints
        + [(line, F32), (line, F32), ((1, atoms_here), jnp.int32)]
        + [(radial_w.shape, F32), (mix_w.shape, F32), (species_w.shape, F32), (out_row.shape, F32)]
        + [pltpu.SemaphoreType.DMA((12,))],
        centre_tile, other_tile, pair_live, send_tiles, positions, ref_forces, species, features,
        radial_w, mix_w, species_w, out_row,
        space=pltpu.HBM,
        after=(token,),
    )

    long_table = (PAIRS, COMPS * TA, 3 * BASIS * TA)
    env, dinv, gate, curve, inv, rows, fsel, own, *leaving, shape_store, tall, eh, el = call(
        force_kernel,
        "force",
        [
            (PAIRS * COMPS * TA, channels),
            (slots, 3 * channels),
            (slots, channels),
            (slots, channels),
            (slots, 3 * channels),
            (8, CHUNK),
            (slots, channels),
            (8, atoms_here),
            (8, CHUNK),
            (8, CHUNK),
            (8, CHUNK),
            (8, CHUNK),
            (PAIRS, 4 + BASIS, TA, CHUNK),
            ((PAIRS, 3 * BASIS * TA, channels), BF16),
            ((PAIRS, WIDE, channels), BF16),
            ((PAIRS, WIDE, channels), BF16),
        ],
        turning
        + [(long_table, BF16), ((PAIRS, BASIS * TA, 3 * channels), BF16)]
        + [((PAIRS, COMPS * TA, 3 * channels), BF16)]
        + [((PAIRS * COMPS * TA, channels), F32), ((PAIRS, *table), F32)],
        flags, atoms, own_feat, weights, mh, ml, from_second, from_first,
        flops=1 << 31,
    )
    arriving = [exchanged(leaving[i], i // 2, i % 2 == 0) for i in (1, 3, 0, 2)]

    table_shape, lh, ll, token = call(
        table_kernel,
        "table",
        [
            (PAIRS, 4 + 2 * BASIS, TA, CHUNK),
            ((PAIRS, BASIS * TA, WIDE), BF16),
            ((PAIRS, BASIS * TA, WIDE), BF16),
            (8, CHUNK),
        ],
        turning,
        flags, rows,
        flops=1 << 30,
    )

    rows_mix = 3 * channels
    total_count = 3.0 * atoms_here * lax.axis_size("domain") * lax.axis_size("batch")
    forces, keep, give, small, envdot, curl, both = call(
        functools.partial(tangent_kernel, 2.0 / math.sqrt(total_count)),
        "tangent",
        [
            line,
            (rows_mix, HALF),
            (rows_mix, HALF),
            (8, channels),
            (PAIRS * COMPS * TA, channels),
            (slots, channels),
            (16, CHUNK),
        ],
        turning
        + [(long_table, BF16)]
        + [((PAIRS * COMPS * TA, channels), F32)]
        + [((2 * slots, 3 * channels), F32), ((2 * slots, channels), F32)],
        flags, atoms, weights, mh, ml, from_first, from_second, own, *arriving,
        rows, env, gate, curve, inv, shape_store, tall, token,
        flops=1 << 31,
    )

    def radial(p, after):
        return call(
            functools.partial(radial_kernel, p),
            "radial",
            [(BASIS, channels)],
            turning
            + [((BASIS * TA, CHUNK + WIDE), BF16)] * 2
            + [((2 * WIDE, channels), BF16)] * 2
            + [((BASIS * TA, channels), F32)],
            both, table_shape, lh, ll, eh, el, fsel, env, envdot, dinv, curl, mh, ml, after,
            flops=1 << 31 if p == 0 else 0,
        )[0]

    radials = [radial(0, both)]
    piece = rows_mix // (2 * FOUR)
    few = SMALL // FOUR
    near, far, give_near, give_far = call(
        halve_kernel, "halve", [(2 * piece, HALF)] * 3 + [(2 * piece + PAD, HALF)], [],
        keep, shifted(give, "batch", 1), radials[0],
    )
    radials.append(radial(1, far))
    blocks = []
    after = radials[1]
    taken_near = partner(give_near, 1)
    taken_far = partner(give_far, 1)
    for first, kept, taken in ((3, far, taken_far), (1, near, taken_near)):
        blocks += call(
            functools.partial(spread_kernel, first),
            "spread", [(piece + few + PAD * k, HALF) for k in (first - 1, max(first - 2, 0))], [((SMALL, HALF), F32)],
            kept, taken, *radials, small, after,
        )
        after = blocks[0]
    terms = [blocks[3]] + [partner(blocks[3 - k], 2 * k) for k in range(FOUR - 1, 0, -1)]
    (mine,) = call(total_kernel, "total", [(piece + few, HALF)], [], *terms)
    bit = 2 * FOUR
    while bit < lax.axis_size("domain"):
        (mine,) = call(total_kernel, "total", [(piece + few, HALF)], [], mine, partner(mine, bit))
        bit *= 2
    parts = [mine] + [partner(mine, 2 * k) for k in range(1, FOUR)]
    (near,) = call(near_kernel, "near", [(2 * piece + SMALL + PAD, HALF)], [], mine, parts[3])
    their_near = partner(near, 1)
    (rest,) = call(rest_kernel, "rest", [(2 * piece + SMALL, HALF)], [], *parts, near)
    their_rest = partner(rest, 1)
    (whole,) = call(
        pair_kernel, "pair", [(rows_mix + SMALL, HALF)], [], near, rest, their_near, their_rest
    )
    facing = shifted(whole, "batch", 1)
    mix, radial_sum, kinds, out = call(
        join_kernel,
        "join",
        [(rows_mix, channels), (BASIS, channels), (SPECIES, channels), (1, channels)],
        [pltpu.SemaphoreType.DMA((2,))],
        whole,
        facing,
        loose=1,
    )
    return forces.transpose(1, 0, 2), radial_sum, mix, kinds, out.reshape(channels)


def solution(mesh):
    return jax.shard_map(
        on_device,
        mesh=mesh,
        in_specs=(
            P(("parts", "batch"), None, "domain"),
            P(("parts", "batch"), "domain", None),
            P(("parts", "batch"), "domain"),
            P(("parts", "batch"), None, "domain"),
            P(("parts", "batch"), "domain"),
            P(("parts", "batch"), "domain"),
            P(("parts", "batch"), "domain"),
            P(("parts", "batch"), "domain"),
            P(),
            P(),
            P(),
            P(),
        ),
        out_specs=(
            P(("parts", "batch"), None, "domain"),
            P("parts", None),
            P("parts", None),
            P("parts", None),
            P("parts"),
        ),
        check_vma=False,
    )
```

```python
import functools
import math

import jax
import jax.numpy as jnp
from jax import lax
from jax.experimental import pallas as pl
from jax.experimental.pallas import tpu as pltpu
from jax.sharding import PartitionSpec as P

TA = 64
SEND = 2
PAIRS = 2
COMPS = 9
STRIP = 16
WIDE = 10 * TA
BASIS = 8
SPECIES = 4
HALF = 128
CHUNK = 2 * TA

cutoff = 2.5
soften = 0.25
env_scale = 0.25
root_three = math.sqrt(3.0)
F32 = jnp.float32
BF16 = jnp.bfloat16
NN = (((1,), (0,)), ((), ()))
NT = (((1,), (1,)), ((), ()))
TN = (((0,), (0,)), ((), ()))
GROUP = (0, 1, 1, 1, 2, 2, 2, 2, 2)


def split(value):
    high = value.astype(BF16)
    return high, (value - high.astype(F32)).astype(BF16)


def product(left, right, dims):
    (lh, ll), (rh, rl) = left, right

    def one(x, y):
        return lax.dot_general(x, y, dims, preferred_element_type=F32)

    return one(lh, rh) + (one(lh, rl) + one(ll, rh))


def long_product(left, right, dims):
    return lax.dot_general(left, right, dims, preferred_element_type=F32)


def put_left(ref, p, rows, lane, width, value):
    hi, lo = split(value)
    span = ref.shape[2] // 3
    for third, part in enumerate((hi, lo, hi)):
        at = third * span + lane
        ref[p, rows, at : at + width] = part


def flag(condition):
    return jnp.where(condition, 1.0, 0.0).astype(F32)


def place(shift, width):
    return lax.bitwise_and(lax.shift_right_logical(lax.axis_index("domain"), shift), width - 1)


def lane_half():
    lane = lax.broadcasted_iota(jnp.int32, (1, CHUNK), 1)
    low = flag(lane < TA)
    return low, 1.0 - low


def twice(chunk, half):
    low, high = lane_half()
    swapped = pltpu.roll(chunk, TA, 1)
    return chunk * low + swapped * high if half == 0 else swapped * low + chunk * high


def pick(chunks, position):
    total = None
    for q, chunk in enumerate(chunks):
        for half in range(2):
            term = twice(chunk, half) * flag(position == 2 * q + half)
            total = term if total is None else total + term
    return total


def paired(first, second):
    low, high = lane_half()
    return first * low + second * high


def chunk_mask(position, q):
    low, high = lane_half()
    return low * flag(position == 2 * q) + high * flag(position == 2 * q + 1)


def geometry(lane_rows, columns, sign, live, same, first):
    offset = [(row - column) * sign for row, column in zip(lane_rows, columns)]
    dist_sq = offset[0] * offset[0] + offset[1] * offset[1] + offset[2] * offset[2] + soften
    distance = jnp.sqrt(dist_sq)
    inverse = 1.0 / distance
    unit = [x * inverse for x in offset]
    row = lax.broadcasted_iota(jnp.int32, (STRIP, CHUNK), 0) + first
    lane = lax.broadcasted_iota(jnp.int32, (STRIP, CHUNK), 1)
    lane = jnp.where(lane >= TA, lane - TA, lane)
    mask = live * (1.0 - same * flag(row == lane))
    base = jnp.maximum(1.0 - dist_sq * (1.0 / (cutoff * cutoff)), 0.0)
    weight = base * base * base * mask * inverse
    slope = -(6.0 / (cutoff * cutoff)) * base * base * mask - weight * inverse
    angle = distance * (math.pi / cutoff)
    return unit, inverse, weight, slope, jnp.sin(angle), jnp.cos(angle)


def harmonics(v):
    x, y, z = v
    return [
        None,
        x,
        y,
        z,
        root_three * x * y,
        root_three * y * z,
        root_three * z * x,
        0.5 * root_three * (x * x - y * y),
        z * z - 0.5 * (x * x + y * y),
    ]


def harmonics_tangent(v, t):
    x, y, z = v
    a, b, c = t
    return [
        None,
        a,
        b,
        c,
        root_three * (a * y + x * b),
        root_three * (b * z + y * c),
        root_three * (c * x + z * a),
        root_three * (x * a - y * b),
        2.0 * z * c - (x * a + y * b),
    ]


def paired_orders(sine, cosine, weight, slope):
    low, high = lane_half()
    double_s, double_c = 2.0 * sine * cosine, 1.0 - 2.0 * sine * sine
    now_s = sine * low + double_s * high
    now_c = cosine * low + double_c * high
    old_s = -sine * low
    old_c = cosine * low + high
    values, slopes = [], []
    for k in range(BASIS // 2):
        order = ((2 * k + 1) * low + (2 * k + 2) * high) * (math.pi / cutoff)
        values.append(now_s * weight)
        slopes.append(now_c * (weight * order) + now_s * slope)
        now_s, old_s = 2.0 * double_c * now_s - old_s, now_s
        now_c, old_c = 2.0 * double_c * now_c - old_c, now_c
    return values, slopes


def single_orders(sine, cosine, weight, slope):
    now_s, now_c = sine, cosine
    old_s, old_c = jnp.zeros_like(sine), jnp.ones_like(cosine)
    values, slopes = [], []
    for n in range(1, BASIS + 1):
        values.append(now_s * weight)
        slopes.append(now_c * (weight * (n * math.pi / cutoff)) + now_s * slope)
        now_s, old_s = 2.0 * cosine * now_s - old_s, now_s
        now_c, old_c = 2.0 * cosine * now_c - old_c, now_c
    return values, slopes


def columns_of(rows, square, turned):
    square[...] = jnp.zeros_like(square)
    square[0 : rows.shape[0], :] = rows
    turned[...] = square[...].T


def pair_rows(first, p):
    return twice(first, p)


def radial_feat(feat, radial, p, tall, wide):
    own = feat[p * TA : (p + 1) * TA, :]
    span, channels = BASIS * TA, feat.shape[1]
    for n in range(BASIS):
        hi, lo = split(own * radial[n : n + 1, :])
        for third, part in enumerate((hi, hi, lo)):
            tall[p, third * span + n * TA : third * span + (n + 1) * TA, :] = part
            wide[p, n * TA : (n + 1) * TA, third * channels : (third + 1) * channels] = part


OTHER, CENTRE, LIVE, SAME, SHARED, SENT = 0, 2, 4, 6, 8, 9
GHOST_ROWS = 8


def fetch(pairs, sems):
    copies = [pltpu.make_async_copy(src, dst, sems.at[i]) for i, (src, dst) in enumerate(pairs)]
    for copy in copies:
        copy.start()
    return copies


def upward(shift):
    return 1.0 - flag(place(shift, 2) == 1)


def either(choice, first, second):
    return first * choice + second * (1.0 - choice)


def gather_kernel(send, pos, feat, ref, to_second, to_first, token, send_v, pos_v, feat_v, ref_v, sems):
    copies = fetch([(send, send_v), (pos, pos_v), (ref, ref_v), (feat, feat_v)], sems)
    for copy in copies[:3]:
        copy.wait()
    low, high = lane_half()
    up = upward(0)
    sent = [send_v[0:1, j : j + 1].astype(F32) for j in range(2 * SEND)]
    tiles_of = []
    for out, choice in ((to_first, 1.0 - up), (to_second, up)):
        tiles = [either(choice, sent[j], sent[SEND + j]) for j in range(SEND)]
        tiles_of.append(tiles)
        out[SEND * TA :, :] = jnp.zeros((GHOST_ROWS, out.shape[1]), F32)
        for i in range(3):
            at = SEND * TA + i
            for lanes, source in ((slice(0, CHUNK), pos_v), (slice(CHUNK, 2 * CHUNK), ref_v)):
                chunks = [source[i, :, q * CHUNK : (q + 1) * CHUNK] for q in range(2)]
                out[at : at + 1, lanes] = paired(pick(chunks, tiles[0]), pick(chunks, tiles[1]))
        for other in range(2 * SEND):
            same = low * flag(sent[other] == tiles[0]) + high * flag(sent[other] == tiles[1])
            out[SEND * TA + 3 + other : SEND * TA + 4 + other, 0:CHUNK] = same
    token[...] = jnp.zeros_like(token)
    copies[3].wait()
    for out, tiles in zip((to_first, to_second), tiles_of):
        for j in range(SEND):
            out[j * TA : (j + 1) * TA, :] = pick_rows(feat_v.at[0], tiles[j], 0.0)


def pick_rows(ref, position, first):
    total = None
    for t in range(ref.shape[0] // TA):
        term = ref[t * TA : (t + 1) * TA, :] * flag(position == first + float(t))
        total = term if total is None else total + term
    return total


def stage_kernel(
    centre, other, live, send, pos, ref, species, feat, radial_w, mix_w, species_w, out_w, after,
    flags, atoms, own_feat, weights, mh, ml,
    centre_v, other_v, live_v, send_v, pos_v, ref_v, species_v, radial_v, mix_v, species_w_v, out_v, sems,
):
    copies = fetch(
        [
            (centre, centre_v), (other, other_v), (live, live_v), (send, send_v), (pos, pos_v), (ref, ref_v),
            (species, species_v), (radial_w, radial_v), (species_w, species_w_v), (out_w, out_v),
            (feat.at[0], own_feat), (mix_w, mix_v),
        ],
        sems,
    )
    for copy in copies[:-1]:
        copy.wait()
    flags[...] = jnp.zeros_like(flags)
    centres = [centre_v[0:1, p : p + 1].astype(F32) for p in range(PAIRS)]
    others = [other_v[0:1, p : p + 1].astype(F32) for p in range(PAIRS)]
    for p in range(PAIRS):
        for row, value in (
            (OTHER, others[p]),
            (CENTRE, centres[p]),
            (LIVE, live_v[0:1, p : p + 1].astype(F32)),
            (SAME, flag(others[p] == centres[p] + SEND)),
        ):
            flags[row + p : row + p + 1, :] = jnp.broadcast_to(value, (1, CHUNK))
    flags[SHARED : SHARED + 1, :] = jnp.broadcast_to(flag(centres[0] == centres[1]), (1, CHUNK))
    for j in range(2 * SEND):
        value = send_v[0:1, j : j + 1].astype(F32)
        flags[SENT + j : SENT + j + 1, :] = jnp.broadcast_to(value, (1, CHUNK))
    atoms[...] = jnp.zeros_like(atoms)
    for i in range(3):
        atoms[i : i + 1, :] = pos_v[i]
        atoms[4 + i : 5 + i, :] = ref_v[i]
    atoms[3:4, :] = species_v[...].astype(F32)
    weights[...] = jnp.zeros_like(weights)
    weights[0:BASIS, :] = radial_v[...]
    weights[BASIS : BASIS + SPECIES, :] = species_w_v[...]
    weights[BASIS + SPECIES : BASIS + SPECIES + 1, :] = out_v[...]
    copies[-1].wait()
    hi, lo = split(mix_v[...])
    mh[...] = hi
    ml[...] = lo


def force_kernel(
    flags, atoms, feat, weights, mh, ml, from_second, from_first,
    env, dinv, gate, curve, inv, rows, fsel, own, one_first, one_second, two_first, two_second, shape_store, tall, eh, el,
    square, turned, squares, table, wide, steady, raw, back,
):
    ghost = SEND * TA
    up = upward(0)
    near, far = from_first[ghost : ghost + 3, 0:CHUNK], from_second[ghost : ghost + 3, 0:CHUNK]
    chunks = [either(up, far, near), atoms[0:3, 0:CHUNK], atoms[0:3, CHUNK:], either(up, near, far)]
    kinds = [atoms[3:4, q * CHUNK : (q + 1) * CHUNK] for q in range(2)]

    def number(row):
        return flags[row : row + 1, :]

    centres = [number(CENTRE + p) for p in range(PAIRS)]
    others = [number(OTHER + p) for p in range(PAIRS)]
    shared = flags[SHARED : SHARED + 1, 0:1]
    rows[...] = jnp.zeros_like(rows)
    rows[0:3, :] = paired(*(pick(chunks, others[p]) for p in range(PAIRS)))
    rows[3:6, :] = paired(*(pick(chunks[1:3], centres[p]) for p in range(PAIRS)))
    rows[6:7, :] = paired(*(pick(kinds, centres[p]) for p in range(PAIRS)))
    columns_of(rows[...], square, turned)

    for p in range(PAIRS):
        o = flags[OTHER + p : OTHER + p + 1, 0:1]
        fsel[p * TA : (p + 1) * TA, :] = (
            pick_rows(from_first.at[0:ghost], o, (SEND + 4) * up)
            + pick_rows(feat, o, float(SEND))
            + pick_rows(from_second.at[0:ghost], o, (SEND + 4) * (1.0 - up))
        )

    for p in range(PAIRS):
        lane_rows = [twice(rows[i : i + 1, :], p) for i in range(3)]
        for r in range(0, TA, STRIP):
            strip = slice(p * TA + r, p * TA + r + STRIP)
            columns = [turned[strip, 3 + i : 4 + i] for i in range(3)]
            unit, inverse, weight, slope, sine, cosine = geometry(
                lane_rows, columns, 1.0, number(LIVE + p), number(SAME + p), r
            )
            angular = harmonics(unit)
            values, slopes = paired_orders(sine, cosine, weight, slope)
            for i, part in enumerate(unit + [inverse] + values + slopes):
                shape_store[p, i, r : r + STRIP, :] = part
            for m in range(COMPS):
                at = slice(m * TA + r, m * TA + r + STRIP)
                for k in range(BASIS // 2):
                    entry = values[k] if m == 0 else angular[m] * values[k]
                    put_left(table, p, at, k * CHUNK, CHUNK, entry)
        radial_feat(fsel, weights, p, tall, wide)
        raw[p * COMPS * TA : (p + 1) * COMPS * TA, :] = long_product(table[p], tall[p], NN)

    for m in range(COMPS):
        first = raw[m * TA : (m + 1) * TA, :]
        second = raw[(COMPS + m) * TA : (COMPS + m + 1) * TA, :]
        env[m * TA : (m + 1) * TA, :] = env_scale * (first + shared * second)
        env[(COMPS + m) * TA : (COMPS + m + 1) * TA, :] = env_scale * (second + shared * first)
    for p in range(PAIRS):
        sums = [None] * 3
        for m in range(COMPS):
            block = env[(p * COMPS + m) * TA : (p * COMPS + m + 1) * TA, :]
            sums[GROUP[m]] = block * block if sums[GROUP[m]] is None else sums[GROUP[m]] + block * block
        for g in range(3):
            inv[p * TA : (p + 1) * TA, g * 256 : (g + 1) * 256] = sums[g]
    hidden = product(split(inv[...]), (mh[...], ml[...]), NN)
    kind = turned[:, 6:7]
    for s in range(SPECIES):
        hidden = hidden + flag(kind == float(s)) * weights[BASIS + s : BASIS + s + 1, :]
    out_row = weights[BASIS + SPECIES : BASIS + SPECIES + 1, :]
    sigma = 1.0 / (1.0 + jnp.exp(-hidden))
    first_order = sigma * (1.0 + hidden * (1.0 - sigma))
    gate[...] = first_order
    curve[...] = sigma * (1.0 - sigma) * (2.0 + hidden * (1.0 - 2.0 * sigma)) * out_row
    dinv[...] = product(split(first_order * out_row), (mh[...], ml[...]), NT)

    tile_grads = [jnp.zeros((3, CHUNK), F32) for _ in range(4)]
    other_rows = []
    for p in range(PAIRS):
        for m in range(COMPS):
            block = env[(p * COMPS + m) * TA : (p * COMPS + m + 1) * TA, :]
            part = dinv[p * TA : (p + 1) * TA, GROUP[m] * 256 : (GROUP[m] + 1) * 256]
            at = slice(m * TA, (m + 1) * TA)
            hi, lo = split((2.0 * env_scale) * block * part)
            eh[p, at, :] = hi
            el[p, at, :] = lo
            for third, piece in enumerate((hi, lo, hi)):
                steady[p, at, third * 256 : (third + 1) * 256] = piece
        for ref in (eh, el):
            ref[p, COMPS * TA :, :] = jnp.zeros((WIDE - COMPS * TA, ref.shape[2]), BF16)
        back[p] = long_product(steady[p], wide[p], NT)
        summed = [jnp.zeros((1, CHUNK), F32) for _ in range(3)]
        for r in range(0, TA, STRIP):
            strip = slice(r, r + STRIP)
            x, y, z, inverse = (shape_store[p, i, strip, :] for i in range(4))
            values = [shape_store[p, 4 + k, strip, :] for k in range(BASIS // 2)]
            slopes = [shape_store[p, 8 + k, strip, :] for k in range(BASIS // 2)]
            angular = harmonics((x, y, z))
            d_radius = None
            g = []
            for m in range(COMPS):
                along, across = None, None
                for k in range(BASIS // 2):
                    block = back[p, m * TA + r : m * TA + r + STRIP, k * CHUNK : (k + 1) * CHUNK]
                    along = block * slopes[k] if along is None else along + block * slopes[k]
                    across = block * values[k] if across is None else across + block * values[k]
                g.append(across)
                term = along if m == 0 else along * angular[m]
                d_radius = term if d_radius is None else d_radius + term
            toward = [
                g[1] + root_three * (y * g[4] + z * g[6] + x * g[7]) - x * g[8],
                g[2] + root_three * (x * g[4] + z * g[5] - y * g[7]) - y * g[8],
                g[3] + root_three * (y * g[5] + x * g[6]) + 2.0 * (z * g[8]),
            ]
            radial_part = d_radius - inverse * (toward[0] * x + toward[1] * y + toward[2] * z)
            for i, v in enumerate((x, y, z)):
                d_offset = inverse * toward[i] + v * radial_part
                summed[i] = summed[i] + jnp.sum(d_offset, axis=0, keepdims=True)
                squares[i, p * TA + r : p * TA + r + STRIP, :] = d_offset
        other_rows.append([part + pltpu.roll(part, TA, 1) for part in summed])
    for i in range(3):
        centre_both = -jnp.sum(squares[i].T, axis=0, keepdims=True)
        component = flag(lax.broadcasted_iota(jnp.int32, (3, CHUNK), 0) == i)
        for p in range(PAIRS):
            centre_row = twice(centre_both, p)
            for q in range(4):
                at = chunk_mask(others[p], q) * other_rows[p][i]
                if q in (1, 2):
                    at = at + chunk_mask(centres[p] + SEND, q) * centre_row
                tile_grads[q] = tile_grads[q] + at * component
    own[...] = jnp.zeros_like(own)
    own[0:3, 0:CHUNK] = tile_grads[1]
    own[0:3, CHUNK:] = tile_grads[2]
    own[3:6, 0:CHUNK] = tile_grads[0]
    own[3:6, CHUNK:] = tile_grads[3]
    leaving = []
    for first, ghost_grad in ((0, tile_grads[0]), (SEND, tile_grads[3])):
        listed = paired(*(pick(tile_grads[1:3], number(SENT + first + j)) for j in range(SEND)))
        leaving.append((listed, ghost_grad))
    for shift, outs in ((0, (one_first, one_second)), (1, (two_first, two_second))):
        choice = upward(shift)
        for out, above in zip(outs, (choice, 1.0 - choice)):
            out[...] = jnp.zeros_like(out)
            out[0:3, :] = either(above, leaving[1][0], leaving[0][0])
            out[3:6, :] = either(above, leaving[1][1], leaving[0][1])


def tangent_kernel(
    scale, flags, atoms, weights, mh, ml, from_first, from_second, own, one_second, two_second, one_first, two_first,
    rows, env, gate, curve, inv, shape_store, tall, after,
    forces, keep, give, small, envdot, curl, both,
    square, turned, table, raw, left, right,
):
    ghost = SEND * TA
    def number(row):
        return flags[row : row + 1, :]

    centres = [number(CENTRE + p) for p in range(PAIRS)]
    others = [number(OTHER + p) for p in range(PAIRS)]
    shared = flags[SHARED : SHARED + 1, 0:1]
    mine = [own[0:3, 0:CHUNK], own[0:3, CHUNK:]]
    up, up_two = upward(0), upward(1)
    low_one = either(up, one_second[...], one_first[...])
    high_one = either(up, one_first[...], one_second[...])
    low_two = either(up_two, two_second[...], two_first[...])
    high_two = either(up_two, two_first[...], two_second[...])
    low_tail = either(up, from_second[ghost:, :], from_first[ghost:, :])
    high_tail = either(up, from_first[ghost:, :], from_second[ghost:, :])
    arrived = [twice(low_one[3:6, :], j) for j in range(SEND)]
    arrived += [twice(high_one[3:6, :], j) for j in range(SEND)]
    for j in range(2 * SEND):
        for q in range(2):
            mine[q] = mine[q] + chunk_mask(number(SENT + j), q) * arrived[j]
    below = low_one[0:3, :]
    above = high_one[0:3, :]
    to_below = [twice(low_two[3:6, :], j) for j in range(SEND)]
    to_below += [twice(own[3:6, 0:CHUNK], j) for j in range(SEND)]
    to_above = [twice(own[3:6, CHUNK:], j) for j in range(SEND)]
    to_above += [twice(high_two[3:6, :], j) for j in range(SEND)]
    for j in range(2 * SEND):
        below = below + low_tail[3 + j : 4 + j, 0:CHUNK] * to_below[j]
        above = above + high_tail[3 + j : 4 + j, 0:CHUNK] * to_above[j]
    for q in range(2):
        for i in range(3):
            forces[i, :, q * CHUNK : (q + 1) * CHUNK] = -mine[q][i : i + 1, :]
    error = [
        below + low_tail[0:3, CHUNK:],
        mine[0] + atoms[4:7, 0:CHUNK],
        mine[1] + atoms[4:7, CHUNK:],
        above + high_tail[0:3, CHUNK:],
    ]
    error = [part * scale for part in error]
    both[...] = jnp.zeros_like(both)
    both[0:8, :] = rows[...]
    both[8:11, :] = paired(*(pick(error, others[p]) for p in range(PAIRS)))
    both[11:14, :] = paired(*(pick(error[1:3], centres[p]) for p in range(PAIRS)))
    columns_of(both[...], square, turned)

    for p in range(PAIRS):
        lane_move = [twice(both[8 + i : 9 + i, :], p) for i in range(3)]
        for r in range(0, TA, STRIP):
            strip = slice(r, r + STRIP)
            here = slice(p * TA + r, p * TA + r + STRIP)
            column_move = [turned[here, 11 + i : 12 + i] for i in range(3)]
            unit = [shape_store[p, i, strip, :] for i in range(3)]
            inverse = shape_store[p, 3, strip, :]
            move = [a - b for a, b in zip(lane_move, column_move)]
            stretch = unit[0] * move[0] + unit[1] * move[1] + unit[2] * move[2]
            turn = [(m - v * stretch) * inverse for m, v in zip(move, unit)]
            angular, turning = harmonics(unit), harmonics_tangent(unit, turn)
            for k in range(BASIS // 2):
                value = shape_store[p, 4 + k, strip, :]
                slope = shape_store[p, 8 + k, strip, :] * stretch
                for m in range(COMPS):
                    at = slice(m * TA + r, m * TA + r + STRIP)
                    entry = slope if m == 0 else angular[m] * slope + turning[m] * value
                    put_left(table, p, at, k * CHUNK, CHUNK, entry)
        raw[p * COMPS * TA : (p + 1) * COMPS * TA, :] = long_product(table[p], tall[p], NN)

    for m in range(COMPS):
        first = raw[m * TA : (m + 1) * TA, :]
        second = raw[(COMPS + m) * TA : (COMPS + m + 1) * TA, :]
        envdot[m * TA : (m + 1) * TA, :] = env_scale * (first + shared * second)
        envdot[(COMPS + m) * TA : (COMPS + m + 1) * TA, :] = env_scale * (second + shared * first)
    invdot = left
    half = PAIRS * TA
    for p in range(PAIRS):
        sums = [None] * 3
        for m in range(COMPS):
            at = slice((p * COMPS + m) * TA, (p * COMPS + m + 1) * TA)
            term = 2.0 * env[at, :] * envdot[at, :]
            sums[GROUP[m]] = term if sums[GROUP[m]] is None else sums[GROUP[m]] + term
        for g in range(3):
            invdot[half + p * TA : half + (p + 1) * TA, g * 256 : (g + 1) * 256] = sums[g]
    invdot[0:half, :] = inv[...]
    hidden_move = product(split(invdot[half:, :]), (mh[...], ml[...]), NN)
    bend = curve[...] * hidden_move
    curl[...] = bend
    once = 1.0 - shared * flag(lax.broadcasted_iota(jnp.int32, (half, 1), 0) >= TA)
    right[0:half, :] = bend * once
    right[half:, :] = gate[...] * weights[BASIS + SPECIES : BASIS + SPECIES + 1, :] * once
    raw[0 : left.shape[1], :] = product(split(left[...]), split(right[...]), TN)
    core = lax.axis_index("batch")
    for out, part in ((keep, core), (give, 1 - core)):
        out[...] = raw[0 : left.shape[1], block_of_lanes(part)]
    small[...] = jnp.zeros_like(small)
    kind = turned[:, 6:7]
    for s in range(SPECIES):
        small[s : s + 1, :] = jnp.sum(right[0:half, :] * flag(kind == float(s)), axis=0, keepdims=True)
    small[SPECIES : SPECIES + 1, :] = jnp.sum(gate[...] * hidden_move * once, axis=0, keepdims=True)


def table_kernel(flags, rows, shape_store, lh, ll, token, square, turned):
    low, high = lane_half()
    token[...] = jnp.zeros_like(token)
    columns_of(rows[...], square, turned)
    for p in range(PAIRS):
        lane_rows = [twice(rows[3 + i : 4 + i, :], p) for i in range(3)]
        for r in range(0, TA, STRIP):
            columns = [turned[p * TA + r : p * TA + r + STRIP, i : i + 1] for i in range(3)]
            unit, inverse, weight, slope, sine, cosine = geometry(
                lane_rows, columns, -1.0, flags[LIVE + p : LIVE + p + 1, :], flags[SAME + p : SAME + p + 1, :], r
            )
            angular = harmonics(unit)
            values, slopes = single_orders(sine, cosine, weight, slope)
            for i, part in enumerate(unit + [inverse] + values + slopes):
                shape_store[p, i, r : r + STRIP, :] = part
            for m in range(0, COMPS + 1, 2):
                factor = low if m == 0 else angular[m] * low
                if m + 1 < COMPS:
                    factor = factor + angular[m + 1] * high
                for n in range(BASIS):
                    hi, lo = split(factor * values[n])
                    lh[p, n * TA + r : n * TA + r + STRIP, m * TA : (m + 2) * TA] = hi
                    ll[p, n * TA + r : n * TA + r + STRIP, m * TA : (m + 2) * TA] = lo


def radial_kernel(
    p, both, shape_store, lh, ll, eh, el, fsel, env, envdot, dinv, curl, mh, ml, after,
    grad_radial,
    square, turned, sh, sl, gh, gl, raw,
):
    low, high = lane_half()
    columns_of(both[...], square, turned)
    here = slice(p * TA, (p + 1) * TA)
    turn_inv = product(split(curl[here, :]), (mh[...], ml[...]), NT)
    lane_move = [twice(both[11 + i : 12 + i, :], p) for i in range(3)]
    sh[:, 0:CHUNK] = lh[p, :, WIDE - CHUNK :]
    sl[:, 0:CHUNK] = ll[p, :, WIDE - CHUNK :]
    for r in range(0, TA, STRIP):
        strip = slice(r, r + STRIP)
        column_move = [turned[p * TA + r : p * TA + r + STRIP, 8 + i : 9 + i] for i in range(3)]
        unit = [shape_store[p, i, strip, :] for i in range(3)]
        inverse = shape_store[p, 3, strip, :]
        move = [b - a for a, b in zip(lane_move, column_move)]
        stretch = unit[0] * move[0] + unit[1] * move[1] + unit[2] * move[2]
        turn = [(m - v * stretch) * inverse for m, v in zip(move, unit)]
        angular, turning = harmonics(unit), harmonics_tangent(unit, turn)
        on_values, on_slopes = [turning[1] * high], [(low + angular[1] * high) * stretch]
        for m in range(2, COMPS + 1, 2):
            on_value, on_slope = turning[m] * low, angular[m] * low
            if m + 1 < COMPS:
                on_value = on_value + turning[m + 1] * high
                on_slope = on_slope + angular[m + 1] * high
            on_values.append(on_value)
            on_slopes.append(on_slope * stretch)
        for n in range(BASIS):
            value, slope = shape_store[p, 4 + n, strip, :], shape_store[p, 4 + BASIS + n, strip, :]
            for j, (on_value, on_slope) in enumerate(zip(on_values, on_slopes)):
                hi, lo = split(on_value * value + on_slope * slope)
                sh[n * TA + r : n * TA + r + STRIP, (j + 1) * CHUNK : (j + 2) * CHUNK] = hi
                sl[n * TA + r : n * TA + r + STRIP, (j + 1) * CHUNK : (j + 2) * CHUNK] = lo
    for m in range(COMPS):
        at = slice((p * COMPS + m) * TA, (p * COMPS + m + 1) * TA)
        group = slice(GROUP[m] * 256, (GROUP[m] + 1) * 256)
        steady = (2.0 * env_scale) * dinv[here, group]
        bent = (2.0 * env_scale) * turn_inv[:, group]
        hi, lo = split(env[at, :] * bent + envdot[at, :] * steady)
        gh[m * TA : (m + 1) * TA, :] = hi
        gl[m * TA : (m + 1) * TA, :] = lo
    for ref, tail in ((gh, eh), (gl, el)):
        ref[COMPS * TA : WIDE, :] = jnp.zeros((WIDE - COMPS * TA, ref.shape[1]), BF16)
        ref[WIDE:, :] = tail[p]
    first = WIDE - CHUNK
    raw[...] = product((lh[p, :, 0:first], ll[p, :, 0:first]), (gh[0:first, :], gl[0:first, :]), NN) + product(
        (sh[...], sl[...]), (gh[first:, :], gl[first:, :]), NN
    )
    for n in range(BASIS):
        grad_radial[n : n + 1, :] = jnp.sum(
            raw[n * TA : (n + 1) * TA, :] * fsel[here, :], axis=0, keepdims=True
        )


SMALL = 32
PAD = 8
FOUR = 4


def block_of(part, rows):
    return pl.ds(pl.multiple_of(part * rows, 8), rows)


def block_from(start, rows):
    return pl.ds(pl.multiple_of(start, 8), rows)


def block_of_lanes(part):
    return pl.ds(pl.multiple_of(part * HALF, HALF), HALF)


def total_of(refs, at):
    total = refs[0][at, :]
    for ref in refs[1:]:
        total = total + ref[at, :]
    return total


def halve_kernel(keep, taken, after, *outs):
    half, piece = keep.shape[0] // 2, keep.shape[0] // (2 * FOUR)
    mine, me = place(0, 2), place(1, FOUR)
    for i, out in enumerate(outs):
        part = mine if i < 2 else 1 - mine
        for j in range(2):
            k = 1 + 2 * (i % 2) - j
            at = block_from(part * half + lax.bitwise_xor(me, k) * piece, piece)
            out[j * piece : (j + 1) * piece, :] = keep[at, :] + taken[at, :]
        if out.shape[0] > 2 * piece:
            out[2 * piece :, :] = jnp.zeros((out.shape[0] - 2 * piece, HALF), F32)


def spread_kernel(first, keep, taken, radial_0, radial_1, small, after, out_0, out_1, tiny):
    for h in range(2):
        lanes = slice(h * HALF, (h + 1) * HALF)
        tiny[16 * h : 16 * h + 8, :] = radial_0[:, lanes] + radial_1[:, lanes]
        tiny[16 * h + 8 : 16 * h + 16, :] = small[:, lanes]
    me = place(1, FOUR)
    few = SMALL // FOUR
    rows = keep.shape[0] // 2
    for j, out in enumerate((out_0, out_1)):
        out[0:rows, :] = total_of([keep, taken], slice(j * rows, (j + 1) * rows))
        out[rows : rows + few, :] = tiny[block_of(lax.bitwise_xor(me, first - j), few), :]
        if out.shape[0] > rows + few:
            out[rows + few :, :] = jnp.zeros((out.shape[0] - rows - few, HALF), F32)


def total_kernel(*refs):
    refs[-1][...] = total_of(refs[:-1], slice(0, refs[-1].shape[0]))


def near_kernel(mine, third, out):
    rows = mine.shape[0] - SMALL // FOUR
    out[0:rows, :] = mine[0:rows, :]
    out[rows : 2 * rows, :] = third[0:rows, :]
    out[2 * rows :, :] = jnp.zeros((out.shape[0] - 2 * rows, HALF), F32)


def rest_kernel(mine, first, second, third, after, out):
    few = SMALL // FOUR
    rows = mine.shape[0] - few
    out[0:rows, :] = second[0:rows, :]
    out[rows : 2 * rows, :] = first[0:rows, :]
    me = place(1, FOUR)
    for k, ref in enumerate((mine, first, second, third)):
        out[block_from(2 * rows + lax.bitwise_xor(me, k) * few, few), :] = ref[rows:, :]


def pair_kernel(near, rest, their_near, their_rest, out):
    piece = (rest.shape[0] - SMALL) // 2
    half = FOUR * piece
    mine, me = place(0, 2), place(1, FOUR)
    for refs, part in (((near, rest), mine), ((their_near, their_rest), 1 - mine)):
        for ref, ks in zip(refs, ((0, 3), (2, 1))):
            for j, k in enumerate(ks):
                at = block_from(part * half + lax.bitwise_xor(me, k) * piece, piece)
                out[at, :] = ref[j * piece : (j + 1) * piece, :]
    out[2 * half :, :] = rest[2 * piece :, :] + their_rest[2 * piece :, :]


def join_kernel(whole, facing, mix, radial, kinds, out):
    rows = mix.shape[0]
    core = lax.axis_index("batch")
    for ref, part in ((whole, core), (facing, 1 - core)):
        mix[:, block_of_lanes(part)] = ref[0:rows, :]
    both = whole[rows:, :] + facing[rows:, :]
    for h in range(2):
        lanes = slice(h * HALF, (h + 1) * HALF)
        few = both[16 * h : 16 * h + 16, :]
        radial[:, lanes] = few[0:BASIS]
        kinds[:, lanes] = few[BASIS : BASIS + SPECIES]
        out[:, lanes] = few[BASIS + SPECIES : BASIS + SPECIES + 1]


def spec(space):
    return pl.BlockSpec(memory_space=space)


def call(kernel, name, outs, scratch, *operands, space=pltpu.VMEM, after=(), flops=0):
    if space is pltpu.HBM:
        operands = [pltpu.with_memory_space_constraint(operand, space) for operand in operands]
    outs = [out if len(out) == 2 and isinstance(out[0], tuple) else (out, F32) for out in outs]
    return pl.pallas_call(
        kernel,
        name=name,
        out_shape=[jax.ShapeDtypeStruct(*out) for out in outs],
        in_specs=[spec(space)] * len(operands) + [spec(pltpu.VMEM)] * len(after),
        out_specs=[spec(pltpu.VMEM)] * len(outs),
        scratch_shapes=[pltpu.VMEM(*item) if isinstance(item, tuple) else item for item in scratch],
        compiler_params=pltpu.CompilerParams(vmem_limit_bytes=28 * 1024 * 1024),
        cost_estimate=pl.CostEstimate(flops=flops, bytes_accessed=1 << 20 if flops else 1 << 10, transcendentals=0),
    )(*operands, *after)


def shifted(block, axis, by):
    count = lax.axis_size(axis)
    return lax.ppermute(block, axis, [(i, (i + by) % count) for i in range(count)])


def exchanged(block, shift, first):
    count, step = lax.axis_size("domain"), 1 << shift
    up = [((i >> shift) & 1 == 0) == first for i in range(count)]
    return lax.ppermute(block, "domain", [(i, (i + step if up[i] else i - step) % count) for i in range(count)])


def partner(block, mask):
    return lax.ppermute(block, "domain", [(i, i ^ mask) for i in range(lax.axis_size("domain"))])


def on_device(
    positions,
    features,
    species,
    ref_forces,
    centre_tile,
    other_tile,
    pair_live,
    send_tiles,
    radial_w,
    mix_w,
    species_w,
    out_w,
):
    atoms_here = positions.shape[2]
    channels = features.shape[2]
    table = (COMPS * TA, BASIS * TA)
    sent = (SEND * TA + GHOST_ROWS, channels)
    slots = PAIRS * TA
    line = (3, 1, atoms_here)
    turning = [((CHUNK, CHUNK), F32)] * 2
    out_row = out_w.reshape(1, channels)
    positions = positions.transpose(1, 0, 2)
    ref_forces = ref_forces.transpose(1, 0, 2)
    ints = [((1, n), jnp.int32) for n in (PAIRS, PAIRS, PAIRS, 2 * SEND)]

    to_second, to_first, token = call(
        gather_kernel,
        "gather",
        [sent, sent, (8, CHUNK)],
        [
            ints[3],
            (line, F32),
            ((1, atoms_here, channels), F32),
            (line, F32),
            pltpu.SemaphoreType.DMA((4,)),
        ],
        send_tiles, positions, features, ref_forces,
        space=pltpu.HBM,
    )
    from_second = exchanged(to_second, 0, False)
    from_first = exchanged(to_first, 0, True)
    flags, atoms, own_feat, weights, mh, ml = call(
        stage_kernel,
        "stage",
        [
            (16, CHUNK),
            (8, atoms_here),
            (atoms_here, channels),
            (16, channels),
            (mix_w.shape, BF16),
            (mix_w.shape, BF16),
        ],
        ints
        + [(line, F32), (line, F32), ((1, atoms_here), jnp.int32)]
        + [(radial_w.shape, F32), (mix_w.shape, F32), (species_w.shape, F32), (out_row.shape, F32)]
        + [pltpu.SemaphoreType.DMA((12,))],
        centre_tile, other_tile, pair_live, send_tiles, positions, ref_forces, species, features,
        radial_w, mix_w, species_w, out_row,
        space=pltpu.HBM,
        after=(token,),
    )

    long_table = (PAIRS, COMPS * TA, 3 * BASIS * TA)
    env, dinv, gate, curve, inv, rows, fsel, own, *leaving, shape_store, tall, eh, el = call(
        force_kernel,
        "force",
        [
            (PAIRS * COMPS * TA, channels),
            (slots, 3 * channels),
            (slots, channels),
            (slots, channels),
            (slots, 3 * channels),
            (8, CHUNK),
            (slots, channels),
            (8, atoms_here),
            (8, CHUNK),
            (8, CHUNK),
            (8, CHUNK),
            (8, CHUNK),
            (PAIRS, 4 + BASIS, TA, CHUNK),
            ((PAIRS, 3 * BASIS * TA, channels), BF16),
            ((PAIRS, WIDE, channels), BF16),
            ((PAIRS, WIDE, channels), BF16),
        ],
        turning
        + [((3, CHUNK, CHUNK), F32)]
        + [(long_table, BF16), ((PAIRS, BASIS * TA, 3 * channels), BF16)]
        + [((PAIRS, COMPS * TA, 3 * channels), BF16)]
        + [((PAIRS * COMPS * TA, channels), F32), ((PAIRS, *table), F32)],
        flags, atoms, own_feat, weights, mh, ml, from_second, from_first,
        flops=1 << 31,
    )
    arriving = [exchanged(leaving[i], i // 2, i % 2 == 0) for i in (1, 3, 0, 2)]

    table_shape, lh, ll, token = call(
        table_kernel,
        "table",
        [
            (PAIRS, 4 + 2 * BASIS, TA, CHUNK),
            ((PAIRS, BASIS * TA, WIDE), BF16),
            ((PAIRS, BASIS * TA, WIDE), BF16),
            (8, CHUNK),
        ],
        turning,
        flags, rows,
        flops=1 << 30,
    )

    rows_mix = 3 * channels
    total_count = 3.0 * atoms_here * lax.axis_size("domain") * lax.axis_size("batch")
    forces, keep, give, small, envdot, curl, both = call(
        functools.partial(tangent_kernel, 2.0 / math.sqrt(total_count)),
        "tangent",
        [
            line,
            (rows_mix, HALF),
            (rows_mix, HALF),
            (8, channels),
            (PAIRS * COMPS * TA, channels),
            (slots, channels),
            (16, CHUNK),
        ],
        turning
        + [(long_table, BF16)]
        + [((PAIRS * COMPS * TA, channels), F32)]
        + [((2 * slots, 3 * channels), F32), ((2 * slots, channels), F32)],
        flags, atoms, weights, mh, ml, from_first, from_second, own, *arriving,
        rows, env, gate, curve, inv, shape_store, tall, token,
        flops=1 << 31,
    )

    def radial(p, after):
        return call(
            functools.partial(radial_kernel, p),
            "radial",
            [(BASIS, channels)],
            turning
            + [((BASIS * TA, CHUNK + WIDE), BF16)] * 2
            + [((2 * WIDE, channels), BF16)] * 2
            + [((BASIS * TA, channels), F32)],
            both, table_shape, lh, ll, eh, el, fsel, env, envdot, dinv, curl, mh, ml, after,
            flops=1 << 31 if p == 0 else 0,
        )[0]

    radials = [radial(0, both)]
    piece = rows_mix // (2 * FOUR)
    few = SMALL // FOUR
    near, far, give_near, give_far = call(
        halve_kernel, "halve", [(2 * piece, HALF)] * 3 + [(2 * piece + PAD, HALF)], [],
        keep, shifted(give, "batch", 1), radials[0],
    )
    radials.append(radial(1, far))
    blocks = []
    after = radials[1]
    taken_near = partner(give_near, 1)
    taken_far = partner(give_far, 1)
    for first, kept, taken in ((3, far, taken_far), (1, near, taken_near)):
        blocks += call(
            functools.partial(spread_kernel, first),
            "spread", [(piece + few + PAD * k, HALF) for k in (first - 1, max(first - 2, 0))], [((SMALL, HALF), F32)],
            kept, taken, *radials, small, after,
        )
        after = blocks[0]
    terms = [blocks[3]] + [partner(blocks[3 - k], 2 * k) for k in range(FOUR - 1, 0, -1)]
    (mine,) = call(total_kernel, "total", [(piece + few, HALF)], [], *terms)
    bit = 2 * FOUR
    while bit < lax.axis_size("domain"):
        (mine,) = call(total_kernel, "total", [(piece + few, HALF)], [], mine, partner(mine, bit))
        bit *= 2
    parts = [mine] + [partner(mine, 2 * k) for k in range(1, FOUR)]
    (near,) = call(near_kernel, "near", [(2 * piece + SMALL + PAD, HALF)], [], mine, parts[3])
    their_near = partner(near, 1)
    (rest,) = call(rest_kernel, "rest", [(2 * piece + SMALL, HALF)], [], *parts, near)
    their_rest = partner(rest, 1)
    (whole,) = call(
        pair_kernel, "pair", [(rows_mix + SMALL, HALF)], [], near, rest, their_near, their_rest
    )
    facing = shifted(whole, "batch", 1)
    mix, radial_sum, kinds, out = call(
        join_kernel,
        "join",
        [(rows_mix, channels), (BASIS, channels), (SPECIES, channels), (1, channels)],
        [],
        whole,
        facing,
    )
    return forces.transpose(1, 0, 2), radial_sum, mix, kinds, out.reshape(channels)


def solution(mesh):
    return jax.shard_map(
        on_device,
        mesh=mesh,
        in_specs=(
            P(("parts", "batch"), None, "domain"),
            P(("parts", "batch"), "domain", None),
            P(("parts", "batch"), "domain"),
            P(("parts", "batch"), None, "domain"),
            P(("parts", "batch"), "domain"),
            P(("parts", "batch"), "domain"),
            P(("parts", "batch"), "domain"),
            P(("parts", "batch"), "domain"),
            P(),
            P(),
            P(),
            P(),
        ),
        out_specs=(
            P(("parts", "batch"), None, "domain"),
            P("parts", None),
            P("parts", None),
            P("parts", None),
            P("parts"),
        ),
        check_vma=False,
    )
```

```python
import functools
import math

import jax
import jax.numpy as jnp
from jax import lax
from jax.experimental import pallas as pl
from jax.experimental.pallas import tpu as pltpu
from jax.sharding import PartitionSpec as P

TA = 64
SEND = 2
PAIRS = 2
COMPS = 9
STRIP = 16
WIDE = 10 * TA
BASIS = 8
SPECIES = 4
HALF = 128
CHUNK = 2 * TA

cutoff = 2.5
soften = 0.25
env_scale = 0.25
root_three = math.sqrt(3.0)
F32 = jnp.float32
BF16 = jnp.bfloat16
NN = (((1,), (0,)), ((), ()))
NT = (((1,), (1,)), ((), ()))
TN = (((0,), (0,)), ((), ()))
GROUP = (0, 1, 1, 1, 2, 2, 2, 2, 2)


def split(value):
    high = value.astype(BF16)
    return high, (value - high.astype(F32)).astype(BF16)


def product(left, right, dims):
    (lh, ll), (rh, rl) = left, right

    def one(x, y):
        return lax.dot_general(x, y, dims, preferred_element_type=F32)

    return one(lh, rh) + (one(lh, rl) + one(ll, rh))


def long_product(left, right, dims):
    return lax.dot_general(left, right, dims, preferred_element_type=F32)


def put_left(ref, p, rows, lane, width, value):
    hi, lo = split(value)
    span = ref.shape[2] // 3
    for third, part in enumerate((hi, lo, hi)):
        at = third * span + lane
        ref[p, rows, at : at + width] = part


def flag(condition):
    return jnp.where(condition, 1.0, 0.0).astype(F32)


def place(shift, width):
    return lax.bitwise_and(lax.shift_right_logical(lax.axis_index("domain"), shift), width - 1)


def lane_half():
    lane = lax.broadcasted_iota(jnp.int32, (1, CHUNK), 1)
    low = flag(lane < TA)
    return low, 1.0 - low


def twice(chunk, half):
    low, high = lane_half()
    swapped = pltpu.roll(chunk, TA, 1)
    return chunk * low + swapped * high if half == 0 else swapped * low + chunk * high


def pick(chunks, position):
    total = None
    for q, chunk in enumerate(chunks):
        for half in range(2):
            term = twice(chunk, half) * flag(position == 2 * q + half)
            total = term if total is None else total + term
    return total


def paired(first, second):
    low, high = lane_half()
    return first * low + second * high


def chunk_mask(position, q):
    low, high = lane_half()
    return low * flag(position == 2 * q) + high * flag(position == 2 * q + 1)


def series(angle):
    square = angle * angle
    sine, cosine = 1.0 / math.factorial(13), -1.0 / math.factorial(14)
    for order in range(11, 0, -2):
        sine = sine * square + (-1.0) ** (order // 2) / math.factorial(order)
    for order in range(12, -1, -2):
        cosine = cosine * square + (-1.0) ** (order // 2) / math.factorial(order)
    return sine * angle, cosine


def geometry(lane_rows, columns, sign, live, same, first):
    offset = [(row - column) * sign for row, column in zip(lane_rows, columns)]
    dist_sq = offset[0] * offset[0] + offset[1] * offset[1] + offset[2] * offset[2] + soften
    inverse = lax.rsqrt(dist_sq)
    inverse = inverse * (1.5 - 0.5 * dist_sq * inverse * inverse)
    unit = [x * inverse for x in offset]
    row = lax.broadcasted_iota(jnp.int32, (STRIP, CHUNK), 0) + first
    lane = lax.broadcasted_iota(jnp.int32, (STRIP, CHUNK), 1)
    lane = jnp.where(lane >= TA, lane - TA, lane)
    mask = live * (1.0 - same * flag(row == lane))
    base = jnp.maximum(1.0 - dist_sq * (1.0 / (cutoff * cutoff)), 0.0)
    weight = base * base * base * mask * inverse
    slope = -(6.0 / (cutoff * cutoff)) * base * base * mask - weight * inverse
    turned = jnp.minimum(dist_sq * inverse, cutoff) * (math.pi / cutoff) - 0.5 * math.pi
    sine, cosine = series(turned)
    return unit, inverse, weight, slope, cosine, -sine


def harmonics(v):
    x, y, z = v
    return [
        None,
        x,
        y,
        z,
        root_three * x * y,
        root_three * y * z,
        root_three * z * x,
        0.5 * root_three * (x * x - y * y),
        z * z - 0.5 * (x * x + y * y),
    ]


def harmonics_tangent(v, t):
    x, y, z = v
    a, b, c = t
    return [
        None,
        a,
        b,
        c,
        root_three * (a * y + x * b),
        root_three * (b * z + y * c),
        root_three * (c * x + z * a),
        root_three * (x * a - y * b),
        2.0 * z * c - (x * a + y * b),
    ]


def paired_orders(sine, cosine, weight, slope):
    low, high = lane_half()
    double_s, double_c = 2.0 * sine * cosine, 1.0 - 2.0 * sine * sine
    now_s = sine * low + double_s * high
    now_c = cosine * low + double_c * high
    old_s = -sine * low
    old_c = cosine * low + high
    values, slopes = [], []
    for k in range(BASIS // 2):
        order = ((2 * k + 1) * low + (2 * k + 2) * high) * (math.pi / cutoff)
        values.append(now_s * weight)
        slopes.append(now_c * (weight * order) + now_s * slope)
        now_s, old_s = 2.0 * double_c * now_s - old_s, now_s
        now_c, old_c = 2.0 * double_c * now_c - old_c, now_c
    return values, slopes


def single_orders(sine, cosine, weight, slope):
    now_s, now_c = sine, cosine
    old_s, old_c = jnp.zeros_like(sine), jnp.ones_like(cosine)
    values, slopes = [], []
    for n in range(1, BASIS + 1):
        values.append(now_s * weight)
        slopes.append(now_c * (weight * (n * math.pi / cutoff)) + now_s * slope)
        now_s, old_s = 2.0 * cosine * now_s - old_s, now_s
        now_c, old_c = 2.0 * cosine * now_c - old_c, now_c
    return values, slopes


def columns_of(rows, square, turned):
    square[...] = jnp.zeros_like(square)
    square[0 : rows.shape[0], :] = rows
    turned[...] = square[...].T


def pair_rows(first, p):
    return twice(first, p)


def radial_feat(feat, radial, p, tall, wide):
    own = feat[p * TA : (p + 1) * TA, :]
    span, channels = BASIS * TA, feat.shape[1]
    for n in range(BASIS):
        hi, lo = split(own * radial[n : n + 1, :])
        for third, part in enumerate((hi, hi, lo)):
            tall[p, third * span + n * TA : third * span + (n + 1) * TA, :] = part
            wide[p, n * TA : (n + 1) * TA, third * channels : (third + 1) * channels] = part


OTHER, CENTRE, LIVE, SAME, SHARED, SENT = 0, 2, 4, 6, 8, 9
GHOST_ROWS = 8


def fetch(pairs, sems):
    copies = [pltpu.make_async_copy(src, dst, sems.at[i]) for i, (src, dst) in enumerate(pairs)]
    for copy in copies:
        copy.start()
    return copies


def upward(shift):
    return 1.0 - flag(place(shift, 2) == 1)


def either(choice, first, second):
    return first * choice + second * (1.0 - choice)


def gather_kernel(send, pos, feat, ref, to_second, to_first, token, send_v, pos_v, feat_v, ref_v, sems):
    copies = fetch([(send, send_v), (pos, pos_v), (ref, ref_v), (feat, feat_v)], sems)
    for copy in copies[:3]:
        copy.wait()
    low, high = lane_half()
    up = upward(0)
    sent = [send_v[0:1, j : j + 1].astype(F32) for j in range(2 * SEND)]
    tiles_of = []
    for out, choice in ((to_first, 1.0 - up), (to_second, up)):
        tiles = [either(choice, sent[j], sent[SEND + j]) for j in range(SEND)]
        tiles_of.append(tiles)
        out[SEND * TA :, :] = jnp.zeros((GHOST_ROWS, out.shape[1]), F32)
        for i in range(3):
            at = SEND * TA + i
            for lanes, source in ((slice(0, CHUNK), pos_v), (slice(CHUNK, 2 * CHUNK), ref_v)):
                chunks = [source[i, :, q * CHUNK : (q + 1) * CHUNK] for q in range(2)]
                out[at : at + 1, lanes] = paired(pick(chunks, tiles[0]), pick(chunks, tiles[1]))
        for other in range(2 * SEND):
            same = low * flag(sent[other] == tiles[0]) + high * flag(sent[other] == tiles[1])
            out[SEND * TA + 3 + other : SEND * TA + 4 + other, 0:CHUNK] = same
    token[...] = jnp.zeros_like(token)
    copies[3].wait()
    for out, tiles in zip((to_first, to_second), tiles_of):
        for j in range(SEND):
            out[j * TA : (j + 1) * TA, :] = pick_rows(feat_v.at[0], tiles[j], 0.0)


def pick_rows(ref, position, first):
    total = None
    for t in range(ref.shape[0] // TA):
        term = ref[t * TA : (t + 1) * TA, :] * flag(position == first + float(t))
        total = term if total is None else total + term
    return total


def stage_kernel(
    centre, other, live, send, pos, ref, species, feat, radial_w, mix_w, species_w, out_w, after,
    flags, atoms, own_feat, weights, mh, ml,
    centre_v, other_v, live_v, send_v, pos_v, ref_v, species_v, radial_v, mix_v, species_w_v, out_v, sems,
):
    copies = fetch(
        [
            (centre, centre_v), (other, other_v), (live, live_v), (send, send_v), (pos, pos_v), (ref, ref_v),
            (species, species_v), (radial_w, radial_v), (species_w, species_w_v), (out_w, out_v),
            (feat.at[0], own_feat), (mix_w, mix_v),
        ],
        sems,
    )
    for copy in copies[:-1]:
        copy.wait()
    flags[...] = jnp.zeros_like(flags)
    centres = [centre_v[0:1, p : p + 1].astype(F32) for p in range(PAIRS)]
    others = [other_v[0:1, p : p + 1].astype(F32) for p in range(PAIRS)]
    for p in range(PAIRS):
        for row, value in (
            (OTHER, others[p]),
            (CENTRE, centres[p]),
            (LIVE, live_v[0:1, p : p + 1].astype(F32)),
            (SAME, flag(others[p] == centres[p] + SEND)),
        ):
            flags[row + p : row + p + 1, :] = jnp.broadcast_to(value, (1, CHUNK))
    flags[SHARED : SHARED + 1, :] = jnp.broadcast_to(flag(centres[0] == centres[1]), (1, CHUNK))
    for j in range(2 * SEND):
        value = send_v[0:1, j : j + 1].astype(F32)
        flags[SENT + j : SENT + j + 1, :] = jnp.broadcast_to(value, (1, CHUNK))
    atoms[...] = jnp.zeros_like(atoms)
    for i in range(3):
        atoms[i : i + 1, :] = pos_v[i]
        atoms[4 + i : 5 + i, :] = ref_v[i]
    atoms[3:4, :] = species_v[...].astype(F32)
    weights[...] = jnp.zeros_like(weights)
    weights[0:BASIS, :] = radial_v[...]
    weights[BASIS : BASIS + SPECIES, :] = species_w_v[...]
    weights[BASIS + SPECIES : BASIS + SPECIES + 1, :] = out_v[...]
    copies[-1].wait()
    hi, lo = split(mix_v[...])
    mh[...] = hi
    ml[...] = lo


def force_kernel(
    flags, atoms, feat, weights, mh, ml, from_second, from_first,
    env, dinv, gate, curve, inv, rows, fsel, own, one_first, one_second, two_first, two_second, shape_store, tall, eh, el,
    square, turned, squares, table, wide, steady, raw, back,
):
    ghost = SEND * TA
    up = upward(0)
    near, far = from_first[ghost : ghost + 3, 0:CHUNK], from_second[ghost : ghost + 3, 0:CHUNK]
    chunks = [either(up, far, near), atoms[0:3, 0:CHUNK], atoms[0:3, CHUNK:], either(up, near, far)]
    kinds = [atoms[3:4, q * CHUNK : (q + 1) * CHUNK] for q in range(2)]

    def number(row):
        return flags[row : row + 1, :]

    centres = [number(CENTRE + p) for p in range(PAIRS)]
    others = [number(OTHER + p) for p in range(PAIRS)]
    shared = flags[SHARED : SHARED + 1, 0:1]
    rows[...] = jnp.zeros_like(rows)
    rows[0:3, :] = paired(*(pick(chunks, others[p]) for p in range(PAIRS)))
    rows[3:6, :] = paired(*(pick(chunks[1:3], centres[p]) for p in range(PAIRS)))
    rows[6:7, :] = paired(*(pick(kinds, centres[p]) for p in range(PAIRS)))
    columns_of(rows[...], square, turned)

    for p in range(PAIRS):
        o = flags[OTHER + p : OTHER + p + 1, 0:1]
        fsel[p * TA : (p + 1) * TA, :] = (
            pick_rows(from_first.at[0:ghost], o, (SEND + 4) * up)
            + pick_rows(feat, o, float(SEND))
            + pick_rows(from_second.at[0:ghost], o, (SEND + 4) * (1.0 - up))
        )

    for p in range(PAIRS):
        lane_rows = [twice(rows[i : i + 1, :], p) for i in range(3)]
        for r in range(0, TA, STRIP):
            strip = slice(p * TA + r, p * TA + r + STRIP)
            columns = [turned[strip, 3 + i : 4 + i] for i in range(3)]
            unit, inverse, weight, slope, sine, cosine = geometry(
                lane_rows, columns, 1.0, number(LIVE + p), number(SAME + p), r
            )
            angular = harmonics(unit)
            values, slopes = paired_orders(sine, cosine, weight, slope)
            for i, part in enumerate(unit + [inverse] + values + slopes):
                shape_store[p, i, r : r + STRIP, :] = part
            for m in range(COMPS):
                at = slice(m * TA + r, m * TA + r + STRIP)
                for k in range(BASIS // 2):
                    entry = values[k] if m == 0 else angular[m] * values[k]
                    put_left(table, p, at, k * CHUNK, CHUNK, entry)
        radial_feat(fsel, weights, p, tall, wide)
        raw[p * COMPS * TA : (p + 1) * COMPS * TA, :] = long_product(table[p], tall[p], NN)

    for m in range(COMPS):
        first = raw[m * TA : (m + 1) * TA, :]
        second = raw[(COMPS + m) * TA : (COMPS + m + 1) * TA, :]
        env[m * TA : (m + 1) * TA, :] = env_scale * (first + shared * second)
        env[(COMPS + m) * TA : (COMPS + m + 1) * TA, :] = env_scale * (second + shared * first)
    for p in range(PAIRS):
        sums = [None] * 3
        for m in range(COMPS):
            block = env[(p * COMPS + m) * TA : (p * COMPS + m + 1) * TA, :]
            sums[GROUP[m]] = block * block if sums[GROUP[m]] is None else sums[GROUP[m]] + block * block
        for g in range(3):
            inv[p * TA : (p + 1) * TA, g * 256 : (g + 1) * 256] = sums[g]
    hidden = product(split(inv[...]), (mh[...], ml[...]), NN)
    kind = turned[:, 6:7]
    for s in range(SPECIES):
        hidden = hidden + flag(kind == float(s)) * weights[BASIS + s : BASIS + s + 1, :]
    out_row = weights[BASIS + SPECIES : BASIS + SPECIES + 1, :]
    sigma = 1.0 / (1.0 + jnp.exp(-hidden))
    first_order = sigma * (1.0 + hidden * (1.0 - sigma))
    gate[...] = first_order
    curve[...] = sigma * (1.0 - sigma) * (2.0 + hidden * (1.0 - 2.0 * sigma)) * out_row
    dinv[...] = product(split(first_order * out_row), (mh[...], ml[...]), NT)

    tile_grads = [jnp.zeros((3, CHUNK), F32) for _ in range(4)]
    other_rows = []
    for p in range(PAIRS):
        for m in range(COMPS):
            block = env[(p * COMPS + m) * TA : (p * COMPS + m + 1) * TA, :]
            part = dinv[p * TA : (p + 1) * TA, GROUP[m] * 256 : (GROUP[m] + 1) * 256]
            at = slice(m * TA, (m + 1) * TA)
            hi, lo = split((2.0 * env_scale) * block * part)
            eh[p, at, :] = hi
            el[p, at, :] = lo
            for third, piece in enumerate((hi, lo, hi)):
                steady[p, at, third * 256 : (third + 1) * 256] = piece
        for ref in (eh, el):
            ref[p, COMPS * TA :, :] = jnp.zeros((WIDE - COMPS * TA, ref.shape[2]), BF16)
        back[p] = long_product(steady[p], wide[p], NT)
        summed = [jnp.zeros((1, CHUNK), F32) for _ in range(3)]
        for r in range(0, TA, STRIP):
            strip = slice(r, r + STRIP)
            x, y, z, inverse = (shape_store[p, i, strip, :] for i in range(4))
            values = [shape_store[p, 4 + k, strip, :] for k in range(BASIS // 2)]
            slopes = [shape_store[p, 8 + k, strip, :] for k in range(BASIS // 2)]
            angular = harmonics((x, y, z))
            d_radius = None
            g = []
            for m in range(COMPS):
                along, across = None, None
                for k in range(BASIS // 2):
                    block = back[p, m * TA + r : m * TA + r + STRIP, k * CHUNK : (k + 1) * CHUNK]
                    along = block * slopes[k] if along is None else along + block * slopes[k]
                    across = block * values[k] if across is None else across + block * values[k]
                g.append(across)
                term = along if m == 0 else along * angular[m]
                d_radius = term if d_radius is None else d_radius + term
            toward = [
                g[1] + root_three * (y * g[4] + z * g[6] + x * g[7]) - x * g[8],
                g[2] + root_three * (x * g[4] + z * g[5] - y * g[7]) - y * g[8],
                g[3] + root_three * (y * g[5] + x * g[6]) + 2.0 * (z * g[8]),
            ]
            radial_part = d_radius - inverse * (toward[0] * x + toward[1] * y + toward[2] * z)
            for i, v in enumerate((x, y, z)):
                d_offset = inverse * toward[i] + v * radial_part
                summed[i] = summed[i] + jnp.sum(d_offset, axis=0, keepdims=True)
                squares[i, p * TA + r : p * TA + r + STRIP, :] = d_offset
        other_rows.append([part + pltpu.roll(part, TA, 1) for part in summed])
    for i in range(3):
        centre_both = -jnp.sum(squares[i].T, axis=0, keepdims=True)
        component = flag(lax.broadcasted_iota(jnp.int32, (3, CHUNK), 0) == i)
        for p in range(PAIRS):
            centre_row = twice(centre_both, p)
            for q in range(4):
                at = chunk_mask(others[p], q) * other_rows[p][i]
                if q in (1, 2):
                    at = at + chunk_mask(centres[p] + SEND, q) * centre_row
                tile_grads[q] = tile_grads[q] + at * component
    own[...] = jnp.zeros_like(own)
    own[0:3, 0:CHUNK] = tile_grads[1]
    own[0:3, CHUNK:] = tile_grads[2]
    own[3:6, 0:CHUNK] = tile_grads[0]
    own[3:6, CHUNK:] = tile_grads[3]
    leaving = []
    for first, ghost_grad in ((0, tile_grads[0]), (SEND, tile_grads[3])):
        listed = paired(*(pick(tile_grads[1:3], number(SENT + first + j)) for j in range(SEND)))
        leaving.append((listed, ghost_grad))
    for shift, outs in ((0, (one_first, one_second)), (1, (two_first, two_second))):
        choice = upward(shift)
        for out, above in zip(outs, (choice, 1.0 - choice)):
            out[...] = jnp.zeros_like(out)
            out[0:3, :] = either(above, leaving[1][0], leaving[0][0])
            out[3:6, :] = either(above, leaving[1][1], leaving[0][1])


def tangent_kernel(
    scale, flags, atoms, weights, mh, ml, from_first, from_second, own, one_second, two_second, one_first, two_first,
    rows, env, gate, curve, inv, shape_store, tall, after,
    forces, keep, give, small, envdot, curl, both,
    square, turned, table, raw, left, right,
):
    ghost = SEND * TA
    def number(row):
        return flags[row : row + 1, :]

    centres = [number(CENTRE + p) for p in range(PAIRS)]
    others = [number(OTHER + p) for p in range(PAIRS)]
    shared = flags[SHARED : SHARED + 1, 0:1]
    mine = [own[0:3, 0:CHUNK], own[0:3, CHUNK:]]
    up, up_two = upward(0), upward(1)
    low_one = either(up, one_second[...], one_first[...])
    high_one = either(up, one_first[...], one_second[...])
    low_two = either(up_two, two_second[...], two_first[...])
    high_two = either(up_two, two_first[...], two_second[...])
    low_tail = either(up, from_second[ghost:, :], from_first[ghost:, :])
    high_tail = either(up, from_first[ghost:, :], from_second[ghost:, :])
    arrived = [twice(low_one[3:6, :], j) for j in range(SEND)]
    arrived += [twice(high_one[3:6, :], j) for j in range(SEND)]
    for j in range(2 * SEND):
        for q in range(2):
            mine[q] = mine[q] + chunk_mask(number(SENT + j), q) * arrived[j]
    below = low_one[0:3, :]
    above = high_one[0:3, :]
    to_below = [twice(low_two[3:6, :], j) for j in range(SEND)]
    to_below += [twice(own[3:6, 0:CHUNK], j) for j in range(SEND)]
    to_above = [twice(own[3:6, CHUNK:], j) for j in range(SEND)]
    to_above += [twice(high_two[3:6, :], j) for j in range(SEND)]
    for j in range(2 * SEND):
        below = below + low_tail[3 + j : 4 + j, 0:CHUNK] * to_below[j]
        above = above + high_tail[3 + j : 4 + j, 0:CHUNK] * to_above[j]
    for q in range(2):
        for i in range(3):
            forces[i, :, q * CHUNK : (q + 1) * CHUNK] = -mine[q][i : i + 1, :]
    error = [
        below + low_tail[0:3, CHUNK:],
        mine[0] + atoms[4:7, 0:CHUNK],
        mine[1] + atoms[4:7, CHUNK:],
        above + high_tail[0:3, CHUNK:],
    ]
    error = [part * scale for part in error]
    both[...] = jnp.zeros_like(both)
    both[0:8, :] = rows[...]
    both[8:11, :] = paired(*(pick(error, others[p]) for p in range(PAIRS)))
    both[11:14, :] = paired(*(pick(error[1:3], centres[p]) for p in range(PAIRS)))
    columns_of(both[...], square, turned)

    for p in range(PAIRS):
        lane_move = [twice(both[8 + i : 9 + i, :], p) for i in range(3)]
        for r in range(0, TA, STRIP):
            strip = slice(r, r + STRIP)
            here = slice(p * TA + r, p * TA + r + STRIP)
            column_move = [turned[here, 11 + i : 12 + i] for i in range(3)]
            unit = [shape_store[p, i, strip, :] for i in range(3)]
            inverse = shape_store[p, 3, strip, :]
            move = [a - b for a, b in zip(lane_move, column_move)]
            stretch = unit[0] * move[0] + unit[1] * move[1] + unit[2] * move[2]
            turn = [(m - v * stretch) * inverse for m, v in zip(move, unit)]
            angular, turning = harmonics(unit), harmonics_tangent(unit, turn)
            for k in range(BASIS // 2):
                value = shape_store[p, 4 + k, strip, :]
                slope = shape_store[p, 8 + k, strip, :] * stretch
                for m in range(COMPS):
                    at = slice(m * TA + r, m * TA + r + STRIP)
                    entry = slope if m == 0 else angular[m] * slope + turning[m] * value
                    put_left(table, p, at, k * CHUNK, CHUNK, entry)
        raw[p * COMPS * TA : (p + 1) * COMPS * TA, :] = long_product(table[p], tall[p], NN)

    for m in range(COMPS):
        first = raw[m * TA : (m + 1) * TA, :]
        second = raw[(COMPS + m) * TA : (COMPS + m + 1) * TA, :]
        envdot[m * TA : (m + 1) * TA, :] = env_scale * (first + shared * second)
        envdot[(COMPS + m) * TA : (COMPS + m + 1) * TA, :] = env_scale * (second + shared * first)
    invdot = left
    half = PAIRS * TA
    for p in range(PAIRS):
        sums = [None] * 3
        for m in range(COMPS):
            at = slice((p * COMPS + m) * TA, (p * COMPS + m + 1) * TA)
            term = 2.0 * env[at, :] * envdot[at, :]
            sums[GROUP[m]] = term if sums[GROUP[m]] is None else sums[GROUP[m]] + term
        for g in range(3):
            invdot[half + p * TA : half + (p + 1) * TA, g * 256 : (g + 1) * 256] = sums[g]
    invdot[0:half, :] = inv[...]
    hidden_move = product(split(invdot[half:, :]), (mh[...], ml[...]), NN)
    bend = curve[...] * hidden_move
    curl[...] = bend
    once = 1.0 - shared * flag(lax.broadcasted_iota(jnp.int32, (half, 1), 0) >= TA)
    right[0:half, :] = bend * once
    right[half:, :] = gate[...] * weights[BASIS + SPECIES : BASIS + SPECIES + 1, :] * once
    raw[0 : left.shape[1], :] = product(split(left[...]), split(right[...]), TN)
    core = lax.axis_index("batch")
    for out, part in ((keep, core), (give, 1 - core)):
        out[...] = raw[0 : left.shape[1], block_of_lanes(part)]
    small[...] = jnp.zeros_like(small)
    kind = turned[:, 6:7]
    for s in range(SPECIES):
        small[s : s + 1, :] = jnp.sum(right[0:half, :] * flag(kind == float(s)), axis=0, keepdims=True)
    small[SPECIES : SPECIES + 1, :] = jnp.sum(gate[...] * hidden_move * once, axis=0, keepdims=True)


def table_kernel(flags, rows, shape_store, lh, ll, token, square, turned):
    low, high = lane_half()
    token[...] = jnp.zeros_like(token)
    columns_of(rows[...], square, turned)
    for p in range(PAIRS):
        lane_rows = [twice(rows[3 + i : 4 + i, :], p) for i in range(3)]
        for r in range(0, TA, STRIP):
            columns = [turned[p * TA + r : p * TA + r + STRIP, i : i + 1] for i in range(3)]
            unit, inverse, weight, slope, sine, cosine = geometry(
                lane_rows, columns, -1.0, flags[LIVE + p : LIVE + p + 1, :], flags[SAME + p : SAME + p + 1, :], r
            )
            angular = harmonics(unit)
            values, slopes = single_orders(sine, cosine, weight, slope)
            for i, part in enumerate(unit + [inverse] + values + slopes):
                shape_store[p, i, r : r + STRIP, :] = part
            for m in range(0, COMPS + 1, 2):
                factor = low if m == 0 else angular[m] * low
                if m + 1 < COMPS:
                    factor = factor + angular[m + 1] * high
                for n in range(BASIS):
                    hi, lo = split(factor * values[n])
                    lh[p, n * TA + r : n * TA + r + STRIP, m * TA : (m + 2) * TA] = hi
                    ll[p, n * TA + r : n * TA + r + STRIP, m * TA : (m + 2) * TA] = lo


def radial_kernel(
    p, both, shape_store, lh, ll, eh, el, fsel, env, envdot, dinv, curl, mh, ml, after,
    grad_radial,
    square, turned, sh, sl, gh, gl, raw,
):
    low, high = lane_half()
    columns_of(both[...], square, turned)
    here = slice(p * TA, (p + 1) * TA)
    turn_inv = product(split(curl[here, :]), (mh[...], ml[...]), NT)
    lane_move = [twice(both[11 + i : 12 + i, :], p) for i in range(3)]
    sh[:, 0:CHUNK] = lh[p, :, WIDE - CHUNK :]
    sl[:, 0:CHUNK] = ll[p, :, WIDE - CHUNK :]
    for r in range(0, TA, STRIP):
        strip = slice(r, r + STRIP)
        column_move = [turned[p * TA + r : p * TA + r + STRIP, 8 + i : 9 + i] for i in range(3)]
        unit = [shape_store[p, i, strip, :] for i in range(3)]
        inverse = shape_store[p, 3, strip, :]
        move = [b - a for a, b in zip(lane_move, column_move)]
        stretch = unit[0] * move[0] + unit[1] * move[1] + unit[2] * move[2]
        turn = [(m - v * stretch) * inverse for m, v in zip(move, unit)]
        angular, turning = harmonics(unit), harmonics_tangent(unit, turn)
        on_values, on_slopes = [turning[1] * high], [(low + angular[1] * high) * stretch]
        for m in range(2, COMPS + 1, 2):
            on_value, on_slope = turning[m] * low, angular[m] * low
            if m + 1 < COMPS:
                on_value = on_value + turning[m + 1] * high
                on_slope = on_slope + angular[m + 1] * high
            on_values.append(on_value)
            on_slopes.append(on_slope * stretch)
        for n in range(BASIS):
            value, slope = shape_store[p, 4 + n, strip, :], shape_store[p, 4 + BASIS + n, strip, :]
            for j, (on_value, on_slope) in enumerate(zip(on_values, on_slopes)):
                hi, lo = split(on_value * value + on_slope * slope)
                sh[n * TA + r : n * TA + r + STRIP, (j + 1) * CHUNK : (j + 2) * CHUNK] = hi
                sl[n * TA + r : n * TA + r + STRIP, (j + 1) * CHUNK : (j + 2) * CHUNK] = lo
    for m in range(COMPS):
        at = slice((p * COMPS + m) * TA, (p * COMPS + m + 1) * TA)
        group = slice(GROUP[m] * 256, (GROUP[m] + 1) * 256)
        steady = (2.0 * env_scale) * dinv[here, group]
        bent = (2.0 * env_scale) * turn_inv[:, group]
        hi, lo = split(env[at, :] * bent + envdot[at, :] * steady)
        gh[m * TA : (m + 1) * TA, :] = hi
        gl[m * TA : (m + 1) * TA, :] = lo
    for ref, tail in ((gh, eh), (gl, el)):
        ref[COMPS * TA : WIDE, :] = jnp.zeros((WIDE - COMPS * TA, ref.shape[1]), BF16)
        ref[WIDE:, :] = tail[p]
    first = WIDE - CHUNK
    raw[...] = product((lh[p, :, 0:first], ll[p, :, 0:first]), (gh[0:first, :], gl[0:first, :]), NN) + product(
        (sh[...], sl[...]), (gh[first:, :], gl[first:, :]), NN
    )
    for n in range(BASIS):
        grad_radial[n : n + 1, :] = jnp.sum(
            raw[n * TA : (n + 1) * TA, :] * fsel[here, :], axis=0, keepdims=True
        )


SMALL = 32
PAD = 8
FOUR = 4


def block_of(part, rows):
    return pl.ds(pl.multiple_of(part * rows, 8), rows)


def block_from(start, rows):
    return pl.ds(pl.multiple_of(start, 8), rows)


def block_of_lanes(part):
    return pl.ds(pl.multiple_of(part * HALF, HALF), HALF)


def total_of(refs, at):
    total = refs[0][at, :]
    for ref in refs[1:]:
        total = total + ref[at, :]
    return total


def halve_kernel(keep, taken, after, *outs):
    half, piece = keep.shape[0] // 2, keep.shape[0] // (2 * FOUR)
    mine, me = place(0, 2), place(1, FOUR)
    for i, out in enumerate(outs):
        part = mine if i < 2 else 1 - mine
        for j in range(2):
            k = 1 + 2 * (i % 2) - j
            at = block_from(part * half + lax.bitwise_xor(me, k) * piece, piece)
            out[j * piece : (j + 1) * piece, :] = keep[at, :] + taken[at, :]
        if out.shape[0] > 2 * piece:
            out[2 * piece :, :] = jnp.zeros((out.shape[0] - 2 * piece, HALF), F32)


def spread_kernel(first, keep, taken, radial_0, radial_1, small, after, out_0, out_1, tiny):
    for h in range(2):
        lanes = slice(h * HALF, (h + 1) * HALF)
        tiny[16 * h : 16 * h + 8, :] = radial_0[:, lanes] + radial_1[:, lanes]
        tiny[16 * h + 8 : 16 * h + 16, :] = small[:, lanes]
    me = place(1, FOUR)
    few = SMALL // FOUR
    rows = keep.shape[0] // 2
    for j, out in enumerate((out_0, out_1)):
        out[0:rows, :] = total_of([keep, taken], slice(j * rows, (j + 1) * rows))
        out[rows : rows + few, :] = tiny[block_of(lax.bitwise_xor(me, first - j), few), :]
        if out.shape[0] > rows + few:
            out[rows + few :, :] = jnp.zeros((out.shape[0] - rows - few, HALF), F32)


def total_kernel(*refs):
    refs[-1][...] = total_of(refs[:-1], slice(0, refs[-1].shape[0]))


def near_kernel(mine, third, out):
    rows = mine.shape[0] - SMALL // FOUR
    out[0:rows, :] = mine[0:rows, :]
    out[rows : 2 * rows, :] = third[0:rows, :]
    out[2 * rows :, :] = jnp.zeros((out.shape[0] - 2 * rows, HALF), F32)


def rest_kernel(mine, first, second, third, after, out):
    few = SMALL // FOUR
    rows = mine.shape[0] - few
    out[0:rows, :] = second[0:rows, :]
    out[rows : 2 * rows, :] = first[0:rows, :]
    me = place(1, FOUR)
    for k, ref in enumerate((mine, first, second, third)):
        out[block_from(2 * rows + lax.bitwise_xor(me, k) * few, few), :] = ref[rows:, :]


def pair_kernel(near, rest, their_near, their_rest, out):
    piece = (rest.shape[0] - SMALL) // 2
    half = FOUR * piece
    mine, me = place(0, 2), place(1, FOUR)
    for refs, part in (((near, rest), mine), ((their_near, their_rest), 1 - mine)):
        for ref, ks in zip(refs, ((0, 3), (2, 1))):
            for j, k in enumerate(ks):
                at = block_from(part * half + lax.bitwise_xor(me, k) * piece, piece)
                out[at, :] = ref[j * piece : (j + 1) * piece, :]
    out[2 * half :, :] = rest[2 * piece :, :] + their_rest[2 * piece :, :]


def join_kernel(whole, facing, mix, radial, kinds, out):
    rows = mix.shape[0]
    core = lax.axis_index("batch")
    for ref, part in ((whole, core), (facing, 1 - core)):
        mix[:, block_of_lanes(part)] = ref[0:rows, :]
    both = whole[rows:, :] + facing[rows:, :]
    for h in range(2):
        lanes = slice(h * HALF, (h + 1) * HALF)
        few = both[16 * h : 16 * h + 16, :]
        radial[:, lanes] = few[0:BASIS]
        kinds[:, lanes] = few[BASIS : BASIS + SPECIES]
        out[:, lanes] = few[BASIS + SPECIES : BASIS + SPECIES + 1]


def spec(space):
    return pl.BlockSpec(memory_space=space)


def call(kernel, name, outs, scratch, *operands, space=pltpu.VMEM, after=(), flops=0):
    if space is pltpu.HBM:
        operands = [pltpu.with_memory_space_constraint(operand, space) for operand in operands]
    outs = [out if len(out) == 2 and isinstance(out[0], tuple) else (out, F32) for out in outs]
    return pl.pallas_call(
        kernel,
        name=name,
        out_shape=[jax.ShapeDtypeStruct(*out) for out in outs],
        in_specs=[spec(space)] * len(operands) + [spec(pltpu.VMEM)] * len(after),
        out_specs=[spec(pltpu.VMEM)] * len(outs),
        scratch_shapes=[pltpu.VMEM(*item) if isinstance(item, tuple) else item for item in scratch],
        compiler_params=pltpu.CompilerParams(vmem_limit_bytes=28 * 1024 * 1024),
        cost_estimate=pl.CostEstimate(flops=flops, bytes_accessed=1 << 20 if flops else 1 << 10, transcendentals=0),
    )(*operands, *after)


def shifted(block, axis, by):
    count = lax.axis_size(axis)
    return lax.ppermute(block, axis, [(i, (i + by) % count) for i in range(count)])


def exchanged(block, shift, first):
    count, step = lax.axis_size("domain"), 1 << shift
    up = [((i >> shift) & 1 == 0) == first for i in range(count)]
    return lax.ppermute(block, "domain", [(i, (i + step if up[i] else i - step) % count) for i in range(count)])


def partner(block, mask):
    return lax.ppermute(block, "domain", [(i, i ^ mask) for i in range(lax.axis_size("domain"))])


def on_device(
    positions,
    features,
    species,
    ref_forces,
    centre_tile,
    other_tile,
    pair_live,
    send_tiles,
    radial_w,
    mix_w,
    species_w,
    out_w,
):
    atoms_here = positions.shape[2]
    channels = features.shape[2]
    table = (COMPS * TA, BASIS * TA)
    sent = (SEND * TA + GHOST_ROWS, channels)
    slots = PAIRS * TA
    line = (3, 1, atoms_here)
    turning = [((CHUNK, CHUNK), F32)] * 2
    out_row = out_w.reshape(1, channels)
    positions = positions.transpose(1, 0, 2)
    ref_forces = ref_forces.transpose(1, 0, 2)
    ints = [((1, n), jnp.int32) for n in (PAIRS, PAIRS, PAIRS, 2 * SEND)]

    to_second, to_first, token = call(
        gather_kernel,
        "gather",
        [sent, sent, (8, CHUNK)],
        [
            ints[3],
            (line, F32),
            ((1, atoms_here, channels), F32),
            (line, F32),
            pltpu.SemaphoreType.DMA((4,)),
        ],
        send_tiles, positions, features, ref_forces,
        space=pltpu.HBM,
    )
    from_second = exchanged(to_second, 0, False)
    from_first = exchanged(to_first, 0, True)
    flags, atoms, own_feat, weights, mh, ml = call(
        stage_kernel,
        "stage",
        [
            (16, CHUNK),
            (8, atoms_here),
            (atoms_here, channels),
            (16, channels),
            (mix_w.shape, BF16),
            (mix_w.shape, BF16),
        ],
        ints
        + [(line, F32), (line, F32), ((1, atoms_here), jnp.int32)]
        + [(radial_w.shape, F32), (mix_w.shape, F32), (species_w.shape, F32), (out_row.shape, F32)]
        + [pltpu.SemaphoreType.DMA((12,))],
        centre_tile, other_tile, pair_live, send_tiles, positions, ref_forces, species, features,
        radial_w, mix_w, species_w, out_row,
        space=pltpu.HBM,
        after=(token,),
    )

    long_table = (PAIRS, COMPS * TA, 3 * BASIS * TA)
    env, dinv, gate, curve, inv, rows, fsel, own, *leaving, shape_store, tall, eh, el = call(
        force_kernel,
        "force",
        [
            (PAIRS * COMPS * TA, channels),
            (slots, 3 * channels),
            (slots, channels),
            (slots, channels),
            (slots, 3 * channels),
            (8, CHUNK),
            (slots, channels),
            (8, atoms_here),
            (8, CHUNK),
            (8, CHUNK),
            (8, CHUNK),
            (8, CHUNK),
            (PAIRS, 4 + BASIS, TA, CHUNK),
            ((PAIRS, 3 * BASIS * TA, channels), BF16),
            ((PAIRS, WIDE, channels), BF16),
            ((PAIRS, WIDE, channels), BF16),
        ],
        turning
        + [((3, CHUNK, CHUNK), F32)]
        + [(long_table, BF16), ((PAIRS, BASIS * TA, 3 * channels), BF16)]
        + [((PAIRS, COMPS * TA, 3 * channels), BF16)]
        + [((PAIRS * COMPS * TA, channels), F32), ((PAIRS, *table), F32)],
        flags, atoms, own_feat, weights, mh, ml, from_second, from_first,
        flops=1 << 31,
    )
    arriving = [exchanged(leaving[i], i // 2, i % 2 == 0) for i in (1, 3, 0, 2)]

    table_shape, lh, ll, token = call(
        table_kernel,
        "table",
        [
            (PAIRS, 4 + 2 * BASIS, TA, CHUNK),
            ((PAIRS, BASIS * TA, WIDE), BF16),
            ((PAIRS, BASIS * TA, WIDE), BF16),
            (8, CHUNK),
        ],
        turning,
        flags, rows,
        flops=1 << 30,
    )

    rows_mix = 3 * channels
    total_count = 3.0 * atoms_here * lax.axis_size("domain") * lax.axis_size("batch")
    forces, keep, give, small, envdot, curl, both = call(
        functools.partial(tangent_kernel, 2.0 / math.sqrt(total_count)),
        "tangent",
        [
            line,
            (rows_mix, HALF),
            (rows_mix, HALF),
            (8, channels),
            (PAIRS * COMPS * TA, channels),
            (slots, channels),
            (16, CHUNK),
        ],
        turning
        + [(long_table, BF16)]
        + [((PAIRS * COMPS * TA, channels), F32)]
        + [((2 * slots, 3 * channels), F32), ((2 * slots, channels), F32)],
        flags, atoms, weights, mh, ml, from_first, from_second, own, *arriving,
        rows, env, gate, curve, inv, shape_store, tall, token,
        flops=1 << 31,
    )

    def radial(p, after):
        return call(
            functools.partial(radial_kernel, p),
            "radial",
            [(BASIS, channels)],
            turning
            + [((BASIS * TA, CHUNK + WIDE), BF16)] * 2
            + [((2 * WIDE, channels), BF16)] * 2
            + [((BASIS * TA, channels), F32)],
            both, table_shape, lh, ll, eh, el, fsel, env, envdot, dinv, curl, mh, ml, after,
            flops=1 << 31 if p == 0 else 0,
        )[0]

    radials = [radial(0, both)]
    piece = rows_mix // (2 * FOUR)
    few = SMALL // FOUR
    near, far, give_near, give_far = call(
        halve_kernel, "halve", [(2 * piece, HALF)] * 3 + [(2 * piece + PAD, HALF)], [],
        keep, shifted(give, "batch", 1), radials[0],
    )
    radials.append(radial(1, far))
    blocks = []
    after = radials[1]
    taken_near = partner(give_near, 1)
    taken_far = partner(give_far, 1)
    for first, kept, taken in ((3, far, taken_far), (1, near, taken_near)):
        blocks += call(
            functools.partial(spread_kernel, first),
            "spread", [(piece + few + PAD * k, HALF) for k in (first - 1, max(first - 2, 0))], [((SMALL, HALF), F32)],
            kept, taken, *radials, small, after,
        )
        after = blocks[0]
    terms = [blocks[3]] + [partner(blocks[3 - k], 2 * k) for k in range(FOUR - 1, 0, -1)]
    (mine,) = call(total_kernel, "total", [(piece + few, HALF)], [], *terms)
    bit = 2 * FOUR
    while bit < lax.axis_size("domain"):
        (mine,) = call(total_kernel, "total", [(piece + few, HALF)], [], mine, partner(mine, bit))
        bit *= 2
    parts = [mine] + [partner(mine, 2 * k) for k in range(1, FOUR)]
    (near,) = call(near_kernel, "near", [(2 * piece + SMALL + PAD, HALF)], [], mine, parts[3])
    their_near = partner(near, 1)
    (rest,) = call(rest_kernel, "rest", [(2 * piece + SMALL, HALF)], [], *parts, near)
    their_rest = partner(rest, 1)
    (whole,) = call(
        pair_kernel, "pair", [(rows_mix + SMALL, HALF)], [], near, rest, their_near, their_rest
    )
    facing = shifted(whole, "batch", 1)
    mix, radial_sum, kinds, out = call(
        join_kernel,
        "join",
        [(rows_mix, channels), (BASIS, channels), (SPECIES, channels), (1, channels)],
        [],
        whole,
        facing,
    )
    return forces.transpose(1, 0, 2), radial_sum, mix, kinds, out.reshape(channels)


def solution(mesh):
    return jax.shard_map(
        on_device,
        mesh=mesh,
        in_specs=(
            P(("parts", "batch"), None, "domain"),
            P(("parts", "batch"), "domain", None),
            P(("parts", "batch"), "domain"),
            P(("parts", "batch"), None, "domain"),
            P(("parts", "batch"), "domain"),
            P(("parts", "batch"), "domain"),
            P(("parts", "batch"), "domain"),
            P(("parts", "batch"), "domain"),
            P(),
            P(),
            P(),
            P(),
        ),
        out_specs=(
            P(("parts", "batch"), None, "domain"),
            P("parts", None),
            P("parts", None),
            P("parts", None),
            P("parts"),
        ),
        check_vma=False,
    )
```

```python
import functools
import math

import jax
import jax.numpy as jnp
from jax import lax
from jax.experimental import pallas as pl
from jax.experimental.pallas import tpu as pltpu
from jax.sharding import PartitionSpec as P

TA = 64
SEND = 2
PAIRS = 2
COMPS = 9
STRIP = 16
WIDE = 10 * TA
BASIS = 8
SPECIES = 4
HALF = 128
CHUNK = 2 * TA

cutoff = 2.5
soften = 0.25
env_scale = 0.25
root_three = math.sqrt(3.0)
F32 = jnp.float32
BF16 = jnp.bfloat16
NN = (((1,), (0,)), ((), ()))
NT = (((1,), (1,)), ((), ()))
TN = (((0,), (0,)), ((), ()))
GROUP = (0, 1, 1, 1, 2, 2, 2, 2, 2)


def split(value):
    high = value.astype(BF16)
    return high, (value - high.astype(F32)).astype(BF16)


def product(left, right, dims):
    (lh, ll), (rh, rl) = left, right

    def one(x, y):
        return lax.dot_general(x, y, dims, preferred_element_type=F32)

    return one(lh, rh) + (one(lh, rl) + one(ll, rh))


def long_product(left, right, dims):
    return lax.dot_general(left, right, dims, preferred_element_type=F32)


def put_left(ref, p, rows, lane, width, value):
    hi, lo = split(value)
    for third, part in enumerate((hi, lo, hi)):
        at = third * (ref.shape[2] // 3) + lane
        ref[p, rows, at : at + width] = part


def flag(condition):
    return jnp.where(condition, 1.0, 0.0).astype(F32)


def place(shift, width):
    return lax.bitwise_and(lax.shift_right_logical(lax.axis_index("domain"), shift), width - 1)


def lane_half():
    lane = lax.broadcasted_iota(jnp.int32, (1, CHUNK), 1)
    low = flag(lane < TA)
    return low, 1.0 - low


def twice(chunk, half):
    low, high = lane_half()
    swapped = pltpu.roll(chunk, TA, 1)
    return chunk * low + swapped * high if half == 0 else swapped * low + chunk * high


def twice_at(chunk, p):
    first = flag(p == 0)
    return twice(chunk, 0) * first + twice(chunk, 1) * (1.0 - first)


def slots(body):
    def step(p, carry):
        body(p)
        return carry

    lax.fori_loop(0, PAIRS, step, 0)


def span(start, size):
    return pl.ds(pl.multiple_of(start, 16), size)


def pick(chunks, position):
    total = None
    for q, chunk in enumerate(chunks):
        for half in range(2):
            term = twice(chunk, half) * flag(position == 2 * q + half)
            total = term if total is None else total + term
    return total


def paired(first, second):
    low, high = lane_half()
    return first * low + second * high


def chunk_mask(position, q):
    low, high = lane_half()
    return low * flag(position == 2 * q) + high * flag(position == 2 * q + 1)


def series(angle):
    square = angle * angle
    sine, cosine = 1.0 / math.factorial(13), -1.0 / math.factorial(14)
    for order in range(11, 0, -2):
        sine = sine * square + (-1.0) ** (order // 2) / math.factorial(order)
    for order in range(12, -1, -2):
        cosine = cosine * square + (-1.0) ** (order // 2) / math.factorial(order)
    return sine * angle, cosine


def geometry(lane_rows, columns, sign, live, same, first):
    offset = [(row - column) * sign for row, column in zip(lane_rows, columns)]
    dist_sq = offset[0] * offset[0] + offset[1] * offset[1] + offset[2] * offset[2] + soften
    inverse = lax.rsqrt(dist_sq)
    inverse = inverse * (1.5 - 0.5 * dist_sq * inverse * inverse)
    unit = [x * inverse for x in offset]
    row = lax.broadcasted_iota(jnp.int32, (STRIP, CHUNK), 0) + first
    lane = lax.broadcasted_iota(jnp.int32, (STRIP, CHUNK), 1)
    lane = jnp.where(lane >= TA, lane - TA, lane)
    mask = live * (1.0 - same * flag(row == lane))
    base = jnp.maximum(1.0 - dist_sq * (1.0 / (cutoff * cutoff)), 0.0)
    weight = base * base * base * mask * inverse
    slope = -(6.0 / (cutoff * cutoff)) * base * base * mask - weight * inverse
    turned = jnp.minimum(dist_sq * inverse, cutoff) * (math.pi / cutoff) - 0.5 * math.pi
    sine, cosine = series(turned)
    return unit, inverse, weight, slope, cosine, -sine


def harmonics(v):
    x, y, z = v
    return [
        None,
        x,
        y,
        z,
        root_three * x * y,
        root_three * y * z,
        root_three * z * x,
        0.5 * root_three * (x * x - y * y),
        z * z - 0.5 * (x * x + y * y),
    ]


def harmonics_tangent(v, t):
    x, y, z = v
    a, b, c = t
    return [
        None,
        a,
        b,
        c,
        root_three * (a * y + x * b),
        root_three * (b * z + y * c),
        root_three * (c * x + z * a),
        root_three * (x * a - y * b),
        2.0 * z * c - (x * a + y * b),
    ]


def paired_orders(sine, cosine, weight, slope):
    low, high = lane_half()
    double_s, double_c = 2.0 * sine * cosine, 1.0 - 2.0 * sine * sine
    now_s = sine * low + double_s * high
    now_c = cosine * low + double_c * high
    old_s = -sine * low
    old_c = cosine * low + high
    values, slopes = [], []
    for k in range(BASIS // 2):
        order = ((2 * k + 1) * low + (2 * k + 2) * high) * (math.pi / cutoff)
        values.append(now_s * weight)
        slopes.append(now_c * (weight * order) + now_s * slope)
        now_s, old_s = 2.0 * double_c * now_s - old_s, now_s
        now_c, old_c = 2.0 * double_c * now_c - old_c, now_c
    return values, slopes


def single_orders(sine, cosine, weight, slope):
    now_s, now_c = sine, cosine
    old_s, old_c = jnp.zeros_like(sine), jnp.ones_like(cosine)
    values, slopes = [], []
    for n in range(1, BASIS + 1):
        values.append(now_s * weight)
        slopes.append(now_c * (weight * (n * math.pi / cutoff)) + now_s * slope)
        now_s, old_s = 2.0 * cosine * now_s - old_s, now_s
        now_c, old_c = 2.0 * cosine * now_c - old_c, now_c
    return values, slopes


def columns_of(rows, square, turned):
    square[...] = jnp.zeros_like(square)
    square[0 : rows.shape[0], :] = rows
    turned[...] = square[...].T


def pair_rows(first, p):
    return twice(first, p)


def radial_feat(feat, radial, p, tall, wide):
    own = feat[span(p * TA, TA), :]
    third_rows, channels = BASIS * TA, feat.shape[1]
    for n in range(BASIS):
        hi, lo = split(own * radial[n : n + 1, :])
        for third, part in enumerate((hi, hi, lo)):
            tall[p, third * third_rows + n * TA : third * third_rows + (n + 1) * TA, :] = part
            wide[p, n * TA : (n + 1) * TA, third * channels : (third + 1) * channels] = part


OTHER, CENTRE, LIVE, SAME, SHARED, SENT = 0, 2, 4, 6, 8, 9
GHOST_ROWS = 8


def fetch(pairs, sems):
    copies = [pltpu.make_async_copy(src, dst, sems.at[i]) for i, (src, dst) in enumerate(pairs)]
    for copy in copies:
        copy.start()
    return copies


def upward(shift):
    return 1.0 - flag(place(shift, 2) == 1)


def either(choice, first, second):
    return first * choice + second * (1.0 - choice)


def gather_kernel(send, pos, feat, ref, to_second, to_first, token, send_v, pos_v, feat_v, ref_v, sems):
    copies = fetch([(send, send_v), (pos, pos_v), (ref, ref_v), (feat, feat_v)], sems)
    for copy in copies[:3]:
        copy.wait()
    low, high = lane_half()
    up = upward(0)
    sent = [send_v[0:1, j : j + 1].astype(F32) for j in range(2 * SEND)]
    tiles_of = []
    for out, choice in ((to_first, 1.0 - up), (to_second, up)):
        tiles = [either(choice, sent[j], sent[SEND + j]) for j in range(SEND)]
        tiles_of.append(tiles)
        out[SEND * TA :, :] = jnp.zeros((GHOST_ROWS, out.shape[1]), F32)
        for i in range(3):
            at = SEND * TA + i
            for lanes, source in ((slice(0, CHUNK), pos_v), (slice(CHUNK, 2 * CHUNK), ref_v)):
                chunks = [source[i, :, q * CHUNK : (q + 1) * CHUNK] for q in range(2)]
                out[at : at + 1, lanes] = paired(pick(chunks, tiles[0]), pick(chunks, tiles[1]))
        for other in range(2 * SEND):
            same = low * flag(sent[other] == tiles[0]) + high * flag(sent[other] == tiles[1])
            out[SEND * TA + 3 + other : SEND * TA + 4 + other, 0:CHUNK] = same
    token[...] = jnp.zeros_like(token)
    copies[3].wait()
    for out, tiles in zip((to_first, to_second), tiles_of):
        for j in range(SEND):
            out[j * TA : (j + 1) * TA, :] = pick_rows(feat_v.at[0], tiles[j], 0.0)


def pick_rows(ref, position, first):
    total = None
    for t in range(ref.shape[0] // TA):
        term = ref[t * TA : (t + 1) * TA, :] * flag(position == first + float(t))
        total = term if total is None else total + term
    return total


def stage_kernel(
    centre, other, live, send, pos, ref, species, feat, radial_w, mix_w, species_w, out_w, after,
    flags, atoms, own_feat, weights, mh, ml,
    centre_v, other_v, live_v, send_v, pos_v, ref_v, species_v, radial_v, mix_v, species_w_v, out_v, sems,
):
    copies = fetch(
        [
            (centre, centre_v), (other, other_v), (live, live_v), (send, send_v), (pos, pos_v), (ref, ref_v),
            (species, species_v), (radial_w, radial_v), (species_w, species_w_v), (out_w, out_v),
            (feat.at[0], own_feat), (mix_w, mix_v),
        ],
        sems,
    )
    for copy in copies[:-1]:
        copy.wait()
    flags[...] = jnp.zeros_like(flags)
    centres = [centre_v[0:1, p : p + 1].astype(F32) for p in range(PAIRS)]
    others = [other_v[0:1, p : p + 1].astype(F32) for p in range(PAIRS)]
    for p in range(PAIRS):
        for row, value in (
            (OTHER, others[p]),
            (CENTRE, centres[p]),
            (LIVE, live_v[0:1, p : p + 1].astype(F32)),
            (SAME, flag(others[p] == centres[p] + SEND)),
        ):
            flags[row + p : row + p + 1, :] = jnp.broadcast_to(value, (1, CHUNK))
    flags[SHARED : SHARED + 1, :] = jnp.broadcast_to(flag(centres[0] == centres[1]), (1, CHUNK))
    for j in range(2 * SEND):
        value = send_v[0:1, j : j + 1].astype(F32)
        flags[SENT + j : SENT + j + 1, :] = jnp.broadcast_to(value, (1, CHUNK))
    atoms[...] = jnp.zeros_like(atoms)
    for i in range(3):
        atoms[i : i + 1, :] = pos_v[i]
        atoms[4 + i : 5 + i, :] = ref_v[i]
    atoms[3:4, :] = species_v[...].astype(F32)
    weights[...] = jnp.zeros_like(weights)
    weights[0:BASIS, :] = radial_v[...]
    weights[BASIS : BASIS + SPECIES, :] = species_w_v[...]
    weights[BASIS + SPECIES : BASIS + SPECIES + 1, :] = out_v[...]
    copies[-1].wait()
    hi, lo = split(mix_v[...])
    mh[...] = hi
    ml[...] = lo


def force_kernel(
    flags, atoms, feat, weights, mh, ml, from_second, from_first,
    env, dinv, gate, curve, inv, rows, fsel, own, one_first, one_second, two_first, two_second, shape_store, tall, eh, el,
    square, turned, squares, others_sum, table, wide, steady, raw, back,
):
    ghost = SEND * TA
    up = upward(0)
    near, far = from_first[ghost : ghost + 3, 0:CHUNK], from_second[ghost : ghost + 3, 0:CHUNK]
    chunks = [either(up, far, near), atoms[0:3, 0:CHUNK], atoms[0:3, CHUNK:], either(up, near, far)]
    kinds = [atoms[3:4, q * CHUNK : (q + 1) * CHUNK] for q in range(2)]

    def number(row):
        return flags[row : row + 1, :]

    centres = [number(CENTRE + p) for p in range(PAIRS)]
    others = [number(OTHER + p) for p in range(PAIRS)]
    shared = flags[SHARED : SHARED + 1, 0:1]
    rows[...] = jnp.zeros_like(rows)
    rows[0:3, :] = paired(*(pick(chunks, others[p]) for p in range(PAIRS)))
    rows[3:6, :] = paired(*(pick(chunks[1:3], centres[p]) for p in range(PAIRS)))
    rows[6:7, :] = paired(*(pick(kinds, centres[p]) for p in range(PAIRS)))
    columns_of(rows[...], square, turned)

    for p in range(PAIRS):
        o = flags[OTHER + p : OTHER + p + 1, 0:1]
        fsel[p * TA : (p + 1) * TA, :] = (
            pick_rows(from_first.at[0:ghost], o, (SEND + 4) * up)
            + pick_rows(feat, o, float(SEND))
            + pick_rows(from_second.at[0:ghost], o, (SEND + 4) * (1.0 - up))
        )

    def forward(p):
        lane_rows = [twice_at(rows[i : i + 1, :], p) for i in range(3)]
        live, same = flags[pl.ds(LIVE + p, 1), :], flags[pl.ds(SAME + p, 1), :]
        for r in range(0, TA, STRIP):
            strip = span(p * TA + r, STRIP)
            columns = [turned[strip, 3 + i : 4 + i] for i in range(3)]
            unit, inverse, weight, slope, sine, cosine = geometry(lane_rows, columns, 1.0, live, same, r)
            angular = harmonics(unit)
            values, slopes = paired_orders(sine, cosine, weight, slope)
            for i, part in enumerate(unit + [inverse] + values + slopes):
                shape_store[p, i, r : r + STRIP, :] = part
            for m in range(COMPS):
                at = slice(m * TA + r, m * TA + r + STRIP)
                for k in range(BASIS // 2):
                    entry = values[k] if m == 0 else angular[m] * values[k]
                    put_left(table, p, at, k * CHUNK, CHUNK, entry)
        radial_feat(fsel, weights, p, tall, wide)
        raw[span(p * COMPS * TA, COMPS * TA), :] = long_product(table[p], tall[p], NN)

    slots(forward)

    for m in range(COMPS):
        first = raw[m * TA : (m + 1) * TA, :]
        second = raw[(COMPS + m) * TA : (COMPS + m + 1) * TA, :]
        env[m * TA : (m + 1) * TA, :] = env_scale * (first + shared * second)
        env[(COMPS + m) * TA : (COMPS + m + 1) * TA, :] = env_scale * (second + shared * first)
    for p in range(PAIRS):
        sums = [None] * 3
        for m in range(COMPS):
            block = env[(p * COMPS + m) * TA : (p * COMPS + m + 1) * TA, :]
            sums[GROUP[m]] = block * block if sums[GROUP[m]] is None else sums[GROUP[m]] + block * block
        for g in range(3):
            inv[p * TA : (p + 1) * TA, g * 256 : (g + 1) * 256] = sums[g]
    hidden = product(split(inv[...]), (mh[...], ml[...]), NN)
    kind = turned[:, 6:7]
    for s in range(SPECIES):
        hidden = hidden + flag(kind == float(s)) * weights[BASIS + s : BASIS + s + 1, :]
    out_row = weights[BASIS + SPECIES : BASIS + SPECIES + 1, :]
    sigma = 1.0 / (1.0 + jnp.exp(-hidden))
    first_order = sigma * (1.0 + hidden * (1.0 - sigma))
    gate[...] = first_order
    curve[...] = sigma * (1.0 - sigma) * (2.0 + hidden * (1.0 - 2.0 * sigma)) * out_row
    dinv[...] = product(split(first_order * out_row), (mh[...], ml[...]), NT)

    tile_grads = [jnp.zeros((3, CHUNK), F32) for _ in range(4)]

    def backward(p):
        here = span(p * TA, TA)
        for m in range(COMPS):
            block = env[span((p * COMPS + m) * TA, TA), :]
            part = dinv[here, GROUP[m] * 256 : (GROUP[m] + 1) * 256]
            at = slice(m * TA, (m + 1) * TA)
            hi, lo = split((2.0 * env_scale) * block * part)
            eh[p, at, :] = hi
            el[p, at, :] = lo
            for third, piece in enumerate((hi, lo, hi)):
                steady[p, at, third * 256 : (third + 1) * 256] = piece
        for ref in (eh, el):
            ref[p, COMPS * TA :, :] = jnp.zeros((WIDE - COMPS * TA, ref.shape[2]), BF16)
        back[p] = long_product(steady[p], wide[p], NT)
        summed = [jnp.zeros((1, CHUNK), F32) for _ in range(3)]
        for r in range(0, TA, STRIP):
            strip = slice(r, r + STRIP)
            x, y, z, inverse = (shape_store[p, i, strip, :] for i in range(4))
            values = [shape_store[p, 4 + k, strip, :] for k in range(BASIS // 2)]
            slopes = [shape_store[p, 8 + k, strip, :] for k in range(BASIS // 2)]
            angular = harmonics((x, y, z))
            d_radius = None
            g = []
            for m in range(COMPS):
                along, across = None, None
                for k in range(BASIS // 2):
                    block = back[p, m * TA + r : m * TA + r + STRIP, k * CHUNK : (k + 1) * CHUNK]
                    along = block * slopes[k] if along is None else along + block * slopes[k]
                    across = block * values[k] if across is None else across + block * values[k]
                g.append(across)
                term = along if m == 0 else along * angular[m]
                d_radius = term if d_radius is None else d_radius + term
            toward = [
                g[1] + root_three * (y * g[4] + z * g[6] + x * g[7]) - x * g[8],
                g[2] + root_three * (x * g[4] + z * g[5] - y * g[7]) - y * g[8],
                g[3] + root_three * (y * g[5] + x * g[6]) + 2.0 * (z * g[8]),
            ]
            radial_part = d_radius - inverse * (toward[0] * x + toward[1] * y + toward[2] * z)
            for i, v in enumerate((x, y, z)):
                d_offset = inverse * toward[i] + v * radial_part
                summed[i] = summed[i] + jnp.sum(d_offset, axis=0, keepdims=True)
                squares[i, span(p * TA + r, STRIP), :] = d_offset
        for i, part in enumerate(summed):
            others_sum[p, i : i + 1, :] = part + pltpu.roll(part, TA, 1)

    slots(backward)
    for i in range(3):
        centre_both = -jnp.sum(squares[i].T, axis=0, keepdims=True)
        component = flag(lax.broadcasted_iota(jnp.int32, (3, CHUNK), 0) == i)
        for p in range(PAIRS):
            centre_row = twice(centre_both, p)
            for q in range(4):
                at = chunk_mask(others[p], q) * others_sum[p, i : i + 1, :]
                if q in (1, 2):
                    at = at + chunk_mask(centres[p] + SEND, q) * centre_row
                tile_grads[q] = tile_grads[q] + at * component
    own[...] = jnp.zeros_like(own)
    own[0:3, 0:CHUNK] = tile_grads[1]
    own[0:3, CHUNK:] = tile_grads[2]
    own[3:6, 0:CHUNK] = tile_grads[0]
    own[3:6, CHUNK:] = tile_grads[3]
    leaving = []
    for first, ghost_grad in ((0, tile_grads[0]), (SEND, tile_grads[3])):
        listed = paired(*(pick(tile_grads[1:3], number(SENT + first + j)) for j in range(SEND)))
        leaving.append((listed, ghost_grad))
    for shift, outs in ((0, (one_first, one_second)), (1, (two_first, two_second))):
        choice = upward(shift)
        for out, above in zip(outs, (choice, 1.0 - choice)):
            out[...] = jnp.zeros_like(out)
            out[0:3, :] = either(above, leaving[1][0], leaving[0][0])
            out[3:6, :] = either(above, leaving[1][1], leaving[0][1])


def tangent_kernel(
    scale, flags, atoms, weights, mh, ml, from_first, from_second, own, one_second, two_second, one_first, two_first,
    rows, env, gate, curve, inv, shape_store, tall, after,
    forces, keep, give, small, envdot, curl, both,
    square, turned, table, raw, left, right,
):
    ghost = SEND * TA
    def number(row):
        return flags[row : row + 1, :]

    centres = [number(CENTRE + p) for p in range(PAIRS)]
    others = [number(OTHER + p) for p in range(PAIRS)]
    shared = flags[SHARED : SHARED + 1, 0:1]
    mine = [own[0:3, 0:CHUNK], own[0:3, CHUNK:]]
    up, up_two = upward(0), upward(1)
    low_one = either(up, one_second[...], one_first[...])
    high_one = either(up, one_first[...], one_second[...])
    low_two = either(up_two, two_second[...], two_first[...])
    high_two = either(up_two, two_first[...], two_second[...])
    low_tail = either(up, from_second[ghost:, :], from_first[ghost:, :])
    high_tail = either(up, from_first[ghost:, :], from_second[ghost:, :])
    arrived = [twice(low_one[3:6, :], j) for j in range(SEND)]
    arrived += [twice(high_one[3:6, :], j) for j in range(SEND)]
    for j in range(2 * SEND):
        for q in range(2):
            mine[q] = mine[q] + chunk_mask(number(SENT + j), q) * arrived[j]
    below = low_one[0:3, :]
    above = high_one[0:3, :]
    to_below = [twice(low_two[3:6, :], j) for j in range(SEND)]
    to_below += [twice(own[3:6, 0:CHUNK], j) for j in range(SEND)]
    to_above = [twice(own[3:6, CHUNK:], j) for j in range(SEND)]
    to_above += [twice(high_two[3:6, :], j) for j in range(SEND)]
    for j in range(2 * SEND):
        below = below + low_tail[3 + j : 4 + j, 0:CHUNK] * to_below[j]
        above = above + high_tail[3 + j : 4 + j, 0:CHUNK] * to_above[j]
    for q in range(2):
        for i in range(3):
            forces[i, :, q * CHUNK : (q + 1) * CHUNK] = -mine[q][i : i + 1, :]
    error = [
        below + low_tail[0:3, CHUNK:],
        mine[0] + atoms[4:7, 0:CHUNK],
        mine[1] + atoms[4:7, CHUNK:],
        above + high_tail[0:3, CHUNK:],
    ]
    error = [part * scale for part in error]
    both[...] = jnp.zeros_like(both)
    both[0:8, :] = rows[...]
    both[8:11, :] = paired(*(pick(error, others[p]) for p in range(PAIRS)))
    both[11:14, :] = paired(*(pick(error[1:3], centres[p]) for p in range(PAIRS)))
    columns_of(both[...], square, turned)

    def moved(p):
        lane_move = [twice_at(both[8 + i : 9 + i, :], p) for i in range(3)]
        for r in range(0, TA, STRIP):
            strip = slice(r, r + STRIP)
            here = span(p * TA + r, STRIP)
            column_move = [turned[here, 11 + i : 12 + i] for i in range(3)]
            unit = [shape_store[p, i, strip, :] for i in range(3)]
            inverse = shape_store[p, 3, strip, :]
            move = [a - b for a, b in zip(lane_move, column_move)]
            stretch = unit[0] * move[0] + unit[1] * move[1] + unit[2] * move[2]
            turn = [(m - v * stretch) * inverse for m, v in zip(move, unit)]
            angular, turning = harmonics(unit), harmonics_tangent(unit, turn)
            for k in range(BASIS // 2):
                value = shape_store[p, 4 + k, strip, :]
                slope = shape_store[p, 8 + k, strip, :] * stretch
                for m in range(COMPS):
                    at = slice(m * TA + r, m * TA + r + STRIP)
                    entry = slope if m == 0 else angular[m] * slope + turning[m] * value
                    put_left(table, p, at, k * CHUNK, CHUNK, entry)
        raw[span(p * COMPS * TA, COMPS * TA), :] = long_product(table[p], tall[p], NN)

    slots(moved)

    for m in range(COMPS):
        first = raw[m * TA : (m + 1) * TA, :]
        second = raw[(COMPS + m) * TA : (COMPS + m + 1) * TA, :]
        envdot[m * TA : (m + 1) * TA, :] = env_scale * (first + shared * second)
        envdot[(COMPS + m) * TA : (COMPS + m + 1) * TA, :] = env_scale * (second + shared * first)
    invdot = left
    half = PAIRS * TA
    for p in range(PAIRS):
        sums = [None] * 3
        for m in range(COMPS):
            at = slice((p * COMPS + m) * TA, (p * COMPS + m + 1) * TA)
            term = 2.0 * env[at, :] * envdot[at, :]
            sums[GROUP[m]] = term if sums[GROUP[m]] is None else sums[GROUP[m]] + term
        for g in range(3):
            invdot[half + p * TA : half + (p + 1) * TA, g * 256 : (g + 1) * 256] = sums[g]
    invdot[0:half, :] = inv[...]
    hidden_move = product(split(invdot[half:, :]), (mh[...], ml[...]), NN)
    bend = curve[...] * hidden_move
    curl[...] = bend
    once = 1.0 - shared * flag(lax.broadcasted_iota(jnp.int32, (half, 1), 0) >= TA)
    right[0:half, :] = bend * once
    right[half:, :] = gate[...] * weights[BASIS + SPECIES : BASIS + SPECIES + 1, :] * once
    raw[0 : left.shape[1], :] = product(split(left[...]), split(right[...]), TN)
    core = lax.axis_index("batch")
    for out, part in ((keep, core), (give, 1 - core)):
        out[...] = raw[0 : left.shape[1], block_of_lanes(part)]
    small[...] = jnp.zeros_like(small)
    kind = turned[:, 6:7]
    for s in range(SPECIES):
        small[s : s + 1, :] = jnp.sum(right[0:half, :] * flag(kind == float(s)), axis=0, keepdims=True)
    small[SPECIES : SPECIES + 1, :] = jnp.sum(gate[...] * hidden_move * once, axis=0, keepdims=True)


def table_kernel(flags, rows, shape_store, lh, ll, token, square, turned):
    low, high = lane_half()
    token[...] = jnp.zeros_like(token)
    columns_of(rows[...], square, turned)
    for p in range(PAIRS):
        lane_rows = [twice(rows[3 + i : 4 + i, :], p) for i in range(3)]
        for r in range(0, TA, STRIP):
            columns = [turned[p * TA + r : p * TA + r + STRIP, i : i + 1] for i in range(3)]
            unit, inverse, weight, slope, sine, cosine = geometry(
                lane_rows, columns, -1.0, flags[LIVE + p : LIVE + p + 1, :], flags[SAME + p : SAME + p + 1, :], r
            )
            angular = harmonics(unit)
            values, slopes = single_orders(sine, cosine, weight, slope)
            for i, part in enumerate(unit + [inverse] + values + slopes):
                shape_store[p, i, r : r + STRIP, :] = part
            for m in range(0, COMPS + 1, 2):
                factor = low if m == 0 else angular[m] * low
                if m + 1 < COMPS:
                    factor = factor + angular[m + 1] * high
                for n in range(BASIS):
                    hi, lo = split(factor * values[n])
                    lh[p, n * TA + r : n * TA + r + STRIP, m * TA : (m + 2) * TA] = hi
                    ll[p, n * TA + r : n * TA + r + STRIP, m * TA : (m + 2) * TA] = lo


def radial_kernel(
    p, both, shape_store, lh, ll, eh, el, fsel, env, envdot, dinv, curl, mh, ml, after,
    grad_radial,
    square, turned, sh, sl, gh, gl, raw,
):
    low, high = lane_half()
    columns_of(both[...], square, turned)
    here = slice(p * TA, (p + 1) * TA)
    turn_inv = product(split(curl[here, :]), (mh[...], ml[...]), NT)
    lane_move = [twice(both[11 + i : 12 + i, :], p) for i in range(3)]
    sh[:, 0:CHUNK] = lh[p, :, WIDE - CHUNK :]
    sl[:, 0:CHUNK] = ll[p, :, WIDE - CHUNK :]
    for r in range(0, TA, STRIP):
        strip = slice(r, r + STRIP)
        column_move = [turned[p * TA + r : p * TA + r + STRIP, 8 + i : 9 + i] for i in range(3)]
        unit = [shape_store[p, i, strip, :] for i in range(3)]
        inverse = shape_store[p, 3, strip, :]
        move = [b - a for a, b in zip(lane_move, column_move)]
        stretch = unit[0] * move[0] + unit[1] * move[1] + unit[2] * move[2]
        turn = [(m - v * stretch) * inverse for m, v in zip(move, unit)]
        angular, turning = harmonics(unit), harmonics_tangent(unit, turn)
        on_values, on_slopes = [turning[1] * high], [(low + angular[1] * high) * stretch]
        for m in range(2, COMPS + 1, 2):
            on_value, on_slope = turning[m] * low, angular[m] * low
            if m + 1 < COMPS:
                on_value = on_value + turning[m + 1] * high
                on_slope = on_slope + angular[m + 1] * high
            on_values.append(on_value)
            on_slopes.append(on_slope * stretch)
        for n in range(BASIS):
            value, slope = shape_store[p, 4 + n, strip, :], shape_store[p, 4 + BASIS + n, strip, :]
            for j, (on_value, on_slope) in enumerate(zip(on_values, on_slopes)):
                hi, lo = split(on_value * value + on_slope * slope)
                sh[n * TA + r : n * TA + r + STRIP, (j + 1) * CHUNK : (j + 2) * CHUNK] = hi
                sl[n * TA + r : n * TA + r + STRIP, (j + 1) * CHUNK : (j + 2) * CHUNK] = lo
    for m in range(COMPS):
        at = slice((p * COMPS + m) * TA, (p * COMPS + m + 1) * TA)
        group = slice(GROUP[m] * 256, (GROUP[m] + 1) * 256)
        steady = (2.0 * env_scale) * dinv[here, group]
        bent = (2.0 * env_scale) * turn_inv[:, group]
        hi, lo = split(env[at, :] * bent + envdot[at, :] * steady)
        gh[m * TA : (m + 1) * TA, :] = hi
        gl[m * TA : (m + 1) * TA, :] = lo
    for ref, tail in ((gh, eh), (gl, el)):
        ref[COMPS * TA : WIDE, :] = jnp.zeros((WIDE - COMPS * TA, ref.shape[1]), BF16)
        ref[WIDE:, :] = tail[p]
    first = WIDE - CHUNK
    raw[...] = product((lh[p, :, 0:first], ll[p, :, 0:first]), (gh[0:first, :], gl[0:first, :]), NN) + product(
        (sh[...], sl[...]), (gh[first:, :], gl[first:, :]), NN
    )
    for n in range(BASIS):
        grad_radial[n : n + 1, :] = jnp.sum(
            raw[n * TA : (n + 1) * TA, :] * fsel[here, :], axis=0, keepdims=True
        )


SMALL = 32
PAD = 8
FOUR = 4


def block_of(part, rows):
    return pl.ds(pl.multiple_of(part * rows, 8), rows)


def block_from(start, rows):
    return pl.ds(pl.multiple_of(start, 8), rows)


def block_of_lanes(part):
    return pl.ds(pl.multiple_of(part * HALF, HALF), HALF)


def total_of(refs, at):
    total = refs[0][at, :]
    for ref in refs[1:]:
        total = total + ref[at, :]
    return total


def halve_kernel(keep, taken, after, *outs):
    half, piece = keep.shape[0] // 2, keep.shape[0] // (2 * FOUR)
    mine, me = place(0, 2), place(1, FOUR)
    for i, out in enumerate(outs):
        part = mine if i < 2 else 1 - mine
        for j in range(2):
            k = 1 + 2 * (i % 2) - j
            at = block_from(part * half + lax.bitwise_xor(me, k) * piece, piece)
            out[j * piece : (j + 1) * piece, :] = keep[at, :] + taken[at, :]
        if out.shape[0] > 2 * piece:
            out[2 * piece :, :] = jnp.zeros((out.shape[0] - 2 * piece, HALF), F32)


def spread_kernel(first, keep, taken, radial_0, radial_1, small, after, out_0, out_1, tiny):
    for h in range(2):
        lanes = slice(h * HALF, (h + 1) * HALF)
        tiny[16 * h : 16 * h + 8, :] = radial_0[:, lanes] + radial_1[:, lanes]
        tiny[16 * h + 8 : 16 * h + 16, :] = small[:, lanes]
    me = place(1, FOUR)
    few = SMALL // FOUR
    rows = keep.shape[0] // 2
    for j, out in enumerate((out_0, out_1)):
        out[0:rows, :] = total_of([keep, taken], slice(j * rows, (j + 1) * rows))
        out[rows : rows + few, :] = tiny[block_of(lax.bitwise_xor(me, first - j), few), :]
        if out.shape[0] > rows + few:
            out[rows + few :, :] = jnp.zeros((out.shape[0] - rows - few, HALF), F32)


def total_kernel(*refs):
    refs[-1][...] = total_of(refs[:-1], slice(0, refs[-1].shape[0]))


def near_kernel(mine, third, out):
    rows = mine.shape[0] - SMALL // FOUR
    out[0:rows, :] = mine[0:rows, :]
    out[rows : 2 * rows, :] = third[0:rows, :]
    out[2 * rows :, :] = jnp.zeros((out.shape[0] - 2 * rows, HALF), F32)


def rest_kernel(mine, first, second, third, after, out):
    few = SMALL // FOUR
    rows = mine.shape[0] - few
    out[0:rows, :] = second[0:rows, :]
    out[rows : 2 * rows, :] = first[0:rows, :]
    me = place(1, FOUR)
    for k, ref in enumerate((mine, first, second, third)):
        out[block_from(2 * rows + lax.bitwise_xor(me, k) * few, few), :] = ref[rows:, :]


def pair_kernel(near, rest, their_near, their_rest, out):
    piece = (rest.shape[0] - SMALL) // 2
    half = FOUR * piece
    mine, me = place(0, 2), place(1, FOUR)
    for refs, part in (((near, rest), mine), ((their_near, their_rest), 1 - mine)):
        for ref, ks in zip(refs, ((0, 3), (2, 1))):
            for j, k in enumerate(ks):
                at = block_from(part * half + lax.bitwise_xor(me, k) * piece, piece)
                out[at, :] = ref[j * piece : (j + 1) * piece, :]
    out[2 * half :, :] = rest[2 * piece :, :] + their_rest[2 * piece :, :]


def join_kernel(whole, facing, mix, radial, kinds, out):
    rows = mix.shape[0]
    core = lax.axis_index("batch")
    for ref, part in ((whole, core), (facing, 1 - core)):
        mix[:, block_of_lanes(part)] = ref[0:rows, :]
    both = whole[rows:, :] + facing[rows:, :]
    for h in range(2):
        lanes = slice(h * HALF, (h + 1) * HALF)
        few = both[16 * h : 16 * h + 16, :]
        radial[:, lanes] = few[0:BASIS]
        kinds[:, lanes] = few[BASIS : BASIS + SPECIES]
        out[:, lanes] = few[BASIS + SPECIES : BASIS + SPECIES + 1]


def spec(space):
    return pl.BlockSpec(memory_space=space)


def call(kernel, name, outs, scratch, *operands, space=pltpu.VMEM, after=(), flops=0):
    if space is pltpu.HBM:
        operands = [pltpu.with_memory_space_constraint(operand, space) for operand in operands]
    outs = [out if len(out) == 2 and isinstance(out[0], tuple) else (out, F32) for out in outs]
    return pl.pallas_call(
        kernel,
        name=name,
        out_shape=[jax.ShapeDtypeStruct(*out) for out in outs],
        in_specs=[spec(space)] * len(operands) + [spec(pltpu.VMEM)] * len(after),
        out_specs=[spec(pltpu.VMEM)] * len(outs),
        scratch_shapes=[pltpu.VMEM(*item) if isinstance(item, tuple) else item for item in scratch],
        compiler_params=pltpu.CompilerParams(vmem_limit_bytes=28 * 1024 * 1024),
        cost_estimate=pl.CostEstimate(flops=flops, bytes_accessed=1 << 20 if flops else 1 << 10, transcendentals=0),
    )(*operands, *after)


def shifted(block, axis, by):
    count = lax.axis_size(axis)
    return lax.ppermute(block, axis, [(i, (i + by) % count) for i in range(count)])


def exchanged(block, shift, first):
    count, step = lax.axis_size("domain"), 1 << shift
    up = [((i >> shift) & 1 == 0) == first for i in range(count)]
    return lax.ppermute(block, "domain", [(i, (i + step if up[i] else i - step) % count) for i in range(count)])


def partner(block, mask):
    return lax.ppermute(block, "domain", [(i, i ^ mask) for i in range(lax.axis_size("domain"))])


def on_device(
    positions,
    features,
    species,
    ref_forces,
    centre_tile,
    other_tile,
    pair_live,
    send_tiles,
    radial_w,
    mix_w,
    species_w,
    out_w,
):
    atoms_here = positions.shape[2]
    channels = features.shape[2]
    table = (COMPS * TA, BASIS * TA)
    sent = (SEND * TA + GHOST_ROWS, channels)
    slots = PAIRS * TA
    line = (3, 1, atoms_here)
    turning = [((CHUNK, CHUNK), F32)] * 2
    out_row = out_w.reshape(1, channels)
    positions = positions.transpose(1, 0, 2)
    ref_forces = ref_forces.transpose(1, 0, 2)
    ints = [((1, n), jnp.int32) for n in (PAIRS, PAIRS, PAIRS, 2 * SEND)]

    to_second, to_first, token = call(
        gather_kernel,
        "gather",
        [sent, sent, (8, CHUNK)],
        [
            ints[3],
            (line, F32),
            ((1, atoms_here, channels), F32),
            (line, F32),
            pltpu.SemaphoreType.DMA((4,)),
        ],
        send_tiles, positions, features, ref_forces,
        space=pltpu.HBM,
    )
    from_second = exchanged(to_second, 0, False)
    from_first = exchanged(to_first, 0, True)
    flags, atoms, own_feat, weights, mh, ml = call(
        stage_kernel,
        "stage",
        [
            (16, CHUNK),
            (8, atoms_here),
            (atoms_here, channels),
            (16, channels),
            (mix_w.shape, BF16),
            (mix_w.shape, BF16),
        ],
        ints
        + [(line, F32), (line, F32), ((1, atoms_here), jnp.int32)]
        + [(radial_w.shape, F32), (mix_w.shape, F32), (species_w.shape, F32), (out_row.shape, F32)]
        + [pltpu.SemaphoreType.DMA((12,))],
        centre_tile, other_tile, pair_live, send_tiles, positions, ref_forces, species, features,
        radial_w, mix_w, species_w, out_row,
        space=pltpu.HBM,
        after=(token,),
    )

    long_table = (PAIRS, COMPS * TA, 3 * BASIS * TA)
    env, dinv, gate, curve, inv, rows, fsel, own, *leaving, shape_store, tall, eh, el = call(
        force_kernel,
        "force",
        [
            (PAIRS * COMPS * TA, channels),
            (slots, 3 * channels),
            (slots, channels),
            (slots, channels),
            (slots, 3 * channels),
            (8, CHUNK),
            (slots, channels),
            (8, atoms_here),
            (8, CHUNK),
            (8, CHUNK),
            (8, CHUNK),
            (8, CHUNK),
            (PAIRS, 4 + BASIS, TA, CHUNK),
            ((PAIRS, 3 * BASIS * TA, channels), BF16),
            ((PAIRS, WIDE, channels), BF16),
            ((PAIRS, WIDE, channels), BF16),
        ],
        turning
        + [((3, CHUNK, CHUNK), F32), ((PAIRS, 8, CHUNK), F32)]
        + [(long_table, BF16), ((PAIRS, BASIS * TA, 3 * channels), BF16)]
        + [((PAIRS, COMPS * TA, 3 * channels), BF16)]
        + [((PAIRS * COMPS * TA, channels), F32), ((PAIRS, *table), F32)],
        flags, atoms, own_feat, weights, mh, ml, from_second, from_first,
        flops=1 << 31,
    )
    arriving = [exchanged(leaving[i], i // 2, i % 2 == 0) for i in (1, 3, 0, 2)]

    table_shape, lh, ll, token = call(
        table_kernel,
        "table",
        [
            (PAIRS, 4 + 2 * BASIS, TA, CHUNK),
            ((PAIRS, BASIS * TA, WIDE), BF16),
            ((PAIRS, BASIS * TA, WIDE), BF16),
            (8, CHUNK),
        ],
        turning,
        flags, rows,
        flops=1 << 30,
    )

    rows_mix = 3 * channels
    total_count = 3.0 * atoms_here * lax.axis_size("domain") * lax.axis_size("batch")
    forces, keep, give, small, envdot, curl, both = call(
        functools.partial(tangent_kernel, 2.0 / math.sqrt(total_count)),
        "tangent",
        [
            line,
            (rows_mix, HALF),
            (rows_mix, HALF),
            (8, channels),
            (PAIRS * COMPS * TA, channels),
            (slots, channels),
            (16, CHUNK),
        ],
        turning
        + [(long_table, BF16)]
        + [((PAIRS * COMPS * TA, channels), F32)]
        + [((2 * slots, 3 * channels), F32), ((2 * slots, channels), F32)],
        flags, atoms, weights, mh, ml, from_first, from_second, own, *arriving,
        rows, env, gate, curve, inv, shape_store, tall, token,
        flops=1 << 31,
    )

    def radial(p, after):
        return call(
            functools.partial(radial_kernel, p),
            "radial",
            [(BASIS, channels)],
            turning
            + [((BASIS * TA, CHUNK + WIDE), BF16)] * 2
            + [((2 * WIDE, channels), BF16)] * 2
            + [((BASIS * TA, channels), F32)],
            both, table_shape, lh, ll, eh, el, fsel, env, envdot, dinv, curl, mh, ml, after,
            flops=1 << 31 if p == 0 else 0,
        )[0]

    radials = [radial(0, both)]
    piece = rows_mix // (2 * FOUR)
    few = SMALL // FOUR
    near, far, give_near, give_far = call(
        halve_kernel, "halve", [(2 * piece, HALF)] * 3 + [(2 * piece + PAD, HALF)], [],
        keep, shifted(give, "batch", 1), radials[0],
    )
    radials.append(radial(1, far))
    blocks = []
    after = radials[1]
    taken_near = partner(give_near, 1)
    taken_far = partner(give_far, 1)
    for first, kept, taken in ((3, far, taken_far), (1, near, taken_near)):
        blocks += call(
            functools.partial(spread_kernel, first),
            "spread", [(piece + few + PAD * k, HALF) for k in (first - 1, max(first - 2, 0))], [((SMALL, HALF), F32)],
            kept, taken, *radials, small, after,
        )
        after = blocks[0]
    terms = [blocks[3]] + [partner(blocks[3 - k], 2 * k) for k in range(FOUR - 1, 0, -1)]
    (mine,) = call(total_kernel, "total", [(piece + few, HALF)], [], *terms)
    bit = 2 * FOUR
    while bit < lax.axis_size("domain"):
        (mine,) = call(total_kernel, "total", [(piece + few, HALF)], [], mine, partner(mine, bit))
        bit *= 2
    parts = [mine] + [partner(mine, 2 * k) for k in range(1, FOUR)]
    (near,) = call(near_kernel, "near", [(2 * piece + SMALL + PAD, HALF)], [], mine, parts[3])
    their_near = partner(near, 1)
    (rest,) = call(rest_kernel, "rest", [(2 * piece + SMALL, HALF)], [], *parts, near)
    their_rest = partner(rest, 1)
    (whole,) = call(
        pair_kernel, "pair", [(rows_mix + SMALL, HALF)], [], near, rest, their_near, their_rest
    )
    facing = shifted(whole, "batch", 1)
    mix, radial_sum, kinds, out = call(
        join_kernel,
        "join",
        [(rows_mix, channels), (BASIS, channels), (SPECIES, channels), (1, channels)],
        [],
        whole,
        facing,
    )
    return forces.transpose(1, 0, 2), radial_sum, mix, kinds, out.reshape(channels)


def solution(mesh):
    return jax.shard_map(
        on_device,
        mesh=mesh,
        in_specs=(
            P(("parts", "batch"), None, "domain"),
            P(("parts", "batch"), "domain", None),
            P(("parts", "batch"), "domain"),
            P(("parts", "batch"), None, "domain"),
            P(("parts", "batch"), "domain"),
            P(("parts", "batch"), "domain"),
            P(("parts", "batch"), "domain"),
            P(("parts", "batch"), "domain"),
            P(),
            P(),
            P(),
            P(),
        ),
        out_specs=(
            P(("parts", "batch"), None, "domain"),
            P("parts", None),
            P("parts", None),
            P("parts", None),
            P("parts"),
        ),
        check_vma=False,
    )
```

```python
import functools
import math

import jax
import jax.numpy as jnp
from jax import lax
from jax.experimental import pallas as pl
from jax.experimental.pallas import tpu as pltpu
from jax.sharding import PartitionSpec as P

TA = 64
SEND = 2
PAIRS = 2
COMPS = 9
STRIP = 16
WIDE = 10 * TA
BASIS = 8
SPECIES = 4
HALF = 128
CHUNK = 2 * TA

cutoff = 2.5
soften = 0.25
env_scale = 0.25
root_three = math.sqrt(3.0)
F32 = jnp.float32
BF16 = jnp.bfloat16
NN = (((1,), (0,)), ((), ()))
NT = (((1,), (1,)), ((), ()))
TN = (((0,), (0,)), ((), ()))
GROUP = (0, 1, 1, 1, 2, 2, 2, 2, 2)


def split(value):
    high = value.astype(BF16)
    return high, (value - high.astype(F32)).astype(BF16)


def product(left, right, dims):
    (lh, ll), (rh, rl) = left, right

    def one(x, y):
        return lax.dot_general(x, y, dims, preferred_element_type=F32)

    return one(lh, rh) + (one(lh, rl) + one(ll, rh))


def long_product(left, right, dims):
    return lax.dot_general(left, right, dims, preferred_element_type=F32)


def put_left(ref, p, rows, lane, width, value):
    hi, lo = split(value)
    span = ref.shape[2] // 3
    for third, part in enumerate((hi, lo, hi)):
        at = third * span + lane
        ref[p, rows, at : at + width] = part


def flag(condition):
    return jnp.where(condition, 1.0, 0.0).astype(F32)


def place(shift, width):
    return lax.bitwise_and(lax.shift_right_logical(lax.axis_index("domain"), shift), width - 1)


def lane_half():
    lane = lax.broadcasted_iota(jnp.int32, (1, CHUNK), 1)
    low = flag(lane < TA)
    return low, 1.0 - low


def twice(chunk, half):
    low, high = lane_half()
    swapped = pltpu.roll(chunk, TA, 1)
    return chunk * low + swapped * high if half == 0 else swapped * low + chunk * high


def pick(chunks, position):
    total = None
    for q, chunk in enumerate(chunks):
        for half in range(2):
            term = twice(chunk, half) * flag(position == 2 * q + half)
            total = term if total is None else total + term
    return total


def paired(first, second):
    low, high = lane_half()
    return first * low + second * high


def chunk_mask(position, q):
    low, high = lane_half()
    return low * flag(position == 2 * q) + high * flag(position == 2 * q + 1)


def series(angle):
    square = angle * angle
    sine, cosine = 1.0 / math.factorial(13), -1.0 / math.factorial(14)
    for order in range(11, 0, -2):
        sine = sine * square + (-1.0) ** (order // 2) / math.factorial(order)
    for order in range(12, -1, -2):
        cosine = cosine * square + (-1.0) ** (order // 2) / math.factorial(order)
    return sine * angle, cosine


def geometry(lane_rows, columns, sign, live, same, first):
    offset = [(row - column) * sign for row, column in zip(lane_rows, columns)]
    dist_sq = offset[0] * offset[0] + offset[1] * offset[1] + offset[2] * offset[2] + soften
    inverse = lax.rsqrt(dist_sq)
    inverse = inverse * (1.5 - 0.5 * dist_sq * inverse * inverse)
    unit = [x * inverse for x in offset]
    row = lax.broadcasted_iota(jnp.int32, (STRIP, CHUNK), 0) + first
    lane = lax.broadcasted_iota(jnp.int32, (STRIP, CHUNK), 1)
    lane = jnp.where(lane >= TA, lane - TA, lane)
    mask = live * (1.0 - same * flag(row == lane))
    base = jnp.maximum(1.0 - dist_sq * (1.0 / (cutoff * cutoff)), 0.0)
    weight = base * base * base * mask * inverse
    slope = -(6.0 / (cutoff * cutoff)) * base * base * mask - weight * inverse
    turned = jnp.minimum(dist_sq * inverse, cutoff) * (math.pi / cutoff) - 0.5 * math.pi
    sine, cosine = series(turned)
    return unit, inverse, weight, slope, cosine, -sine


def harmonics(v):
    x, y, z = v
    return [
        None,
        x,
        y,
        z,
        root_three * x * y,
        root_three * y * z,
        root_three * z * x,
        0.5 * root_three * (x * x - y * y),
        z * z - 0.5 * (x * x + y * y),
    ]


def harmonics_tangent(v, t):
    x, y, z = v
    a, b, c = t
    return [
        None,
        a,
        b,
        c,
        root_three * (a * y + x * b),
        root_three * (b * z + y * c),
        root_three * (c * x + z * a),
        root_three * (x * a - y * b),
        2.0 * z * c - (x * a + y * b),
    ]


def paired_orders(sine, cosine, weight, slope):
    low, high = lane_half()
    double_s, double_c = 2.0 * sine * cosine, 1.0 - 2.0 * sine * sine
    now_s = sine * low + double_s * high
    now_c = cosine * low + double_c * high
    old_s = -sine * low
    old_c = cosine * low + high
    values, slopes = [], []
    for k in range(BASIS // 2):
        order = ((2 * k + 1) * low + (2 * k + 2) * high) * (math.pi / cutoff)
        values.append(now_s * weight)
        slopes.append(now_c * (weight * order) + now_s * slope)
        now_s, old_s = 2.0 * double_c * now_s - old_s, now_s
        now_c, old_c = 2.0 * double_c * now_c - old_c, now_c
    return values, slopes


def single_orders(sine, cosine, weight, slope):
    now_s, now_c = sine, cosine
    old_s, old_c = jnp.zeros_like(sine), jnp.ones_like(cosine)
    values, slopes = [], []
    for n in range(1, BASIS + 1):
        values.append(now_s * weight)
        slopes.append(now_c * (weight * (n * math.pi / cutoff)) + now_s * slope)
        now_s, old_s = 2.0 * cosine * now_s - old_s, now_s
        now_c, old_c = 2.0 * cosine * now_c - old_c, now_c
    return values, slopes


def columns_of(rows, square, turned):
    square[...] = jnp.zeros_like(square)
    square[0 : rows.shape[0], :] = rows
    turned[...] = square[...].T


def pair_rows(first, p):
    return twice(first, p)


def radial_feat(feat, radial, p, tall, wide):
    own = feat[p * TA : (p + 1) * TA, :]
    span, channels = BASIS * TA, feat.shape[1]
    for n in range(BASIS):
        hi, lo = split(own * radial[n : n + 1, :])
        for third, part in enumerate((hi, hi, lo)):
            tall[p, third * span + n * TA : third * span + (n + 1) * TA, :] = part
            wide[p, n * TA : (n + 1) * TA, third * channels : (third + 1) * channels] = part


OTHER, CENTRE, LIVE, SAME, SHARED, SENT = 0, 2, 4, 6, 8, 9
GHOST_ROWS = 8


def fetch(pairs, sems):
    copies = [pltpu.make_async_copy(src, dst, sems.at[i]) for i, (src, dst) in enumerate(pairs)]
    for copy in copies:
        copy.start()
    return copies


def upward(shift):
    return 1.0 - flag(place(shift, 2) == 1)


def either(choice, first, second):
    return first * choice + second * (1.0 - choice)


def gather_kernel(send, pos, feat, ref, to_second, to_first, token, send_v, pos_v, feat_v, ref_v, sems):
    copies = fetch([(send, send_v), (pos, pos_v), (ref, ref_v), (feat, feat_v)], sems)
    for copy in copies[:3]:
        copy.wait()
    low, high = lane_half()
    up = upward(0)
    sent = [send_v[0:1, j : j + 1].astype(F32) for j in range(2 * SEND)]
    tiles_of = []
    for out, choice in ((to_first, 1.0 - up), (to_second, up)):
        tiles = [either(choice, sent[j], sent[SEND + j]) for j in range(SEND)]
        tiles_of.append(tiles)
        out[SEND * TA :, :] = jnp.zeros((GHOST_ROWS, out.shape[1]), F32)
        for i in range(3):
            at = SEND * TA + i
            for lanes, source in ((slice(0, CHUNK), pos_v), (slice(CHUNK, 2 * CHUNK), ref_v)):
                chunks = [source[i, :, q * CHUNK : (q + 1) * CHUNK] for q in range(2)]
                out[at : at + 1, lanes] = paired(pick(chunks, tiles[0]), pick(chunks, tiles[1]))
        for other in range(2 * SEND):
            same = low * flag(sent[other] == tiles[0]) + high * flag(sent[other] == tiles[1])
            out[SEND * TA + 3 + other : SEND * TA + 4 + other, 0:CHUNK] = same
    token[...] = jnp.zeros_like(token)
    copies[3].wait()
    for out, tiles in zip((to_first, to_second), tiles_of):
        for j in range(SEND):
            out[j * TA : (j + 1) * TA, :] = pick_rows(feat_v.at[0], tiles[j], 0.0)


def pick_rows(ref, position, first):
    total = None
    for t in range(ref.shape[0] // TA):
        term = ref[t * TA : (t + 1) * TA, :] * flag(position == first + float(t))
        total = term if total is None else total + term
    return total


def stage_kernel(
    centre, other, live, send, pos, ref, species, feat, radial_w, mix_w, species_w, out_w, after,
    flags, atoms, own_feat, weights, mh, ml, nh, nl,
    centre_v, other_v, live_v, send_v, pos_v, ref_v, species_v, radial_v, mix_v, species_w_v, out_v, sems,
):
    copies = fetch(
        [
            (centre, centre_v), (other, other_v), (live, live_v), (send, send_v), (pos, pos_v), (ref, ref_v),
            (species, species_v), (radial_w, radial_v), (species_w, species_w_v), (out_w, out_v),
            (feat.at[0], own_feat), (mix_w, mix_v),
        ],
        sems,
    )
    for copy in copies[:-1]:
        copy.wait()
    flags[...] = jnp.zeros_like(flags)
    centres = [centre_v[0:1, p : p + 1].astype(F32) for p in range(PAIRS)]
    others = [other_v[0:1, p : p + 1].astype(F32) for p in range(PAIRS)]
    for p in range(PAIRS):
        for row, value in (
            (OTHER, others[p]),
            (CENTRE, centres[p]),
            (LIVE, live_v[0:1, p : p + 1].astype(F32)),
            (SAME, flag(others[p] == centres[p] + SEND)),
        ):
            flags[row + p : row + p + 1, :] = jnp.broadcast_to(value, (1, CHUNK))
    flags[SHARED : SHARED + 1, :] = jnp.broadcast_to(flag(centres[0] == centres[1]), (1, CHUNK))
    for j in range(2 * SEND):
        value = send_v[0:1, j : j + 1].astype(F32)
        flags[SENT + j : SENT + j + 1, :] = jnp.broadcast_to(value, (1, CHUNK))
    atoms[...] = jnp.zeros_like(atoms)
    for i in range(3):
        atoms[i : i + 1, :] = pos_v[i]
        atoms[4 + i : 5 + i, :] = ref_v[i]
    atoms[3:4, :] = species_v[...].astype(F32)
    weights[...] = jnp.zeros_like(weights)
    weights[0:BASIS, :] = radial_v[...]
    weights[BASIS : BASIS + SPECIES, :] = species_w_v[...]
    weights[BASIS + SPECIES : BASIS + SPECIES + 1, :] = out_v[...]
    copies[-1].wait()
    for value, (high_part, low_part) in ((mix_v[...], (mh, ml)), (mix_v[...].T, (nh, nl))):
        hi, lo = split(value)
        high_part[...] = hi
        low_part[...] = lo


def force_kernel(
    flags, atoms, feat, weights, mh, ml, nh, nl, from_second, from_first,
    env, dinv, gate, curve, inv, rows, fsel, own, one_first, one_second, two_first, two_second, shape_store, tall, eh, el,
    square, turned, squares, table, wide, steady, raw, back,
):
    ghost = SEND * TA
    up = upward(0)
    near, far = from_first[ghost : ghost + 3, 0:CHUNK], from_second[ghost : ghost + 3, 0:CHUNK]
    chunks = [either(up, far, near), atoms[0:3, 0:CHUNK], atoms[0:3, CHUNK:], either(up, near, far)]
    kinds = [atoms[3:4, q * CHUNK : (q + 1) * CHUNK] for q in range(2)]

    def number(row):
        return flags[row : row + 1, :]

    centres = [number(CENTRE + p) for p in range(PAIRS)]
    others = [number(OTHER + p) for p in range(PAIRS)]
    shared = flags[SHARED : SHARED + 1, 0:1]
    rows[...] = jnp.zeros_like(rows)
    rows[0:3, :] = paired(*(pick(chunks, others[p]) for p in range(PAIRS)))
    rows[3:6, :] = paired(*(pick(chunks[1:3], centres[p]) for p in range(PAIRS)))
    rows[6:7, :] = paired(*(pick(kinds, centres[p]) for p in range(PAIRS)))
    columns_of(rows[...], square, turned)

    for p in range(PAIRS):
        o = flags[OTHER + p : OTHER + p + 1, 0:1]
        fsel[p * TA : (p + 1) * TA, :] = (
            pick_rows(from_first.at[0:ghost], o, (SEND + 4) * up)
            + pick_rows(feat, o, float(SEND))
            + pick_rows(from_second.at[0:ghost], o, (SEND + 4) * (1.0 - up))
        )

    for p in range(PAIRS):
        lane_rows = [twice(rows[i : i + 1, :], p) for i in range(3)]
        for r in range(0, TA, STRIP):
            strip = slice(p * TA + r, p * TA + r + STRIP)
            columns = [turned[strip, 3 + i : 4 + i] for i in range(3)]
            unit, inverse, weight, slope, sine, cosine = geometry(
                lane_rows, columns, 1.0, number(LIVE + p), number(SAME + p), r
            )
            angular = harmonics(unit)
            values, slopes = paired_orders(sine, cosine, weight, slope)
            for i, part in enumerate(unit + [inverse] + values + slopes):
                shape_store[p, i, r : r + STRIP, :] = part
            for m in range(COMPS):
                at = slice(m * TA + r, m * TA + r + STRIP)
                for k in range(BASIS // 2):
                    entry = values[k] if m == 0 else angular[m] * values[k]
                    put_left(table, p, at, k * CHUNK, CHUNK, entry)
        radial_feat(fsel, weights, p, tall, wide)
        raw[p * COMPS * TA : (p + 1) * COMPS * TA, :] = long_product(table[p], tall[p], NN)

    for m in range(COMPS):
        first = raw[m * TA : (m + 1) * TA, :]
        second = raw[(COMPS + m) * TA : (COMPS + m + 1) * TA, :]
        env[m * TA : (m + 1) * TA, :] = env_scale * (first + shared * second)
        env[(COMPS + m) * TA : (COMPS + m + 1) * TA, :] = env_scale * (second + shared * first)
    for p in range(PAIRS):
        sums = [None] * 3
        for m in range(COMPS):
            block = env[(p * COMPS + m) * TA : (p * COMPS + m + 1) * TA, :]
            sums[GROUP[m]] = block * block if sums[GROUP[m]] is None else sums[GROUP[m]] + block * block
        for g in range(3):
            inv[p * TA : (p + 1) * TA, g * 256 : (g + 1) * 256] = sums[g]
    hidden = product(split(inv[...]), (mh[...], ml[...]), NN)
    kind = turned[:, 6:7]
    for s in range(SPECIES):
        hidden = hidden + flag(kind == float(s)) * weights[BASIS + s : BASIS + s + 1, :]
    out_row = weights[BASIS + SPECIES : BASIS + SPECIES + 1, :]
    sigma = 1.0 / (1.0 + jnp.exp(-hidden))
    first_order = sigma * (1.0 + hidden * (1.0 - sigma))
    gate[...] = first_order
    curve[...] = sigma * (1.0 - sigma) * (2.0 + hidden * (1.0 - 2.0 * sigma)) * out_row
    dinv[...] = product(split(first_order * out_row), (nh[...], nl[...]), NN)

    tile_grads = [jnp.zeros((3, CHUNK), F32) for _ in range(4)]
    other_rows = []
    for p in range(PAIRS):
        for m in range(COMPS):
            block = env[(p * COMPS + m) * TA : (p * COMPS + m + 1) * TA, :]
            part = dinv[p * TA : (p + 1) * TA, GROUP[m] * 256 : (GROUP[m] + 1) * 256]
            at = slice(m * TA, (m + 1) * TA)
            hi, lo = split((2.0 * env_scale) * block * part)
            eh[p, at, :] = hi
            el[p, at, :] = lo
            for third, piece in enumerate((hi, lo, hi)):
                steady[p, at, third * 256 : (third + 1) * 256] = piece
        for ref in (eh, el):
            ref[p, COMPS * TA :, :] = jnp.zeros((WIDE - COMPS * TA, ref.shape[2]), BF16)
        back[p] = long_product(steady[p], wide[p], NT)
        summed = [jnp.zeros((1, CHUNK), F32) for _ in range(3)]
        for r in range(0, TA, STRIP):
            strip = slice(r, r + STRIP)
            x, y, z, inverse = (shape_store[p, i, strip, :] for i in range(4))
            values = [shape_store[p, 4 + k, strip, :] for k in range(BASIS // 2)]
            slopes = [shape_store[p, 8 + k, strip, :] for k in range(BASIS // 2)]
            angular = harmonics((x, y, z))
            d_radius = None
            g = []
            for m in range(COMPS):
                along, across = None, None
                for k in range(BASIS // 2):
                    block = back[p, m * TA + r : m * TA + r + STRIP, k * CHUNK : (k + 1) * CHUNK]
                    along = block * slopes[k] if along is None else along + block * slopes[k]
                    across = block * values[k] if across is None else across + block * values[k]
                g.append(across)
                term = along if m == 0 else along * angular[m]
                d_radius = term if d_radius is None else d_radius + term
            toward = [
                g[1] + root_three * (y * g[4] + z * g[6] + x * g[7]) - x * g[8],
                g[2] + root_three * (x * g[4] + z * g[5] - y * g[7]) - y * g[8],
                g[3] + root_three * (y * g[5] + x * g[6]) + 2.0 * (z * g[8]),
            ]
            radial_part = d_radius - inverse * (toward[0] * x + toward[1] * y + toward[2] * z)
            for i, v in enumerate((x, y, z)):
                d_offset = inverse * toward[i] + v * radial_part
                summed[i] = summed[i] + jnp.sum(d_offset, axis=0, keepdims=True)
                squares[i, p * TA + r : p * TA + r + STRIP, :] = d_offset
        other_rows.append([part + pltpu.roll(part, TA, 1) for part in summed])
    for i in range(3):
        centre_both = -jnp.sum(squares[i].T, axis=0, keepdims=True)
        component = flag(lax.broadcasted_iota(jnp.int32, (3, CHUNK), 0) == i)
        for p in range(PAIRS):
            centre_row = twice(centre_both, p)
            for q in range(4):
                at = chunk_mask(others[p], q) * other_rows[p][i]
                if q in (1, 2):
                    at = at + chunk_mask(centres[p] + SEND, q) * centre_row
                tile_grads[q] = tile_grads[q] + at * component
    own[...] = jnp.zeros_like(own)
    own[0:3, 0:CHUNK] = tile_grads[1]
    own[0:3, CHUNK:] = tile_grads[2]
    own[3:6, 0:CHUNK] = tile_grads[0]
    own[3:6, CHUNK:] = tile_grads[3]
    leaving = []
    for first, ghost_grad in ((0, tile_grads[0]), (SEND, tile_grads[3])):
        listed = paired(*(pick(tile_grads[1:3], number(SENT + first + j)) for j in range(SEND)))
        leaving.append((listed, ghost_grad))
    for shift, outs in ((0, (one_first, one_second)), (1, (two_first, two_second))):
        choice = upward(shift)
        for out, above in zip(outs, (choice, 1.0 - choice)):
            out[...] = jnp.zeros_like(out)
            out[0:3, :] = either(above, leaving[1][0], leaving[0][0])
            out[3:6, :] = either(above, leaving[1][1], leaving[0][1])


def tangent_kernel(
    scale, flags, atoms, weights, mh, ml, from_first, from_second, own, one_second, two_second, one_first, two_first,
    rows, env, gate, curve, inv_high, inv_low, shape_store, tall,
    forces, keep, give, small, envdot, curl, both,
    square, turned, table, raw, invdot, left_high, left_low, right,
):
    ghost = SEND * TA
    def number(row):
        return flags[row : row + 1, :]

    centres = [number(CENTRE + p) for p in range(PAIRS)]
    others = [number(OTHER + p) for p in range(PAIRS)]
    shared = flags[SHARED : SHARED + 1, 0:1]
    mine = [own[0:3, 0:CHUNK], own[0:3, CHUNK:]]
    up, up_two = upward(0), upward(1)
    low_one = either(up, one_second[...], one_first[...])
    high_one = either(up, one_first[...], one_second[...])
    low_two = either(up_two, two_second[...], two_first[...])
    high_two = either(up_two, two_first[...], two_second[...])
    low_tail = either(up, from_second[ghost:, :], from_first[ghost:, :])
    high_tail = either(up, from_first[ghost:, :], from_second[ghost:, :])
    arrived = [twice(low_one[3:6, :], j) for j in range(SEND)]
    arrived += [twice(high_one[3:6, :], j) for j in range(SEND)]
    for j in range(2 * SEND):
        for q in range(2):
            mine[q] = mine[q] + chunk_mask(number(SENT + j), q) * arrived[j]
    below = low_one[0:3, :]
    above = high_one[0:3, :]
    to_below = [twice(low_two[3:6, :], j) for j in range(SEND)]
    to_below += [twice(own[3:6, 0:CHUNK], j) for j in range(SEND)]
    to_above = [twice(own[3:6, CHUNK:], j) for j in range(SEND)]
    to_above += [twice(high_two[3:6, :], j) for j in range(SEND)]
    for j in range(2 * SEND):
        below = below + low_tail[3 + j : 4 + j, 0:CHUNK] * to_below[j]
        above = above + high_tail[3 + j : 4 + j, 0:CHUNK] * to_above[j]
    for q in range(2):
        for i in range(3):
            forces[i, :, q * CHUNK : (q + 1) * CHUNK] = -mine[q][i : i + 1, :]
    error = [
        below + low_tail[0:3, CHUNK:],
        mine[0] + atoms[4:7, 0:CHUNK],
        mine[1] + atoms[4:7, CHUNK:],
        above + high_tail[0:3, CHUNK:],
    ]
    error = [part * scale for part in error]
    both[...] = jnp.zeros_like(both)
    both[0:8, :] = rows[...]
    both[8:11, :] = paired(*(pick(error, others[p]) for p in range(PAIRS)))
    both[11:14, :] = paired(*(pick(error[1:3], centres[p]) for p in range(PAIRS)))
    columns_of(both[...], square, turned)

    for p in range(PAIRS):
        lane_move = [twice(both[8 + i : 9 + i, :], p) for i in range(3)]
        for r in range(0, TA, STRIP):
            strip = slice(r, r + STRIP)
            here = slice(p * TA + r, p * TA + r + STRIP)
            column_move = [turned[here, 11 + i : 12 + i] for i in range(3)]
            unit = [shape_store[p, i, strip, :] for i in range(3)]
            inverse = shape_store[p, 3, strip, :]
            move = [a - b for a, b in zip(lane_move, column_move)]
            stretch = unit[0] * move[0] + unit[1] * move[1] + unit[2] * move[2]
            turn = [(m - v * stretch) * inverse for m, v in zip(move, unit)]
            angular, turning = harmonics(unit), harmonics_tangent(unit, turn)
            for k in range(BASIS // 2):
                value = shape_store[p, 4 + k, strip, :]
                slope = shape_store[p, 8 + k, strip, :] * stretch
                for m in range(COMPS):
                    at = slice(m * TA + r, m * TA + r + STRIP)
                    entry = slope if m == 0 else angular[m] * slope + turning[m] * value
                    put_left(table, p, at, k * CHUNK, CHUNK, entry)
        raw[p * COMPS * TA : (p + 1) * COMPS * TA, :] = long_product(table[p], tall[p], NN)

    for m in range(COMPS):
        first = raw[m * TA : (m + 1) * TA, :]
        second = raw[(COMPS + m) * TA : (COMPS + m + 1) * TA, :]
        envdot[m * TA : (m + 1) * TA, :] = env_scale * (first + shared * second)
        envdot[(COMPS + m) * TA : (COMPS + m + 1) * TA, :] = env_scale * (second + shared * first)
    half = PAIRS * TA
    for p in range(PAIRS):
        sums = [None] * 3
        for m in range(COMPS):
            at = slice((p * COMPS + m) * TA, (p * COMPS + m + 1) * TA)
            term = 2.0 * env[at, :] * envdot[at, :]
            sums[GROUP[m]] = term if sums[GROUP[m]] is None else sums[GROUP[m]] + term
        for g in range(3):
            invdot[p * TA : (p + 1) * TA, g * 256 : (g + 1) * 256] = sums[g]
    hidden_move = product(split(invdot[...]), (mh[...], ml[...]), NN)
    bend = curve[...] * hidden_move
    curl[...] = bend
    once = 1.0 - shared * flag(lax.broadcasted_iota(jnp.int32, (half, 1), 0) >= TA)
    right[0:half, :] = bend * once
    right[half:, :] = gate[...] * weights[BASIS + SPECIES : BASIS + SPECIES + 1, :] * once
    hi, lo = split(invdot[...].T)
    for ref, given, made in ((left_high, inv_high, hi), (left_low, inv_low, lo)):
        ref[:, 0:half] = given[...]
        ref[:, half:] = made
    raw[0 : left_high.shape[0], :] = product((left_high[...], left_low[...]), split(right[...]), NN)
    core = lax.axis_index("batch")
    for out, part in ((keep, core), (give, 1 - core)):
        out[...] = raw[0 : left_high.shape[0], block_of_lanes(part)]
    small[...] = jnp.zeros_like(small)
    kind = turned[:, 6:7]
    for s in range(SPECIES):
        small[s : s + 1, :] = jnp.sum(right[0:half, :] * flag(kind == float(s)), axis=0, keepdims=True)
    small[SPECIES : SPECIES + 1, :] = jnp.sum(gate[...] * hidden_move * once, axis=0, keepdims=True)


def table_kernel(flags, rows, inv, shape_store, lh, ll, inv_high, inv_low, square, turned):
    low, high = lane_half()
    hi, lo = split(inv[...].T)
    inv_high[...] = hi
    inv_low[...] = lo
    columns_of(rows[...], square, turned)
    for p in range(PAIRS):
        lane_rows = [twice(rows[3 + i : 4 + i, :], p) for i in range(3)]
        for r in range(0, TA, STRIP):
            columns = [turned[p * TA + r : p * TA + r + STRIP, i : i + 1] for i in range(3)]
            unit, inverse, weight, slope, sine, cosine = geometry(
                lane_rows, columns, -1.0, flags[LIVE + p : LIVE + p + 1, :], flags[SAME + p : SAME + p + 1, :], r
            )
            angular = harmonics(unit)
            values, slopes = single_orders(sine, cosine, weight, slope)
            for i, part in enumerate(unit + [inverse] + values + slopes):
                shape_store[p, i, r : r + STRIP, :] = part
            for m in range(0, COMPS + 1, 2):
                factor = low if m == 0 else angular[m] * low
                if m + 1 < COMPS:
                    factor = factor + angular[m + 1] * high
                for n in range(BASIS):
                    hi, lo = split(factor * values[n])
                    lh[p, n * TA + r : n * TA + r + STRIP, m * TA : (m + 2) * TA] = hi
                    ll[p, n * TA + r : n * TA + r + STRIP, m * TA : (m + 2) * TA] = lo


def radial_kernel(
    p, both, shape_store, lh, ll, eh, el, fsel, env, envdot, dinv, curl, nh, nl, after,
    grad_radial,
    square, turned, sh, sl, gh, gl, raw,
):
    low, high = lane_half()
    columns_of(both[...], square, turned)
    here = slice(p * TA, (p + 1) * TA)
    turn_inv = product(split(curl[here, :]), (nh[...], nl[...]), NN)
    lane_move = [twice(both[11 + i : 12 + i, :], p) for i in range(3)]
    sh[:, 0:CHUNK] = lh[p, :, WIDE - CHUNK :]
    sl[:, 0:CHUNK] = ll[p, :, WIDE - CHUNK :]
    for r in range(0, TA, STRIP):
        strip = slice(r, r + STRIP)
        column_move = [turned[p * TA + r : p * TA + r + STRIP, 8 + i : 9 + i] for i in range(3)]
        unit = [shape_store[p, i, strip, :] for i in range(3)]
        inverse = shape_store[p, 3, strip, :]
        move = [b - a for a, b in zip(lane_move, column_move)]
        stretch = unit[0] * move[0] + unit[1] * move[1] + unit[2] * move[2]
        turn = [(m - v * stretch) * inverse for m, v in zip(move, unit)]
        angular, turning = harmonics(unit), harmonics_tangent(unit, turn)
        on_values, on_slopes = [turning[1] * high], [(low + angular[1] * high) * stretch]
        for m in range(2, COMPS + 1, 2):
            on_value, on_slope = turning[m] * low, angular[m] * low
            if m + 1 < COMPS:
                on_value = on_value + turning[m + 1] * high
                on_slope = on_slope + angular[m + 1] * high
            on_values.append(on_value)
            on_slopes.append(on_slope * stretch)
        for n in range(BASIS):
            value, slope = shape_store[p, 4 + n, strip, :], shape_store[p, 4 + BASIS + n, strip, :]
            for j, (on_value, on_slope) in enumerate(zip(on_values, on_slopes)):
                hi, lo = split(on_value * value + on_slope * slope)
                sh[n * TA + r : n * TA + r + STRIP, (j + 1) * CHUNK : (j + 2) * CHUNK] = hi
                sl[n * TA + r : n * TA + r + STRIP, (j + 1) * CHUNK : (j + 2) * CHUNK] = lo
    for m in range(COMPS):
        at = slice((p * COMPS + m) * TA, (p * COMPS + m + 1) * TA)
        group = slice(GROUP[m] * 256, (GROUP[m] + 1) * 256)
        steady = (2.0 * env_scale) * dinv[here, group]
        bent = (2.0 * env_scale) * turn_inv[:, group]
        hi, lo = split(env[at, :] * bent + envdot[at, :] * steady)
        gh[m * TA : (m + 1) * TA, :] = hi
        gl[m * TA : (m + 1) * TA, :] = lo
    for ref, tail in ((gh, eh), (gl, el)):
        ref[COMPS * TA : WIDE, :] = jnp.zeros((WIDE - COMPS * TA, ref.shape[1]), BF16)
        ref[WIDE:, :] = tail[p]
    first = WIDE - CHUNK
    raw[...] = product((lh[p, :, 0:first], ll[p, :, 0:first]), (gh[0:first, :], gl[0:first, :]), NN) + product(
        (sh[...], sl[...]), (gh[first:, :], gl[first:, :]), NN
    )
    for n in range(BASIS):
        grad_radial[n : n + 1, :] = jnp.sum(
            raw[n * TA : (n + 1) * TA, :] * fsel[here, :], axis=0, keepdims=True
        )


SMALL = 32
PAD = 8
FOUR = 4


def block_of(part, rows):
    return pl.ds(pl.multiple_of(part * rows, 8), rows)


def block_from(start, rows):
    return pl.ds(pl.multiple_of(start, 8), rows)


def block_of_lanes(part):
    return pl.ds(pl.multiple_of(part * HALF, HALF), HALF)


def total_of(refs, at):
    total = refs[0][at, :]
    for ref in refs[1:]:
        total = total + ref[at, :]
    return total


def halve_kernel(keep, taken, after, *outs):
    half, piece = keep.shape[0] // 2, keep.shape[0] // (2 * FOUR)
    mine, me = place(0, 2), place(1, FOUR)
    for i, out in enumerate(outs):
        part = mine if i < 2 else 1 - mine
        for j in range(2):
            k = 1 + 2 * (i % 2) - j
            at = block_from(part * half + lax.bitwise_xor(me, k) * piece, piece)
            out[j * piece : (j + 1) * piece, :] = keep[at, :] + taken[at, :]
        if out.shape[0] > 2 * piece:
            out[2 * piece :, :] = jnp.zeros((out.shape[0] - 2 * piece, HALF), F32)


def spread_kernel(first, keep, taken, radial_0, radial_1, small, after, out_0, out_1, tiny):
    for h in range(2):
        lanes = slice(h * HALF, (h + 1) * HALF)
        tiny[16 * h : 16 * h + 8, :] = radial_0[:, lanes] + radial_1[:, lanes]
        tiny[16 * h + 8 : 16 * h + 16, :] = small[:, lanes]
    me = place(1, FOUR)
    few = SMALL // FOUR
    rows = keep.shape[0] // 2
    for j, out in enumerate((out_0, out_1)):
        out[0:rows, :] = total_of([keep, taken], slice(j * rows, (j + 1) * rows))
        out[rows : rows + few, :] = tiny[block_of(lax.bitwise_xor(me, first - j), few), :]
        if out.shape[0] > rows + few:
            out[rows + few :, :] = jnp.zeros((out.shape[0] - rows - few, HALF), F32)


def total_kernel(*refs):
    refs[-1][...] = total_of(refs[:-1], slice(0, refs[-1].shape[0]))


def near_kernel(mine, third, out):
    rows = mine.shape[0] - SMALL // FOUR
    out[0:rows, :] = mine[0:rows, :]
    out[rows : 2 * rows, :] = third[0:rows, :]
    out[2 * rows :, :] = jnp.zeros((out.shape[0] - 2 * rows, HALF), F32)


def rest_kernel(mine, first, second, third, after, out):
    few = SMALL // FOUR
    rows = mine.shape[0] - few
    out[0:rows, :] = second[0:rows, :]
    out[rows : 2 * rows, :] = first[0:rows, :]
    me = place(1, FOUR)
    for k, ref in enumerate((mine, first, second, third)):
        out[block_from(2 * rows + lax.bitwise_xor(me, k) * few, few), :] = ref[rows:, :]


def pair_kernel(near, rest, their_near, their_rest, out):
    piece = (rest.shape[0] - SMALL) // 2
    half = FOUR * piece
    mine, me = place(0, 2), place(1, FOUR)
    for refs, part in (((near, rest), mine), ((their_near, their_rest), 1 - mine)):
        for ref, ks in zip(refs, ((0, 3), (2, 1))):
            for j, k in enumerate(ks):
                at = block_from(part * half + lax.bitwise_xor(me, k) * piece, piece)
                out[at, :] = ref[j * piece : (j + 1) * piece, :]
    out[2 * half :, :] = rest[2 * piece :, :] + their_rest[2 * piece :, :]


def join_kernel(whole, facing, mix, radial, kinds, out):
    rows = mix.shape[0]
    core = lax.axis_index("batch")
    for ref, part in ((whole, core), (facing, 1 - core)):
        mix[:, block_of_lanes(part)] = ref[0:rows, :]
    both = whole[rows:, :] + facing[rows:, :]
    for h in range(2):
        lanes = slice(h * HALF, (h + 1) * HALF)
        few = both[16 * h : 16 * h + 16, :]
        radial[:, lanes] = few[0:BASIS]
        kinds[:, lanes] = few[BASIS : BASIS + SPECIES]
        out[:, lanes] = few[BASIS + SPECIES : BASIS + SPECIES + 1]


def spec(space):
    return pl.BlockSpec(memory_space=space)


def call(kernel, name, outs, scratch, *operands, space=pltpu.VMEM, after=(), flops=0):
    if space is pltpu.HBM:
        operands = [pltpu.with_memory_space_constraint(operand, space) for operand in operands]
    outs = [out if len(out) == 2 and isinstance(out[0], tuple) else (out, F32) for out in outs]
    return pl.pallas_call(
        kernel,
        name=name,
        out_shape=[jax.ShapeDtypeStruct(*out) for out in outs],
        in_specs=[spec(space)] * len(operands) + [spec(pltpu.VMEM)] * len(after),
        out_specs=[spec(pltpu.VMEM)] * len(outs),
        scratch_shapes=[pltpu.VMEM(*item) if isinstance(item, tuple) else item for item in scratch],
        compiler_params=pltpu.CompilerParams(vmem_limit_bytes=28 * 1024 * 1024),
        cost_estimate=pl.CostEstimate(flops=flops, bytes_accessed=1 << 20 if flops else 1 << 10, transcendentals=0),
    )(*operands, *after)


def shifted(block, axis, by):
    count = lax.axis_size(axis)
    return lax.ppermute(block, axis, [(i, (i + by) % count) for i in range(count)])


def exchanged(block, shift, first):
    count, step = lax.axis_size("domain"), 1 << shift
    up = [((i >> shift) & 1 == 0) == first for i in range(count)]
    return lax.ppermute(block, "domain", [(i, (i + step if up[i] else i - step) % count) for i in range(count)])


def partner(block, mask):
    return lax.ppermute(block, "domain", [(i, i ^ mask) for i in range(lax.axis_size("domain"))])


def on_device(
    positions,
    features,
    species,
    ref_forces,
    centre_tile,
    other_tile,
    pair_live,
    send_tiles,
    radial_w,
    mix_w,
    species_w,
    out_w,
):
    atoms_here = positions.shape[2]
    channels = features.shape[2]
    table = (COMPS * TA, BASIS * TA)
    sent = (SEND * TA + GHOST_ROWS, channels)
    slots = PAIRS * TA
    line = (3, 1, atoms_here)
    turning = [((CHUNK, CHUNK), F32)] * 2
    out_row = out_w.reshape(1, channels)
    positions = positions.transpose(1, 0, 2)
    ref_forces = ref_forces.transpose(1, 0, 2)
    ints = [((1, n), jnp.int32) for n in (PAIRS, PAIRS, PAIRS, 2 * SEND)]

    to_second, to_first, token = call(
        gather_kernel,
        "gather",
        [sent, sent, (8, CHUNK)],
        [
            ints[3],
            (line, F32),
            ((1, atoms_here, channels), F32),
            (line, F32),
            pltpu.SemaphoreType.DMA((4,)),
        ],
        send_tiles, positions, features, ref_forces,
        space=pltpu.HBM,
    )
    from_second = exchanged(to_second, 0, False)
    from_first = exchanged(to_first, 0, True)
    flags, atoms, own_feat, weights, mh, ml, nh, nl = call(
        stage_kernel,
        "stage",
        [
            (16, CHUNK),
            (8, atoms_here),
            (atoms_here, channels),
            (16, channels),
            (mix_w.shape, BF16),
            (mix_w.shape, BF16),
            (mix_w.shape[::-1], BF16),
            (mix_w.shape[::-1], BF16),
        ],
        ints
        + [(line, F32), (line, F32), ((1, atoms_here), jnp.int32)]
        + [(radial_w.shape, F32), (mix_w.shape, F32), (species_w.shape, F32), (out_row.shape, F32)]
        + [pltpu.SemaphoreType.DMA((12,))],
        centre_tile, other_tile, pair_live, send_tiles, positions, ref_forces, species, features,
        radial_w, mix_w, species_w, out_row,
        space=pltpu.HBM,
        after=(token,),
    )

    long_table = (PAIRS, COMPS * TA, 3 * BASIS * TA)
    env, dinv, gate, curve, inv, rows, fsel, own, *leaving, shape_store, tall, eh, el = call(
        force_kernel,
        "force",
        [
            (PAIRS * COMPS * TA, channels),
            (slots, 3 * channels),
            (slots, channels),
            (slots, channels),
            (slots, 3 * channels),
            (8, CHUNK),
            (slots, channels),
            (8, atoms_here),
            (8, CHUNK),
            (8, CHUNK),
            (8, CHUNK),
            (8, CHUNK),
            (PAIRS, 4 + BASIS, TA, CHUNK),
            ((PAIRS, 3 * BASIS * TA, channels), BF16),
            ((PAIRS, WIDE, channels), BF16),
            ((PAIRS, WIDE, channels), BF16),
        ],
        turning
        + [((3, CHUNK, CHUNK), F32)]
        + [(long_table, BF16), ((PAIRS, BASIS * TA, 3 * channels), BF16)]
        + [((PAIRS, COMPS * TA, 3 * channels), BF16)]
        + [((PAIRS * COMPS * TA, channels), F32), ((PAIRS, *table), F32)],
        flags, atoms, own_feat, weights, mh, ml, nh, nl, from_second, from_first,
        flops=1 << 31,
    )
    arriving = [exchanged(leaving[i], i // 2, i % 2 == 0) for i in (1, 3, 0, 2)]

    table_shape, lh, ll, inv_high, inv_low = call(
        table_kernel,
        "table",
        [
            (PAIRS, 4 + 2 * BASIS, TA, CHUNK),
            ((PAIRS, BASIS * TA, WIDE), BF16),
            ((PAIRS, BASIS * TA, WIDE), BF16),
            ((3 * channels, slots), BF16),
            ((3 * channels, slots), BF16),
        ],
        turning,
        flags, rows, inv,
        flops=1 << 30,
    )

    rows_mix = 3 * channels
    total_count = 3.0 * atoms_here * lax.axis_size("domain") * lax.axis_size("batch")
    forces, keep, give, small, envdot, curl, both = call(
        functools.partial(tangent_kernel, 2.0 / math.sqrt(total_count)),
        "tangent",
        [
            line,
            (rows_mix, HALF),
            (rows_mix, HALF),
            (8, channels),
            (PAIRS * COMPS * TA, channels),
            (slots, channels),
            (16, CHUNK),
        ],
        turning
        + [(long_table, BF16)]
        + [((PAIRS * COMPS * TA, channels), F32)]
        + [((slots, 3 * channels), F32)]
        + [((3 * channels, 2 * slots), BF16)] * 2
        + [((2 * slots, channels), F32)],
        flags, atoms, weights, mh, ml, from_first, from_second, own, *arriving,
        rows, env, gate, curve, inv_high, inv_low, shape_store, tall,
        flops=1 << 31,
    )

    def radial(p, after):
        return call(
            functools.partial(radial_kernel, p),
            "radial",
            [(BASIS, channels)],
            turning
            + [((BASIS * TA, CHUNK + WIDE), BF16)] * 2
            + [((2 * WIDE, channels), BF16)] * 2
            + [((BASIS * TA, channels), F32)],
            both, table_shape, lh, ll, eh, el, fsel, env, envdot, dinv, curl, nh, nl, after,
            flops=1 << 31 if p == 0 else 0,
        )[0]

    radials = [radial(0, both)]
    piece = rows_mix // (2 * FOUR)
    few = SMALL // FOUR
    near, far, give_near, give_far = call(
        halve_kernel, "halve", [(2 * piece, HALF)] * 3 + [(2 * piece + PAD, HALF)], [],
        keep, shifted(give, "batch", 1), radials[0],
    )
    radials.append(radial(1, far))
    blocks = []
    after = radials[1]
    taken_near = partner(give_near, 1)
    taken_far = partner(give_far, 1)
    for first, kept, taken in ((3, far, taken_far), (1, near, taken_near)):
        blocks += call(
            functools.partial(spread_kernel, first),
            "spread", [(piece + few + PAD * k, HALF) for k in (first - 1, max(first - 2, 0))], [((SMALL, HALF), F32)],
            kept, taken, *radials, small, after,
        )
        after = blocks[0]
    terms = [blocks[3]] + [partner(blocks[3 - k], 2 * k) for k in range(FOUR - 1, 0, -1)]
    (mine,) = call(total_kernel, "total", [(piece + few, HALF)], [], *terms)
    bit = 2 * FOUR
    while bit < lax.axis_size("domain"):
        (mine,) = call(total_kernel, "total", [(piece + few, HALF)], [], mine, partner(mine, bit))
        bit *= 2
    parts = [mine] + [partner(mine, 2 * k) for k in range(1, FOUR)]
    (near,) = call(near_kernel, "near", [(2 * piece + SMALL + PAD, HALF)], [], mine, parts[3])
    their_near = partner(near, 1)
    (rest,) = call(rest_kernel, "rest", [(2 * piece + SMALL, HALF)], [], *parts, near)
    their_rest = partner(rest, 1)
    (whole,) = call(
        pair_kernel, "pair", [(rows_mix + SMALL, HALF)], [], near, rest, their_near, their_rest
    )
    facing = shifted(whole, "batch", 1)
    mix, radial_sum, kinds, out = call(
        join_kernel,
        "join",
        [(rows_mix, channels), (BASIS, channels), (SPECIES, channels), (1, channels)],
        [],
        whole,
        facing,
    )
    return forces.transpose(1, 0, 2), radial_sum, mix, kinds, out.reshape(channels)


def solution(mesh):
    return jax.shard_map(
        on_device,
        mesh=mesh,
        in_specs=(
            P(("parts", "batch"), None, "domain"),
            P(("parts", "batch"), "domain", None),
            P(("parts", "batch"), "domain"),
            P(("parts", "batch"), None, "domain"),
            P(("parts", "batch"), "domain"),
            P(("parts", "batch"), "domain"),
            P(("parts", "batch"), "domain"),
            P(("parts", "batch"), "domain"),
            P(),
            P(),
            P(),
            P(),
        ),
        out_specs=(
            P(("parts", "batch"), None, "domain"),
            P("parts", None),
            P("parts", None),
            P("parts", None),
            P("parts"),
        ),
        check_vma=False,
    )
```

```python
import functools
import math

import jax
import jax.numpy as jnp
from jax import lax
from jax.experimental import pallas as pl
from jax.experimental.pallas import tpu as pltpu
from jax.sharding import PartitionSpec as P

TA = 64
SEND = 2
PAIRS = 2
COMPS = 9
STRIP = 16
WIDE = 10 * TA
BASIS = 8
SPECIES = 4
HALF = 128
CHUNK = 2 * TA

cutoff = 2.5
soften = 0.25
env_scale = 0.25
root_three = math.sqrt(3.0)
F32 = jnp.float32
BF16 = jnp.bfloat16
NN = (((1,), (0,)), ((), ()))
NT = (((1,), (1,)), ((), ()))
TN = (((0,), (0,)), ((), ()))
GROUP = (0, 1, 1, 1, 2, 2, 2, 2, 2)


def split(value):
    high = value.astype(BF16)
    return high, (value - high.astype(F32)).astype(BF16)


def product(left, right, dims):
    (lh, ll), (rh, rl) = left, right

    def one(x, y):
        return lax.dot_general(x, y, dims, preferred_element_type=F32)

    return one(lh, rh) + (one(lh, rl) + one(ll, rh))


def long_product(left, right, dims):
    return lax.dot_general(left, right, dims, preferred_element_type=F32)


def put_left(ref, p, rows, lane, width, value):
    hi, lo = split(value)
    span = ref.shape[2] // 3
    for third, part in enumerate((hi, lo, hi)):
        at = third * span + lane
        ref[p, rows, at : at + width] = part


def flag(condition):
    return jnp.where(condition, 1.0, 0.0).astype(F32)


def place(shift, width):
    return lax.bitwise_and(lax.shift_right_logical(lax.axis_index("domain"), shift), width - 1)


def lane_half():
    lane = lax.broadcasted_iota(jnp.int32, (1, CHUNK), 1)
    low = flag(lane < TA)
    return low, 1.0 - low


def twice(chunk, half):
    low, high = lane_half()
    swapped = pltpu.roll(chunk, TA, 1)
    return chunk * low + swapped * high if half == 0 else swapped * low + chunk * high


def pick(chunks, position):
    total = None
    for q, chunk in enumerate(chunks):
        for half in range(2):
            term = twice(chunk, half) * flag(position == 2 * q + half)
            total = term if total is None else total + term
    return total


def paired(first, second):
    low, high = lane_half()
    return first * low + second * high


def chunk_mask(position, q):
    low, high = lane_half()
    return low * flag(position == 2 * q) + high * flag(position == 2 * q + 1)


def series(angle):
    square = angle * angle
    sine, cosine = 1.0 / math.factorial(13), -1.0 / math.factorial(14)
    for order in range(11, 0, -2):
        sine = sine * square + (-1.0) ** (order // 2) / math.factorial(order)
    for order in range(12, -1, -2):
        cosine = cosine * square + (-1.0) ** (order // 2) / math.factorial(order)
    return sine * angle, cosine


def geometry(lane_rows, columns, sign, live, same, first):
    offset = [(row - column) * sign for row, column in zip(lane_rows, columns)]
    dist_sq = offset[0] * offset[0] + offset[1] * offset[1] + offset[2] * offset[2] + soften
    inverse = lax.rsqrt(dist_sq)
    inverse = inverse * (1.5 - 0.5 * dist_sq * inverse * inverse)
    unit = [x * inverse for x in offset]
    row = lax.broadcasted_iota(jnp.int32, (STRIP, CHUNK), 0) + first
    lane = lax.broadcasted_iota(jnp.int32, (STRIP, CHUNK), 1)
    lane = jnp.where(lane >= TA, lane - TA, lane)
    mask = live * (1.0 - same * flag(row == lane))
    base = jnp.maximum(1.0 - dist_sq * (1.0 / (cutoff * cutoff)), 0.0)
    weight = base * base * base * mask * inverse
    slope = -(6.0 / (cutoff * cutoff)) * base * base * mask - weight * inverse
    turned = jnp.minimum(dist_sq * inverse, cutoff) * (math.pi / cutoff) - 0.5 * math.pi
    sine, cosine = series(turned)
    return unit, inverse, weight, slope, cosine, -sine


def harmonics(v):
    x, y, z = v
    return [
        None,
        x,
        y,
        z,
        root_three * x * y,
        root_three * y * z,
        root_three * z * x,
        0.5 * root_three * (x * x - y * y),
        z * z - 0.5 * (x * x + y * y),
    ]


def harmonics_tangent(v, t):
    x, y, z = v
    a, b, c = t
    return [
        None,
        a,
        b,
        c,
        root_three * (a * y + x * b),
        root_three * (b * z + y * c),
        root_three * (c * x + z * a),
        root_three * (x * a - y * b),
        2.0 * z * c - (x * a + y * b),
    ]


def paired_orders(sine, cosine, weight, slope):
    low, high = lane_half()
    double_s, double_c = 2.0 * sine * cosine, 1.0 - 2.0 * sine * sine
    now_s = sine * low + double_s * high
    now_c = cosine * low + double_c * high
    old_s = -sine * low
    old_c = cosine * low + high
    values, slopes = [], []
    for k in range(BASIS // 2):
        order = ((2 * k + 1) * low + (2 * k + 2) * high) * (math.pi / cutoff)
        values.append(now_s * weight)
        slopes.append(now_c * (weight * order) + now_s * slope)
        now_s, old_s = 2.0 * double_c * now_s - old_s, now_s
        now_c, old_c = 2.0 * double_c * now_c - old_c, now_c
    return values, slopes


def single_orders(sine, cosine, weight, slope):
    now_s, now_c = sine, cosine
    old_s, old_c = jnp.zeros_like(sine), jnp.ones_like(cosine)
    values, slopes = [], []
    for n in range(1, BASIS + 1):
        values.append(now_s * weight)
        slopes.append(now_c * (weight * (n * math.pi / cutoff)) + now_s * slope)
        now_s, old_s = 2.0 * cosine * now_s - old_s, now_s
        now_c, old_c = 2.0 * cosine * now_c - old_c, now_c
    return values, slopes


def columns_of(rows, square, turned):
    square[...] = jnp.zeros_like(square)
    square[0 : rows.shape[0], :] = rows
    turned[...] = square[...].T


def pair_rows(first, p):
    return twice(first, p)


def radial_feat(feat, turned_feat, radial, spread_w, p, tall, flat):
    own = feat[p * TA : (p + 1) * TA, :]
    span, channels = BASIS * TA, feat.shape[1]
    for n in range(BASIS):
        hi, lo = split(own * radial[n : n + 1, :])
        for third, part in enumerate((hi, hi, lo)):
            tall[p, third * span + n * TA : third * span + (n + 1) * TA, :] = part
    both = twice(turned_feat, p)
    for k in range(BASIS // 2):
        hi, lo = split(both * spread_w[k])
        for third, part in enumerate((hi, hi, lo)):
            flat[p, third * channels : (third + 1) * channels, k * CHUNK : (k + 1) * CHUNK] = part


OTHER, CENTRE, LIVE, SAME, SHARED, SENT = 0, 2, 4, 6, 8, 9
GHOST_ROWS = 8


def fetch(pairs, sems):
    copies = [pltpu.make_async_copy(src, dst, sems.at[i]) for i, (src, dst) in enumerate(pairs)]
    for copy in copies:
        copy.start()
    return copies


def upward(shift):
    return 1.0 - flag(place(shift, 2) == 1)


def either(choice, first, second):
    return first * choice + second * (1.0 - choice)


def gather_kernel(send, pos, feat, ref, to_second, to_first, token, send_v, pos_v, feat_v, ref_v, sems):
    copies = fetch([(send, send_v), (pos, pos_v), (ref, ref_v), (feat, feat_v)], sems)
    for copy in copies[:3]:
        copy.wait()
    low, high = lane_half()
    up = upward(0)
    sent = [send_v[0:1, j : j + 1].astype(F32) for j in range(2 * SEND)]
    tiles_of = []
    for out, choice in ((to_first, 1.0 - up), (to_second, up)):
        tiles = [either(choice, sent[j], sent[SEND + j]) for j in range(SEND)]
        tiles_of.append(tiles)
        out[SEND * TA :, :] = jnp.zeros((GHOST_ROWS, out.shape[1]), F32)
        for i in range(3):
            at = SEND * TA + i
            for lanes, source in ((slice(0, CHUNK), pos_v), (slice(CHUNK, 2 * CHUNK), ref_v)):
                chunks = [source[i, :, q * CHUNK : (q + 1) * CHUNK] for q in range(2)]
                out[at : at + 1, lanes] = paired(pick(chunks, tiles[0]), pick(chunks, tiles[1]))
        for other in range(2 * SEND):
            same = low * flag(sent[other] == tiles[0]) + high * flag(sent[other] == tiles[1])
            out[SEND * TA + 3 + other : SEND * TA + 4 + other, 0:CHUNK] = same
    token[...] = jnp.zeros_like(token)
    copies[3].wait()
    for out, tiles in zip((to_first, to_second), tiles_of):
        for j in range(SEND):
            out[j * TA : (j + 1) * TA, :] = pick_rows(feat_v.at[0], tiles[j], 0.0)


def pick_rows(ref, position, first):
    total = None
    for t in range(ref.shape[0] // TA):
        term = ref[t * TA : (t + 1) * TA, :] * flag(position == first + float(t))
        total = term if total is None else total + term
    return total


def stage_kernel(
    centre, other, live, send, pos, ref, species, feat, radial_w, mix_w, species_w, out_w, after,
    flags, atoms, own_feat, weights, spread_w, mh, ml, nh, nl,
    centre_v, other_v, live_v, send_v, pos_v, ref_v, species_v, radial_v, mix_v, species_w_v, out_v, square, sems,
):
    copies = fetch(
        [
            (centre, centre_v), (other, other_v), (live, live_v), (send, send_v), (pos, pos_v), (ref, ref_v),
            (species, species_v), (radial_w, radial_v), (species_w, species_w_v), (out_w, out_v),
            (feat.at[0], own_feat), (mix_w, mix_v),
        ],
        sems,
    )
    for copy in copies[:-1]:
        copy.wait()
    flags[...] = jnp.zeros_like(flags)
    centres = [centre_v[0:1, p : p + 1].astype(F32) for p in range(PAIRS)]
    others = [other_v[0:1, p : p + 1].astype(F32) for p in range(PAIRS)]
    for p in range(PAIRS):
        for row, value in (
            (OTHER, others[p]),
            (CENTRE, centres[p]),
            (LIVE, live_v[0:1, p : p + 1].astype(F32)),
            (SAME, flag(others[p] == centres[p] + SEND)),
        ):
            flags[row + p : row + p + 1, :] = jnp.broadcast_to(value, (1, CHUNK))
    flags[SHARED : SHARED + 1, :] = jnp.broadcast_to(flag(centres[0] == centres[1]), (1, CHUNK))
    for j in range(2 * SEND):
        value = send_v[0:1, j : j + 1].astype(F32)
        flags[SENT + j : SENT + j + 1, :] = jnp.broadcast_to(value, (1, CHUNK))
    atoms[...] = jnp.zeros_like(atoms)
    for i in range(3):
        atoms[i : i + 1, :] = pos_v[i]
        atoms[4 + i : 5 + i, :] = ref_v[i]
    atoms[3:4, :] = species_v[...].astype(F32)
    weights[...] = jnp.zeros_like(weights)
    weights[0:BASIS, :] = radial_v[...]
    weights[BASIS : BASIS + SPECIES, :] = species_w_v[...]
    weights[BASIS + SPECIES : BASIS + SPECIES + 1, :] = out_v[...]
    square[...] = jnp.zeros_like(square)
    square[0:BASIS, :] = radial_v[...]
    turned = square[...].T
    low, high = lane_half()
    for k in range(BASIS // 2):
        spread_w[k] = turned[:, 2 * k : 2 * k + 1] * low + turned[:, 2 * k + 1 : 2 * k + 2] * high
    copies[-1].wait()
    for value, (high_part, low_part) in ((mix_v[...], (mh, ml)), (mix_v[...].T, (nh, nl))):
        hi, lo = split(value)
        high_part[...] = hi
        low_part[...] = lo


def force_kernel(
    flags, atoms, feat, weights, spread_w, mh, ml, nh, nl, from_second, from_first,
    env, dinv, gate, curve, inv, rows, fsel, own, one_first, one_second, two_first, two_second, shape_store, tall, eh, el,
    square, turned, squares, table, flat, steady, raw, back,
):
    ghost = SEND * TA
    up = upward(0)
    near, far = from_first[ghost : ghost + 3, 0:CHUNK], from_second[ghost : ghost + 3, 0:CHUNK]
    chunks = [either(up, far, near), atoms[0:3, 0:CHUNK], atoms[0:3, CHUNK:], either(up, near, far)]
    kinds = [atoms[3:4, q * CHUNK : (q + 1) * CHUNK] for q in range(2)]

    def number(row):
        return flags[row : row + 1, :]

    centres = [number(CENTRE + p) for p in range(PAIRS)]
    others = [number(OTHER + p) for p in range(PAIRS)]
    shared = flags[SHARED : SHARED + 1, 0:1]
    rows[...] = jnp.zeros_like(rows)
    rows[0:3, :] = paired(*(pick(chunks, others[p]) for p in range(PAIRS)))
    rows[3:6, :] = paired(*(pick(chunks[1:3], centres[p]) for p in range(PAIRS)))
    rows[6:7, :] = paired(*(pick(kinds, centres[p]) for p in range(PAIRS)))
    columns_of(rows[...], square, turned)

    for p in range(PAIRS):
        o = flags[OTHER + p : OTHER + p + 1, 0:1]
        fsel[p * TA : (p + 1) * TA, :] = (
            pick_rows(from_first.at[0:ghost], o, (SEND + 4) * up)
            + pick_rows(feat, o, float(SEND))
            + pick_rows(from_second.at[0:ghost], o, (SEND + 4) * (1.0 - up))
        )

    turned_feat = fsel[...].T
    for p in range(PAIRS):
        lane_rows = [twice(rows[i : i + 1, :], p) for i in range(3)]
        for r in range(0, TA, STRIP):
            strip = slice(p * TA + r, p * TA + r + STRIP)
            columns = [turned[strip, 3 + i : 4 + i] for i in range(3)]
            unit, inverse, weight, slope, sine, cosine = geometry(
                lane_rows, columns, 1.0, number(LIVE + p), number(SAME + p), r
            )
            angular = harmonics(unit)
            values, slopes = paired_orders(sine, cosine, weight, slope)
            for i, part in enumerate(unit + [inverse] + values + slopes):
                shape_store[p, i, r : r + STRIP, :] = part
            for m in range(COMPS):
                at = slice(m * TA + r, m * TA + r + STRIP)
                for k in range(BASIS // 2):
                    entry = values[k] if m == 0 else angular[m] * values[k]
                    put_left(table, p, at, k * CHUNK, CHUNK, entry)
        radial_feat(fsel, turned_feat, weights, spread_w, p, tall, flat)
        raw[p * COMPS * TA : (p + 1) * COMPS * TA, :] = long_product(table[p], tall[p], NN)

    for m in range(COMPS):
        first = raw[m * TA : (m + 1) * TA, :]
        second = raw[(COMPS + m) * TA : (COMPS + m + 1) * TA, :]
        env[m * TA : (m + 1) * TA, :] = env_scale * (first + shared * second)
        env[(COMPS + m) * TA : (COMPS + m + 1) * TA, :] = env_scale * (second + shared * first)
    for p in range(PAIRS):
        sums = [None] * 3
        for m in range(COMPS):
            block = env[(p * COMPS + m) * TA : (p * COMPS + m + 1) * TA, :]
            sums[GROUP[m]] = block * block if sums[GROUP[m]] is None else sums[GROUP[m]] + block * block
        for g in range(3):
            inv[p * TA : (p + 1) * TA, g * 256 : (g + 1) * 256] = sums[g]
    hidden = product(split(inv[...]), (mh[...], ml[...]), NN)
    kind = turned[:, 6:7]
    for s in range(SPECIES):
        hidden = hidden + flag(kind == float(s)) * weights[BASIS + s : BASIS + s + 1, :]
    out_row = weights[BASIS + SPECIES : BASIS + SPECIES + 1, :]
    sigma = 1.0 / (1.0 + jnp.exp(-hidden))
    first_order = sigma * (1.0 + hidden * (1.0 - sigma))
    gate[...] = first_order
    curve[...] = sigma * (1.0 - sigma) * (2.0 + hidden * (1.0 - 2.0 * sigma)) * out_row
    dinv[...] = product(split(first_order * out_row), (nh[...], nl[...]), NN)

    tile_grads = [jnp.zeros((3, CHUNK), F32) for _ in range(4)]
    other_rows = []
    for p in range(PAIRS):
        for m in range(COMPS):
            block = env[(p * COMPS + m) * TA : (p * COMPS + m + 1) * TA, :]
            part = dinv[p * TA : (p + 1) * TA, GROUP[m] * 256 : (GROUP[m] + 1) * 256]
            at = slice(m * TA, (m + 1) * TA)
            hi, lo = split((2.0 * env_scale) * block * part)
            eh[p, at, :] = hi
            el[p, at, :] = lo
            for third, piece in enumerate((hi, lo, hi)):
                steady[p, at, third * 256 : (third + 1) * 256] = piece
        for ref in (eh, el):
            ref[p, COMPS * TA :, :] = jnp.zeros((WIDE - COMPS * TA, ref.shape[2]), BF16)
        back[p] = long_product(steady[p], flat[p], NN)
        summed = [jnp.zeros((1, CHUNK), F32) for _ in range(3)]
        for r in range(0, TA, STRIP):
            strip = slice(r, r + STRIP)
            x, y, z, inverse = (shape_store[p, i, strip, :] for i in range(4))
            values = [shape_store[p, 4 + k, strip, :] for k in range(BASIS // 2)]
            slopes = [shape_store[p, 8 + k, strip, :] for k in range(BASIS // 2)]
            angular = harmonics((x, y, z))
            d_radius = None
            g = []
            for m in range(COMPS):
                along, across = None, None
                for k in range(BASIS // 2):
                    block = back[p, m * TA + r : m * TA + r + STRIP, k * CHUNK : (k + 1) * CHUNK]
                    along = block * slopes[k] if along is None else along + block * slopes[k]
                    across = block * values[k] if across is None else across + block * values[k]
                g.append(across)
                term = along if m == 0 else along * angular[m]
                d_radius = term if d_radius is None else d_radius + term
            toward = [
                g[1] + root_three * (y * g[4] + z * g[6] + x * g[7]) - x * g[8],
                g[2] + root_three * (x * g[4] + z * g[5] - y * g[7]) - y * g[8],
                g[3] + root_three * (y * g[5] + x * g[6]) + 2.0 * (z * g[8]),
            ]
            radial_part = d_radius - inverse * (toward[0] * x + toward[1] * y + toward[2] * z)
            for i, v in enumerate((x, y, z)):
                d_offset = inverse * toward[i] + v * radial_part
                summed[i] = summed[i] + jnp.sum(d_offset, axis=0, keepdims=True)
                squares[i, p * TA + r : p * TA + r + STRIP, :] = d_offset
        other_rows.append([part + pltpu.roll(part, TA, 1) for part in summed])
    for i in range(3):
        centre_both = -jnp.sum(squares[i].T, axis=0, keepdims=True)
        component = flag(lax.broadcasted_iota(jnp.int32, (3, CHUNK), 0) == i)
        for p in range(PAIRS):
            centre_row = twice(centre_both, p)
            for q in range(4):
                at = chunk_mask(others[p], q) * other_rows[p][i]
                if q in (1, 2):
                    at = at + chunk_mask(centres[p] + SEND, q) * centre_row
                tile_grads[q] = tile_grads[q] + at * component
    own[...] = jnp.zeros_like(own)
    own[0:3, 0:CHUNK] = tile_grads[1]
    own[0:3, CHUNK:] = tile_grads[2]
    own[3:6, 0:CHUNK] = tile_grads[0]
    own[3:6, CHUNK:] = tile_grads[3]
    leaving = []
    for first, ghost_grad in ((0, tile_grads[0]), (SEND, tile_grads[3])):
        listed = paired(*(pick(tile_grads[1:3], number(SENT + first + j)) for j in range(SEND)))
        leaving.append((listed, ghost_grad))
    for shift, outs in ((0, (one_first, one_second)), (1, (two_first, two_second))):
        choice = upward(shift)
        for out, above in zip(outs, (choice, 1.0 - choice)):
            out[...] = jnp.zeros_like(out)
            out[0:3, :] = either(above, leaving[1][0], leaving[0][0])
            out[3:6, :] = either(above, leaving[1][1], leaving[0][1])


def tangent_kernel(
    scale, flags, atoms, weights, mh, ml, from_first, from_second, own, one_second, two_second, one_first, two_first,
    rows, env, gate, curve, inv, shape_store, tall, after,
    forces, keep, give, small, envdot, curl, both,
    square, turned, table, raw, left, right,
):
    ghost = SEND * TA
    def number(row):
        return flags[row : row + 1, :]

    centres = [number(CENTRE + p) for p in range(PAIRS)]
    others = [number(OTHER + p) for p in range(PAIRS)]
    shared = flags[SHARED : SHARED + 1, 0:1]
    mine = [own[0:3, 0:CHUNK], own[0:3, CHUNK:]]
    up, up_two = upward(0), upward(1)
    low_one = either(up, one_second[...], one_first[...])
    high_one = either(up, one_first[...], one_second[...])
    low_two = either(up_two, two_second[...], two_first[...])
    high_two = either(up_two, two_first[...], two_second[...])
    low_tail = either(up, from_second[ghost:, :], from_first[ghost:, :])
    high_tail = either(up, from_first[ghost:, :], from_second[ghost:, :])
    arrived = [twice(low_one[3:6, :], j) for j in range(SEND)]
    arrived += [twice(high_one[3:6, :], j) for j in range(SEND)]
    for j in range(2 * SEND):
        for q in range(2):
            mine[q] = mine[q] + chunk_mask(number(SENT + j), q) * arrived[j]
    below = low_one[0:3, :]
    above = high_one[0:3, :]
    to_below = [twice(low_two[3:6, :], j) for j in range(SEND)]
    to_below += [twice(own[3:6, 0:CHUNK], j) for j in range(SEND)]
    to_above = [twice(own[3:6, CHUNK:], j) for j in range(SEND)]
    to_above += [twice(high_two[3:6, :], j) for j in range(SEND)]
    for j in range(2 * SEND):
        below = below + low_tail[3 + j : 4 + j, 0:CHUNK] * to_below[j]
        above = above + high_tail[3 + j : 4 + j, 0:CHUNK] * to_above[j]
    for q in range(2):
        for i in range(3):
            forces[i, :, q * CHUNK : (q + 1) * CHUNK] = -mine[q][i : i + 1, :]
    error = [
        below + low_tail[0:3, CHUNK:],
        mine[0] + atoms[4:7, 0:CHUNK],
        mine[1] + atoms[4:7, CHUNK:],
        above + high_tail[0:3, CHUNK:],
    ]
    error = [part * scale for part in error]
    both[...] = jnp.zeros_like(both)
    both[0:8, :] = rows[...]
    both[8:11, :] = paired(*(pick(error, others[p]) for p in range(PAIRS)))
    both[11:14, :] = paired(*(pick(error[1:3], centres[p]) for p in range(PAIRS)))
    columns_of(both[...], square, turned)

    for p in range(PAIRS):
        lane_move = [twice(both[8 + i : 9 + i, :], p) for i in range(3)]
        for r in range(0, TA, STRIP):
            strip = slice(r, r + STRIP)
            here = slice(p * TA + r, p * TA + r + STRIP)
            column_move = [turned[here, 11 + i : 12 + i] for i in range(3)]
            unit = [shape_store[p, i, strip, :] for i in range(3)]
            inverse = shape_store[p, 3, strip, :]
            move = [a - b for a, b in zip(lane_move, column_move)]
            stretch = unit[0] * move[0] + unit[1] * move[1] + unit[2] * move[2]
            turn = [(m - v * stretch) * inverse for m, v in zip(move, unit)]
            angular, turning = harmonics(unit), harmonics_tangent(unit, turn)
            for k in range(BASIS // 2):
                value = shape_store[p, 4 + k, strip, :]
                slope = shape_store[p, 8 + k, strip, :] * stretch
                for m in range(COMPS):
                    at = slice(m * TA + r, m * TA + r + STRIP)
                    entry = slope if m == 0 else angular[m] * slope + turning[m] * value
                    put_left(table, p, at, k * CHUNK, CHUNK, entry)
        raw[p * COMPS * TA : (p + 1) * COMPS * TA, :] = long_product(table[p], tall[p], NN)

    for m in range(COMPS):
        first = raw[m * TA : (m + 1) * TA, :]
        second = raw[(COMPS + m) * TA : (COMPS + m + 1) * TA, :]
        envdot[m * TA : (m + 1) * TA, :] = env_scale * (first + shared * second)
        envdot[(COMPS + m) * TA : (COMPS + m + 1) * TA, :] = env_scale * (second + shared * first)
    half = PAIRS * TA
    for p in range(PAIRS):
        sums = [None] * 3
        for m in range(COMPS):
            at = slice((p * COMPS + m) * TA, (p * COMPS + m + 1) * TA)
            term = 2.0 * env[at, :] * envdot[at, :]
            sums[GROUP[m]] = term if sums[GROUP[m]] is None else sums[GROUP[m]] + term
        for g in range(3):
            left[half + p * TA : half + (p + 1) * TA, g * 256 : (g + 1) * 256] = sums[g]
    left[0:half, :] = inv[...]
    hidden_move = product(split(left[half:, :]), (mh[...], ml[...]), NN)
    bend = curve[...] * hidden_move
    curl[...] = bend
    once = 1.0 - shared * flag(lax.broadcasted_iota(jnp.int32, (half, 1), 0) >= TA)
    right[0:half, :] = bend * once
    right[half:, :] = gate[...] * weights[BASIS + SPECIES : BASIS + SPECIES + 1, :] * once
    raw[0 : left.shape[1], :] = product(split(left[...]), split(right[...]), TN)
    core = lax.axis_index("batch")
    for out, part in ((keep, core), (give, 1 - core)):
        out[...] = raw[0 : left.shape[1], block_of_lanes(part)]
    small[...] = jnp.zeros_like(small)
    kind = turned[:, 6:7]
    for s in range(SPECIES):
        small[s : s + 1, :] = jnp.sum(right[0:half, :] * flag(kind == float(s)), axis=0, keepdims=True)
    small[SPECIES : SPECIES + 1, :] = jnp.sum(gate[...] * hidden_move * once, axis=0, keepdims=True)


def table_kernel(flags, rows, shape_store, lh, ll, token, square, turned):
    low, high = lane_half()
    token[...] = jnp.zeros_like(token)
    columns_of(rows[...], square, turned)
    for p in range(PAIRS):
        lane_rows = [twice(rows[3 + i : 4 + i, :], p) for i in range(3)]
        for r in range(0, TA, STRIP):
            columns = [turned[p * TA + r : p * TA + r + STRIP, i : i + 1] for i in range(3)]
            unit, inverse, weight, slope, sine, cosine = geometry(
                lane_rows, columns, -1.0, flags[LIVE + p : LIVE + p + 1, :], flags[SAME + p : SAME + p + 1, :], r
            )
            angular = harmonics(unit)
            values, slopes = single_orders(sine, cosine, weight, slope)
            for i, part in enumerate(unit + [inverse] + values + slopes):
                shape_store[p, i, r : r + STRIP, :] = part
            for m in range(0, COMPS + 1, 2):
                factor = low if m == 0 else angular[m] * low
                if m + 1 < COMPS:
                    factor = factor + angular[m + 1] * high
                for n in range(BASIS):
                    hi, lo = split(factor * values[n])
                    lh[p, n * TA + r : n * TA + r + STRIP, m * TA : (m + 2) * TA] = hi
                    ll[p, n * TA + r : n * TA + r + STRIP, m * TA : (m + 2) * TA] = lo


def radial_kernel(
    p, both, shape_store, lh, ll, eh, el, fsel, env, envdot, dinv, curl, nh, nl, after,
    grad_radial,
    square, turned, sh, sl, gh, gl, raw,
):
    low, high = lane_half()
    columns_of(both[...], square, turned)
    here = slice(p * TA, (p + 1) * TA)
    turn_inv = product(split(curl[here, :]), (nh[...], nl[...]), NN)
    lane_move = [twice(both[11 + i : 12 + i, :], p) for i in range(3)]
    sh[:, 0:CHUNK] = lh[p, :, WIDE - CHUNK :]
    sl[:, 0:CHUNK] = ll[p, :, WIDE - CHUNK :]
    for r in range(0, TA, STRIP):
        strip = slice(r, r + STRIP)
        column_move = [turned[p * TA + r : p * TA + r + STRIP, 8 + i : 9 + i] for i in range(3)]
        unit = [shape_store[p, i, strip, :] for i in range(3)]
        inverse = shape_store[p, 3, strip, :]
        move = [b - a for a, b in zip(lane_move, column_move)]
        stretch = unit[0] * move[0] + unit[1] * move[1] + unit[2] * move[2]
        turn = [(m - v * stretch) * inverse for m, v in zip(move, unit)]
        angular, turning = harmonics(unit), harmonics_tangent(unit, turn)
        on_values, on_slopes = [turning[1] * high], [(low + angular[1] * high) * stretch]
        for m in range(2, COMPS + 1, 2):
            on_value, on_slope = turning[m] * low, angular[m] * low
            if m + 1 < COMPS:
                on_value = on_value + turning[m + 1] * high
                on_slope = on_slope + angular[m + 1] * high
            on_values.append(on_value)
            on_slopes.append(on_slope * stretch)
        for n in range(BASIS):
            value, slope = shape_store[p, 4 + n, strip, :], shape_store[p, 4 + BASIS + n, strip, :]
            for j, (on_value, on_slope) in enumerate(zip(on_values, on_slopes)):
                hi, lo = split(on_value * value + on_slope * slope)
                sh[n * TA + r : n * TA + r + STRIP, (j + 1) * CHUNK : (j + 2) * CHUNK] = hi
                sl[n * TA + r : n * TA + r + STRIP, (j + 1) * CHUNK : (j + 2) * CHUNK] = lo
    for m in range(COMPS):
        at = slice((p * COMPS + m) * TA, (p * COMPS + m + 1) * TA)
        group = slice(GROUP[m] * 256, (GROUP[m] + 1) * 256)
        steady = (2.0 * env_scale) * dinv[here, group]
        bent = (2.0 * env_scale) * turn_inv[:, group]
        hi, lo = split(env[at, :] * bent + envdot[at, :] * steady)
        gh[m * TA : (m + 1) * TA, :] = hi
        gl[m * TA : (m + 1) * TA, :] = lo
    for ref, tail in ((gh, eh), (gl, el)):
        ref[COMPS * TA : WIDE, :] = jnp.zeros((WIDE - COMPS * TA, ref.shape[1]), BF16)
        ref[WIDE:, :] = tail[p]
    first = WIDE - CHUNK
    raw[...] = product((lh[p, :, 0:first], ll[p, :, 0:first]), (gh[0:first, :], gl[0:first, :]), NN) + product(
        (sh[...], sl[...]), (gh[first:, :], gl[first:, :]), NN
    )
    for n in range(BASIS):
        grad_radial[n : n + 1, :] = jnp.sum(
            raw[n * TA : (n + 1) * TA, :] * fsel[here, :], axis=0, keepdims=True
        )


SMALL = 32
PAD = 8
FOUR = 4


def block_of(part, rows):
    return pl.ds(pl.multiple_of(part * rows, 8), rows)


def block_from(start, rows):
    return pl.ds(pl.multiple_of(start, 8), rows)


def block_of_lanes(part):
    return pl.ds(pl.multiple_of(part * HALF, HALF), HALF)


def total_of(refs, at):
    total = refs[0][at, :]
    for ref in refs[1:]:
        total = total + ref[at, :]
    return total


def halve_kernel(keep, taken, after, *outs):
    half, piece = keep.shape[0] // 2, keep.shape[0] // (2 * FOUR)
    mine, me = place(0, 2), place(1, FOUR)
    for i, out in enumerate(outs):
        part = mine if i < 2 else 1 - mine
        for j in range(2):
            k = 1 + 2 * (i % 2) - j
            at = block_from(part * half + lax.bitwise_xor(me, k) * piece, piece)
            out[j * piece : (j + 1) * piece, :] = keep[at, :] + taken[at, :]
        if out.shape[0] > 2 * piece:
            out[2 * piece :, :] = jnp.zeros((out.shape[0] - 2 * piece, HALF), F32)


def spread_kernel(first, keep, taken, radial_0, radial_1, small, after, out_0, out_1, tiny):
    for h in range(2):
        lanes = slice(h * HALF, (h + 1) * HALF)
        tiny[16 * h : 16 * h + 8, :] = radial_0[:, lanes] + radial_1[:, lanes]
        tiny[16 * h + 8 : 16 * h + 16, :] = small[:, lanes]
    me = place(1, FOUR)
    few = SMALL // FOUR
    rows = keep.shape[0] // 2
    for j, out in enumerate((out_0, out_1)):
        out[0:rows, :] = total_of([keep, taken], slice(j * rows, (j + 1) * rows))
        out[rows : rows + few, :] = tiny[block_of(lax.bitwise_xor(me, first - j), few), :]
        if out.shape[0] > rows + few:
            out[rows + few :, :] = jnp.zeros((out.shape[0] - rows - few, HALF), F32)


def total_kernel(*refs):
    refs[-1][...] = total_of(refs[:-1], slice(0, refs[-1].shape[0]))


def near_kernel(mine, third, out):
    rows = mine.shape[0] - SMALL // FOUR
    out[0:rows, :] = mine[0:rows, :]
    out[rows : 2 * rows, :] = third[0:rows, :]
    out[2 * rows :, :] = jnp.zeros((out.shape[0] - 2 * rows, HALF), F32)


def rest_kernel(mine, first, second, third, after, out):
    few = SMALL // FOUR
    rows = mine.shape[0] - few
    out[0:rows, :] = second[0:rows, :]
    out[rows : 2 * rows, :] = first[0:rows, :]
    me = place(1, FOUR)
    for k, ref in enumerate((mine, first, second, third)):
        out[block_from(2 * rows + lax.bitwise_xor(me, k) * few, few), :] = ref[rows:, :]


def pair_kernel(near, rest, their_near, their_rest, out):
    piece = (rest.shape[0] - SMALL) // 2
    half = FOUR * piece
    mine, me = place(0, 2), place(1, FOUR)
    for refs, part in (((near, rest), mine), ((their_near, their_rest), 1 - mine)):
        for ref, ks in zip(refs, ((0, 3), (2, 1))):
            for j, k in enumerate(ks):
                at = block_from(part * half + lax.bitwise_xor(me, k) * piece, piece)
                out[at, :] = ref[j * piece : (j + 1) * piece, :]
    out[2 * half :, :] = rest[2 * piece :, :] + their_rest[2 * piece :, :]


def join_kernel(whole, facing, mix, radial, kinds, out):
    rows = mix.shape[0]
    core = lax.axis_index("batch")
    for ref, part in ((whole, core), (facing, 1 - core)):
        mix[:, block_of_lanes(part)] = ref[0:rows, :]
    both = whole[rows:, :] + facing[rows:, :]
    for h in range(2):
        lanes = slice(h * HALF, (h + 1) * HALF)
        few = both[16 * h : 16 * h + 16, :]
        radial[:, lanes] = few[0:BASIS]
        kinds[:, lanes] = few[BASIS : BASIS + SPECIES]
        out[:, lanes] = few[BASIS + SPECIES : BASIS + SPECIES + 1]


def spec(space):
    return pl.BlockSpec(memory_space=space)


def call(kernel, name, outs, scratch, *operands, space=pltpu.VMEM, after=(), flops=0):
    if space is pltpu.HBM:
        operands = [pltpu.with_memory_space_constraint(operand, space) for operand in operands]
    outs = [out if len(out) == 2 and isinstance(out[0], tuple) else (out, F32) for out in outs]
    return pl.pallas_call(
        kernel,
        name=name,
        out_shape=[jax.ShapeDtypeStruct(*out) for out in outs],
        in_specs=[spec(space)] * len(operands) + [spec(pltpu.VMEM)] * len(after),
        out_specs=[spec(pltpu.VMEM)] * len(outs),
        scratch_shapes=[pltpu.VMEM(*item) if isinstance(item, tuple) else item for item in scratch],
        compiler_params=pltpu.CompilerParams(vmem_limit_bytes=28 * 1024 * 1024),
        cost_estimate=pl.CostEstimate(flops=flops, bytes_accessed=1 << 20 if flops else 1 << 10, transcendentals=0),
    )(*operands, *after)


def shifted(block, axis, by):
    count = lax.axis_size(axis)
    return lax.ppermute(block, axis, [(i, (i + by) % count) for i in range(count)])


def exchanged(block, shift, first):
    count, step = lax.axis_size("domain"), 1 << shift
    up = [((i >> shift) & 1 == 0) == first for i in range(count)]
    return lax.ppermute(block, "domain", [(i, (i + step if up[i] else i - step) % count) for i in range(count)])


def partner(block, mask):
    return lax.ppermute(block, "domain", [(i, i ^ mask) for i in range(lax.axis_size("domain"))])


def on_device(
    positions,
    features,
    species,
    ref_forces,
    centre_tile,
    other_tile,
    pair_live,
    send_tiles,
    radial_w,
    mix_w,
    species_w,
    out_w,
):
    atoms_here = positions.shape[2]
    channels = features.shape[2]
    table = (COMPS * TA, BASIS * TA)
    sent = (SEND * TA + GHOST_ROWS, channels)
    slots = PAIRS * TA
    line = (3, 1, atoms_here)
    turning = [((CHUNK, CHUNK), F32)] * 2
    out_row = out_w.reshape(1, channels)
    positions = positions.transpose(1, 0, 2)
    ref_forces = ref_forces.transpose(1, 0, 2)
    ints = [((1, n), jnp.int32) for n in (PAIRS, PAIRS, PAIRS, 2 * SEND)]

    to_second, to_first, token = call(
        gather_kernel,
        "gather",
        [sent, sent, (8, CHUNK)],
        [
            ints[3],
            (line, F32),
            ((1, atoms_here, channels), F32),
            (line, F32),
            pltpu.SemaphoreType.DMA((4,)),
        ],
        send_tiles, positions, features, ref_forces,
        space=pltpu.HBM,
    )
    from_second = exchanged(to_second, 0, False)
    from_first = exchanged(to_first, 0, True)
    flags, atoms, own_feat, weights, spread_w, mh, ml, nh, nl = call(
        stage_kernel,
        "stage",
        [
            (16, CHUNK),
            (8, atoms_here),
            (atoms_here, channels),
            (16, channels),
            (BASIS // 2, channels, CHUNK),
            (mix_w.shape, BF16),
            (mix_w.shape, BF16),
            (mix_w.shape[::-1], BF16),
            (mix_w.shape[::-1], BF16),
        ],
        ints
        + [(line, F32), (line, F32), ((1, atoms_here), jnp.int32)]
        + [(radial_w.shape, F32), (mix_w.shape, F32), (species_w.shape, F32), (out_row.shape, F32)]
        + [((CHUNK, channels), F32), pltpu.SemaphoreType.DMA((12,))],
        centre_tile, other_tile, pair_live, send_tiles, positions, ref_forces, species, features,
        radial_w, mix_w, species_w, out_row,
        space=pltpu.HBM,
        after=(token,),
    )

    long_table = (PAIRS, COMPS * TA, 3 * BASIS * TA)
    env, dinv, gate, curve, inv, rows, fsel, own, *leaving, shape_store, tall, eh, el = call(
        force_kernel,
        "force",
        [
            (PAIRS * COMPS * TA, channels),
            (slots, 3 * channels),
            (slots, channels),
            (slots, channels),
            (slots, 3 * channels),
            (8, CHUNK),
            (slots, channels),
            (8, atoms_here),
            (8, CHUNK),
            (8, CHUNK),
            (8, CHUNK),
            (8, CHUNK),
            (PAIRS, 4 + BASIS, TA, CHUNK),
            ((PAIRS, 3 * BASIS * TA, channels), BF16),
            ((PAIRS, WIDE, channels), BF16),
            ((PAIRS, WIDE, channels), BF16),
        ],
        turning
        + [((3, CHUNK, CHUNK), F32)]
        + [(long_table, BF16), ((PAIRS, 3 * channels, BASIS * TA), BF16)]
        + [((PAIRS, COMPS * TA, 3 * channels), BF16)]
        + [((PAIRS * COMPS * TA, channels), F32), ((PAIRS, *table), F32)],
        flags, atoms, own_feat, weights, spread_w, mh, ml, nh, nl, from_second, from_first,
        flops=1 << 31,
    )
    arriving = [exchanged(leaving[i], i // 2, i % 2 == 0) for i in (1, 3, 0, 2)]

    table_shape, lh, ll, token = call(
        table_kernel,
        "table",
        [
            (PAIRS, 4 + 2 * BASIS, TA, CHUNK),
            ((PAIRS, BASIS * TA, WIDE), BF16),
            ((PAIRS, BASIS * TA, WIDE), BF16),
            (8, CHUNK),
        ],
        turning,
        flags, rows,
        flops=1 << 30,
    )

    rows_mix = 3 * channels
    total_count = 3.0 * atoms_here * lax.axis_size("domain") * lax.axis_size("batch")
    forces, keep, give, small, envdot, curl, both = call(
        functools.partial(tangent_kernel, 2.0 / math.sqrt(total_count)),
        "tangent",
        [
            line,
            (rows_mix, HALF),
            (rows_mix, HALF),
            (8, channels),
            (PAIRS * COMPS * TA, channels),
            (slots, channels),
            (16, CHUNK),
        ],
        turning
        + [(long_table, BF16)]
        + [((PAIRS * COMPS * TA, channels), F32)]
        + [((2 * slots, 3 * channels), F32), ((2 * slots, channels), F32)],
        flags, atoms, weights, mh, ml, from_first, from_second, own, *arriving,
        rows, env, gate, curve, inv, shape_store, tall, token,
        flops=1 << 31,
    )

    def radial(p, after):
        return call(
            functools.partial(radial_kernel, p),
            "radial",
            [(BASIS, channels)],
            turning
            + [((BASIS * TA, CHUNK + WIDE), BF16)] * 2
            + [((2 * WIDE, channels), BF16)] * 2
            + [((BASIS * TA, channels), F32)],
            both, table_shape, lh, ll, eh, el, fsel, env, envdot, dinv, curl, nh, nl, after,
            flops=1 << 31 if p == 0 else 0,
        )[0]

    radials = [radial(0, both)]
    piece = rows_mix // (2 * FOUR)
    few = SMALL // FOUR
    near, far, give_near, give_far = call(
        halve_kernel, "halve", [(2 * piece, HALF)] * 3 + [(2 * piece + PAD, HALF)], [],
        keep, shifted(give, "batch", 1), radials[0],
    )
    radials.append(radial(1, far))
    blocks = []
    after = radials[1]
    taken_near = partner(give_near, 1)
    taken_far = partner(give_far, 1)
    for first, kept, taken in ((3, far, taken_far), (1, near, taken_near)):
        blocks += call(
            functools.partial(spread_kernel, first),
            "spread", [(piece + few + PAD * k, HALF) for k in (first - 1, max(first - 2, 0))], [((SMALL, HALF), F32)],
            kept, taken, *radials, small, after,
        )
        after = blocks[0]
    terms = [blocks[3]] + [partner(blocks[3 - k], 2 * k) for k in range(FOUR - 1, 0, -1)]
    (mine,) = call(total_kernel, "total", [(piece + few, HALF)], [], *terms)
    bit = 2 * FOUR
    while bit < lax.axis_size("domain"):
        (mine,) = call(total_kernel, "total", [(piece + few, HALF)], [], mine, partner(mine, bit))
        bit *= 2
    parts = [mine] + [partner(mine, 2 * k) for k in range(1, FOUR)]
    (near,) = call(near_kernel, "near", [(2 * piece + SMALL + PAD, HALF)], [], mine, parts[3])
    their_near = partner(near, 1)
    (rest,) = call(rest_kernel, "rest", [(2 * piece + SMALL, HALF)], [], *parts, near)
    their_rest = partner(rest, 1)
    (whole,) = call(
        pair_kernel, "pair", [(rows_mix + SMALL, HALF)], [], near, rest, their_near, their_rest
    )
    facing = shifted(whole, "batch", 1)
    mix, radial_sum, kinds, out = call(
        join_kernel,
        "join",
        [(rows_mix, channels), (BASIS, channels), (SPECIES, channels), (1, channels)],
        [],
        whole,
        facing,
    )
    return forces.transpose(1, 0, 2), radial_sum, mix, kinds, out.reshape(channels)


def solution(mesh):
    return jax.shard_map(
        on_device,
        mesh=mesh,
        in_specs=(
            P(("parts", "batch"), None, "domain"),
            P(("parts", "batch"), "domain", None),
            P(("parts", "batch"), "domain"),
            P(("parts", "batch"), None, "domain"),
            P(("parts", "batch"), "domain"),
            P(("parts", "batch"), "domain"),
            P(("parts", "batch"), "domain"),
            P(("parts", "batch"), "domain"),
            P(),
            P(),
            P(),
            P(),
        ),
        out_specs=(
            P(("parts", "batch"), None, "domain"),
            P("parts", None),
            P("parts", None),
            P("parts", None),
            P("parts"),
        ),
        check_vma=False,
    )
```
